32 devices in a mesh: dp: 4 (over y, x), ctx: 2 (over core), head: 4 (over z).
Axes of the slice: x: 2, y: 2, z: 4, core: 2. Of those that a mesh axis runs over, the one named last changes fastest.
Arguments:
- enc_query: bfloat16 [2048, 4096], P(('dp', 'ctx'), 'head'), parts along dimension 0, may hold values from -30 to 30
- enc_key: bfloat16 [2048, 4096], P(('dp', 'ctx'), 'head'), parts along dimension 0, may hold values from -6 to 6
- enc_value: bfloat16 [2048, 4096], P(('dp', 'ctx'), 'head'), parts along dimension 0, may hold values from -6 to 6
- doc_ids: int32 [2048], P(('dp', 'ctx')), parts along dimension 0, may hold values from 0 to 5, never falling along the last dimension, each value on 1 to 256 neighbouring positions
- key_map: bfloat16 [4096, 2048], P('ctx', 'head'), may hold values from -0.09375 to 0.09375
- value_map: bfloat16 [4096, 2048], P('ctx', 'head'), may hold values from -0.09375 to 0.09375
- tgt_query: bfloat16 [512, 2048], P(('dp', 'ctx'), 'head'), parts along dimension 0, may hold values from -150 to 150
Outputs:
- cross_out: bfloat16 [512, 2048], P(('dp', 'ctx'), 'head'), parts along dimension 0
The draws below stay inside these ranges and needn't reach their ends.
There are 4 independent parts, one for each index of `dp`. The reference program is written for one: setup_inputs(seed, part) draws one part's arguments, and reference() takes and returns one part's arrays. A program takes and returns all parts, laid end to end along the dimension named above; an argument that names none is the same for every part. Nothing has to cross between parts.
Inputs may be any that keep to these rules, and one draw needn't show every extreme that they name: `doc_ids`: document ids never fall along the pack; each document holds 1 to 256 consecutive positions and one holds exactly 256.
All inputs are finite; a program needn't handle non-finite values.
Results may differ from the reference program's by a relative error of at most 0.011.
Values may be sent and summed in bfloat16 or wider, within the bound.
No kernel may reach another device: no remote copies, remote signals or barrier semaphores. Data moves between devices by JAX's collectives and lax.ppermute only.
A program may use at most 64 MiB of HBM per device.

```python
import math
import jax
import jax.numpy as jnp
import numpy as np
from jax import lax

HEADS = 16
HEAD_DIM = 256
CROSS_HEADS = 8
TOK_DEV = 256
TGT_DEV = 64
S_IN = 512
S_TG = 128
DOCS = 6
N_CTX = 2


def key_rows(key):
    shape = (S_IN, HEADS * HEAD_DIM)
    return jnp.clip(jax.random.normal(jax.random.fold_in(key, 7), shape, jnp.float32), -6.0, 6.0)


def draw_enc_key(key, part):
    return key_rows(key).astype(jnp.bfloat16)


def draw_enc_query(key, part):
    shape = (S_IN, HEADS * HEAD_DIM)
    fresh = jnp.clip(jax.random.normal(jax.random.fold_in(key, 8), shape, jnp.float32), -6.0, 6.0)
    return fresh.astype(jnp.bfloat16)


def draw_tgt_query(key, part):
    shape = (S_TG, CROSS_HEADS * HEAD_DIM)
    fresh = jnp.clip(jax.random.normal(jax.random.fold_in(key, 11), shape, jnp.float32), -6.0, 6.0)
    return fresh.astype(jnp.bfloat16)


def levels(key, extent, pieces, least, top_value):
    factor_of = 1.0
    for position, blocks in pieces:
        heights = jax.random.uniform(jax.random.fold_in(jax.random.fold_in(key, 6), position), (blocks,), jnp.float32, least / len(pieces), top_value / len(pieces))
        factor_of = factor_of * jnp.repeat(jnp.exp(heights), extent[position] // blocks).reshape((-1,) + (1,) * (len(extent) - 1 - position))
    return factor_of


def length_profile(amount, total, most, skew):
    loads = [(1 << 20) // math.isqrt(grade ** skew) + 1 for grade in range(2, amount + 1)]
    surplus, given = total - most - (amount - 1), [1] * (amount - 1)
    while surplus > 0:
        movable = [i for i in range(amount - 1) if given[i] < most]
        mass, left = sum([loads[i] for i in movable]), surplus
        for i in movable:
            extra = min(most - given[i], max(1, left * loads[i] // mass), surplus)
            given[i] = given[i] + extra
            surplus = surplus - extra
    return np.array([most] + given)


def uneven(stream_key, count, total, limit, lean):
    if count == 2:
        one = jax.random.randint(stream_key, (), max(1, total - limit), min(limit, total - 1) + 1)
        return jnp.stack([one, total - one])
    lengths = jnp.asarray(length_profile(count, total, limit, lean), jnp.int32)
    couples = (count - 1) // 2
    source_of, receiver = lengths[1:1 + 2 * couples:2], lengths[2:2 + 2 * couples:2]
    margin = jnp.minimum(source_of - 1, limit - receiver)
    shifted = jax.random.randint(jax.random.fold_in(stream_key, 1), (couples,), 0, 1 << 20) % (margin + 1)
    lengths = lengths.at[1:1 + 2 * couples:2].set(source_of - shifted).at[2:2 + 2 * couples:2].set(receiver + shifted)
    return lengths[jax.random.permutation(jax.random.fold_in(stream_key, 2), count)]


def centred(stream_key, shape, spread, most, shards=(), kind=jnp.bfloat16):
    level = levels(stream_key, shape, shards, -0.22, 0.18) if shards else 1.0
    result = jax.random.normal(stream_key, shape, jnp.float32) * spread * level
    return jnp.minimum(jnp.maximum(result, -most), most).astype(kind)


def setup_inputs(seed: int = 0, part: int = 0) -> dict:
    seeds = jax.random.split(jax.random.key(seed), 8)
    own_keys = jax.random.split(jax.random.fold_in(seeds[7], part), 8)
    return {
        "enc_query": draw_enc_query(jax.random.fold_in(jax.random.fold_in(seeds[7], part), 71), part),
        "enc_key": draw_enc_key(jax.random.fold_in(jax.random.fold_in(seeds[7], part), 71), part),
        "enc_value": centred(own_keys[2], (S_IN, HEADS * HEAD_DIM), 1.0, 6.0, ((0, 2), (1, 4))),
        "doc_ids": jnp.searchsorted(jnp.cumsum(uneven(own_keys[3], DOCS, S_IN, TOK_DEV, 2)), jnp.arange(S_IN), side="right").astype(jnp.int32),
        "key_map": centred(seeds[4], (HEADS * HEAD_DIM, CROSS_HEADS * HEAD_DIM), (HEADS * HEAD_DIM) ** -0.5, 0.09375, ((0, 2), (1, 4))),
        "value_map": centred(seeds[5], (HEADS * HEAD_DIM, CROSS_HEADS * HEAD_DIM), (HEADS * HEAD_DIM) ** -0.5, 0.09375, ((0, 2), (1, 4))),
        "tgt_query": draw_tgt_query(jax.random.fold_in(jax.random.fold_in(seeds[7], part), 71), part),
    }


NEG_FILL = -1e30


def attend(query, keys, values, query_mark, key_mark):
    scale = HEAD_DIM ** -0.5
    scores = jnp.einsum("rhe,khe->hrk", query.astype(jnp.float32), keys.astype(jnp.float32), precision=lax.Precision.HIGHEST) * scale
    same = query_mark[:, None] == key_mark[None, :]
    scores = jnp.where(same[None], scores, NEG_FILL)
    top = jnp.max(scores, axis=2, keepdims=True)
    weights = jnp.exp(scores - top)
    total = jnp.sum(weights, axis=2)
    rounded = lax.optimization_barrier(weights.astype(jnp.bfloat16)).astype(jnp.float32)
    summed = jnp.einsum("hrk,khe->rhe", rounded, values.astype(jnp.float32), precision=lax.Precision.HIGHEST)
    return summed / jnp.transpose(total)[:, :, None]


def padded_rows(array, fill_value):
    edge = jnp.full((TOK_DEV,) + array.shape[1:], fill_value, array.dtype)
    return jnp.concatenate([edge, array, edge], 0)


def reference(enc_query, enc_key, enc_value, doc_ids, key_map, value_map, tgt_query):
    blocks = N_CTX
    query = enc_query.reshape(blocks, TOK_DEV, HEADS, HEAD_DIM)
    keys = padded_rows(enc_key.reshape(S_IN, HEADS, HEAD_DIM), 0.0)
    values = padded_rows(enc_value.reshape(S_IN, HEADS, HEAD_DIM), 0.0)
    marks = padded_rows(doc_ids, -1)
    query_marks = doc_ids.reshape(blocks, TOK_DEV)

    def encoder_block(index):
        start = (index * TOK_DEV).astype(jnp.int32)
        window_keys = lax.dynamic_slice_in_dim(keys, start, 3 * TOK_DEV, 0)
        window_values = lax.dynamic_slice_in_dim(values, start, 3 * TOK_DEV, 0)
        window_marks = lax.dynamic_slice_in_dim(marks, start, 3 * TOK_DEV, 0)
        return attend(query[index], window_keys, window_values, query_marks[index], window_marks).astype(jnp.bfloat16)

    enc_out = lax.map(encoder_block, jnp.arange(blocks, dtype=jnp.int32)).reshape(S_IN, HEADS * HEAD_DIM)
    memory_key = jnp.dot(enc_out, key_map, preferred_element_type=jnp.float32).astype(jnp.bfloat16)
    memory_value = jnp.dot(enc_out, value_map, preferred_element_type=jnp.float32).astype(jnp.bfloat16)
    memory_keys = padded_rows(memory_key.reshape(S_IN, CROSS_HEADS, HEAD_DIM), 0.0)
    memory_values = padded_rows(memory_value.reshape(S_IN, CROSS_HEADS, HEAD_DIM), 0.0)
    target_doc = doc_ids.reshape(S_TG, 4)[:, 0]
    target_marks = target_doc.reshape(blocks, TGT_DEV)
    target = tgt_query.reshape(blocks, TGT_DEV, CROSS_HEADS, HEAD_DIM)

    def cross_block(index):
        start = (index * TOK_DEV).astype(jnp.int32)
        window_keys = lax.dynamic_slice_in_dim(memory_keys, start, 3 * TOK_DEV, 0)
        window_values = lax.dynamic_slice_in_dim(memory_values, start, 3 * TOK_DEV, 0)
        window_marks = lax.dynamic_slice_in_dim(marks, start, 3 * TOK_DEV, 0)
        return attend(target[index], window_keys, window_values, target_marks[index], window_marks).astype(jnp.bfloat16)

    cross_out = lax.map(cross_block, jnp.arange(blocks, dtype=jnp.int32))
    return cross_out.reshape(S_TG, CROSS_HEADS * HEAD_DIM)
```

```python
import functools

import jax
import jax.numpy as jnp
from jax import lax
from jax.experimental import pallas as pl
from jax.experimental.pallas import tpu as pltpu
from jax.sharding import PartitionSpec as P

HEAD_DIM = 256
NEG_FILL = -1e30
F32 = jnp.float32
BF16 = jnp.bfloat16
STATS = 128


def ring_order(count):
    return list(range(0, count, 2)) + list(range(1, count, 2))[::-1]


def links_of(count):
    if count == 2:
        return [[(0, 1), (1, 0)]]
    return [[(i, i + 1) for i in range(count - 1)], [(i + 1, i) for i in range(count - 1)]]


def dot_t(a, b):
    return lax.dot_general(a, b, (((1,), (1,)), ((), ())), preferred_element_type=F32)


def attend_kernel(blocks, scale, mask_ref, q_ref, *refs):
    keys, values, out_ref = refs[:blocks], refs[blocks : 2 * blocks], refs[-1]
    scores = jnp.concatenate([dot_t(q_ref[...], k[...]) for k in keys], axis=1) * scale
    scores = jnp.where(mask_ref[...] > 0, scores, NEG_FILL)
    weights = jnp.exp(scores - jnp.max(scores, axis=1, keepdims=True))
    total = jnp.sum(weights, axis=1, keepdims=True)
    rounded = weights.astype(BF16)
    summed = jnp.zeros(out_ref.shape, F32)
    width = keys[0].shape[0]
    for i, v in enumerate(values):
        summed += jnp.dot(rounded[:, i * width : (i + 1) * width], v[...], preferred_element_type=F32)
    out_ref[...] = (summed / total).astype(BF16)


def encoder_attend(query, keys, values, mask, first, heads):
    rows = query.shape[0]
    blocks = len(keys)
    block = pl.BlockSpec((rows, HEAD_DIM), lambda h: (0, first + h))
    return pl.pallas_call(
        functools.partial(attend_kernel, blocks, HEAD_DIM**-0.5),
        grid=(heads,),
        in_specs=[pl.BlockSpec(mask.shape, lambda h: (0, 0))] + [block] * (1 + 2 * blocks),
        out_specs=pl.BlockSpec((rows, HEAD_DIM), lambda h: (0, h)),
        out_shape=jax.ShapeDtypeStruct((rows, heads * HEAD_DIM), BF16),
        name="encoder_attend",
    )(mask, query, *keys, *values)


def project_kernel(parts, has_acc, rows_ref, *refs):
    acc_ref, out_ref = (refs[0], refs[-1])
    refs = refs[1:-1] if has_acc else refs[:-1]
    half = out_ref.shape[1] // 2
    for side in range(2):
        columns = slice(side * half, (side + 1) * half)
        total = acc_ref[:, columns] if has_acc else jnp.zeros((out_ref.shape[0], half), F32)
        for i in range(parts):
            total += jnp.dot(refs[3 * i][...], refs[3 * i + 1 + side][...], preferred_element_type=F32)
        out_ref[:, columns] = total


def project(acc, chunks, places, key_full, value_full):
    rows, depth = chunks[0].shape
    width = key_full.shape[1]
    whole = pl.BlockSpec((rows, 2 * width), lambda i, s: (0, 0))
    specs, operands = [], []
    if acc is not None:
        specs.append(whole)
        operands.append(acc)
    for i, chunk in enumerate(chunks):
        piece = pl.BlockSpec((depth, width), lambda g, s, i=i: (s[i], 0))
        specs += [pl.BlockSpec((rows, depth), lambda g, s: (0, 0)), piece, piece]
        operands += [chunk, key_full, value_full]
    return pl.pallas_call(
        functools.partial(project_kernel, len(chunks), acc is not None),
        grid_spec=pltpu.PrefetchScalarGridSpec(
            num_scalar_prefetch=1, grid=(1,), in_specs=specs, out_specs=whole
        ),
        out_shape=jax.ShapeDtypeStruct((rows, 2 * width), F32),
        compiler_params=pltpu.CompilerParams(vmem_limit_bytes=32 << 20),
        name="project",
    )(jnp.stack(places).astype(jnp.int32), *operands)


def cross_kernel(scale, places_ref, acc_ref, e_ref, kmap_ref, vmap_ref, tgt_ref, mask_ref, out_ref):
    width = kmap_ref.shape[1]
    mem_key = (acc_ref[:, :width] + jnp.dot(e_ref[...], kmap_ref[...], preferred_element_type=F32)).astype(BF16)
    mem_value = (acc_ref[:, width:] + jnp.dot(e_ref[...], vmap_ref[...], preferred_element_type=F32)).astype(BF16)
    heads = width // HEAD_DIM
    lane = lax.broadcasted_iota(jnp.int32, (out_ref.shape[0], STATS), 1)
    stats = jnp.zeros((out_ref.shape[0], STATS), F32)
    for h in range(heads):
        columns = slice(h * HEAD_DIM, (h + 1) * HEAD_DIM)
        scores = dot_t(tgt_ref[:, columns], mem_key[:, columns]) * scale
        scores = jnp.where(mask_ref[...] > 0, scores, NEG_FILL)
        top = jnp.max(scores, axis=1, keepdims=True)
        weights = jnp.exp(scores - top)
        total = jnp.sum(weights, axis=1, keepdims=True)
        out_ref[:, columns] = jnp.dot(weights.astype(BF16), mem_value[:, columns], preferred_element_type=F32)
        stats = jnp.where(lane == h, top, jnp.where(lane == heads + h, total, stats))
    out_ref[:, width:] = stats


def cross_attend(acc, chunk, place, key_full, value_full, targets, mask):
    rows, depth = chunk.shape
    width = key_full.shape[1]
    count = targets.shape[0]
    piece = pl.BlockSpec((depth, width), lambda g, s: (s[0], 0))
    whole = lambda shape: pl.BlockSpec(shape, lambda g, s: (0, 0))
    return pl.pallas_call(
        functools.partial(cross_kernel, HEAD_DIM**-0.5),
        grid_spec=pltpu.PrefetchScalarGridSpec(
            num_scalar_prefetch=1,
            grid=(1,),
            in_specs=[whole(acc.shape), whole(chunk.shape), piece, piece, whole(targets.shape), whole(mask.shape)],
            out_specs=whole((count, width + STATS)),
        ),
        out_shape=jax.ShapeDtypeStruct((count, width + STATS), F32),
        compiler_params=pltpu.CompilerParams(vmem_limit_bytes=32 << 20),
        name="cross_attend",
    )(place.reshape(1).astype(jnp.int32), acc, chunk, key_full, value_full, targets, mask)


def combine_kernel(count, valid_ref, *refs):
    parts, out_ref = refs[:-1], refs[-1]
    width = out_ref.shape[1]
    heads = width // HEAD_DIM
    for h in range(heads):
        columns = slice(h * HEAD_DIM, (h + 1) * HEAD_DIM)
        tops = [r[:, width + h : width + h + 1] for r in parts]
        tops = [tops[0]] + [jnp.where(valid_ref[i] > 0, t, NEG_FILL) for i, t in enumerate(tops[1:])]
        top = functools.reduce(jnp.maximum, tops)
        factors = [jnp.exp(t - top) for t in tops]
        total = sum(f * r[:, width + heads + h : width + heads + h + 1] for f, r in zip(factors, parts))
        summed = sum(f * r[:, columns] for f, r in zip(factors, parts))
        out_ref[:, columns] = (summed / total).astype(BF16)


def combine(own, others, valid):
    count, wide = own.shape
    return pl.pallas_call(
        functools.partial(combine_kernel, 1 + len(others)),
        in_specs=[pl.BlockSpec(memory_space=pltpu.SMEM)] + [pl.BlockSpec(memory_space=pltpu.VMEM)] * (1 + len(others)),
        out_specs=pl.BlockSpec(memory_space=pltpu.VMEM),
        out_shape=jax.ShapeDtypeStruct((count, wide - STATS), BF16),
        name="combine",
    )(valid, own, *others)


def on_device(enc_query, enc_key, enc_value, doc_ids, key_map, value_map, tgt_query):
    rows, features = enc_query.shape
    tgt_rows = tgt_query.shape[0]
    n_ctx, n_head = lax.axis_size("ctx"), lax.axis_size("head")
    ctx, head = lax.axis_index("ctx"), lax.axis_index("head")
    links = links_of(n_ctx)
    bring = lambda x, pairs: lax.ppermute(x, "ctx", pairs)

    marks = doc_ids + 1
    all_marks = [marks] + [bring(marks, pairs) for pairs in links]
    keys = [enc_key] + [bring(enc_key, pairs) for pairs in links]
    values = [enc_value] + [bring(enc_value, pairs) for pairs in links]
    targets = jnp.concatenate([tgt_query] + [bring(tgt_query, pairs) for pairs in links], 0)

    mask = (marks[:, None] == jnp.concatenate(all_marks)[None, :]).astype(F32)
    step = rows // tgt_rows
    tgt_marks = jnp.concatenate([m.reshape(tgt_rows, step)[:, 0] for m in all_marks])
    tgt_mask = (tgt_marks[:, None] == marks[None, :]).astype(F32)

    if n_ctx == 2:
        def whole_map(own):
            other = bring(own, links[0])
            low = jnp.where(ctx == 0, own, other)
            high = jnp.where(ctx == 0, other, own)
            return jnp.concatenate([low, high], 0)
    else:
        def whole_map(own):
            return lax.all_gather(own, "ctx", axis=0, tiled=True)
    key_full, value_full = whole_map(key_map), whole_map(value_map)

    chunks = 2
    heads_chunk = features // HEAD_DIM // chunks
    order = ring_order(n_head)
    pairs = [(order[i], order[(i + 1) % n_head]) for i in range(n_head)]
    before = [0] * n_head
    for source, target in pairs:
        before[target] = source
    before = jnp.array(before, jnp.int32)

    held = [encoder_attend(enc_query, keys, values, mask, j * heads_chunk, heads_chunk) for j in range(chunks)]
    owner, acc = head, None
    for turn in range(n_head - 1):
        later = [lax.ppermute(h, "head", pairs) for h in held]
        acc = project(acc, held, [owner * chunks + j for j in range(chunks)], key_full, value_full)
        held, owner = later, before[owner]
    acc = project(acc, held[:-1], [owner * chunks + j for j in range(chunks - 1)], key_full, value_full)
    partial = cross_attend(acc, held[-1], owner * chunks + chunks - 1, key_full, value_full, targets, tgt_mask)

    others, valid = [], []
    for i, pairs in enumerate(links):
        back = [(target, source) for source, target in pairs]
        piece = partial[(i + 1) * tgt_rows : (i + 2) * tgt_rows]
        others.append(bring(piece, back))
        valid.append(1 if n_ctx == 2 else jnp.where(ctx == (n_ctx - 1 if i == 0 else 0), 0, 1))
    valid = jnp.stack([jnp.asarray(v, jnp.int32) for v in valid])
    return combine(partial[:tgt_rows], others, valid)


def solution(mesh):
    in_specs = (
        P(("dp", "ctx"), "head"),
        P(("dp", "ctx"), "head"),
        P(("dp", "ctx"), "head"),
        P(("dp", "ctx")),
        P("ctx", "head"),
        P("ctx", "head"),
        P(("dp", "ctx"), "head"),
    )
    out_specs = P(("dp", "ctx"), "head")
    return jax.shard_map(
        on_device, mesh=mesh, in_specs=in_specs, out_specs=out_specs, check_vma=False
    )
```

```python
import functools

import jax
import jax.numpy as jnp
from jax import lax
from jax.experimental import pallas as pl
from jax.experimental.pallas import tpu as pltpu
from jax.sharding import PartitionSpec as P

HEAD_DIM = 256
NEG_FILL = -1e30
F32 = jnp.float32
BF16 = jnp.bfloat16
STATS = 128
VMEM = pl.BlockSpec(memory_space=pltpu.VMEM)


def links_of(count):
    if count == 2:
        return [[(0, 1), (1, 0)]]
    return [[(i, i + 1) for i in range(count - 1)], [(i + 1, i) for i in range(count - 1)]]


def dot_t(a, b):
    return lax.dot_general(a, b, (((1,), (1,)), ((), ())), preferred_element_type=F32)


def same_mark(row_marks, column_marks):
    down = jnp.transpose(jnp.broadcast_to(row_marks, (STATS, row_marks.shape[1])))
    pieces = [down == column_marks[:, i : i + STATS] for i in range(0, column_marks.shape[1], STATS)]
    return jnp.concatenate(pieces, axis=1)


def attend_kernel(blocks, first, scale, *refs):
    marks, q_ref = refs[:blocks], refs[blocks]
    keys, values = refs[blocks + 1 : 2 * blocks + 1], refs[2 * blocks + 1 : 3 * blocks + 1]
    out_ref = refs[-1]
    own = marks[0][...]
    same = jnp.concatenate([same_mark(own, m[...]) for m in marks], axis=1)
    width = keys[0].shape[0]
    for h in range(out_ref.shape[1] // HEAD_DIM):
        at = slice((first + h) * HEAD_DIM, (first + h + 1) * HEAD_DIM)
        query = q_ref[:, at]
        scores = jnp.concatenate([dot_t(query, k[:, at]) for k in keys], axis=1) * scale
        scores = jnp.where(same, scores, NEG_FILL)
        weights = jnp.exp(scores - jnp.max(scores, axis=1, keepdims=True))
        total = jnp.sum(weights, axis=1, keepdims=True)
        rounded = weights.astype(BF16)
        summed = 0.0
        for i, v in enumerate(values):
            summed += jnp.dot(rounded[:, i * width : (i + 1) * width], v[:, at], preferred_element_type=F32)
        out_ref[:, h * HEAD_DIM : (h + 1) * HEAD_DIM] = (summed / total).astype(BF16)


def encoder_attend(query, keys, values, marks, first, heads):
    rows = query.shape[0]
    operands = [*marks, query, *keys, *values]
    pairs = rows * rows * len(keys) * heads
    return pl.pallas_call(
        functools.partial(attend_kernel, len(keys), first, HEAD_DIM**-0.5),
        in_specs=[VMEM] * len(operands),
        out_specs=VMEM,
        out_shape=jax.ShapeDtypeStruct((rows, heads * HEAD_DIM), BF16),
        compiler_params=pltpu.CompilerParams(vmem_limit_bytes=32 << 20),
        cost_estimate=pl.CostEstimate(
            flops=4 * pairs * HEAD_DIM, bytes_accessed=2 * rows * heads * HEAD_DIM * 6, transcendentals=pairs
        ),
        name="encoder_attend",
    )(*operands)


def project_kernel(parts, has_acc, rows_ref, *refs):
    acc_ref, out_ref = (refs[0], refs[-1])
    refs = refs[1:-1] if has_acc else refs[:-1]
    half = out_ref.shape[1] // 2
    for side in range(2):
        columns = slice(side * half, (side + 1) * half)
        total = acc_ref[:, columns] if has_acc else jnp.zeros((out_ref.shape[0], half), F32)
        for i in range(parts):
            total += jnp.dot(refs[3 * i][...], refs[3 * i + 1 + side][...], preferred_element_type=F32)
        out_ref[:, columns] = total


def project(acc, chunks, places, key_full, value_full):
    rows, depth = chunks[0].shape
    width = key_full.shape[1]
    whole = pl.BlockSpec((rows, 2 * width), lambda i, s: (0, 0))
    specs, operands = [], []
    if acc is not None:
        specs.append(whole)
        operands.append(acc)
    for i, chunk in enumerate(chunks):
        piece = pl.BlockSpec((depth, width), lambda g, s, i=i: (s[i], 0))
        specs += [pl.BlockSpec((rows, depth), lambda g, s: (0, 0)), piece, piece]
        operands += [chunk, key_full, value_full]
    return pl.pallas_call(
        functools.partial(project_kernel, len(chunks), acc is not None),
        grid_spec=pltpu.PrefetchScalarGridSpec(
            num_scalar_prefetch=1, grid=(1,), in_specs=specs, out_specs=whole
        ),
        out_shape=jax.ShapeDtypeStruct((rows, 2 * width), F32),
        compiler_params=pltpu.CompilerParams(vmem_limit_bytes=32 << 20),
        cost_estimate=pl.CostEstimate(
            flops=4 * rows * depth * width * len(chunks),
            bytes_accessed=8 * depth * width * len(chunks),
            transcendentals=0,
        ),
        name="project",
    )(jnp.stack(places).astype(jnp.int32), *operands)


def cross_kernel(scale, places_ref, acc_ref, e_ref, kmap_ref, vmap_ref, *refs):
    parts = len(refs) // 3
    own_ref, targets, marks, outs = refs[0], refs[1 : 1 + parts], refs[1 + parts : 1 + 2 * parts], refs[1 + 2 * parts :]
    width = kmap_ref.shape[1]
    mem_key = (acc_ref[:, :width] + jnp.dot(e_ref[...], kmap_ref[...], preferred_element_type=F32)).astype(BF16)
    mem_value = (acc_ref[:, width:] + jnp.dot(e_ref[...], vmap_ref[...], preferred_element_type=F32)).astype(BF16)
    heads = width // HEAD_DIM
    for tgt_ref, mark_ref, out_ref in zip(targets, marks, outs):
        same = mark_ref[...] == own_ref[...]
        lane = lax.broadcasted_iota(jnp.int32, (out_ref.shape[0], STATS), 1)
        stats = jnp.zeros((out_ref.shape[0], STATS), F32)
        for h in range(heads):
            columns = slice(h * HEAD_DIM, (h + 1) * HEAD_DIM)
            scores = dot_t(tgt_ref[:, columns], mem_key[:, columns]) * scale
            scores = jnp.where(same, scores, NEG_FILL)
            top = jnp.max(scores, axis=1, keepdims=True)
            weights = jnp.exp(scores - top)
            total = jnp.sum(weights, axis=1, keepdims=True)
            out_ref[:, columns] = jnp.dot(weights.astype(BF16), mem_value[:, columns], preferred_element_type=F32)
            stats = jnp.where(lane == h, top, jnp.where(lane == heads + h, total, stats))
        out_ref[:, width:] = stats


def cross_attend(acc, chunk, place, key_full, value_full, own_marks, targets, tgt_marks):
    rows, depth = chunk.shape
    width = key_full.shape[1]
    count = targets[0].shape[0]
    piece = pl.BlockSpec((depth, width), lambda g, s: (s[0], 0))
    whole = lambda x: pl.BlockSpec(x.shape, lambda g, s: (0, 0))
    result = jax.ShapeDtypeStruct((count, width + STATS), F32)
    return pl.pallas_call(
        functools.partial(cross_kernel, HEAD_DIM**-0.5),
        grid_spec=pltpu.PrefetchScalarGridSpec(
            num_scalar_prefetch=1,
            grid=(1,),
            in_specs=[whole(acc), whole(chunk), piece, piece] + [whole(x) for x in [own_marks, *targets, *tgt_marks]],
            out_specs=[whole(result)] * len(targets),
        ),
        out_shape=[result] * len(targets),
        compiler_params=pltpu.CompilerParams(vmem_limit_bytes=32 << 20),
        name="cross_attend",
    )(place.reshape(1).astype(jnp.int32), acc, chunk, key_full, value_full, own_marks, *targets, *tgt_marks)


def combine_kernel(*refs):
    parts, out_ref = refs[:-1], refs[-1]
    width = out_ref.shape[1]
    heads = width // HEAD_DIM
    for h in range(heads):
        columns = slice(h * HEAD_DIM, (h + 1) * HEAD_DIM)
        tops = [r[:, width + h : width + h + 1] for r in parts]
        top = functools.reduce(jnp.maximum, tops)
        factors = [jnp.exp(t - top) for t in tops]
        total = sum(f * r[:, width + heads + h : width + heads + h + 1] for f, r in zip(factors, parts))
        summed = sum(f * r[:, columns] for f, r in zip(factors, parts))
        out_ref[:, columns] = (summed / total).astype(BF16)


def combine(parts):
    count, wide = parts[0].shape
    return pl.pallas_call(
        combine_kernel,
        in_specs=[VMEM] * len(parts),
        out_specs=VMEM,
        out_shape=jax.ShapeDtypeStruct((count, wide - STATS), BF16),
        name="combine",
    )(*parts)


def on_device(enc_query, enc_key, enc_value, doc_ids, key_map, value_map, tgt_query):
    rows, features = enc_query.shape
    tgt_rows = tgt_query.shape[0]
    n_ctx, n_head = lax.axis_size("ctx"), lax.axis_size("head")
    ctx, head = lax.axis_index("ctx"), lax.axis_index("head")
    links = links_of(n_ctx)
    bring = lambda x, pairs: lax.ppermute(x, "ctx", pairs)

    marks = (doc_ids + 1).reshape(1, rows)
    all_marks = [marks] + [bring(marks, pairs) for pairs in links]
    keys = [enc_key] + [bring(enc_key, pairs) for pairs in links]
    values = [enc_value] + [bring(enc_value, pairs) for pairs in links]

    chunks = 2
    heads_chunk = features // HEAD_DIM // chunks
    held = [encoder_attend(enc_query, keys, values, all_marks, j * heads_chunk, heads_chunk) for j in range(chunks)]

    key_map, value_map, tgt_query, _ = lax.optimization_barrier((key_map, value_map, tgt_query, held[-1]))
    targets = [tgt_query] + [bring(tgt_query, pairs) for pairs in links]
    step = rows // tgt_rows
    tgt_marks = [m.reshape(tgt_rows, step)[:, :1] for m in all_marks]
    if n_ctx == 2:
        key_full, value_full = (jnp.concatenate([own, bring(own, links[0])], 0) for own in (key_map, value_map))
    else:
        key_full, value_full = (lax.all_gather(own, "ctx", axis=0, tiled=True) for own in (key_map, value_map))

    def place(owner, chunk):
        block = owner * chunks + chunk
        if n_ctx == 2:
            block = lax.rem(block + ctx * (n_head * chunks // 2), n_head * chunks)
        return block

    ways = [1 if j % 2 == 0 else -1 for j in range(chunks)]
    rings = [[(i, (i + way) % n_head) for i in range(n_head)] for way in ways]
    acc = None
    for turn in range(n_head - 1):
        later = [lax.ppermute(h, "head", ring) for h, ring in zip(held, rings)]
        places = [place(lax.rem(head + n_head - way * turn, n_head), j) for j, way in enumerate(ways)]
        acc = project(acc, held, places, key_full, value_full)
        held = later
    places = [place(lax.rem(head + n_head - way * (n_head - 1), n_head), j) for j, way in enumerate(ways)]
    acc = project(acc, held[:-1], places[:-1], key_full, value_full)
    own, *rest = cross_attend(acc, held[-1], places[-1], key_full, value_full, marks, targets, tgt_marks)

    parts = [own]
    for i, (pairs, piece) in enumerate(zip(links, rest)):
        other = bring(piece, [(target, source) for source, target in pairs])
        if n_ctx > 2:
            last = n_ctx - 1 if i == 0 else 0
            column = lax.broadcasted_iota(jnp.int32, other.shape, 1)
            other = jnp.where((ctx == last) & (column >= tgt_query.shape[1]), NEG_FILL, other)
        parts.append(other)
    return combine(parts)


def solution(mesh):
    in_specs = (
        P(("dp", "ctx"), "head"),
        P(("dp", "ctx"), "head"),
        P(("dp", "ctx"), "head"),
        P(("dp", "ctx")),
        P("ctx", "head"),
        P("ctx", "head"),
        P(("dp", "ctx"), "head"),
    )
    out_specs = P(("dp", "ctx"), "head")
    return jax.shard_map(
        on_device, mesh=mesh, in_specs=in_specs, out_specs=out_specs, check_vma=False
    )
```

```python
import functools

import jax
import jax.numpy as jnp
from jax import lax
from jax.experimental import pallas as pl
from jax.experimental.pallas import tpu as pltpu
from jax.sharding import PartitionSpec as P

HEAD_DIM = 256
NEG_FILL = -1e30
F32 = jnp.float32
BF16 = jnp.bfloat16
LANES = 128
SCALE = HEAD_DIM**-0.5
VMEM = pl.BlockSpec(memory_space=pltpu.VMEM)
HBM = pl.BlockSpec(memory_space=pltpu.HBM)


def ring_order(count):
    return list(range(0, count, 2)) + list(range(1, count, 2))[::-1]


def links_of(count):
    if count == 2:
        return [[(0, 1), (1, 0)]]
    return [[(i, i + 1) for i in range(count - 1)], [(i + 1, i) for i in range(count - 1)]]


def dot_t(a, b):
    return lax.dot_general(a, b, (((1,), (1,)), ((), ())), preferred_element_type=F32)


def dot(a, b):
    return jnp.dot(a, b, preferred_element_type=F32)


def head_columns(h):
    return slice(h * HEAD_DIM, (h + 1) * HEAD_DIM)


def down_lanes(row):
    return jnp.transpose(jnp.broadcast_to(row, (LANES, row.shape[1])))


def same_mark(down, row):
    return jnp.concatenate([down == row[:, i : i + LANES] for i in range(0, row.shape[1], LANES)], axis=1)


def softmax_block(scores, same):
    scores = jnp.where(same, scores * SCALE, NEG_FILL)
    top = jnp.max(scores, axis=1, keepdims=True)
    weights = jnp.exp(scores - top)
    return top, weights, jnp.sum(weights, axis=1, keepdims=True)


def call(kernel, name, outs, operands, flops=0, exps=0, specs=None, scratch=(), limit=8 << 20):
    out_shape = [jax.ShapeDtypeStruct(*o) for o in outs]
    moved = sum(x.size * x.dtype.itemsize for x in [*operands, *out_shape])
    return pl.pallas_call(
        kernel,
        in_specs=specs or [VMEM] * len(operands),
        out_specs=[VMEM] * len(outs),
        out_shape=out_shape,
        scratch_shapes=list(scratch),
        compiler_params=pltpu.CompilerParams(vmem_limit_bytes=limit),
        cost_estimate=pl.CostEstimate(flops=flops, bytes_accessed=moved, transcendentals=exps),
        name=name,
    )(*operands)


def attend_own_kernel(marks_ref, q_hbm, k_hbm, v_hbm, q_ref, sum_ref, stat_ref, k_ref, v_ref, sems):
    heads = q_ref.shape[1] // HEAD_DIM
    copies = []
    for h in range(heads):
        at = head_columns(h)
        for i, (source, target) in enumerate(((q_hbm, q_ref), (k_hbm, k_ref), (v_hbm, v_ref))):
            copies.append(pltpu.make_async_copy(source.at[:, at], target.at[:, at], sems.at[3 * h + i]))
    for copy in copies:
        copy.start()
    marks = marks_ref[...]
    same = same_mark(down_lanes(marks), marks)
    lane = lax.broadcasted_iota(jnp.int32, stat_ref.shape, 1)
    stats = jnp.zeros(stat_ref.shape, F32)
    for h in range(heads):
        at = head_columns(h)
        copies[3 * h].wait()
        copies[3 * h + 1].wait()
        top, weights, total = softmax_block(dot_t(q_ref[:, at], k_ref[:, at]), same)
        copies[3 * h + 2].wait()
        sum_ref[:, at] = dot(weights.astype(BF16), v_ref[:, at])
        stats = jnp.where(lane == h, top, jnp.where(lane == heads + h, total, stats))
    stat_ref[...] = stats


def attend_near_kernel(near, *refs):
    marks, (q_ref, sum_ref, stat_ref) = refs[: near + 1], refs[near + 1 : near + 4]
    keys, values = refs[near + 4 : 2 * near + 4], refs[2 * near + 4 : 3 * near + 4]
    outs = refs[3 * near + 4 :]
    heads = q_ref.shape[1] // HEAD_DIM
    down = down_lanes(marks[0][...])
    same = jnp.concatenate([same_mark(down, m[...]) for m in marks[1:]], axis=1)
    rows = q_ref.shape[0]
    each = heads // len(outs)
    for h in range(heads):
        at = head_columns(h)
        scores = jnp.concatenate([dot_t(q_ref[:, at], k[:, at]) for k in keys], axis=1)
        scores = jnp.where(same, scores * SCALE, NEG_FILL)
        own_top, own_total = stat_ref[:, h : h + 1], stat_ref[:, heads + h : heads + h + 1]
        top = jnp.maximum(jnp.max(scores, axis=1, keepdims=True), own_top)
        weights = jnp.exp(scores - top)
        factor = jnp.exp(own_top - top)
        total = factor * own_total + jnp.sum(weights, axis=1, keepdims=True)
        rounded = weights.astype(BF16)
        summed = factor * sum_ref[:, at]
        for i, v in enumerate(values):
            summed += dot(rounded[:, i * rows : (i + 1) * rows], v[:, at])
        outs[h // each][:, head_columns(h % each)] = (summed / total).astype(BF16)


def encoder_attend(query, key, value, marks, keys, values, near_marks, chunks):
    rows, width = query.shape
    heads = width // HEAD_DIM
    pairs = rows * rows * heads
    copied, summed, stats = call(
        attend_own_kernel,
        "attend_own",
        [((rows, width), BF16), ((rows, width), F32), ((rows, LANES), F32)],
        [marks, *(pltpu.with_memory_space_constraint(x, pltpu.HBM) for x in (query, key, value))],
        flops=4 * pairs * HEAD_DIM,
        exps=pairs,
        specs=[VMEM, HBM, HBM, HBM],
        scratch=[pltpu.VMEM((rows, width), BF16)] * 2 + [pltpu.SemaphoreType.DMA((3 * heads,))],
    )
    return call(
        functools.partial(attend_near_kernel, len(keys)),
        "attend_near",
        [((rows, width // chunks), BF16)] * chunks,
        [marks, *near_marks, copied, summed, stats, *keys, *values],
        flops=4 * pairs * HEAD_DIM * len(keys),
        exps=pairs * len(keys),
    )


def target_mask_kernel(step, own_ref, *refs):
    marks, out_ref, down_ref = refs[:-2], refs[-2], refs[-1]
    own = own_ref[...]
    count = out_ref.shape[0] // len(marks)
    for i, mark_ref in enumerate(marks):
        down_ref[...] = down_lanes(mark_ref[...])
        down = down_ref[pl.ds(0, count, stride=step), :]
        out_ref[i * count : (i + 1) * count, :] = same_mark(down, own).astype(F32)


def target_mask(marks, all_marks, tgt_rows):
    rows = marks.shape[1]
    return call(
        functools.partial(target_mask_kernel, rows // tgt_rows),
        "target_mask",
        [((tgt_rows * len(all_marks), rows), F32)],
        [marks, *all_marks],
        scratch=[pltpu.VMEM((rows, LANES), jnp.int32)],
    )[0]


def add_products(acc_of, store, e_ref, place, key_shards, value_shards):
    shard, block = place
    depth = e_ref.shape[1]
    at = pl.ds(pl.multiple_of(block * depth, depth), depth)

    def add(i):
        for side, shards in enumerate((key_shards, value_shards)):
            store(side, acc_of(side) + dot(e_ref[...], shards[i][at, :]))

    if len(key_shards) == 1:
        add(0)
    else:
        for i in range(len(key_shards)):
            pl.when(shard == i)(functools.partial(add, i))


def project_kernel(chunks, shards, has_acc, places, *refs):
    out_ref = refs[-1]
    e_refs, maps = refs[:chunks], refs[chunks : chunks + 2 * shards]
    half = out_ref.shape[1] // 2
    side_of = lambda side: slice(side * half, (side + 1) * half)

    def store(side, value):
        out_ref[:, side_of(side)] = value

    for i, (e_ref, place) in enumerate(zip(e_refs, places())):
        if i:
            acc_of = lambda side: out_ref[:, side_of(side)]
        elif has_acc:
            acc_of = lambda side: refs[-2][:, side_of(side)]
        else:
            acc_of = lambda side: 0.0
        add_products(acc_of, store, e_ref, place, maps[:shards], maps[shards:])


def project(acc, chunks, places, key_shards, value_shards):
    rows, depth = chunks[0].shape
    width = key_shards[0].shape[1]
    operands = [*chunks, *key_shards, *value_shards] + ([] if acc is None else [acc])
    return call(
        functools.partial(project_kernel, len(chunks), len(key_shards), acc is not None, places),
        "project",
        [((rows, 2 * width), F32)],
        operands,
        flops=4 * rows * depth * width * len(chunks),
    )[0]


def cross_kernel(shards, places, e_ref, *refs):
    maps, (acc_ref, tgt_ref, mask_ref) = refs[: 2 * shards], refs[2 * shards : 2 * shards + 3]
    outs, mem_ref = refs[2 * shards + 3 : -1], refs[-1]
    half = mem_ref.shape[1] // 2
    side_of = lambda side: slice(side * half, (side + 1) * half)

    def store(side, value):
        mem_ref[:, side_of(side)] = value.astype(BF16)

    (place,) = places()
    add_products(lambda side: acc_ref[:, side_of(side)], store, e_ref, place, maps[:shards], maps[shards:])
    heads = half // HEAD_DIM
    count = outs[0].shape[0]
    lane = lax.broadcasted_iota(jnp.int32, (tgt_ref.shape[0], LANES), 1)
    stats = jnp.zeros(lane.shape, F32)
    same = mask_ref[...] > 0
    for h in range(heads):
        at = head_columns(h)
        top, weights, total = softmax_block(dot_t(tgt_ref[:, at], mem_ref[:, at]), same)
        summed = dot(weights.astype(BF16), mem_ref[:, head_columns(heads + h)])
        for i, out_ref in enumerate(outs):
            out_ref[:, at] = summed[i * count : (i + 1) * count]
        stats = jnp.where(lane == h, top, jnp.where(lane == heads + h, total, stats))
    for i, out_ref in enumerate(outs):
        out_ref[:, half:] = stats[i * count : (i + 1) * count]


def cross_attend(acc, chunk, places, key_shards, value_shards, targets, mask, parts):
    rows, depth = chunk.shape
    width = key_shards[0].shape[1]
    count = targets.shape[0] // parts
    return call(
        functools.partial(cross_kernel, len(key_shards), places),
        "cross_attend",
        [((count, width + LANES), F32)] * parts,
        [chunk, *key_shards, *value_shards, acc, targets, mask],
        flops=4 * rows * depth * width,
        scratch=[pltpu.VMEM((rows, 2 * width), BF16)],
    )


def combine_kernel(*refs):
    parts, out_ref = refs[:-1], refs[-1]
    width = out_ref.shape[1]
    heads = width // HEAD_DIM
    for h in range(heads):
        at = head_columns(h)
        tops = [r[:, width + h : width + h + 1] for r in parts]
        top = functools.reduce(jnp.maximum, tops)
        factors = [jnp.exp(t - top) for t in tops]
        total = sum(f * r[:, width + heads + h : width + heads + h + 1] for f, r in zip(factors, parts))
        summed = sum(f * r[:, at] for f, r in zip(factors, parts))
        out_ref[:, at] = (summed / total).astype(BF16)


def on_device(enc_query, enc_key, enc_value, doc_ids, key_map, value_map, tgt_query):
    rows, features = enc_query.shape
    tgt_rows, width = tgt_query.shape
    n_ctx, n_head = lax.axis_size("ctx"), lax.axis_size("head")
    links = links_of(n_ctx)
    bring = lambda x: [lax.ppermute(x, "ctx", pairs) for pairs in links]

    marks = (doc_ids if n_ctx == 2 else doc_ids + 1).reshape(1, rows)
    keys, values, near_marks = bring(enc_key), bring(enc_value), bring(marks)
    chunks = 2
    held = encoder_attend(enc_query, enc_key, enc_value, marks, keys, values, near_marks, chunks)

    key_map, value_map, tgt_query, *held = lax.optimization_barrier((key_map, value_map, tgt_query, *held))
    targets = jnp.concatenate([tgt_query, *bring(tgt_query)], 0)
    mask = target_mask(marks, [marks, *near_marks], tgt_rows)
    if n_ctx == 2:
        key_shards, value_shards = [key_map, *bring(key_map)], [value_map, *bring(value_map)]
    else:
        key_shards, value_shards = ([lax.all_gather(x, "ctx", axis=0, tiled=True)] for x in (key_map, value_map))
    shard_blocks = n_head * chunks // len(key_shards)

    order = ring_order(n_head)
    ring = [(order[i], order[(i + 1) % n_head]) for i in range(n_head)]
    before = {target: source for source, target in ring}

    def places(turn, which):
        head, ctx = lax.axis_index("head"), lax.axis_index("ctx")
        owner = 0
        for i in range(n_head):
            source = i
            for _ in range(turn):
                source = before[source]
            owner = owner + jnp.where(head == i, source, 0)
        found = []
        for j in which:
            block = owner * chunks + j
            shard = jnp.where(lax.div(block, shard_blocks) == ctx, 0, 1) if len(key_shards) == 2 else None
            found.append((shard, lax.rem(block, shard_blocks)))
        return found

    acc, every = None, tuple(range(chunks))
    for turn in range(n_head - 1):
        later = [lax.ppermute(h, "head", ring) for h in held]
        acc = project(acc, held, functools.partial(places, turn, every), key_shards, value_shards)
        held = later
    last = n_head - 1
    acc = project(acc, held[:-1], functools.partial(places, last, every[:-1]), key_shards, value_shards)
    parts = cross_attend(
        acc, held[-1], functools.partial(places, last, every[-1:]), key_shards, value_shards, targets, mask, 1 + len(links)
    )

    combined = [parts[0]]
    for i, (pairs, piece) in enumerate(zip(links, parts[1:])):
        other = lax.ppermute(piece, "ctx", [(target, source) for source, target in pairs])
        if n_ctx > 2:
            end = n_ctx - 1 if i == 0 else 0
            column = lax.broadcasted_iota(jnp.int32, other.shape, 1)
            other = jnp.where((lax.axis_index("ctx") == end) & (column >= width), NEG_FILL, other)
        combined.append(other)
    return call(combine_kernel, "combine", [((tgt_rows, width), BF16)], combined, limit=4 << 20)[0]


def solution(mesh):
    in_specs = (
        P(("dp", "ctx"), "head"),
        P(("dp", "ctx"), "head"),
        P(("dp", "ctx"), "head"),
        P(("dp", "ctx")),
        P("ctx", "head"),
        P("ctx", "head"),
        P(("dp", "ctx"), "head"),
    )
    out_specs = P(("dp", "ctx"), "head")
    return jax.shard_map(
        on_device, mesh=mesh, in_specs=in_specs, out_specs=out_specs, check_vma=False
    )
```

```python
import functools

import jax
import jax.numpy as jnp
from jax import lax
from jax.experimental import pallas as pl
from jax.experimental.pallas import tpu as pltpu
from jax.sharding import PartitionSpec as P

HEAD_DIM = 256
NEG_FILL = -1e30
F32 = jnp.float32
BF16 = jnp.bfloat16
LANES = 128
SCALE = HEAD_DIM**-0.5
VMEM = pl.BlockSpec(memory_space=pltpu.VMEM)
HBM = pl.BlockSpec(memory_space=pltpu.HBM)


def ring_order(count):
    return list(range(0, count, 2)) + list(range(1, count, 2))[::-1]


def links_of(count):
    if count == 2:
        return [[(0, 1), (1, 0)]]
    return [[(i, i + 1) for i in range(count - 1)], [(i + 1, i) for i in range(count - 1)]]


def dot_t(a, b):
    return lax.dot_general(a, b, (((1,), (1,)), ((), ())), preferred_element_type=F32)


def dot(a, b):
    return jnp.dot(a, b, preferred_element_type=F32)


def head_columns(h):
    return slice(h * HEAD_DIM, (h + 1) * HEAD_DIM)


def down_lanes(row):
    return jnp.transpose(jnp.broadcast_to(row, (LANES, row.shape[1])))


def same_mark(down, row):
    return jnp.concatenate([down == row[:, i : i + LANES] for i in range(0, row.shape[1], LANES)], axis=1)


def softmax_block(scores, same):
    scores = jnp.where(same, scores * SCALE, NEG_FILL)
    top = jnp.max(scores, axis=1, keepdims=True)
    weights = jnp.exp(scores - top)
    return top, weights, jnp.sum(weights, axis=1, keepdims=True)


def call(kernel, name, outs, operands, flops=0, exps=0, specs=None, scratch=(), limit=8 << 20):
    out_shape = [jax.ShapeDtypeStruct(*o) for o in outs]
    moved = sum(x.size * x.dtype.itemsize for x in [*operands, *out_shape])
    return pl.pallas_call(
        kernel,
        in_specs=specs or [VMEM] * len(operands),
        out_specs=[VMEM] * len(outs),
        out_shape=out_shape,
        scratch_shapes=list(scratch),
        compiler_params=pltpu.CompilerParams(vmem_limit_bytes=limit),
        cost_estimate=pl.CostEstimate(flops=flops, bytes_accessed=moved, transcendentals=exps),
        name=name,
    )(*operands)


def fetch_kernel(count, *refs):
    sources, targets, sems = refs[:count], refs[count : 2 * count], refs[-1]
    copies = [pltpu.make_async_copy(s, t, sems.at[i]) for i, (s, t) in enumerate(zip(sources, targets))]
    for copy in copies:
        copy.start()
    for copy in copies:
        copy.wait()


def fetch(*arrays):
    return call(
        functools.partial(fetch_kernel, len(arrays)),
        "fetch",
        [(x.shape, x.dtype) for x in arrays],
        [pltpu.with_memory_space_constraint(x, pltpu.HBM) for x in arrays],
        specs=[HBM] * len(arrays),
        scratch=[pltpu.SemaphoreType.DMA((len(arrays),))],
    )


def attend_kernel(blocks, *refs):
    marks, q_ref = refs[:blocks], refs[blocks]
    keys, values = refs[blocks + 1 : 2 * blocks + 1], refs[2 * blocks + 1 : 3 * blocks + 1]
    outs = refs[3 * blocks + 1 :]
    down = down_lanes(marks[0][...])
    same = jnp.concatenate([same_mark(down, m[...]) for m in marks], axis=1)
    rows = q_ref.shape[0]
    heads = q_ref.shape[1] // HEAD_DIM
    each = heads // len(outs)
    for h in range(heads):
        at = head_columns(h)
        scores = jnp.concatenate([dot_t(q_ref[:, at], k[:, at]) for k in keys], axis=1)
        _, weights, total = softmax_block(scores, same)
        rounded = weights.astype(BF16)
        summed = sum(dot(rounded[:, i * rows : (i + 1) * rows], v[:, at]) for i, v in enumerate(values))
        outs[h // each][:, head_columns(h % each)] = (summed / total).astype(BF16)


def encoder_attend(query, keys, values, marks, chunks):
    rows, width = query.shape
    pairs = rows * rows * len(keys) * (width // HEAD_DIM)
    return list(
        call(
            functools.partial(attend_kernel, len(keys)),
            "encoder_attend",
            [((rows, width // chunks), BF16)] * chunks,
            [*marks, query, *keys, *values],
            flops=4 * pairs * HEAD_DIM,
            exps=pairs,
        )
    )


def target_mask_kernel(step, own_ref, *refs):
    marks, out_ref, down_ref = refs[:-2], refs[-2], refs[-1]
    own = own_ref[...]
    count = out_ref.shape[0] // len(marks)
    for i, mark_ref in enumerate(marks):
        down_ref[...] = down_lanes(mark_ref[...])
        down = down_ref[pl.ds(0, count, stride=step), :]
        out_ref[i * count : (i + 1) * count, :] = same_mark(down, own).astype(F32)


def target_mask(marks, all_marks, tgt_rows):
    rows = marks.shape[1]
    return call(
        functools.partial(target_mask_kernel, rows // tgt_rows),
        "target_mask",
        [((tgt_rows * len(all_marks), rows), F32)],
        [marks, *all_marks],
        scratch=[pltpu.VMEM((rows, LANES), jnp.int32)],
    )[0]


def add_products(acc_of, store, e_refs, place, key_shards, value_shards):
    shard, row = place
    depth = e_refs[0].shape[1]
    at = pl.ds(pl.multiple_of(row, depth), depth * len(e_refs))
    chunks = jnp.concatenate([r[...] for r in e_refs], axis=1)

    def add(i):
        for side, shards in enumerate((key_shards, value_shards)):
            store(side, acc_of(side) + dot(chunks, shards[i][at, :]))

    if len(key_shards) == 1:
        add(0)
    else:
        for i in range(len(key_shards)):
            pl.when(shard == i)(functools.partial(add, i))


def project_kernel(chunks, shards, has_acc, place, *refs):
    out_ref = refs[-1]
    e_refs, maps = refs[:chunks], refs[chunks : chunks + 2 * shards]
    half = out_ref.shape[1] // 2
    side_of = lambda side: slice(side * half, (side + 1) * half)

    def store(side, value):
        out_ref[:, side_of(side)] = value

    acc_of = lambda side: refs[-2][:, side_of(side)] if has_acc else 0.0
    add_products(acc_of, store, e_refs, place(), maps[:shards], maps[shards:])


def project(acc, chunks, place, key_shards, value_shards):
    rows, depth = chunks[0].shape
    width = key_shards[0].shape[1]
    operands = [*chunks, *key_shards, *value_shards] + ([] if acc is None else [acc])
    return call(
        functools.partial(project_kernel, len(chunks), len(key_shards), acc is not None, place),
        "project",
        [((rows, 2 * width), F32)],
        operands,
        flops=4 * rows * depth * width * len(chunks),
    )[0]


def cross_kernel(shards, place, e_ref, *refs):
    maps, (acc_ref, tgt_ref, mask_ref) = refs[: 2 * shards], refs[2 * shards : 2 * shards + 3]
    outs, mem_ref = refs[2 * shards + 3 : -1], refs[-1]
    half = mem_ref.shape[1] // 2
    side_of = lambda side: slice(side * half, (side + 1) * half)

    def store(side, value):
        mem_ref[:, side_of(side)] = value.astype(BF16)

    add_products(lambda side: acc_ref[:, side_of(side)], store, [e_ref], place(), maps[:shards], maps[shards:])
    heads = half // HEAD_DIM
    count = outs[0].shape[0]
    lane = lax.broadcasted_iota(jnp.int32, (tgt_ref.shape[0], LANES), 1)
    stats = jnp.zeros(lane.shape, F32)
    same = mask_ref[...] > 0
    for h in range(heads):
        at = head_columns(h)
        top, weights, total = softmax_block(dot_t(tgt_ref[:, at], mem_ref[:, at]), same)
        summed = dot(weights.astype(BF16), mem_ref[:, head_columns(heads + h)])
        for i, out_ref in enumerate(outs):
            out_ref[:, at] = summed[i * count : (i + 1) * count]
        stats = jnp.where(lane == h, top, jnp.where(lane == heads + h, total, stats))
    for i, out_ref in enumerate(outs):
        out_ref[:, half:] = stats[i * count : (i + 1) * count]


def cross_attend(acc, chunk, place, key_shards, value_shards, targets, mask, parts):
    rows, depth = chunk.shape
    width = key_shards[0].shape[1]
    count = targets.shape[0] // parts
    return call(
        functools.partial(cross_kernel, len(key_shards), place),
        "cross_attend",
        [((count, width + LANES), F32)] * parts,
        [chunk, *key_shards, *value_shards, acc, targets, mask],
        flops=4 * rows * depth * width,
        scratch=[pltpu.VMEM((rows, 2 * width), BF16)],
    )


def combine_kernel(*refs):
    parts, out_ref = refs[:-1], refs[-1]
    width = out_ref.shape[1]
    heads = width // HEAD_DIM
    for h in range(heads):
        at = head_columns(h)
        tops = [r[:, width + h : width + h + 1] for r in parts]
        top = functools.reduce(jnp.maximum, tops)
        factors = [jnp.exp(t - top) for t in tops]
        total = sum(f * r[:, width + heads + h : width + heads + h + 1] for f, r in zip(factors, parts))
        summed = sum(f * r[:, at] for f, r in zip(factors, parts))
        out_ref[:, at] = (summed / total).astype(BF16)


def on_device(enc_query, enc_key, enc_value, doc_ids, key_map, value_map, tgt_query):
    rows, features = enc_query.shape
    tgt_rows, width = tgt_query.shape
    n_ctx, n_head = lax.axis_size("ctx"), lax.axis_size("head")
    links = links_of(n_ctx)
    bring = lambda x: [lax.ppermute(x, "ctx", pairs) for pairs in links]

    marks = (doc_ids if n_ctx == 2 else doc_ids + 1).reshape(1, rows)
    keys, values, near_marks = bring(enc_key), bring(enc_value), bring(marks)
    query, own_key, own_value, marks = fetch(enc_query, enc_key, enc_value, marks)
    chunks = 2
    held = encoder_attend(query, [own_key, *keys], [own_value, *values], [marks, *near_marks], chunks)

    key_map, value_map, tgt_query, *_ = lax.optimization_barrier(
        (key_map, value_map, tgt_query, *keys, *values, *near_marks, query)
    )
    near_targets = bring(tgt_query)
    if n_ctx == 2:
        key_shards, value_shards = [key_map, *bring(key_map)], [value_map, *bring(value_map)]
    else:
        key_shards, value_shards = ([lax.all_gather(x, "ctx", axis=0, tiled=True)] for x in (key_map, value_map))
    targets = jnp.concatenate([tgt_query, *near_targets], 0)
    mask = target_mask(marks, [marks, *near_marks], tgt_rows)

    order = ring_order(n_head)
    ring = [(order[i], order[(i + 1) % n_head]) for i in range(n_head)]
    before = {target: source for source, target in ring}

    def place(turn, first):
        head, ctx = lax.axis_index("head"), lax.axis_index("ctx")
        owner = 0
        for i in range(n_head):
            source = i
            for _ in range(turn):
                source = before[source]
            owner = owner + jnp.where(head == i, source, 0)
        row = owner * features + first
        if len(key_shards) == 1:
            return None, row
        shard_rows = n_head * features // 2
        return jnp.where(lax.div(row, shard_rows) == ctx, 0, 1), lax.rem(row, shard_rows)

    acc, last = None, n_head - 1
    for turn in range(last):
        if turn == last - 1:
            pieces = [p for h in held for p in jnp.split(h, 2, axis=1)]
        else:
            pieces = held
        later = [lax.ppermute(p, "head", ring) for p in pieces]
        acc = project(acc, held, functools.partial(place, turn, 0), key_shards, value_shards)
        held = later
    acc = project(acc, held[:-1], functools.partial(place, last, 0), key_shards, value_shards)
    first = features - held[-1].shape[1]
    parts = cross_attend(
        acc, held[-1], functools.partial(place, last, first), key_shards, value_shards, targets, mask, 1 + len(links)
    )

    combined = [parts[0]]
    for i, (pairs, piece) in enumerate(zip(links, parts[1:])):
        other = lax.ppermute(piece, "ctx", [(target, source) for source, target in pairs])
        if n_ctx > 2:
            end = n_ctx - 1 if i == 0 else 0
            column = lax.broadcasted_iota(jnp.int32, other.shape, 1)
            other = jnp.where((lax.axis_index("ctx") == end) & (column >= width), NEG_FILL, other)
        combined.append(other)
    return call(combine_kernel, "combine", [((tgt_rows, width), BF16)], combined, limit=4 << 20)[0]


def solution(mesh):
    in_specs = (
        P(("dp", "ctx"), "head"),
        P(("dp", "ctx"), "head"),
        P(("dp", "ctx"), "head"),
        P(("dp", "ctx")),
        P("ctx", "head"),
        P("ctx", "head"),
        P(("dp", "ctx"), "head"),
    )
    out_specs = P(("dp", "ctx"), "head")
    return jax.shard_map(
        on_device, mesh=mesh, in_specs=in_specs, out_specs=out_specs, check_vma=False
    )
```

```python
import functools

import jax
import jax.numpy as jnp
from jax import lax
from jax.experimental import pallas as pl
from jax.experimental.pallas import tpu as pltpu
from jax.sharding import PartitionSpec as P

HEAD_DIM = 256
NEG_FILL = -1e30
F32 = jnp.float32
BF16 = jnp.bfloat16
LANES = 128
SCALE = HEAD_DIM**-0.5
VMEM = pl.BlockSpec(memory_space=pltpu.VMEM)
HBM = pl.BlockSpec(memory_space=pltpu.HBM)


def ring_order(count):
    return list(range(0, count, 2)) + list(range(1, count, 2))[::-1]


def links_of(count):
    if count == 2:
        return [[(0, 1), (1, 0)]]
    return [[(i, i + 1) for i in range(count - 1)], [(i + 1, i) for i in range(count - 1)]]


def dot_t(a, b):
    return lax.dot_general(a, b, (((1,), (1,)), ((), ())), preferred_element_type=F32)


def dot(a, b):
    return jnp.dot(a, b, preferred_element_type=F32)


def head_columns(h):
    return slice(h * HEAD_DIM, (h + 1) * HEAD_DIM)


def down_lanes(row):
    return jnp.transpose(jnp.broadcast_to(row, (LANES, row.shape[1])))


def same_mark(down, row):
    return jnp.concatenate([down == row[:, i : i + LANES] for i in range(0, row.shape[1], LANES)], axis=1)


def softmax_block(scores, same):
    scores = jnp.where(same, scores * SCALE, NEG_FILL)
    top = jnp.max(scores, axis=1, keepdims=True)
    weights = jnp.exp(scores - top)
    return top, weights, jnp.sum(weights, axis=1, keepdims=True)


def call(kernel, name, outs, operands, flops=0, exps=0, specs=None, scratch=(), limit=8 << 20):
    out_shape = [jax.ShapeDtypeStruct(*o) for o in outs]
    moved = sum(x.size * x.dtype.itemsize for x in [*operands, *out_shape])
    return pl.pallas_call(
        kernel,
        in_specs=specs or [VMEM] * len(operands),
        out_specs=[VMEM] * len(outs),
        out_shape=out_shape,
        scratch_shapes=list(scratch),
        compiler_params=pltpu.CompilerParams(vmem_limit_bytes=limit),
        cost_estimate=pl.CostEstimate(flops=flops, bytes_accessed=moved, transcendentals=exps),
        name=name,
    )(*operands)


def fetch_kernel(count, *refs):
    sources, targets, sems = refs[:count], refs[count : 2 * count], refs[-1]
    copies = [pltpu.make_async_copy(s, t, sems.at[i]) for i, (s, t) in enumerate(zip(sources, targets))]
    for copy in copies:
        copy.start()
    for copy in copies:
        copy.wait()


def fetch(*arrays):
    return call(
        functools.partial(fetch_kernel, len(arrays)),
        "fetch",
        [(x.shape, x.dtype) for x in arrays],
        [pltpu.with_memory_space_constraint(x, pltpu.HBM) for x in arrays],
        specs=[HBM] * len(arrays),
        scratch=[pltpu.SemaphoreType.DMA((len(arrays),))],
    )


def attend_kernel(blocks, first, *refs):
    marks, q_ref = refs[:blocks], refs[blocks]
    keys, values = refs[blocks + 1 : 2 * blocks + 1], refs[2 * blocks + 1 : 3 * blocks + 1]
    out_ref = refs[-1]
    down = down_lanes(marks[0][...])
    same = jnp.concatenate([same_mark(down, m[...]) for m in marks], axis=1)
    rows = q_ref.shape[0]
    for h in range(out_ref.shape[1] // HEAD_DIM):
        at = head_columns(first + h)
        scores = jnp.concatenate([dot_t(q_ref[:, at], k[:, at]) for k in keys], axis=1)
        _, weights, total = softmax_block(scores, same)
        rounded = weights.astype(BF16)
        summed = sum(dot(rounded[:, i * rows : (i + 1) * rows], v[:, at]) for i, v in enumerate(values))
        out_ref[:, head_columns(h)] = (summed / total).astype(BF16)


def encoder_attend(query, keys, values, marks, first, heads):
    rows = query.shape[0]
    pairs = rows * rows * len(keys) * heads
    return call(
        functools.partial(attend_kernel, len(keys), first),
        "encoder_attend",
        [((rows, heads * HEAD_DIM), BF16)],
        [*marks, query, *keys, *values],
        flops=4 * pairs * HEAD_DIM,
        exps=pairs,
    )[0]


def target_mask_kernel(step, own_ref, *refs):
    marks, out_ref, down_ref = refs[:-2], refs[-2], refs[-1]
    own = own_ref[...]
    count = out_ref.shape[0] // len(marks)
    for i, mark_ref in enumerate(marks):
        down_ref[...] = down_lanes(mark_ref[...])
        down = down_ref[pl.ds(0, count, stride=step), :]
        out_ref[i * count : (i + 1) * count, :] = same_mark(down, own).astype(F32)


def target_mask(marks, all_marks, tgt_rows):
    rows = marks.shape[1]
    return call(
        functools.partial(target_mask_kernel, rows // tgt_rows),
        "target_mask",
        [((tgt_rows * len(all_marks), rows), F32)],
        [marks, *all_marks],
        scratch=[pltpu.VMEM((rows, LANES), jnp.int32)],
    )[0]


def add_products(acc_of, store, e_refs, place, key_shards, value_shards):
    shard, row = place
    depth = e_refs[0].shape[1]
    at = pl.ds(pl.multiple_of(row, depth), depth * len(e_refs))
    chunks = jnp.concatenate([r[...] for r in e_refs], axis=1)

    def add(i):
        for side, shards in enumerate((key_shards, value_shards)):
            store(side, acc_of(side) + dot(chunks, shards[i][at, :]))

    if len(key_shards) == 1:
        add(0)
    else:
        for i in range(len(key_shards)):
            pl.when(shard == i)(functools.partial(add, i))


def project_kernel(chunks, shards, has_acc, place, *refs):
    out_ref = refs[-1]
    e_refs, maps = refs[:chunks], refs[chunks : chunks + 2 * shards]
    half = out_ref.shape[1] // 2
    side_of = lambda side: slice(side * half, (side + 1) * half)

    def store(side, value):
        out_ref[:, side_of(side)] = value

    acc_of = lambda side: refs[-2][:, side_of(side)] if has_acc else 0.0
    add_products(acc_of, store, e_refs, place(), maps[:shards], maps[shards:])


def project(acc, chunks, place, key_shards, value_shards):
    rows, depth = chunks[0].shape
    width = key_shards[0].shape[1]
    operands = [*chunks, *key_shards, *value_shards] + ([] if acc is None else [acc])
    return call(
        functools.partial(project_kernel, len(chunks), len(key_shards), acc is not None, place),
        "project",
        [((rows, 2 * width), F32)],
        operands,
        flops=4 * rows * depth * width * len(chunks),
    )[0]


def pick_kernel(shards, place, *refs):
    maps, out_ref = refs[:-1], refs[-1]
    shard, row = place()
    depth, width = out_ref.shape[0], out_ref.shape[1] // 2
    at = pl.ds(pl.multiple_of(row, depth), depth)

    def copy(i):
        out_ref[:, :width] = maps[i][at, :]
        out_ref[:, width:] = maps[shards + i][at, :]

    if shards == 1:
        copy(0)
    else:
        for i in range(shards):
            pl.when(shard == i)(functools.partial(copy, i))


def pick(place, depth, key_shards, value_shards):
    return call(
        functools.partial(pick_kernel, len(key_shards), place),
        "pick",
        [((depth, 2 * key_shards[0].shape[1]), BF16)],
        [*key_shards, *value_shards],
    )[0]


def cross_kernel(acc_ref, e_ref, map_ref, tgt_ref, mask_ref, *outs):
    half = map_ref.shape[1] // 2
    heads = half // HEAD_DIM
    count = outs[0].shape[0]
    chunk = e_ref[...]

    def memory(at):
        return (acc_ref[:, at] + dot(chunk, map_ref[:, at])).astype(BF16)

    lane = lax.broadcasted_iota(jnp.int32, (tgt_ref.shape[0], LANES), 1)
    stats = jnp.zeros(lane.shape, F32)
    same = mask_ref[...] > 0
    keys = [memory(head_columns(h)) for h in range(heads)]
    values = [memory(head_columns(heads + h)) for h in range(heads)]
    for h in range(heads):
        at = head_columns(h)
        top, weights, total = softmax_block(dot_t(tgt_ref[:, at], keys[h]), same)
        summed = dot(weights.astype(BF16), values[h])
        for i, out_ref in enumerate(outs):
            out_ref[:, at] = summed[i * count : (i + 1) * count]
        stats = jnp.where(lane == h, top, jnp.where(lane == heads + h, total, stats))
    for i, out_ref in enumerate(outs):
        out_ref[:, half:] = stats[i * count : (i + 1) * count]


def cross_attend(acc, chunk, maps, targets, mask, parts):
    width = targets.shape[1]
    count = targets.shape[0] // parts
    return call(
        cross_kernel,
        "cross_attend",
        [((count, width + LANES), F32)] * parts,
        [acc, chunk, maps, targets, mask],
        flops=2 * chunk.size * 2 * width,
    )


def combine_kernel(*refs):
    parts, out_ref = refs[:-1], refs[-1]
    width = out_ref.shape[1]
    heads = width // HEAD_DIM
    for h in range(heads):
        at = head_columns(h)
        tops = [r[:, width + h : width + h + 1] for r in parts]
        top = functools.reduce(jnp.maximum, tops)
        factors = [jnp.exp(t - top) for t in tops]
        total = sum(f * r[:, width + heads + h : width + heads + h + 1] for f, r in zip(factors, parts))
        summed = sum(f * r[:, at] for f, r in zip(factors, parts))
        out_ref[:, at] = (summed / total).astype(BF16)


def on_device(enc_query, enc_key, enc_value, doc_ids, key_map, value_map, tgt_query):
    rows, features = enc_query.shape
    tgt_rows, width = tgt_query.shape
    n_ctx, n_head = lax.axis_size("ctx"), lax.axis_size("head")
    links = links_of(n_ctx)
    bring = lambda x: [lax.ppermute(x, "ctx", pairs) for pairs in links]

    marks = (doc_ids if n_ctx == 2 else doc_ids + 1).reshape(1, rows)
    keys, values, near_marks = bring(enc_key), bring(enc_value), bring(marks)
    query, own_key, own_value, marks = fetch(enc_query, enc_key, enc_value, marks)
    key_map, value_map, tgt_query, *_ = lax.optimization_barrier(
        (key_map, value_map, tgt_query, *keys, *values, *near_marks, query)
    )
    near_targets = bring(tgt_query)
    if n_ctx == 2:
        key_shards, value_shards = [key_map, *bring(key_map)], [value_map, *bring(value_map)]
    else:
        key_shards, value_shards = ([lax.all_gather(x, "ctx", axis=0, tiled=True)] for x in (key_map, value_map))
    targets = jnp.concatenate([tgt_query, *near_targets], 0)
    mask = target_mask(marks, [marks, *near_marks], tgt_rows)

    chunks = 2
    heads = features // HEAD_DIM // chunks
    held = [
        encoder_attend(query, [own_key, *keys], [own_value, *values], [marks, *near_marks], j * heads, heads)
        for j in range(chunks)
    ]

    order = ring_order(n_head)
    ring = [(order[i], order[(i + 1) % n_head]) for i in range(n_head)]
    before = {target: source for source, target in ring}

    def place(turn, first):
        head, ctx = lax.axis_index("head"), lax.axis_index("ctx")
        owner = 0
        for i in range(n_head):
            source = i
            for _ in range(turn):
                source = before[source]
            owner = owner + jnp.where(head == i, source, 0)
        row = owner * features + first
        if len(key_shards) == 1:
            return None, row
        shard_rows = n_head * features // 2
        return jnp.where(lax.div(row, shard_rows) == ctx, 0, 1), lax.rem(row, shard_rows)

    acc, last = None, n_head - 1
    for turn in range(last):
        if turn == last - 1:
            pieces = [p for h in held for p in jnp.split(h, 2, axis=1)]
        else:
            pieces = held
        later = [lax.ppermute(p, "head", ring) for p in pieces]
        acc = project(acc, held, functools.partial(place, turn, 0), key_shards, value_shards)
        held = later
    acc = project(acc, held[:-1], functools.partial(place, last, 0), key_shards, value_shards)
    depth = held[-1].shape[1]
    last_maps = pick(functools.partial(place, last, features - depth), depth, key_shards, value_shards)
    parts = cross_attend(acc, held[-1], last_maps, targets, mask, 1 + len(links))

    combined = [parts[0]]
    for i, (pairs, piece) in enumerate(zip(links, parts[1:])):
        other = lax.ppermute(piece, "ctx", [(target, source) for source, target in pairs])
        if n_ctx > 2:
            end = n_ctx - 1 if i == 0 else 0
            column = lax.broadcasted_iota(jnp.int32, other.shape, 1)
            other = jnp.where((lax.axis_index("ctx") == end) & (column >= width), NEG_FILL, other)
        combined.append(other)
    return call(combine_kernel, "combine", [((tgt_rows, width), BF16)], combined, limit=4 << 20)[0]


def solution(mesh):
    in_specs = (
        P(("dp", "ctx"), "head"),
        P(("dp", "ctx"), "head"),
        P(("dp", "ctx"), "head"),
        P(("dp", "ctx")),
        P("ctx", "head"),
        P("ctx", "head"),
        P(("dp", "ctx"), "head"),
    )
    out_specs = P(("dp", "ctx"), "head")
    return jax.shard_map(
        on_device, mesh=mesh, in_specs=in_specs, out_specs=out_specs, check_vma=False
    )
```

```python
import functools

import jax
import jax.numpy as jnp
from jax import lax
from jax.experimental import pallas as pl
from jax.experimental.pallas import tpu as pltpu
from jax.sharding import PartitionSpec as P

HEAD_DIM = 256
NEG_FILL = -1e30
F32 = jnp.float32
BF16 = jnp.bfloat16
LANES = 128
SCALE = HEAD_DIM**-0.5
VMEM = pl.BlockSpec(memory_space=pltpu.VMEM)
HBM = pl.BlockSpec(memory_space=pltpu.HBM)


def ring_order(count):
    return list(range(0, count, 2)) + list(range(1, count, 2))[::-1]


def links_of(count):
    if count == 2:
        return [[(0, 1), (1, 0)]]
    return [[(i, i + 1) for i in range(count - 1)], [(i + 1, i) for i in range(count - 1)]]


def dot_t(a, b):
    return lax.dot_general(a, b, (((1,), (1,)), ((), ())), preferred_element_type=F32)


def dot(a, b):
    return jnp.dot(a, b, preferred_element_type=F32)


def head_columns(h):
    return slice(h * HEAD_DIM, (h + 1) * HEAD_DIM)


def down_lanes(row):
    return jnp.transpose(jnp.broadcast_to(row, (LANES, row.shape[1])))


def same_mark(down, row):
    return jnp.concatenate([down == row[:, i : i + LANES] for i in range(0, row.shape[1], LANES)], axis=1)


def softmax_block(scores, same):
    scores = jnp.where(same, scores * SCALE, NEG_FILL)
    top = jnp.max(scores, axis=1, keepdims=True)
    weights = jnp.exp(scores - top)
    return top, weights, jnp.sum(weights, axis=1, keepdims=True)


def call(kernel, name, outs, operands, flops=0, exps=0, specs=None, scratch=(), limit=8 << 20):
    out_shape = [jax.ShapeDtypeStruct(*o) for o in outs]
    moved = sum(x.size * x.dtype.itemsize for x in [*operands, *out_shape])
    return pl.pallas_call(
        kernel,
        in_specs=specs or [VMEM] * len(operands),
        out_specs=[VMEM] * len(outs),
        out_shape=out_shape,
        scratch_shapes=list(scratch),
        compiler_params=pltpu.CompilerParams(vmem_limit_bytes=limit),
        cost_estimate=pl.CostEstimate(flops=flops, bytes_accessed=moved, transcendentals=exps),
        name=name,
    )(*operands)


def fetch_kernel(count, *refs):
    sources, targets, sems = refs[:count], refs[count : 2 * count], refs[-1]
    copies = [pltpu.make_async_copy(s, t, sems.at[i]) for i, (s, t) in enumerate(zip(sources, targets))]
    for copy in copies:
        copy.start()
    for copy in copies:
        copy.wait()


def fetch(*arrays):
    return call(
        functools.partial(fetch_kernel, len(arrays)),
        "fetch",
        [(x.shape, x.dtype) for x in arrays],
        [pltpu.with_memory_space_constraint(x, pltpu.HBM) for x in arrays],
        specs=[HBM] * len(arrays),
        scratch=[pltpu.SemaphoreType.DMA((len(arrays),))],
    )


def attend_kernel(blocks, first, *refs):
    marks, q_ref = refs[:blocks], refs[blocks]
    keys, values = refs[blocks + 1 : 2 * blocks + 1], refs[2 * blocks + 1 : 3 * blocks + 1]
    out_ref = refs[-1]
    down = down_lanes(marks[0][...])
    same = jnp.concatenate([same_mark(down, m[...]) for m in marks], axis=1)
    rows = q_ref.shape[0]
    for h in range(out_ref.shape[1] // HEAD_DIM):
        at = head_columns(first + h)
        scores = jnp.concatenate([dot_t(q_ref[:, at], k[:, at]) for k in keys], axis=1)
        _, weights, total = softmax_block(scores, same)
        rounded = weights.astype(BF16)
        summed = sum(dot(rounded[:, i * rows : (i + 1) * rows], v[:, at]) for i, v in enumerate(values))
        out_ref[:, head_columns(h)] = (summed / total).astype(BF16)


def encoder_attend(query, keys, values, marks, first, heads):
    rows = query.shape[0]
    pairs = rows * rows * len(keys) * heads
    return call(
        functools.partial(attend_kernel, len(keys), first),
        "encoder_attend",
        [((rows, heads * HEAD_DIM), BF16)],
        [*marks, query, *keys, *values],
        flops=4 * pairs * HEAD_DIM,
        exps=pairs,
    )[0]


def target_mask_kernel(step, own_ref, *refs):
    marks, out_ref, down_ref = refs[:-2], refs[-2], refs[-1]
    own = own_ref[...]
    count = out_ref.shape[0] // len(marks)
    for i, mark_ref in enumerate(marks):
        down_ref[...] = down_lanes(mark_ref[...])
        down = down_ref[pl.ds(0, count, stride=step), :]
        out_ref[i * count : (i + 1) * count, :] = same_mark(down, own).astype(F32)


def target_mask(marks, all_marks, tgt_rows):
    rows = marks.shape[1]
    return call(
        functools.partial(target_mask_kernel, rows // tgt_rows),
        "target_mask",
        [((tgt_rows * len(all_marks), rows), F32)],
        [marks, *all_marks],
        scratch=[pltpu.VMEM((rows, LANES), jnp.int32)],
    )[0]


def add_products(acc_of, store, e_refs, place, key_shards, value_shards):
    shard, row = place
    depth = e_refs[0].shape[1]
    at = pl.ds(pl.multiple_of(row, depth), depth * len(e_refs))
    chunks = jnp.concatenate([r[...] for r in e_refs], axis=1)

    def add(i):
        for side, shards in enumerate((key_shards, value_shards)):
            store(side, acc_of(side) + dot(chunks, shards[i][at, :]))

    if len(key_shards) == 1:
        add(0)
    else:
        for i in range(len(key_shards)):
            pl.when(shard == i)(functools.partial(add, i))


def halve_kernel(source, *outs):
    width = outs[0].shape[1]
    for i, out in enumerate(outs):
        out[...] = source[:, i * width : (i + 1) * width]


def halve(chunk):
    rows, width = chunk.shape
    return call(halve_kernel, "halve", [((rows, width // 2), chunk.dtype)] * 2, [chunk], flops=10**10)


def project_kernel(chunks, shards, has_acc, place, *refs):
    out_ref = refs[-1]
    e_refs, maps = refs[:chunks], refs[chunks : chunks + 2 * shards]
    half = out_ref.shape[1] // 2
    side_of = lambda side: slice(side * half, (side + 1) * half)

    def store(side, value):
        out_ref[:, side_of(side)] = value

    acc_of = lambda side: refs[-2][:, side_of(side)] if has_acc else 0.0
    add_products(acc_of, store, e_refs, place(), maps[:shards], maps[shards:])


def project(acc, chunks, place, key_shards, value_shards):
    rows, depth = chunks[0].shape
    width = key_shards[0].shape[1]
    operands = [*chunks, *key_shards, *value_shards] + ([] if acc is None else [acc])
    return call(
        functools.partial(project_kernel, len(chunks), len(key_shards), acc is not None, place),
        "project",
        [((rows, 2 * width), F32)],
        operands,
        flops=4 * rows * depth * width * len(chunks),
    )[0]


def pick_kernel(shards, place, *refs):
    maps, out_ref = refs[:-1], refs[-1]
    shard, row = place()
    depth, width = out_ref.shape[0], out_ref.shape[1] // 2
    at = pl.ds(pl.multiple_of(row, depth), depth)

    def copy(i):
        out_ref[:, :width] = maps[i][at, :]
        out_ref[:, width:] = maps[shards + i][at, :]

    if shards == 1:
        copy(0)
    else:
        for i in range(shards):
            pl.when(shard == i)(functools.partial(copy, i))


def pick(place, depth, key_shards, value_shards):
    return call(
        functools.partial(pick_kernel, len(key_shards), place),
        "pick",
        [((depth, 2 * key_shards[0].shape[1]), BF16)],
        [*key_shards, *value_shards],
    )[0]


def cross_kernel(acc_ref, e_ref, map_ref, tgt_ref, mask_ref, *outs):
    half = map_ref.shape[1] // 2
    heads = half // HEAD_DIM
    count = outs[0].shape[0]
    chunk = e_ref[...]

    def memory(at):
        return (acc_ref[:, at] + dot(chunk, map_ref[:, at])).astype(BF16)

    lane = lax.broadcasted_iota(jnp.int32, (tgt_ref.shape[0], LANES), 1)
    stats = jnp.zeros(lane.shape, F32)
    same = mask_ref[...] > 0
    keys = [memory(head_columns(h)) for h in range(heads)]
    values = [memory(head_columns(heads + h)) for h in range(heads)]
    for h in range(heads):
        at = head_columns(h)
        top, weights, total = softmax_block(dot_t(tgt_ref[:, at], keys[h]), same)
        summed = dot(weights.astype(BF16), values[h])
        for i, out_ref in enumerate(outs):
            out_ref[:, at] = summed[i * count : (i + 1) * count]
        stats = jnp.where(lane == h, top, jnp.where(lane == heads + h, total, stats))
    for i, out_ref in enumerate(outs):
        out_ref[:, half:] = stats[i * count : (i + 1) * count]


def cross_attend(acc, chunk, maps, targets, mask, parts):
    width = targets.shape[1]
    count = targets.shape[0] // parts
    return call(
        cross_kernel,
        "cross_attend",
        [((count, width + LANES), F32)] * parts,
        [acc, chunk, maps, targets, mask],
        flops=2 * chunk.size * 2 * width,
    )


def combine_kernel(*refs):
    parts, out_ref = refs[:-1], refs[-1]
    width = out_ref.shape[1]
    heads = width // HEAD_DIM
    for h in range(heads):
        at = head_columns(h)
        tops = [r[:, width + h : width + h + 1] for r in parts]
        top = functools.reduce(jnp.maximum, tops)
        factors = [jnp.exp(t - top) for t in tops]
        total = sum(f * r[:, width + heads + h : width + heads + h + 1] for f, r in zip(factors, parts))
        summed = sum(f * r[:, at] for f, r in zip(factors, parts))
        out_ref[:, at] = (summed / total).astype(BF16)


def on_device(enc_query, enc_key, enc_value, doc_ids, key_map, value_map, tgt_query):
    rows, features = enc_query.shape
    tgt_rows, width = tgt_query.shape
    n_ctx, n_head = lax.axis_size("ctx"), lax.axis_size("head")
    links = links_of(n_ctx)
    bring = lambda x: [lax.ppermute(x, "ctx", pairs) for pairs in links]

    marks = (doc_ids if n_ctx == 2 else doc_ids + 1).reshape(1, rows)
    keys, values, near_marks = bring(enc_key), bring(enc_value), bring(marks)
    query, own_key, own_value, marks = fetch(enc_query, enc_key, enc_value, marks)
    near_targets = bring(tgt_query)
    if n_ctx == 2:
        key_shards, value_shards = [key_map, *bring(key_map)], [value_map, *bring(value_map)]
    else:
        key_shards, value_shards = ([lax.all_gather(x, "ctx", axis=0, tiled=True)] for x in (key_map, value_map))
    targets = jnp.concatenate([tgt_query, *near_targets], 0)
    mask = target_mask(marks, [marks, *near_marks], tgt_rows)

    chunks = 2
    heads = features // HEAD_DIM // chunks
    held = [
        encoder_attend(query, [own_key, *keys], [own_value, *values], [marks, *near_marks], j * heads, heads)
        for j in range(chunks)
    ]

    order = ring_order(n_head)
    ring = [(order[i], order[(i + 1) % n_head]) for i in range(n_head)]
    before = {target: source for source, target in ring}

    def place(turn, first):
        head, ctx = lax.axis_index("head"), lax.axis_index("ctx")
        owner = 0
        for i in range(n_head):
            source = i
            for _ in range(turn):
                source = before[source]
            owner = owner + jnp.where(head == i, source, 0)
        row = owner * features + first
        if len(key_shards) == 1:
            return None, row
        shard_rows = n_head * features // 2
        return jnp.where(lax.div(row, shard_rows) == ctx, 0, 1), lax.rem(row, shard_rows)

    acc, last = None, n_head - 1
    for turn in range(last):
        if turn == last - 1:
            pieces = [p for h in held for p in halve(h)]
        else:
            pieces = held
        later = [lax.ppermute(p, "head", ring) for p in pieces]
        acc = project(acc, held, functools.partial(place, turn, 0), key_shards, value_shards)
        held = later
    acc = project(acc, held[:-1], functools.partial(place, last, 0), key_shards, value_shards)
    depth = held[-1].shape[1]
    last_maps = pick(functools.partial(place, last, features - depth), depth, key_shards, value_shards)
    parts = cross_attend(acc, held[-1], last_maps, targets, mask, 1 + len(links))

    combined = [parts[0]]
    for i, (pairs, piece) in enumerate(zip(links, parts[1:])):
        other = lax.ppermute(piece, "ctx", [(target, source) for source, target in pairs])
        if n_ctx > 2:
            end = n_ctx - 1 if i == 0 else 0
            column = lax.broadcasted_iota(jnp.int32, other.shape, 1)
            other = jnp.where((lax.axis_index("ctx") == end) & (column >= width), NEG_FILL, other)
        combined.append(other)
    return call(combine_kernel, "combine", [((tgt_rows, width), BF16)], combined, limit=4 << 20)[0]


def solution(mesh):
    in_specs = (
        P(("dp", "ctx"), "head"),
        P(("dp", "ctx"), "head"),
        P(("dp", "ctx"), "head"),
        P(("dp", "ctx")),
        P("ctx", "head"),
        P("ctx", "head"),
        P(("dp", "ctx"), "head"),
    )
    out_specs = P(("dp", "ctx"), "head")
    return jax.shard_map(
        on_device, mesh=mesh, in_specs=in_specs, out_specs=out_specs, check_vma=False
    )
```

```python
import functools

import jax
import jax.numpy as jnp
from jax import lax
from jax.experimental import pallas as pl
from jax.experimental.pallas import tpu as pltpu
from jax.sharding import PartitionSpec as P

HEAD_DIM = 256
NEG_FILL = -1e30
F32 = jnp.float32
BF16 = jnp.bfloat16
LANES = 128
SCALE = HEAD_DIM**-0.5
VMEM = pl.BlockSpec(memory_space=pltpu.VMEM)
HBM = pl.BlockSpec(memory_space=pltpu.HBM)


def ring_order(count):
    return list(range(0, count, 2)) + list(range(1, count, 2))[::-1]


def links_of(count):
    if count == 2:
        return [[(0, 1), (1, 0)]]
    return [[(i, i + 1) for i in range(count - 1)], [(i + 1, i) for i in range(count - 1)]]


def dot_t(a, b):
    return lax.dot_general(a, b, (((1,), (1,)), ((), ())), preferred_element_type=F32)


def dot(a, b):
    return jnp.dot(a, b, preferred_element_type=F32)


def head_columns(h):
    return slice(h * HEAD_DIM, (h + 1) * HEAD_DIM)


def down_lanes(row):
    return jnp.transpose(jnp.broadcast_to(row, (LANES, row.shape[1])))


def same_mark(down, row):
    return jnp.concatenate([down == row[:, i : i + LANES] for i in range(0, row.shape[1], LANES)], axis=1)


def softmax_block(scores, same):
    scores = jnp.where(same, scores * SCALE, NEG_FILL)
    top = jnp.max(scores, axis=1, keepdims=True)
    weights = jnp.exp(scores - top)
    return top, weights, jnp.sum(weights, axis=1, keepdims=True)


def call(kernel, name, outs, operands, flops=0, exps=0, specs=None, scratch=(), limit=8 << 20):
    out_shape = [jax.ShapeDtypeStruct(*o) for o in outs]
    moved = sum(x.size * x.dtype.itemsize for x in [*operands, *out_shape])
    return pl.pallas_call(
        kernel,
        in_specs=specs or [VMEM] * len(operands),
        out_specs=[VMEM] * len(outs),
        out_shape=out_shape,
        scratch_shapes=list(scratch),
        compiler_params=pltpu.CompilerParams(vmem_limit_bytes=limit),
        cost_estimate=pl.CostEstimate(flops=flops, bytes_accessed=moved, transcendentals=exps),
        name=name,
    )(*operands)


def fetch_kernel(count, *refs):
    sources, targets, sems = refs[:count], refs[count : 2 * count], refs[-1]
    copies = [pltpu.make_async_copy(s, t, sems.at[i]) for i, (s, t) in enumerate(zip(sources, targets))]
    for copy in copies:
        copy.start()
    for copy in copies:
        copy.wait()


def fetch(*arrays):
    return call(
        functools.partial(fetch_kernel, len(arrays)),
        "fetch",
        [(x.shape, x.dtype) for x in arrays],
        [pltpu.with_memory_space_constraint(x, pltpu.HBM) for x in arrays],
        specs=[HBM] * len(arrays),
        scratch=[pltpu.SemaphoreType.DMA((len(arrays),))],
    )


def attend_kernel(blocks, first, *refs):
    marks, q_ref = refs[:blocks], refs[blocks]
    keys, values = refs[blocks + 1 : 2 * blocks + 1], refs[2 * blocks + 1 : 3 * blocks + 1]
    out_ref = refs[-1]
    down = down_lanes(marks[0][...])
    same = jnp.concatenate([same_mark(down, m[...]) for m in marks], axis=1)
    rows = q_ref.shape[0]
    for h in range(out_ref.shape[1] // HEAD_DIM):
        at = head_columns(first + h)
        scores = jnp.concatenate([dot_t(q_ref[:, at], k[:, at]) for k in keys], axis=1)
        _, weights, total = softmax_block(scores, same)
        rounded = weights.astype(BF16)
        summed = sum(dot(rounded[:, i * rows : (i + 1) * rows], v[:, at]) for i, v in enumerate(values))
        out_ref[:, head_columns(h)] = (summed / total).astype(BF16)


def encoder_attend(query, keys, values, marks, first, heads):
    rows = query.shape[0]
    pairs = rows * rows * len(keys) * heads
    return call(
        functools.partial(attend_kernel, len(keys), first),
        "encoder_attend",
        [((rows, heads * HEAD_DIM), BF16)],
        [*marks, query, *keys, *values],
        flops=4 * pairs * HEAD_DIM,
        exps=pairs,
    )[0]


def add_products(acc_of, store, e_refs, place, key_shards, value_shards):
    shard, row = place
    depth = e_refs[0].shape[1]
    at = pl.ds(pl.multiple_of(row, depth), depth * len(e_refs))
    chunks = jnp.concatenate([r[...] for r in e_refs], axis=1)

    def add(i):
        for side, shards in enumerate((key_shards, value_shards)):
            store(side, acc_of(side) + dot(chunks, shards[i][at, :]))

    if len(key_shards) == 1:
        add(0)
    else:
        for i in range(len(key_shards)):
            pl.when(shard == i)(functools.partial(add, i))


def halve_kernel(source, *outs):
    width = outs[0].shape[1]
    for i, out in enumerate(outs):
        out[...] = source[:, i * width : (i + 1) * width]


def halve(chunk):
    rows, width = chunk.shape
    return call(halve_kernel, "halve", [((rows, width // 2), chunk.dtype)] * 2, [chunk], flops=10**10)


def project_kernel(chunks, shards, has_acc, place, *refs):
    out_ref = refs[-1]
    e_refs, maps = refs[:chunks], refs[chunks : chunks + 2 * shards]
    half = out_ref.shape[1] // 2
    side_of = lambda side: slice(side * half, (side + 1) * half)

    def store(side, value):
        out_ref[:, side_of(side)] = value

    acc_of = lambda side: refs[-2][:, side_of(side)] if has_acc else 0.0
    add_products(acc_of, store, e_refs, place(), maps[:shards], maps[shards:])


def project(acc, chunks, place, key_shards, value_shards):
    rows, depth = chunks[0].shape
    width = key_shards[0].shape[1]
    operands = [*chunks, *key_shards, *value_shards] + ([] if acc is None else [acc])
    return call(
        functools.partial(project_kernel, len(chunks), len(key_shards), acc is not None, place),
        "project",
        [((rows, 2 * width), F32)],
        operands,
        flops=4 * rows * depth * width * len(chunks),
    )[0]


def prepare_kernel(shards, parts, step, place, *refs):
    maps, targets, marks = refs[: 2 * shards], refs[2 * shards : 2 * shards + parts], refs[2 * shards + parts : -4]
    map_ref, tgt_ref, mask_ref, down_ref = refs[-4:]
    shard, row = place()
    depth, width = map_ref.shape[0], map_ref.shape[1] // 2
    at = pl.ds(pl.multiple_of(row, depth), depth)

    def copy(i):
        map_ref[:, :width] = maps[i][at, :]
        map_ref[:, width:] = maps[shards + i][at, :]

    if shards == 1:
        copy(0)
    else:
        for i in range(shards):
            pl.when(shard == i)(functools.partial(copy, i))
    own = marks[0][...]
    count = targets[0].shape[0]
    for i, (target_ref, mark_ref) in enumerate(zip(targets, marks)):
        part = slice(i * count, (i + 1) * count)
        tgt_ref[part, :] = target_ref[...]
        down_ref[...] = down_lanes(mark_ref[...])
        down = down_ref[pl.ds(0, count, stride=step), :]
        mask_ref[part, :] = same_mark(down, own).astype(F32)


def prepare(place, depth, key_shards, value_shards, targets, marks):
    rows, count, width = marks[0].shape[1], targets[0].shape[0], targets[0].shape[1]
    total = count * len(targets)
    return call(
        functools.partial(prepare_kernel, len(key_shards), len(targets), rows // count, place),
        "prepare",
        [((depth, 2 * width), BF16), ((total, width), BF16), ((total, rows), F32)],
        [*key_shards, *value_shards, *targets, *marks],
        scratch=[pltpu.VMEM((rows, LANES), jnp.int32)],
    )


def cross_kernel(acc_ref, e_ref, map_ref, tgt_ref, mask_ref, *outs):
    half = map_ref.shape[1] // 2
    heads = half // HEAD_DIM
    count = outs[0].shape[0]
    chunk = e_ref[...]

    def memory(at):
        return (acc_ref[:, at] + dot(chunk, map_ref[:, at])).astype(BF16)

    lane = lax.broadcasted_iota(jnp.int32, (tgt_ref.shape[0], LANES), 1)
    stats = jnp.zeros(lane.shape, F32)
    same = mask_ref[...] > 0
    keys = [memory(head_columns(h)) for h in range(heads)]
    values = [memory(head_columns(heads + h)) for h in range(heads)]
    for h in range(heads):
        at = head_columns(h)
        top, weights, total = softmax_block(dot_t(tgt_ref[:, at], keys[h]), same)
        summed = dot(weights.astype(BF16), values[h])
        for i, out_ref in enumerate(outs):
            out_ref[:, at] = summed[i * count : (i + 1) * count]
        stats = jnp.where(lane == h, top, jnp.where(lane == heads + h, total, stats))
    for i, out_ref in enumerate(outs):
        out_ref[:, half:] = stats[i * count : (i + 1) * count]


def cross_attend(acc, chunk, maps, targets, mask, parts):
    width = targets.shape[1]
    count = targets.shape[0] // parts
    return call(
        cross_kernel,
        "cross_attend",
        [((count, width + LANES), F32)] * parts,
        [acc, chunk, maps, targets, mask],
        flops=2 * chunk.size * 2 * width,
    )


def combine_kernel(*refs):
    parts, out_ref = refs[:-1], refs[-1]
    width = out_ref.shape[1]
    heads = width // HEAD_DIM
    for h in range(heads):
        at = head_columns(h)
        tops = [r[:, width + h : width + h + 1] for r in parts]
        top = functools.reduce(jnp.maximum, tops)
        factors = [jnp.exp(t - top) for t in tops]
        total = sum(f * r[:, width + heads + h : width + heads + h + 1] for f, r in zip(factors, parts))
        summed = sum(f * r[:, at] for f, r in zip(factors, parts))
        out_ref[:, at] = (summed / total).astype(BF16)


def on_device(enc_query, enc_key, enc_value, doc_ids, key_map, value_map, tgt_query):
    rows, features = enc_query.shape
    tgt_rows, width = tgt_query.shape
    n_ctx, n_head = lax.axis_size("ctx"), lax.axis_size("head")
    links = links_of(n_ctx)
    bring = lambda x: [lax.ppermute(x, "ctx", pairs) for pairs in links]

    marks = (doc_ids if n_ctx == 2 else doc_ids + 1).reshape(1, rows)
    keys, values, near_marks = bring(enc_key), bring(enc_value), bring(marks)
    query, own_key, own_value, marks = fetch(enc_query, enc_key, enc_value, marks)
    near_targets = bring(tgt_query)
    if n_ctx == 2:
        key_shards, value_shards = [key_map, *bring(key_map)], [value_map, *bring(value_map)]
    else:
        key_shards, value_shards = ([lax.all_gather(x, "ctx", axis=0, tiled=True)] for x in (key_map, value_map))

    chunks = 2
    heads = features // HEAD_DIM // chunks
    held = [
        encoder_attend(query, [own_key, *keys], [own_value, *values], [marks, *near_marks], j * heads, heads)
        for j in range(chunks)
    ]

    order = ring_order(n_head)
    ring = [(order[i], order[(i + 1) % n_head]) for i in range(n_head)]
    before = {target: source for source, target in ring}

    def place(turn, first):
        head, ctx = lax.axis_index("head"), lax.axis_index("ctx")
        owner = 0
        for i in range(n_head):
            source = i
            for _ in range(turn):
                source = before[source]
            owner = owner + jnp.where(head == i, source, 0)
        row = owner * features + first
        if len(key_shards) == 1:
            return None, row
        shard_rows = n_head * features // 2
        return jnp.where(lax.div(row, shard_rows) == ctx, 0, 1), lax.rem(row, shard_rows)

    acc, last = None, n_head - 1
    for turn in range(last):
        if turn == last - 1:
            pieces = [p for h in held for p in halve(h)]
        else:
            pieces = held
        later = [lax.ppermute(p, "head", ring) for p in pieces]
        acc = project(acc, held, functools.partial(place, turn, 0), key_shards, value_shards)
        held = later
    acc = project(acc, held[:-1], functools.partial(place, last, 0), key_shards, value_shards)
    depth = held[-1].shape[1]
    last_maps, targets, mask = prepare(
        functools.partial(place, last, features - depth),
        depth,
        key_shards,
        value_shards,
        [tgt_query, *near_targets],
        [marks, *near_marks],
    )
    parts = cross_attend(acc, held[-1], last_maps, targets, mask, 1 + len(links))

    combined = [parts[0]]
    for i, (pairs, piece) in enumerate(zip(links, parts[1:])):
        other = lax.ppermute(piece, "ctx", [(target, source) for source, target in pairs])
        if n_ctx > 2:
            end = n_ctx - 1 if i == 0 else 0
            column = lax.broadcasted_iota(jnp.int32, other.shape, 1)
            other = jnp.where((lax.axis_index("ctx") == end) & (column >= width), NEG_FILL, other)
        combined.append(other)
    return call(combine_kernel, "combine", [((tgt_rows, width), BF16)], combined, limit=4 << 20)[0]


def solution(mesh):
    in_specs = (
        P(("dp", "ctx"), "head"),
        P(("dp", "ctx"), "head"),
        P(("dp", "ctx"), "head"),
        P(("dp", "ctx")),
        P("ctx", "head"),
        P("ctx", "head"),
        P(("dp", "ctx"), "head"),
    )
    out_specs = P(("dp", "ctx"), "head")
    return jax.shard_map(
        on_device, mesh=mesh, in_specs=in_specs, out_specs=out_specs, check_vma=False
    )
```

```python
import functools

import jax
import jax.numpy as jnp
from jax import lax
from jax.experimental import pallas as pl
from jax.experimental.pallas import tpu as pltpu
from jax.sharding import PartitionSpec as P

HEAD_DIM = 256
NEG_FILL = -1e30
F32 = jnp.float32
BF16 = jnp.bfloat16
LANES = 128
SCALE = HEAD_DIM**-0.5
VMEM = pl.BlockSpec(memory_space=pltpu.VMEM)
HBM = pl.BlockSpec(memory_space=pltpu.HBM)


def ring_order(count):
    return list(range(0, count, 2)) + list(range(1, count, 2))[::-1]


def links_of(count):
    if count == 2:
        return [[(0, 1), (1, 0)]]
    return [[(i, i + 1) for i in range(count - 1)], [(i + 1, i) for i in range(count - 1)]]


def dot_t(a, b):
    return lax.dot_general(a, b, (((1,), (1,)), ((), ())), preferred_element_type=F32)


def dot(a, b):
    return jnp.dot(a, b, preferred_element_type=F32)


def head_columns(h):
    return slice(h * HEAD_DIM, (h + 1) * HEAD_DIM)


def down_lanes(row):
    return jnp.transpose(jnp.broadcast_to(row, (LANES, row.shape[1])))


def same_mark(down, row):
    return jnp.concatenate([down == row[:, i : i + LANES] for i in range(0, row.shape[1], LANES)], axis=1)


def softmax_block(scores, same):
    scores = jnp.where(same, scores * SCALE, NEG_FILL)
    top = jnp.max(scores, axis=1, keepdims=True)
    weights = jnp.exp(scores - top)
    return top, weights, jnp.sum(weights, axis=1, keepdims=True)


def call(kernel, name, outs, operands, flops=0, exps=0, specs=None, scratch=(), limit=8 << 20):
    out_shape = [jax.ShapeDtypeStruct(*o) for o in outs]
    moved = sum(x.size * x.dtype.itemsize for x in [*operands, *out_shape])
    return pl.pallas_call(
        kernel,
        in_specs=specs or [VMEM] * len(operands),
        out_specs=[VMEM] * len(outs),
        out_shape=out_shape,
        scratch_shapes=list(scratch),
        compiler_params=pltpu.CompilerParams(vmem_limit_bytes=limit),
        cost_estimate=pl.CostEstimate(flops=flops, bytes_accessed=moved, transcendentals=exps),
        name=name,
    )(*operands)


def fetch_kernel(count, *refs):
    sources, targets, sems = refs[:count], refs[count : 2 * count], refs[-1]
    copies = [pltpu.make_async_copy(s, t, sems.at[i]) for i, (s, t) in enumerate(zip(sources, targets))]
    for copy in copies:
        copy.start()
    for copy in copies:
        copy.wait()


def fetch(*arrays):
    return call(
        functools.partial(fetch_kernel, len(arrays)),
        "fetch",
        [(x.shape, x.dtype) for x in arrays],
        [pltpu.with_memory_space_constraint(x, pltpu.HBM) for x in arrays],
        specs=[HBM] * len(arrays),
        scratch=[pltpu.SemaphoreType.DMA((len(arrays),))],
    )


def attend_kernel(blocks, first, *refs):
    marks, q_ref = refs[:blocks], refs[blocks]
    keys, values = refs[blocks + 1 : 2 * blocks + 1], refs[2 * blocks + 1 : 3 * blocks + 1]
    out_ref = refs[-1]
    down = down_lanes(marks[0][...])
    same = jnp.concatenate([same_mark(down, m[...]) for m in marks], axis=1)
    rows = q_ref.shape[0]
    for h in range(out_ref.shape[1] // HEAD_DIM):
        at = head_columns(first + h)
        scores = jnp.concatenate([dot_t(q_ref[:, at], k[:, at]) for k in keys], axis=1)
        _, weights, total = softmax_block(scores, same)
        rounded = weights.astype(BF16)
        summed = sum(dot(rounded[:, i * rows : (i + 1) * rows], v[:, at]) for i, v in enumerate(values))
        out_ref[:, head_columns(h)] = (summed / total).astype(BF16)


def encoder_attend(query, keys, values, marks, first, heads):
    rows = query.shape[0]
    pairs = rows * rows * len(keys) * heads
    return call(
        functools.partial(attend_kernel, len(keys), first),
        "encoder_attend",
        [((rows, heads * HEAD_DIM), BF16)],
        [*marks, query, *keys, *values],
        flops=4 * pairs * HEAD_DIM,
        exps=pairs,
    )[0]


def add_products(acc_of, store, e_refs, place, key_shards, value_shards):
    shard, row = place
    widths = [r.shape[1] for r in e_refs]
    at = pl.ds(pl.multiple_of(row, min(widths)), sum(widths))
    chunks = jnp.concatenate([r[...] for r in e_refs], axis=1)

    def add(i):
        for side, shards in enumerate((key_shards, value_shards)):
            store(side, acc_of(side) + dot(chunks, shards[i][at, :]))

    if len(key_shards) == 1:
        add(0)
    else:
        for i in range(len(key_shards)):
            pl.when(shard == i)(functools.partial(add, i))


def split_kernel(source, *outs):
    width = outs[0].shape[1]
    for i, out in enumerate(outs):
        out[...] = source[:, i * width : (i + 1) * width]


def split(chunk, parts, weight):
    rows, width = chunk.shape
    outs = [((rows, width // parts), chunk.dtype)] * parts
    return call(split_kernel, "split", outs, [chunk], flops=weight * 10**10)


def project_kernel(chunks, shards, has_acc, place, *refs):
    out_ref = refs[-1]
    e_refs, maps = refs[:chunks], refs[chunks : chunks + 2 * shards]
    half = out_ref.shape[1] // 2
    side_of = lambda side: slice(side * half, (side + 1) * half)

    def store(side, value):
        out_ref[:, side_of(side)] = value

    acc_of = lambda side: refs[-2][:, side_of(side)] if has_acc else 0.0
    add_products(acc_of, store, e_refs, place(), maps[:shards], maps[shards:])


def project(acc, chunks, place, key_shards, value_shards):
    rows, width = chunks[0].shape[0], key_shards[0].shape[1]
    operands = [*chunks, *key_shards, *value_shards] + ([] if acc is None else [acc])
    return call(
        functools.partial(project_kernel, len(chunks), len(key_shards), acc is not None, place),
        "project",
        [((rows, 2 * width), F32)],
        operands,
        flops=4 * width * sum(x.size for x in chunks),
    )[0]


def prepare_kernel(shards, parts, step, place, *refs):
    maps, targets, marks = refs[: 2 * shards], refs[2 * shards : 2 * shards + parts], refs[2 * shards + parts : -4]
    map_ref, tgt_ref, mask_ref, down_ref = refs[-4:]
    shard, row = place()
    depth, width = map_ref.shape[0], map_ref.shape[1] // 2
    at = pl.ds(pl.multiple_of(row, depth), depth)

    def copy(i):
        map_ref[:, :width] = maps[i][at, :]
        map_ref[:, width:] = maps[shards + i][at, :]

    if shards == 1:
        copy(0)
    else:
        for i in range(shards):
            pl.when(shard == i)(functools.partial(copy, i))
    own = marks[0][...]
    count = targets[0].shape[0]
    for i, (target_ref, mark_ref) in enumerate(zip(targets, marks)):
        part = slice(i * count, (i + 1) * count)
        tgt_ref[part, :] = target_ref[...]
        down_ref[...] = down_lanes(mark_ref[...])
        down = down_ref[pl.ds(0, count, stride=step), :]
        mask_ref[part, :] = same_mark(down, own).astype(F32)


def prepare(place, depth, key_shards, value_shards, targets, marks):
    rows, count, width = marks[0].shape[1], targets[0].shape[0], targets[0].shape[1]
    total = count * len(targets)
    return call(
        functools.partial(prepare_kernel, len(key_shards), len(targets), rows // count, place),
        "prepare",
        [((depth, 2 * width), BF16), ((total, width), BF16), ((total, rows), F32)],
        [*key_shards, *value_shards, *targets, *marks],
        scratch=[pltpu.VMEM((rows, LANES), jnp.int32)],
    )


def cross_kernel(acc_ref, e_ref, map_ref, tgt_ref, mask_ref, *outs):
    half = map_ref.shape[1] // 2
    heads = half // HEAD_DIM
    count = outs[0].shape[0]
    chunk = e_ref[...]

    def memory(at):
        return (acc_ref[:, at] + dot(chunk, map_ref[:, at])).astype(BF16)

    lane = lax.broadcasted_iota(jnp.int32, (tgt_ref.shape[0], LANES), 1)
    stats = jnp.zeros(lane.shape, F32)
    same = mask_ref[...] > 0
    keys = [memory(head_columns(h)) for h in range(heads)]
    values = [memory(head_columns(heads + h)) for h in range(heads)]
    for h in range(heads):
        at = head_columns(h)
        top, weights, total = softmax_block(dot_t(tgt_ref[:, at], keys[h]), same)
        summed = dot(weights.astype(BF16), values[h])
        for i, out_ref in enumerate(outs):
            out_ref[:, at] = summed[i * count : (i + 1) * count]
        stats = jnp.where(lane == h, top, jnp.where(lane == heads + h, total, stats))
    for i, out_ref in enumerate(outs):
        out_ref[:, half:] = stats[i * count : (i + 1) * count]


def cross_attend(acc, chunk, maps, targets, mask, parts):
    width = targets.shape[1]
    count = targets.shape[0] // parts
    return call(
        cross_kernel,
        "cross_attend",
        [((count, width + LANES), F32)] * parts,
        [acc, chunk, maps, targets, mask],
        flops=2 * chunk.size * 2 * width,
    )


def combine_kernel(*refs):
    parts, out_ref = refs[:-1], refs[-1]
    width = out_ref.shape[1]
    heads = width // HEAD_DIM
    for h in range(heads):
        at = head_columns(h)
        tops = [r[:, width + h : width + h + 1] for r in parts]
        top = functools.reduce(jnp.maximum, tops)
        factors = [jnp.exp(t - top) for t in tops]
        total = sum(f * r[:, width + heads + h : width + heads + h + 1] for f, r in zip(factors, parts))
        summed = sum(f * r[:, at] for f, r in zip(factors, parts))
        out_ref[:, at] = (summed / total).astype(BF16)


def on_device(enc_query, enc_key, enc_value, doc_ids, key_map, value_map, tgt_query):
    rows, features = enc_query.shape
    tgt_rows, width = tgt_query.shape
    n_ctx, n_head = lax.axis_size("ctx"), lax.axis_size("head")
    links = links_of(n_ctx)
    bring = lambda x: [lax.ppermute(x, "ctx", pairs) for pairs in links]

    marks = (doc_ids if n_ctx == 2 else doc_ids + 1).reshape(1, rows)
    keys, values, near_marks = bring(enc_key), bring(enc_value), bring(marks)
    query, own_key, own_value, marks = fetch(enc_query, enc_key, enc_value, marks)
    near_targets = bring(tgt_query)
    if n_ctx == 2:
        key_shards, value_shards = [key_map, *bring(key_map)], [value_map, *bring(value_map)]
    else:
        key_shards, value_shards = ([lax.all_gather(x, "ctx", axis=0, tiled=True)] for x in (key_map, value_map))

    heads = features // HEAD_DIM
    held = [
        encoder_attend(query, [own_key, *keys], [own_value, *values], [marks, *near_marks], first, count)
        for first, count in ((0, 1), (1, heads - 1))
    ]

    order = ring_order(n_head)
    ring = [(order[i], order[(i + 1) % n_head]) for i in range(n_head)]
    before = {target: source for source, target in ring}

    def place(turn, first):
        head, ctx = lax.axis_index("head"), lax.axis_index("ctx")
        owner = 0
        for i in range(n_head):
            source = i
            for _ in range(turn):
                source = before[source]
            owner = owner + jnp.where(head == i, source, 0)
        row = owner * features + first
        if len(key_shards) == 1:
            return None, row
        shard_rows = n_head * features // 2
        return jnp.where(lax.div(row, shard_rows) == ctx, 0, 1), lax.rem(row, shard_rows)

    acc, last = None, n_head - 1
    for turn in range(last):
        if turn == last - 1:
            pieces = [*split(held[0], 2, 2), *split(held[1], heads - 1, 1)]
        else:
            pieces = held if turn == 0 else [*split(held[0], 1, 1), *held[1:]]
        later = [lax.ppermute(p, "head", ring) for p in pieces]
        acc = project(acc, held, functools.partial(place, turn, 0), key_shards, value_shards)
        held = later
    acc = project(acc, held[:-1], functools.partial(place, last, 0), key_shards, value_shards)
    depth = held[-1].shape[1]
    last_maps, targets, mask = prepare(
        functools.partial(place, last, features - depth),
        depth,
        key_shards,
        value_shards,
        [tgt_query, *near_targets],
        [marks, *near_marks],
    )
    parts = cross_attend(acc, held[-1], last_maps, targets, mask, 1 + len(links))

    combined = [parts[0]]
    for i, (pairs, piece) in enumerate(zip(links, parts[1:])):
        other = lax.ppermute(piece, "ctx", [(target, source) for source, target in pairs])
        if n_ctx > 2:
            end = n_ctx - 1 if i == 0 else 0
            column = lax.broadcasted_iota(jnp.int32, other.shape, 1)
            other = jnp.where((lax.axis_index("ctx") == end) & (column >= width), NEG_FILL, other)
        combined.append(other)
    return call(combine_kernel, "combine", [((tgt_rows, width), BF16)], combined, limit=4 << 20)[0]


def solution(mesh):
    in_specs = (
        P(("dp", "ctx"), "head"),
        P(("dp", "ctx"), "head"),
        P(("dp", "ctx"), "head"),
        P(("dp", "ctx")),
        P("ctx", "head"),
        P("ctx", "head"),
        P(("dp", "ctx"), "head"),
    )
    out_specs = P(("dp", "ctx"), "head")
    return jax.shard_map(
        on_device, mesh=mesh, in_specs=in_specs, out_specs=out_specs, check_vma=False
    )
```

```python
import functools

import jax
import jax.numpy as jnp
from jax import lax
from jax.experimental import pallas as pl
from jax.experimental.pallas import tpu as pltpu
from jax.sharding import PartitionSpec as P

HEAD_DIM = 256
NEG_FILL = -1e30
F32 = jnp.float32
BF16 = jnp.bfloat16
LANES = 128
SCALE = HEAD_DIM**-0.5
VMEM = pl.BlockSpec(memory_space=pltpu.VMEM)
HBM = pl.BlockSpec(memory_space=pltpu.HBM)


def ring_order(count):
    return list(range(0, count, 2)) + list(range(1, count, 2))[::-1]


def links_of(count):
    if count == 2:
        return [[(0, 1), (1, 0)]]
    return [[(i, i + 1) for i in range(count - 1)], [(i + 1, i) for i in range(count - 1)]]


def dot_t(a, b):
    return lax.dot_general(a, b, (((1,), (1,)), ((), ())), preferred_element_type=F32)


def dot(a, b):
    return jnp.dot(a, b, preferred_element_type=F32)


def head_columns(h):
    return slice(h * HEAD_DIM, (h + 1) * HEAD_DIM)


def down_lanes(row):
    return jnp.transpose(jnp.broadcast_to(row, (LANES, row.shape[1])))


def same_mark(down, row):
    return jnp.concatenate([down == row[:, i : i + LANES] for i in range(0, row.shape[1], LANES)], axis=1)


def softmax_block(scores, same):
    scores = jnp.where(same, scores * SCALE, NEG_FILL)
    top = jnp.max(scores, axis=1, keepdims=True)
    weights = jnp.exp(scores - top)
    return top, weights, jnp.sum(weights, axis=1, keepdims=True)


def call(kernel, name, outs, operands, flops=0, exps=0, specs=None, scratch=(), limit=8 << 20):
    out_shape = [jax.ShapeDtypeStruct(*o) for o in outs]
    moved = sum(x.size * x.dtype.itemsize for x in [*operands, *out_shape])
    return pl.pallas_call(
        kernel,
        in_specs=specs or [VMEM] * len(operands),
        out_specs=[VMEM] * len(outs),
        out_shape=out_shape,
        scratch_shapes=list(scratch),
        compiler_params=pltpu.CompilerParams(vmem_limit_bytes=limit),
        cost_estimate=pl.CostEstimate(flops=flops, bytes_accessed=moved, transcendentals=exps),
        name=name,
    )(*operands)


def fetch_kernel(count, *refs):
    sources, targets, sems = refs[:count], refs[count : 2 * count], refs[-1]
    copies = [pltpu.make_async_copy(s, t, sems.at[i]) for i, (s, t) in enumerate(zip(sources, targets))]
    for copy in copies:
        copy.start()
    for copy in copies:
        copy.wait()


def fetch(*arrays):
    return call(
        functools.partial(fetch_kernel, len(arrays)),
        "fetch",
        [(x.shape, x.dtype) for x in arrays],
        [pltpu.with_memory_space_constraint(x, pltpu.HBM) for x in arrays],
        specs=[HBM] * len(arrays),
        scratch=[pltpu.SemaphoreType.DMA((len(arrays),))],
    )


def pack_kernel(*refs):
    sources, out_ref, sems = refs[:-2], refs[-2], refs[-1]
    copies, row = [], 0
    for i, source in enumerate(sources):
        rows = source.shape[0]
        copies.append(pltpu.make_async_copy(source, out_ref.at[pl.ds(row, rows), :], sems.at[i]))
        row += rows
    for copy in copies:
        copy.start()
    for copy in copies:
        copy.wait()


def pack(*arrays):
    rows = sum(x.shape[0] for x in arrays)
    return call(
        pack_kernel,
        "pack",
        [((rows, arrays[0].shape[1]), arrays[0].dtype)],
        [pltpu.with_memory_space_constraint(x, pltpu.HBM) for x in arrays],
        specs=[HBM] * len(arrays),
        scratch=[pltpu.SemaphoreType.DMA((len(arrays),))],
    )[0]


def attend_kernel(blocks, first, *refs):
    marks, q_ref = refs[:blocks], refs[blocks]
    keys, values = refs[blocks + 1 : 2 * blocks + 1], refs[2 * blocks + 1 : 3 * blocks + 1]
    out_ref = refs[-1]
    down = down_lanes(marks[0][...])
    same = jnp.concatenate([same_mark(down, m[...]) for m in marks], axis=1)
    rows = q_ref.shape[0]
    for h in range(out_ref.shape[1] // HEAD_DIM):
        at = head_columns(first + h)
        scores = jnp.concatenate([dot_t(q_ref[:, at], k[:, at]) for k in keys], axis=1)
        _, weights, total = softmax_block(scores, same)
        rounded = weights.astype(BF16)
        summed = sum(dot(rounded[:, i * rows : (i + 1) * rows], v[:, at]) for i, v in enumerate(values))
        out_ref[:, head_columns(h)] = (summed / total).astype(BF16)


def encoder_attend(query, keys, values, marks, first, heads):
    rows = query.shape[0]
    pairs = rows * rows * len(keys) * heads
    return call(
        functools.partial(attend_kernel, len(keys), first),
        "encoder_attend",
        [((rows, heads * HEAD_DIM), BF16)],
        [*marks, query, *keys, *values],
        flops=4 * pairs * HEAD_DIM,
        exps=pairs,
    )[0]


def in_shard(shards, shard, act):
    if len(shards) == 1:
        act(shards[0])
    else:
        for i, maps in enumerate(shards):
            pl.when(shard == i)(functools.partial(act, maps))


def halve_kernel(source, *outs):
    width = outs[0].shape[1]
    for i, out in enumerate(outs):
        out[...] = source[:, i * width : (i + 1) * width]


def halve(chunk):
    rows, width = chunk.shape
    return call(halve_kernel, "halve", [((rows, width // 2), chunk.dtype)] * 2, [chunk], flops=3 * 10**10)


def project_kernel(chunks, shards, map_rows, has_acc, place, *refs):
    e_refs, maps, out_ref = refs[:chunks], refs[chunks : chunks + shards], refs[-1]
    half = out_ref.shape[1] // 2
    depth = e_refs[0].shape[1]
    shard, row = place()
    row = pl.multiple_of(row, depth)
    chunk = jnp.concatenate([r[...] for r in e_refs], axis=1)

    def add(map_ref):
        for side in range(2):
            columns = slice(side * half, (side + 1) * half)
            product = dot(chunk, map_ref[pl.ds(side * map_rows + row, depth * chunks), :])
            out_ref[:, columns] = refs[-2][:, columns] + product if has_acc else product

    in_shard(maps, shard, add)


def project(acc, chunks, place, shards, map_rows):
    rows, depth = chunks[0].shape
    width = shards[0].shape[1]
    operands = [*chunks, *shards] + ([] if acc is None else [acc])
    return call(
        functools.partial(project_kernel, len(chunks), len(shards), map_rows, acc is not None, place),
        "project",
        [((rows, 2 * width), F32)],
        operands,
        flops=4 * rows * depth * width * len(chunks),
    )[0]


def prepare_kernel(shards, parts, map_rows, step, place, *refs):
    maps, marks, near = refs[:shards], refs[shards : shards + parts], refs[shards + parts : -4]
    map_ref, tgt_ref, mask_ref, down_ref = refs[-4:]
    shard, row = place()
    depth, width = map_ref.shape[0], map_ref.shape[1] // 2
    row = pl.multiple_of(row, depth)

    def copy(source):
        for side in range(2):
            map_ref[:, side * width : (side + 1) * width] = source[pl.ds(side * map_rows + row, depth), :]

    in_shard(maps, shard, copy)
    own = marks[0][...]
    count = tgt_ref.shape[0] // parts
    below = slice(2 * map_rows, 2 * map_rows + count)
    targets = [maps[0][below, :]] + ([r[...] for r in near] if near else [m[below, :] for m in maps[1:]])
    for i, (target, mark_ref) in enumerate(zip(targets, marks)):
        part = slice(i * count, (i + 1) * count)
        tgt_ref[part, :] = target
        down_ref[...] = down_lanes(mark_ref[...])
        down = down_ref[pl.ds(0, count, stride=step), :]
        mask_ref[part, :] = same_mark(down, own).astype(F32)


def prepare(place, depth, shards, map_rows, count, near_targets, marks):
    rows, width = marks[0].shape[1], shards[0].shape[1]
    total = count * len(marks)
    return call(
        functools.partial(prepare_kernel, len(shards), len(marks), map_rows, rows // count, place),
        "prepare",
        [((depth, 2 * width), BF16), ((total, width), BF16), ((total, rows), F32)],
        [*shards, *marks, *near_targets],
        scratch=[pltpu.VMEM((rows, LANES), jnp.int32)],
    )


def cross_kernel(acc_ref, e_ref, map_ref, tgt_ref, mask_ref, *outs):
    half = map_ref.shape[1] // 2
    heads = half // HEAD_DIM
    count = outs[0].shape[0]
    chunk = e_ref[...]

    def memory(at):
        return (acc_ref[:, at] + dot(chunk, map_ref[:, at])).astype(BF16)

    lane = lax.broadcasted_iota(jnp.int32, (tgt_ref.shape[0], LANES), 1)
    stats = jnp.zeros(lane.shape, F32)
    same = mask_ref[...] > 0
    keys = [memory(head_columns(h)) for h in range(heads)]
    values = [memory(head_columns(heads + h)) for h in range(heads)]
    for h in range(heads):
        at = head_columns(h)
        top, weights, total = softmax_block(dot_t(tgt_ref[:, at], keys[h]), same)
        summed = dot(weights.astype(BF16), values[h])
        for i, out_ref in enumerate(outs):
            out_ref[:, at] = summed[i * count : (i + 1) * count]
        stats = jnp.where(lane == h, top, jnp.where(lane == heads + h, total, stats))
    for i, out_ref in enumerate(outs):
        out_ref[:, half:] = stats[i * count : (i + 1) * count]


def cross_attend(acc, chunk, maps, targets, mask, parts):
    width = targets.shape[1]
    count = targets.shape[0] // parts
    return call(
        cross_kernel,
        "cross_attend",
        [((count, width + LANES), F32)] * parts,
        [acc, chunk, maps, targets, mask],
        flops=2 * chunk.size * 2 * width,
    )


def combine_kernel(*refs):
    parts, out_ref = refs[:-1], refs[-1]
    width = out_ref.shape[1]
    heads = width // HEAD_DIM
    for h in range(heads):
        at = head_columns(h)
        tops = [r[:, width + h : width + h + 1] for r in parts]
        top = functools.reduce(jnp.maximum, tops)
        factors = [jnp.exp(t - top) for t in tops]
        total = sum(f * r[:, width + heads + h : width + heads + h + 1] for f, r in zip(factors, parts))
        summed = sum(f * r[:, at] for f, r in zip(factors, parts))
        out_ref[:, at] = (summed / total).astype(BF16)


def on_device(enc_query, enc_key, enc_value, doc_ids, key_map, value_map, tgt_query):
    rows, features = enc_query.shape
    tgt_rows, width = tgt_query.shape
    n_ctx, n_head = lax.axis_size("ctx"), lax.axis_size("head")
    links = links_of(n_ctx)
    bring = lambda x: [lax.ppermute(x, "ctx", pairs) for pairs in links]

    marks = (doc_ids if n_ctx == 2 else doc_ids + 1).reshape(1, rows)
    keys, values, near_marks = bring(enc_key), bring(enc_value), bring(marks)
    query, own_key, own_value, marks = fetch(enc_query, enc_key, enc_value, marks)
    near_targets = []
    if n_ctx == 2:
        own_maps = pack(key_map, value_map, tgt_query)
        shards = [own_maps, *bring(own_maps)]
    else:
        whole = [lax.all_gather(x, "ctx", axis=0, tiled=True) for x in (key_map, value_map)]
        shards, near_targets = [pack(*whole, tgt_query)], bring(tgt_query)
    map_rows = (shards[0].shape[0] - tgt_rows) // 2

    chunks = 2
    heads = features // HEAD_DIM // chunks
    held = [
        encoder_attend(query, [own_key, *keys], [own_value, *values], [marks, *near_marks], j * heads, heads)
        for j in range(chunks)
    ]

    order = ring_order(n_head)
    ring = [(order[i], order[(i + 1) % n_head]) for i in range(n_head)]
    before = {target: source for source, target in ring}

    def place(turn, first):
        head, ctx = lax.axis_index("head"), lax.axis_index("ctx")
        owner = 0
        for i in range(n_head):
            source = i
            for _ in range(turn):
                source = before[source]
            owner = owner + jnp.where(head == i, source, 0)
        row = owner * features + first
        if len(shards) == 1:
            return None, row
        return jnp.where(lax.div(row, map_rows) == ctx, 0, 1), lax.rem(row, map_rows)

    acc, last = None, n_head - 1
    for turn in range(last):
        if turn == last - 1:
            pieces = [p for h in held for p in halve(h)]
        else:
            pieces = held
        later = [lax.ppermute(p, "head", ring) for p in pieces]
        acc = project(acc, held, functools.partial(place, turn, 0), shards, map_rows)
        held = later
    acc = project(acc, held[:-1], functools.partial(place, last, 0), shards, map_rows)
    depth = held[-1].shape[1]
    last_maps, targets, mask = prepare(
        functools.partial(place, last, features - depth),
        depth,
        shards,
        map_rows,
        tgt_rows,
        near_targets,
        [marks, *near_marks],
    )
    parts = cross_attend(acc, held[-1], last_maps, targets, mask, 1 + len(links))

    combined = [parts[0]]
    for i, (pairs, piece) in enumerate(zip(links, parts[1:])):
        other = lax.ppermute(piece, "ctx", [(target, source) for source, target in pairs])
        if n_ctx > 2:
            end = n_ctx - 1 if i == 0 else 0
            column = lax.broadcasted_iota(jnp.int32, other.shape, 1)
            other = jnp.where((lax.axis_index("ctx") == end) & (column >= width), NEG_FILL, other)
        combined.append(other)
    return call(combine_kernel, "combine", [((tgt_rows, width), BF16)], combined, limit=4 << 20)[0]


def solution(mesh):
    in_specs = (
        P(("dp", "ctx"), "head"),
        P(("dp", "ctx"), "head"),
        P(("dp", "ctx"), "head"),
        P(("dp", "ctx")),
        P("ctx", "head"),
        P("ctx", "head"),
        P(("dp", "ctx"), "head"),
    )
    out_specs = P(("dp", "ctx"), "head")
    return jax.shard_map(
        on_device, mesh=mesh, in_specs=in_specs, out_specs=out_specs, check_vma=False
    )
```

```python
import functools

import jax
import jax.numpy as jnp
from jax import lax
from jax.experimental import pallas as pl
from jax.experimental.pallas import tpu as pltpu
from jax.sharding import PartitionSpec as P

HEAD_DIM = 256
NEG_FILL = -1e30
F32 = jnp.float32
BF16 = jnp.bfloat16
LANES = 128
SCALE = HEAD_DIM**-0.5
WEIGH_FLOPS = 6 * 10**9
VMEM = pl.BlockSpec(memory_space=pltpu.VMEM)
HBM = pl.BlockSpec(memory_space=pltpu.HBM)


def ring_order(count):
    return list(range(0, count, 2)) + list(range(1, count, 2))[::-1]


def links_of(count):
    if count == 2:
        return [[(0, 1), (1, 0)]]
    return [[(i, i + 1) for i in range(count - 1)], [(i + 1, i) for i in range(count - 1)]]


def dot_t(a, b):
    return lax.dot_general(a, b, (((1,), (1,)), ((), ())), preferred_element_type=F32)


def dot(a, b):
    return jnp.dot(a, b, preferred_element_type=F32)


def head_columns(h):
    return slice(h * HEAD_DIM, (h + 1) * HEAD_DIM)


def down_lanes(row):
    return jnp.transpose(jnp.broadcast_to(row, (LANES, row.shape[1])))


def same_mark(down, row):
    return jnp.concatenate([down == row[:, i : i + LANES] for i in range(0, row.shape[1], LANES)], axis=1)


def softmax_block(scores, same):
    scores = jnp.where(same, scores * SCALE, NEG_FILL)
    top = jnp.max(scores, axis=1, keepdims=True)
    weights = jnp.exp(scores - top)
    return top, weights, jnp.sum(weights, axis=1, keepdims=True)


def call(kernel, name, outs, operands, flops=0, exps=0, specs=None, scratch=(), limit=8 << 20):
    out_shape = [jax.ShapeDtypeStruct(*o) for o in outs]
    moved = sum(x.size * x.dtype.itemsize for x in [*operands, *out_shape])
    return pl.pallas_call(
        kernel,
        in_specs=specs or [VMEM] * len(operands),
        out_specs=[VMEM] * len(outs),
        out_shape=out_shape,
        scratch_shapes=list(scratch),
        compiler_params=pltpu.CompilerParams(vmem_limit_bytes=limit),
        cost_estimate=pl.CostEstimate(flops=flops, bytes_accessed=moved, transcendentals=exps),
        name=name,
    )(*operands)


def fetch_kernel(count, *refs):
    sources, targets, sems = refs[:count], refs[count : 2 * count], refs[-1]
    copies = [pltpu.make_async_copy(s, t, sems.at[i]) for i, (s, t) in enumerate(zip(sources, targets))]
    for copy in copies:
        copy.start()
    for copy in copies:
        copy.wait()


def fetch(*arrays):
    return call(
        functools.partial(fetch_kernel, len(arrays)),
        "fetch",
        [(x.shape, x.dtype) for x in arrays],
        [pltpu.with_memory_space_constraint(x, pltpu.HBM) for x in arrays],
        specs=[HBM] * len(arrays),
        scratch=[pltpu.SemaphoreType.DMA((len(arrays),))],
    )


def pack_kernel(*refs):
    sources, out_ref, sems = refs[:-2], refs[-2], refs[-1]
    copies, row = [], 0
    for i, source in enumerate(sources):
        rows = source.shape[0]
        copies.append(pltpu.make_async_copy(source, out_ref.at[pl.ds(row, rows), :], sems.at[i]))
        row += rows
    for copy in copies:
        copy.start()
    for copy in copies:
        copy.wait()


def pack(*arrays):
    rows = sum(x.shape[0] for x in arrays)
    return call(
        pack_kernel,
        "pack",
        [((rows, arrays[0].shape[1]), arrays[0].dtype)],
        [pltpu.with_memory_space_constraint(x, pltpu.HBM) for x in arrays],
        specs=[HBM] * len(arrays),
        scratch=[pltpu.SemaphoreType.DMA((len(arrays),))],
    )[0]


def weigh_kernel(blocks, first, heads, fetches, *refs):
    marks, q_ref, keys = refs[:blocks], refs[blocks], refs[blocks + 1 : 2 * blocks + 1]
    rest = refs[2 * blocks + 1 :]
    weight_ref, total_ref = rest[fetches : fetches + 2]
    if fetches:
        copy = pltpu.make_async_copy(rest[0], rest[-2], rest[-1])
        copy.start()
    down = down_lanes(marks[0][...])
    same = jnp.concatenate([same_mark(down, m[...]) for m in marks], axis=1)
    span = same.shape[1]
    lane = lax.broadcasted_iota(jnp.int32, total_ref.shape, 1)
    totals = jnp.zeros(total_ref.shape, F32)
    for h in range(heads):
        at = head_columns(first + h)
        scores = jnp.concatenate([dot_t(q_ref[:, at], k[:, at]) for k in keys], axis=1)
        _, weights, total = softmax_block(scores, same)
        weight_ref[:, h * span : (h + 1) * span] = weights.astype(BF16)
        totals = jnp.where(lane == h, total, totals)
    total_ref[...] = totals
    if fetches:
        copy.wait()


def weigh(query, keys, marks, first, heads, fetched=None):
    rows, span = query.shape[0], query.shape[0] * len(keys)
    outs = [((rows, heads * span), BF16), ((rows, LANES), F32)]
    operands = [*marks, query, *keys]
    specs, scratch = [VMEM] * len(operands), []
    if fetched is not None:
        operands.append(pltpu.with_memory_space_constraint(fetched, pltpu.HBM))
        specs.append(HBM)
        outs.append((fetched.shape, fetched.dtype))
        scratch.append(pltpu.SemaphoreType.DMA)
    return call(
        functools.partial(weigh_kernel, len(keys), first, heads, len(scratch)),
        "weigh",
        outs,
        operands,
        flops=WEIGH_FLOPS,
        exps=rows * span * heads,
        specs=specs,
        scratch=scratch,
    )


def mix_kernel(first, heads, weight_ref, total_ref, *refs):
    values, out_ref = refs[:-1], refs[-1]
    rows = total_ref.shape[0]
    for h in range(heads):
        start = h * rows * len(values)
        summed = sum(
            dot(weight_ref[:, start + i * rows : start + (i + 1) * rows], v[:, head_columns(first + h)])
            for i, v in enumerate(values)
        )
        out_ref[:, head_columns(h)] = (summed / total_ref[:, h : h + 1]).astype(BF16)


def mix(weights, totals, values, first, heads):
    rows = totals.shape[0]
    return call(
        functools.partial(mix_kernel, first, heads),
        "mix",
        [((rows, heads * HEAD_DIM), BF16)],
        [weights, totals, *values],
        flops=2 * weights.size * HEAD_DIM,
    )[0]


def in_shard(shards, shard, act):
    if len(shards) == 1:
        act(shards[0])
    else:
        for i, maps in enumerate(shards):
            pl.when(shard == i)(functools.partial(act, maps))


def halve_kernel(source, *outs):
    width = outs[0].shape[1]
    for i, out in enumerate(outs):
        out[...] = source[:, i * width : (i + 1) * width]


def halve(chunk):
    rows, width = chunk.shape
    return call(halve_kernel, "halve", [((rows, width // 2), chunk.dtype)] * 2, [chunk], flops=3 * 10**10)


def project_kernel(chunks, shards, map_rows, has_acc, place, *refs):
    e_refs, maps, out_ref = refs[:chunks], refs[chunks : chunks + shards], refs[-1]
    half = out_ref.shape[1] // 2
    depth = e_refs[0].shape[1]
    shard, row = place()
    row = pl.multiple_of(row, depth)
    chunk = jnp.concatenate([r[...] for r in e_refs], axis=1)

    def add(map_ref):
        for side in range(2):
            columns = slice(side * half, (side + 1) * half)
            product = dot(chunk, map_ref[pl.ds(side * map_rows + row, depth * chunks), :])
            out_ref[:, columns] = refs[-2][:, columns] + product if has_acc else product

    in_shard(maps, shard, add)


def project(acc, chunks, place, shards, map_rows):
    rows, depth = chunks[0].shape
    width = shards[0].shape[1]
    operands = [*chunks, *shards] + ([] if acc is None else [acc])
    return call(
        functools.partial(project_kernel, len(chunks), len(shards), map_rows, acc is not None, place),
        "project",
        [((rows, 2 * width), F32)],
        operands,
        flops=4 * rows * depth * width * len(chunks),
    )[0]


def prepare_kernel(shards, parts, map_rows, step, place, *refs):
    maps, marks, near = refs[:shards], refs[shards : shards + parts], refs[shards + parts : -4]
    map_ref, tgt_ref, mask_ref, down_ref = refs[-4:]
    shard, row = place()
    depth, width = map_ref.shape[0], map_ref.shape[1] // 2
    row = pl.multiple_of(row, depth)

    def copy(source):
        for side in range(2):
            map_ref[:, side * width : (side + 1) * width] = source[pl.ds(side * map_rows + row, depth), :]

    in_shard(maps, shard, copy)
    own = marks[0][...]
    count = tgt_ref.shape[0] // parts
    below = slice(2 * map_rows, 2 * map_rows + count)
    targets = [maps[0][below, :]] + ([r[...] for r in near] if near else [m[below, :] for m in maps[1:]])
    for i, (target, mark_ref) in enumerate(zip(targets, marks)):
        part = slice(i * count, (i + 1) * count)
        tgt_ref[part, :] = target
        down_ref[...] = down_lanes(mark_ref[...])
        down = down_ref[pl.ds(0, count, stride=step), :]
        mask_ref[part, :] = same_mark(down, own).astype(F32)


def prepare(place, depth, shards, map_rows, count, near_targets, marks):
    rows, width = marks[0].shape[1], shards[0].shape[1]
    total = count * len(marks)
    return call(
        functools.partial(prepare_kernel, len(shards), len(marks), map_rows, rows // count, place),
        "prepare",
        [((depth, 2 * width), BF16), ((total, width), BF16), ((total, rows), F32)],
        [*shards, *marks, *near_targets],
        scratch=[pltpu.VMEM((rows, LANES), jnp.int32)],
    )


def cross_part(queries, keys, values, same, out_ref):
    heads = len(keys)
    lane = lax.broadcasted_iota(jnp.int32, (out_ref.shape[0], LANES), 1)
    stats = jnp.zeros(lane.shape, F32)
    for h in range(heads):
        at = head_columns(h)
        top, weights, total = softmax_block(dot_t(queries[:, at], keys[h]), same)
        out_ref[:, at] = dot(weights.astype(BF16), values[h])
        stats = jnp.where(lane == h, top, jnp.where(lane == heads + h, total, stats))
    out_ref[:, heads * HEAD_DIM :] = stats


def cross_near_kernel(acc_ref, e_ref, map_ref, tgt_ref, mask_ref, mem_ref, *outs):
    heads = map_ref.shape[1] // 2 // HEAD_DIM
    chunk = e_ref[...]
    memory = []
    for h in range(2 * heads):
        at = head_columns(h)
        memory.append((acc_ref[:, at] + dot(chunk, map_ref[:, at])).astype(BF16))
    count = outs[0].shape[0]
    for i, out_ref in enumerate(outs):
        part = slice((i + 1) * count, (i + 2) * count)
        cross_part(tgt_ref[part, :], memory[:heads], memory[heads:], mask_ref[part, :] > 0, out_ref)
    for h in range(2 * heads):
        mem_ref[:, head_columns(h)] = memory[h]


def cross_near(acc, chunk, maps, targets, mask, parts):
    rows, width = acc.shape[0], targets.shape[1]
    return call(
        cross_near_kernel,
        "cross_near",
        [((rows, 2 * width), BF16)] + [((targets.shape[0] // parts, width + LANES), F32)] * (parts - 1),
        [acc, chunk, maps, targets, mask],
        flops=2 * chunk.size * 2 * width,
    )


def cross_own_kernel(mem_ref, tgt_ref, mask_ref, out_ref):
    heads = mem_ref.shape[1] // 2 // HEAD_DIM
    memory = [mem_ref[:, head_columns(h)] for h in range(2 * heads)]
    part = slice(0, out_ref.shape[0])
    cross_part(tgt_ref[part, :], memory[:heads], memory[heads:], mask_ref[part, :] > 0, out_ref)


def cross_own(memory, targets, mask, parts):
    width = targets.shape[1]
    return call(
        cross_own_kernel,
        "cross_own",
        [((targets.shape[0] // parts, width + LANES), F32)],
        [memory, targets, mask],
        flops=4 * targets.size * memory.shape[0] // parts,
    )[0]


def combine_kernel(*refs):
    parts, out_ref = refs[:-1], refs[-1]
    width = out_ref.shape[1]
    heads = width // HEAD_DIM
    for h in range(heads):
        at = head_columns(h)
        tops = [r[:, width + h : width + h + 1] for r in parts]
        top = functools.reduce(jnp.maximum, tops)
        factors = [jnp.exp(t - top) for t in tops]
        total = sum(f * r[:, width + heads + h : width + heads + h + 1] for f, r in zip(factors, parts))
        summed = sum(f * r[:, at] for f, r in zip(factors, parts))
        out_ref[:, at] = (summed / total).astype(BF16)


def on_device(enc_query, enc_key, enc_value, doc_ids, key_map, value_map, tgt_query):
    rows, features = enc_query.shape
    tgt_rows, width = tgt_query.shape
    n_ctx, n_head = lax.axis_size("ctx"), lax.axis_size("head")
    links = links_of(n_ctx)
    bring = lambda x: [lax.ppermute(x, "ctx", pairs) for pairs in links]

    marks = (doc_ids if n_ctx == 2 else doc_ids + 1).reshape(1, rows)
    keys, near_marks, values = bring(enc_key), bring(marks), bring(enc_value)
    query, own_key, marks = fetch(enc_query, enc_key, marks)
    near_targets = []
    if n_ctx == 2:
        own_maps = pack(key_map, value_map, tgt_query)
        shards = [own_maps, *bring(own_maps)]
    else:
        whole = [lax.all_gather(x, "ctx", axis=0, tiled=True) for x in (key_map, value_map)]
        shards, near_targets = [pack(*whole, tgt_query)], bring(tgt_query)
    map_rows = (shards[0].shape[0] - tgt_rows) // 2

    chunks = 2
    heads = features // HEAD_DIM // chunks
    held = [None] * chunks
    own_value = None
    for j in reversed(range(chunks)):
        weights, totals, *fetched = weigh(
            query,
            [own_key, *keys],
            [marks, *near_marks],
            j * heads,
            heads,
            enc_value if own_value is None else None,
        )
        own_value = fetched[0] if fetched else own_value
        held[j] = mix(weights, totals, [own_value, *values], j * heads, heads)

    order = ring_order(n_head)
    ring = [(order[i], order[(i + 1) % n_head]) for i in range(n_head)]
    before = {target: source for source, target in ring}

    def place(turn, first):
        head, ctx = lax.axis_index("head"), lax.axis_index("ctx")
        owner = 0
        for i in range(n_head):
            source = i
            for _ in range(turn):
                source = before[source]
            owner = owner + jnp.where(head == i, source, 0)
        row = owner * features + first
        if len(shards) == 1:
            return None, row
        return jnp.where(lax.div(row, map_rows) == ctx, 0, 1), lax.rem(row, map_rows)

    acc, last = None, n_head - 1
    for turn in range(last):
        if turn == last - 1:
            pieces = [p for h in held for p in halve(h)]
        else:
            pieces = held
        later = [lax.ppermute(p, "head", ring) for p in pieces]
        acc = project(acc, held, functools.partial(place, turn, 0), shards, map_rows)
        held = later
    acc = project(acc, held[:-1], functools.partial(place, last, 0), shards, map_rows)
    depth = held[-1].shape[1]
    last_maps, targets, mask = prepare(
        functools.partial(place, last, features - depth),
        depth,
        shards,
        map_rows,
        tgt_rows,
        near_targets,
        [marks, *near_marks],
    )
    parts = 1 + len(links)
    memory, *shares = cross_near(acc, held[-1], last_maps, targets, mask, parts)
    combined = [cross_own(memory, targets, mask, parts)]
    for i, (pairs, piece) in enumerate(zip(links, shares)):
        other = lax.ppermute(piece, "ctx", [(target, source) for source, target in pairs])
        if n_ctx > 2:
            end = n_ctx - 1 if i == 0 else 0
            column = lax.broadcasted_iota(jnp.int32, other.shape, 1)
            other = jnp.where((lax.axis_index("ctx") == end) & (column >= width), NEG_FILL, other)
        combined.append(other)
    return call(combine_kernel, "combine", [((tgt_rows, width), BF16)], combined, limit=4 << 20)[0]


def solution(mesh):
    in_specs = (
        P(("dp", "ctx"), "head"),
        P(("dp", "ctx"), "head"),
        P(("dp", "ctx"), "head"),
        P(("dp", "ctx")),
        P("ctx", "head"),
        P("ctx", "head"),
        P(("dp", "ctx"), "head"),
    )
    out_specs = P(("dp", "ctx"), "head")
    return jax.shard_map(
        on_device, mesh=mesh, in_specs=in_specs, out_specs=out_specs, check_vma=False
    )
```

```python
import functools

import jax
import jax.numpy as jnp
from jax import lax
from jax.experimental import pallas as pl
from jax.experimental.pallas import tpu as pltpu
from jax.sharding import PartitionSpec as P

HEAD_DIM = 256
NEG_FILL = -1e30
F32 = jnp.float32
BF16 = jnp.bfloat16
LANES = 128
SCALE = HEAD_DIM**-0.5
WEIGH_FLOPS = 6 * 10**9
VMEM = pl.BlockSpec(memory_space=pltpu.VMEM)
HBM = pl.BlockSpec(memory_space=pltpu.HBM)


def ring_order(count):
    return list(range(0, count, 2)) + list(range(1, count, 2))[::-1]


def links_of(count):
    if count == 2:
        return [[(0, 1), (1, 0)]]
    return [[(i, i + 1) for i in range(count - 1)], [(i + 1, i) for i in range(count - 1)]]


def dot_t(a, b):
    return lax.dot_general(a, b, (((1,), (1,)), ((), ())), preferred_element_type=F32)


def dot(a, b):
    return jnp.dot(a, b, preferred_element_type=F32)


def head_columns(h):
    return slice(h * HEAD_DIM, (h + 1) * HEAD_DIM)


def down_lanes(row):
    return jnp.transpose(jnp.broadcast_to(row, (LANES, row.shape[1])))


def same_mark(down, row):
    return jnp.concatenate([down == row[:, i : i + LANES] for i in range(0, row.shape[1], LANES)], axis=1)


def softmax_block(scores, same):
    scores = jnp.where(same, scores * SCALE, NEG_FILL)
    top = jnp.max(scores, axis=1, keepdims=True)
    weights = jnp.exp(scores - top)
    return top, weights, jnp.sum(weights, axis=1, keepdims=True)


def call(kernel, name, outs, operands, flops=0, exps=0, specs=None, scratch=(), limit=8 << 20):
    out_shape = [jax.ShapeDtypeStruct(*o) for o in outs]
    moved = sum(x.size * x.dtype.itemsize for x in [*operands, *out_shape])
    return pl.pallas_call(
        kernel,
        in_specs=specs or [VMEM] * len(operands),
        out_specs=[VMEM] * len(outs),
        out_shape=out_shape,
        scratch_shapes=list(scratch),
        compiler_params=pltpu.CompilerParams(vmem_limit_bytes=limit),
        cost_estimate=pl.CostEstimate(flops=flops, bytes_accessed=moved, transcendentals=exps),
        name=name,
    )(*operands)


def copies_of(source, target, sems, first, parts=4):
    rows = source.shape[0]
    parts = parts if rows % (16 * parts) == 0 else 1
    step = rows // parts
    made = []
    for i in range(parts):
        at = pl.ds(i * step, step)
        made.append(pltpu.make_async_copy(source.at[at, :], target.at[at, :], sems.at[first + i]))
    return made


def run_all(copies):
    for copy in copies:
        copy.start()
    for copy in copies:
        copy.wait()


def fetch_kernel(count, *refs):
    sources, targets, sems = refs[:count], refs[count : 2 * count], refs[-1]
    copies = []
    for source, target in zip(sources, targets):
        copies += copies_of(source, target, sems, len(copies))
    run_all(copies)


def fetch(*arrays):
    return call(
        functools.partial(fetch_kernel, len(arrays)),
        "fetch",
        [(x.shape, x.dtype) for x in arrays],
        [pltpu.with_memory_space_constraint(x, pltpu.HBM) for x in arrays],
        specs=[HBM] * len(arrays),
        scratch=[pltpu.SemaphoreType.DMA((4 * len(arrays),))],
    )


def pack_kernel(*refs):
    sources, out_ref, sems = refs[:-2], refs[-2], refs[-1]
    copies, row = [], 0
    for source in sources:
        rows = source.shape[0]
        copies += copies_of(source, out_ref.at[pl.ds(row, rows), :], sems, len(copies))
        row += rows
    run_all(copies)


def pack(*arrays):
    rows = sum(x.shape[0] for x in arrays)
    return call(
        pack_kernel,
        "pack",
        [((rows, arrays[0].shape[1]), arrays[0].dtype)],
        [pltpu.with_memory_space_constraint(x, pltpu.HBM) for x in arrays],
        specs=[HBM] * len(arrays),
        scratch=[pltpu.SemaphoreType.DMA((4 * len(arrays),))],
    )[0]


def weigh_kernel(blocks, first, heads, fetches, *refs):
    marks, q_ref, keys = refs[:blocks], refs[blocks], refs[blocks + 1 : 2 * blocks + 1]
    rest = refs[2 * blocks + 1 :]
    weight_ref, total_ref = rest[fetches : fetches + 2]
    if fetches:
        copies = copies_of(rest[0], rest[-2], rest[-1], 0)
        for copy in copies:
            copy.start()
    down = down_lanes(marks[0][...])
    same = jnp.concatenate([same_mark(down, m[...]) for m in marks], axis=1)
    span = same.shape[1]
    lane = lax.broadcasted_iota(jnp.int32, total_ref.shape, 1)
    totals = jnp.zeros(total_ref.shape, F32)
    for h in range(heads):
        at = head_columns(first + h)
        scores = jnp.concatenate([dot_t(q_ref[:, at], k[:, at]) for k in keys], axis=1)
        _, weights, total = softmax_block(scores, same)
        weight_ref[:, h * span : (h + 1) * span] = weights.astype(BF16)
        totals = jnp.where(lane == h, total, totals)
    total_ref[...] = totals
    if fetches:
        for copy in copies:
            copy.wait()


def weigh(query, keys, marks, first, heads, fetched=None):
    rows, span = query.shape[0], query.shape[0] * len(keys)
    outs = [((rows, heads * span), BF16), ((rows, LANES), F32)]
    operands = [*marks, query, *keys]
    specs, scratch = [VMEM] * len(operands), []
    if fetched is not None:
        operands.append(pltpu.with_memory_space_constraint(fetched, pltpu.HBM))
        specs.append(HBM)
        outs.append((fetched.shape, fetched.dtype))
        scratch.append(pltpu.SemaphoreType.DMA((4,)))
    return call(
        functools.partial(weigh_kernel, len(keys), first, heads, len(scratch)),
        "weigh",
        outs,
        operands,
        flops=WEIGH_FLOPS,
        exps=rows * span * heads,
        specs=specs,
        scratch=scratch,
    )


def mix_kernel(first, heads, weight_ref, total_ref, *refs):
    values, out_ref = refs[:-1], refs[-1]
    rows = total_ref.shape[0]
    for h in range(heads):
        start = h * rows * len(values)
        summed = sum(
            dot(weight_ref[:, start + i * rows : start + (i + 1) * rows], v[:, head_columns(first + h)])
            for i, v in enumerate(values)
        )
        out_ref[:, head_columns(h)] = (summed / total_ref[:, h : h + 1]).astype(BF16)


def mix(weights, totals, values, first, heads):
    rows = totals.shape[0]
    return call(
        functools.partial(mix_kernel, first, heads),
        "mix",
        [((rows, heads * HEAD_DIM), BF16)],
        [weights, totals, *values],
        flops=2 * weights.size * HEAD_DIM,
    )[0]


def in_shard(shards, shard, act):
    if len(shards) == 1:
        act(shards[0])
    else:
        for i, maps in enumerate(shards):
            pl.when(shard == i)(functools.partial(act, maps))


def halve_kernel(source, *outs):
    width = outs[0].shape[1]
    for i, out in enumerate(outs):
        out[...] = source[:, i * width : (i + 1) * width]


def halve(chunk):
    rows, width = chunk.shape
    return call(halve_kernel, "halve", [((rows, width // 2), chunk.dtype)] * 2, [chunk], flops=3 * 10**10)


def project_kernel(chunks, shards, map_rows, has_acc, place, *refs):
    e_refs, maps, out_ref = refs[:chunks], refs[chunks : chunks + shards], refs[-1]
    half = out_ref.shape[1] // 2
    depth = e_refs[0].shape[1]
    shard, row = place()
    row = pl.multiple_of(row, depth)
    chunk = jnp.concatenate([r[...] for r in e_refs], axis=1)

    def add(map_ref):
        for side in range(2):
            columns = slice(side * half, (side + 1) * half)
            product = dot(chunk, map_ref[pl.ds(side * map_rows + row, depth * chunks), :])
            out_ref[:, columns] = refs[-2][:, columns] + product if has_acc else product

    in_shard(maps, shard, add)


def project(acc, chunks, place, shards, map_rows):
    rows, depth = chunks[0].shape
    width = shards[0].shape[1]
    operands = [*chunks, *shards] + ([] if acc is None else [acc])
    return call(
        functools.partial(project_kernel, len(chunks), len(shards), map_rows, acc is not None, place),
        "project",
        [((rows, 2 * width), F32)],
        operands,
        flops=4 * rows * depth * width * len(chunks),
    )[0]


def prepare_kernel(shards, parts, map_rows, step, place, *refs):
    maps, marks, near = refs[:shards], refs[shards : shards + parts], refs[shards + parts : -4]
    map_ref, tgt_ref, mask_ref, down_ref = refs[-4:]
    shard, row = place()
    depth, width = map_ref.shape[0], map_ref.shape[1] // 2
    row = pl.multiple_of(row, depth)

    def copy(source):
        for side in range(2):
            map_ref[:, side * width : (side + 1) * width] = source[pl.ds(side * map_rows + row, depth), :]

    in_shard(maps, shard, copy)
    own = marks[0][...]
    count = tgt_ref.shape[0] // parts
    below = slice(2 * map_rows, 2 * map_rows + count)
    targets = [maps[0][below, :]] + ([r[...] for r in near] if near else [m[below, :] for m in maps[1:]])
    for i, (target, mark_ref) in enumerate(zip(targets, marks)):
        part = slice(i * count, (i + 1) * count)
        tgt_ref[part, :] = target
        down_ref[...] = down_lanes(mark_ref[...])
        down = down_ref[pl.ds(0, count, stride=step), :]
        mask_ref[part, :] = same_mark(down, own).astype(F32)


def prepare(place, depth, shards, map_rows, count, near_targets, marks):
    rows, width = marks[0].shape[1], shards[0].shape[1]
    total = count * len(marks)
    return call(
        functools.partial(prepare_kernel, len(shards), len(marks), map_rows, rows // count, place),
        "prepare",
        [((depth, 2 * width), BF16), ((total, width), BF16), ((total, rows), F32)],
        [*shards, *marks, *near_targets],
        scratch=[pltpu.VMEM((rows, LANES), jnp.int32)],
    )


def cross_kernel(acc_ref, e_ref, map_ref, tgt_ref, mask_ref, *outs):
    heads = map_ref.shape[1] // 2 // HEAD_DIM
    chunk = e_ref[...]
    memory = []
    for h in range(2 * heads):
        at = head_columns(h)
        memory.append((acc_ref[:, at] + dot(chunk, map_ref[:, at])).astype(BF16))
    keys, values = memory[:heads], memory[heads:]
    count = outs[0].shape[0]
    same = mask_ref[...] > 0
    lane = lax.broadcasted_iota(jnp.int32, (same.shape[0], LANES), 1)
    stats = jnp.zeros(lane.shape, F32)
    for h in range(heads):
        at = head_columns(h)
        top, weights, total = softmax_block(dot_t(tgt_ref[:, at], keys[h]), same)
        summed = dot(weights.astype(BF16), values[h])
        for i, out_ref in enumerate(outs):
            out_ref[:, at] = summed[i * count : (i + 1) * count]
        stats = jnp.where(lane == h, top, jnp.where(lane == heads + h, total, stats))
    for i, out_ref in enumerate(outs):
        out_ref[:, heads * HEAD_DIM :] = stats[i * count : (i + 1) * count]


def cross_attend(acc, chunk, maps, targets, mask, parts):
    width = targets.shape[1]
    count = targets.shape[0] // parts
    return call(
        cross_kernel,
        "cross_attend",
        [((count, width + LANES), F32)] * parts,
        [acc, chunk, maps, targets, mask],
        flops=2 * chunk.size * 2 * width,
    )


def combine_kernel(*refs):
    parts, out_ref = refs[:-1], refs[-1]
    width = out_ref.shape[1]
    heads = width // HEAD_DIM
    for h in range(heads):
        at = head_columns(h)
        tops = [r[:, width + h : width + h + 1] for r in parts]
        top = functools.reduce(jnp.maximum, tops)
        factors = [jnp.exp(t - top) for t in tops]
        total = sum(f * r[:, width + heads + h : width + heads + h + 1] for f, r in zip(factors, parts))
        summed = sum(f * r[:, at] for f, r in zip(factors, parts))
        out_ref[:, at] = (summed / total).astype(BF16)


def on_device(enc_query, enc_key, enc_value, doc_ids, key_map, value_map, tgt_query):
    rows, features = enc_query.shape
    tgt_rows, width = tgt_query.shape
    n_ctx, n_head = lax.axis_size("ctx"), lax.axis_size("head")
    links = links_of(n_ctx)
    bring = lambda x: [lax.ppermute(x, "ctx", pairs) for pairs in links]

    marks = (doc_ids if n_ctx == 2 else doc_ids + 1).reshape(1, rows)
    keys, near_marks, values = bring(enc_key), bring(marks), bring(enc_value)
    query, own_key, marks = fetch(enc_query, enc_key, marks)
    near_targets = []
    if n_ctx == 2:
        own_maps = pack(key_map, value_map, tgt_query)
        shards = [own_maps, *bring(own_maps)]
    else:
        whole = [lax.all_gather(x, "ctx", axis=0, tiled=True) for x in (key_map, value_map)]
        shards, near_targets = [pack(*whole, tgt_query)], bring(tgt_query)
    map_rows = (shards[0].shape[0] - tgt_rows) // 2

    chunks = 2
    heads = features // HEAD_DIM // chunks
    held = [None] * chunks
    own_value = None
    for j in reversed(range(chunks)):
        weights, totals, *fetched = weigh(
            query,
            [own_key, *keys],
            [marks, *near_marks],
            j * heads,
            heads,
            enc_value if own_value is None else None,
        )
        own_value = fetched[0] if fetched else own_value
        held[j] = mix(weights, totals, [own_value, *values], j * heads, heads)

    order = ring_order(n_head)
    ring = [(order[i], order[(i + 1) % n_head]) for i in range(n_head)]
    before = {target: source for source, target in ring}

    def place(turn, first):
        head, ctx = lax.axis_index("head"), lax.axis_index("ctx")
        owner = 0
        for i in range(n_head):
            source = i
            for _ in range(turn):
                source = before[source]
            owner = owner + jnp.where(head == i, source, 0)
        row = owner * features + first
        if len(shards) == 1:
            return None, row
        return jnp.where(lax.div(row, map_rows) == ctx, 0, 1), lax.rem(row, map_rows)

    acc, last = None, n_head - 1
    for turn in range(last):
        if turn == last - 1:
            pieces = [p for h in held for p in halve(h)]
        else:
            pieces = held
        later = [lax.ppermute(p, "head", ring) for p in pieces]
        acc = project(acc, held, functools.partial(place, turn, 0), shards, map_rows)
        held = later
    acc = project(acc, held[:-1], functools.partial(place, last, 0), shards, map_rows)
    depth = held[-1].shape[1]
    last_maps, targets, mask = prepare(
        functools.partial(place, last, features - depth),
        depth,
        shards,
        map_rows,
        tgt_rows,
        near_targets,
        [marks, *near_marks],
    )
    own, *shares = cross_attend(acc, held[-1], last_maps, targets, mask, 1 + len(links))
    combined = [own]
    for i, (pairs, piece) in enumerate(zip(links, shares)):
        other = lax.ppermute(piece, "ctx", [(target, source) for source, target in pairs])
        if n_ctx > 2:
            end = n_ctx - 1 if i == 0 else 0
            column = lax.broadcasted_iota(jnp.int32, other.shape, 1)
            other = jnp.where((lax.axis_index("ctx") == end) & (column >= width), NEG_FILL, other)
        combined.append(other)
    return call(combine_kernel, "combine", [((tgt_rows, width), BF16)], combined, limit=4 << 20)[0]


def solution(mesh):
    in_specs = (
        P(("dp", "ctx"), "head"),
        P(("dp", "ctx"), "head"),
        P(("dp", "ctx"), "head"),
        P(("dp", "ctx")),
        P("ctx", "head"),
        P("ctx", "head"),
        P(("dp", "ctx"), "head"),
    )
    out_specs = P(("dp", "ctx"), "head")
    return jax.shard_map(
        on_device, mesh=mesh, in_specs=in_specs, out_specs=out_specs, check_vma=False
    )
```

```python
import functools

import jax
import jax.numpy as jnp
from jax import lax
from jax.experimental import pallas as pl
from jax.experimental.pallas import tpu as pltpu
from jax.sharding import PartitionSpec as P

HEAD_DIM = 256
NEG_FILL = -1e30
F32 = jnp.float32
BF16 = jnp.bfloat16
LANES = 128
SCALE = HEAD_DIM**-0.5
WEIGH_FLOPS = 6 * 10**9
VMEM = pl.BlockSpec(memory_space=pltpu.VMEM)
HBM = pl.BlockSpec(memory_space=pltpu.HBM)


def ring_order(count):
    return list(range(0, count, 2)) + list(range(1, count, 2))[::-1]


def links_of(count):
    if count == 2:
        return [[(0, 1), (1, 0)]]
    return [[(i, i + 1) for i in range(count - 1)], [(i + 1, i) for i in range(count - 1)]]


def dot_t(a, b):
    return lax.dot_general(a, b, (((1,), (1,)), ((), ())), preferred_element_type=F32)


def dot(a, b):
    return jnp.dot(a, b, preferred_element_type=F32)


def head_columns(h):
    return slice(h * HEAD_DIM, (h + 1) * HEAD_DIM)


def down_lanes(row):
    return jnp.transpose(jnp.broadcast_to(row, (LANES, row.shape[1])))


def same_mark(down, row):
    return jnp.concatenate([down == row[:, i : i + LANES] for i in range(0, row.shape[1], LANES)], axis=1)


def softmax_block(scores, same):
    scores = jnp.where(same, scores * SCALE, NEG_FILL)
    top = jnp.max(scores, axis=1, keepdims=True)
    weights = jnp.exp(scores - top)
    return top, weights, jnp.sum(weights, axis=1, keepdims=True)


def call(kernel, name, outs, operands, flops=0, exps=0, specs=None, scratch=(), limit=8 << 20):
    out_shape = [jax.ShapeDtypeStruct(*o) for o in outs]
    moved = sum(x.size * x.dtype.itemsize for x in [*operands, *out_shape])
    return pl.pallas_call(
        kernel,
        in_specs=specs or [VMEM] * len(operands),
        out_specs=[VMEM] * len(outs),
        out_shape=out_shape,
        scratch_shapes=list(scratch),
        compiler_params=pltpu.CompilerParams(vmem_limit_bytes=limit),
        cost_estimate=pl.CostEstimate(flops=flops, bytes_accessed=moved, transcendentals=exps),
        name=name,
    )(*operands)


def run_all(copies):
    for copy in copies:
        copy.start()
    for copy in copies:
        copy.wait()


def fetch_kernel(count, *refs):
    sources, targets, sems = refs[:count], refs[count : 2 * count], refs[-1]
    run_all([pltpu.make_async_copy(s, t, sems.at[i]) for i, (s, t) in enumerate(zip(sources, targets))])


def fetch(*arrays):
    return call(
        functools.partial(fetch_kernel, len(arrays)),
        "fetch",
        [(x.shape, x.dtype) for x in arrays],
        [pltpu.with_memory_space_constraint(x, pltpu.HBM) for x in arrays],
        specs=[HBM] * len(arrays),
        scratch=[pltpu.SemaphoreType.DMA((len(arrays),))],
    )


def pack_kernel(*refs):
    sources, out_ref, sems = refs[:-2], refs[-2], refs[-1]
    copies, row = [], 0
    for i, source in enumerate(sources):
        rows = source.shape[0]
        copies.append(pltpu.make_async_copy(source, out_ref.at[pl.ds(row, rows), :], sems.at[i]))
        row += rows
    run_all(copies)


def pack(*arrays):
    rows = sum(x.shape[0] for x in arrays)
    return call(
        pack_kernel,
        "pack",
        [((rows, arrays[0].shape[1]), arrays[0].dtype)],
        [pltpu.with_memory_space_constraint(x, pltpu.HBM) for x in arrays],
        specs=[HBM] * len(arrays),
        scratch=[pltpu.SemaphoreType.DMA((len(arrays),))],
    )[0]


def weigh_kernel(blocks, first, heads, *refs):
    marks, q_ref, keys = refs[:blocks], refs[blocks], refs[blocks + 1 : 2 * blocks + 1]
    weight_ref, total_ref = refs[2 * blocks + 1 :]
    down = down_lanes(marks[0][...])
    same = jnp.concatenate([same_mark(down, m[...]) for m in marks], axis=1)
    span = same.shape[1]
    lane = lax.broadcasted_iota(jnp.int32, total_ref.shape, 1)
    totals = jnp.zeros(total_ref.shape, F32)
    for h in range(heads):
        at = head_columns(first + h)
        scores = jnp.concatenate([dot_t(q_ref[:, at], k[:, at]) for k in keys], axis=1)
        _, weights, total = softmax_block(scores, same)
        weight_ref[:, h * span : (h + 1) * span] = weights.astype(BF16)
        totals = jnp.where(lane == h, total, totals)
    total_ref[...] = totals


def weigh(query, keys, marks, first, heads):
    rows, span = query.shape[0], query.shape[0] * len(keys)
    return call(
        functools.partial(weigh_kernel, len(keys), first, heads),
        "weigh",
        [((rows, heads * span), BF16), ((rows, LANES), F32)],
        [*marks, query, *keys],
        flops=WEIGH_FLOPS,
        exps=rows * span * heads,
    )


def mix_kernel(first, heads, weight_ref, total_ref, *refs):
    values, out_ref = refs[:-1], refs[-1]
    rows = total_ref.shape[0]
    for h in range(heads):
        start = h * rows * len(values)
        summed = sum(
            dot(weight_ref[:, start + i * rows : start + (i + 1) * rows], v[:, head_columns(first + h)])
            for i, v in enumerate(values)
        )
        out_ref[:, head_columns(h)] = (summed / total_ref[:, h : h + 1]).astype(BF16)


def mix(weights, totals, values, first, heads):
    rows = totals.shape[0]
    return call(
        functools.partial(mix_kernel, first, heads),
        "mix",
        [((rows, heads * HEAD_DIM), BF16)],
        [weights, totals, *values],
        flops=2 * weights.size * HEAD_DIM,
    )[0]


def in_shard(shards, shard, act):
    if len(shards) == 1:
        act(shards[0])
    else:
        for i, maps in enumerate(shards):
            pl.when(shard == i)(functools.partial(act, maps))


def halve_kernel(source, *outs):
    width = outs[0].shape[1]
    for i, out in enumerate(outs):
        out[...] = source[:, i * width : (i + 1) * width]


def halve(chunk):
    rows, width = chunk.shape
    return call(halve_kernel, "halve", [((rows, width // 2), chunk.dtype)] * 2, [chunk], flops=3 * 10**10)


def project_kernel(chunks, shards, map_rows, has_acc, place, *refs):
    e_refs, maps, out_ref = refs[:chunks], refs[chunks : chunks + shards], refs[-1]
    half = out_ref.shape[1] // 2
    depth = e_refs[0].shape[1]
    shard, row = place()
    row = pl.multiple_of(row, depth)
    chunk = jnp.concatenate([r[...] for r in e_refs], axis=1)

    def add(map_ref):
        for side in range(2):
            columns = slice(side * half, (side + 1) * half)
            product = dot(chunk, map_ref[pl.ds(side * map_rows + row, depth * chunks), :])
            out_ref[:, columns] = refs[-2][:, columns] + product if has_acc else product

    in_shard(maps, shard, add)


def project(acc, chunks, place, shards, map_rows):
    rows, depth = chunks[0].shape
    width = shards[0].shape[1]
    operands = [*chunks, *shards] + ([] if acc is None else [acc])
    return call(
        functools.partial(project_kernel, len(chunks), len(shards), map_rows, acc is not None, place),
        "project",
        [((rows, 2 * width), F32)],
        operands,
        flops=4 * rows * depth * width * len(chunks),
    )[0]


def prepare_kernel(shards, parts, map_rows, step, place, *refs):
    maps, marks, near = refs[:shards], refs[shards : shards + parts], refs[shards + parts : -4]
    map_ref, tgt_ref, mask_ref, down_ref = refs[-4:]
    shard, row = place()
    depth, width = map_ref.shape[0], map_ref.shape[1] // 2
    row = pl.multiple_of(row, depth)

    def copy(source):
        for side in range(2):
            map_ref[:, side * width : (side + 1) * width] = source[pl.ds(side * map_rows + row, depth), :]

    in_shard(maps, shard, copy)
    own = marks[0][...]
    count = tgt_ref.shape[0] // parts
    below = slice(2 * map_rows, 2 * map_rows + count)
    targets = [maps[0][below, :]] + ([r[...] for r in near] if near else [m[below, :] for m in maps[1:]])
    for i, (target, mark_ref) in enumerate(zip(targets, marks)):
        part = slice(i * count, (i + 1) * count)
        tgt_ref[part, :] = target
        down_ref[...] = down_lanes(mark_ref[...])
        down = down_ref[pl.ds(0, count, stride=step), :]
        mask_ref[part, :] = same_mark(down, own).astype(F32)


def prepare(place, depth, shards, map_rows, count, near_targets, marks):
    rows, width = marks[0].shape[1], shards[0].shape[1]
    total = count * len(marks)
    return call(
        functools.partial(prepare_kernel, len(shards), len(marks), map_rows, rows // count, place),
        "prepare",
        [((depth, 2 * width), BF16), ((total, width), BF16), ((total, rows), F32)],
        [*shards, *marks, *near_targets],
        scratch=[pltpu.VMEM((rows, LANES), jnp.int32)],
    )


def cross_kernel(acc_ref, e_ref, map_ref, tgt_ref, mask_ref, *outs):
    heads = map_ref.shape[1] // 2 // HEAD_DIM
    chunk = e_ref[...]
    memory = []
    for h in range(2 * heads):
        at = head_columns(h)
        memory.append((acc_ref[:, at] + dot(chunk, map_ref[:, at])).astype(BF16))
    keys, values = memory[:heads], memory[heads:]
    count = outs[0].shape[0]
    same = mask_ref[...] > 0
    lane = lax.broadcasted_iota(jnp.int32, (same.shape[0], LANES), 1)
    stats = jnp.zeros(lane.shape, F32)
    for h in range(heads):
        at = head_columns(h)
        top, weights, total = softmax_block(dot_t(tgt_ref[:, at], keys[h]), same)
        summed = dot(weights.astype(BF16), values[h])
        for i, out_ref in enumerate(outs):
            out_ref[:, at] = summed[i * count : (i + 1) * count]
        stats = jnp.where(lane == h, top, jnp.where(lane == heads + h, total, stats))
    for i, out_ref in enumerate(outs):
        out_ref[:, heads * HEAD_DIM :] = stats[i * count : (i + 1) * count]


def cross_attend(acc, chunk, maps, targets, mask, parts):
    width = targets.shape[1]
    count = targets.shape[0] // parts
    return call(
        cross_kernel,
        "cross_attend",
        [((count, width + LANES), F32)] * parts,
        [acc, chunk, maps, targets, mask],
        flops=2 * chunk.size * 2 * width,
    )


def combine_kernel(*refs):
    parts, out_ref = refs[:-1], refs[-1]
    width = out_ref.shape[1]
    heads = width // HEAD_DIM
    for h in range(heads):
        at = head_columns(h)
        tops = [r[:, width + h : width + h + 1] for r in parts]
        top = functools.reduce(jnp.maximum, tops)
        factors = [jnp.exp(t - top) for t in tops]
        total = sum(f * r[:, width + heads + h : width + heads + h + 1] for f, r in zip(factors, parts))
        summed = sum(f * r[:, at] for f, r in zip(factors, parts))
        out_ref[:, at] = (summed / total).astype(BF16)


def on_device(enc_query, enc_key, enc_value, doc_ids, key_map, value_map, tgt_query):
    rows, features = enc_query.shape
    tgt_rows, width = tgt_query.shape
    n_ctx, n_head = lax.axis_size("ctx"), lax.axis_size("head")
    links = links_of(n_ctx)
    bring = lambda x: [lax.ppermute(x, "ctx", pairs) for pairs in links]

    marks = (doc_ids if n_ctx == 2 else doc_ids + 1).reshape(1, rows)
    keys, near_marks, values = bring(enc_key), bring(marks), bring(enc_value)
    query, own_key, own_value, marks = fetch(enc_query, enc_key, enc_value, marks)
    near_targets = []
    if n_ctx == 2:
        own_maps = pack(key_map, value_map, tgt_query)
        shards = [own_maps, *bring(own_maps)]
    else:
        whole = [lax.all_gather(x, "ctx", axis=0, tiled=True) for x in (key_map, value_map)]
        shards, near_targets = [pack(*whole, tgt_query)], bring(tgt_query)
    map_rows = (shards[0].shape[0] - tgt_rows) // 2

    chunks = 2
    heads = features // HEAD_DIM // chunks
    held = [None] * chunks
    for j in reversed(range(chunks)):
        weights, totals = weigh(query, [own_key, *keys], [marks, *near_marks], j * heads, heads)
        held[j] = mix(weights, totals, [own_value, *values], j * heads, heads)

    order = ring_order(n_head)
    ring = [(order[i], order[(i + 1) % n_head]) for i in range(n_head)]
    before = {target: source for source, target in ring}

    def place(turn, first):
        head, ctx = lax.axis_index("head"), lax.axis_index("ctx")
        owner = 0
        for i in range(n_head):
            source = i
            for _ in range(turn):
                source = before[source]
            owner = owner + jnp.where(head == i, source, 0)
        row = owner * features + first
        if len(shards) == 1:
            return None, row
        return jnp.where(lax.div(row, map_rows) == ctx, 0, 1), lax.rem(row, map_rows)

    acc, last = None, n_head - 1
    for turn in range(last):
        if turn == last - 1:
            pieces = [p for h in held for p in halve(h)]
        else:
            pieces = held
        later = [lax.ppermute(p, "head", ring) for p in pieces]
        acc = project(acc, held, functools.partial(place, turn, 0), shards, map_rows)
        held = later
    acc = project(acc, held[:-1], functools.partial(place, last, 0), shards, map_rows)
    depth = held[-1].shape[1]
    last_maps, targets, mask = prepare(
        functools.partial(place, last, features - depth),
        depth,
        shards,
        map_rows,
        tgt_rows,
        near_targets,
        [marks, *near_marks],
    )
    own, *shares = cross_attend(acc, held[-1], last_maps, targets, mask, 1 + len(links))
    combined = [own]
    for i, (pairs, piece) in enumerate(zip(links, shares)):
        other = lax.ppermute(piece, "ctx", [(target, source) for source, target in pairs])
        if n_ctx > 2:
            end = n_ctx - 1 if i == 0 else 0
            column = lax.broadcasted_iota(jnp.int32, other.shape, 1)
            other = jnp.where((lax.axis_index("ctx") == end) & (column >= width), NEG_FILL, other)
        combined.append(other)
    return call(combine_kernel, "combine", [((tgt_rows, width), BF16)], combined, limit=4 << 20)[0]


def solution(mesh):
    in_specs = (
        P(("dp", "ctx"), "head"),
        P(("dp", "ctx"), "head"),
        P(("dp", "ctx"), "head"),
        P(("dp", "ctx")),
        P("ctx", "head"),
        P("ctx", "head"),
        P(("dp", "ctx"), "head"),
    )
    out_specs = P(("dp", "ctx"), "head")
    return jax.shard_map(
        on_device, mesh=mesh, in_specs=in_specs, out_specs=out_specs, check_vma=False
    )
```

```python
import functools

import jax
import jax.numpy as jnp
from jax import lax
from jax.experimental import pallas as pl
from jax.experimental.pallas import tpu as pltpu
from jax.sharding import PartitionSpec as P

HEAD_DIM = 256
NEG_FILL = -1e30
F32 = jnp.float32
BF16 = jnp.bfloat16
LANES = 128
SCALE = HEAD_DIM**-0.5
WEIGH_FLOPS = 6 * 10**9
SPLIT_FLOPS = 30 * 10**9
VMEM = pl.BlockSpec(memory_space=pltpu.VMEM)
HBM = pl.BlockSpec(memory_space=pltpu.HBM)


def ring_order(count):
    return list(range(0, count, 2)) + list(range(1, count, 2))[::-1]


def ring_owners(count):
    order = ring_order(count)
    before = {order[(i + 1) % count]: order[i] for i in range(count)}
    owners = [list(range(count))]
    for _ in range(count - 1):
        owners.append([owners[-1][before[i]] for i in range(count)])
    return owners


def ring_rounds(held, count):
    order = ring_order(count)
    ring = [(order[i], order[(i + 1) % count]) for i in range(count)]
    rounds = [held]
    for turn in range(count - 1):
        pieces = [p for h in rounds[-1] for p in split(h, 2)] if turn == count - 2 else rounds[-1]
        rounds.append([lax.ppermute(p, "head", ring) for p in pieces])
    return rounds


def line_owners():
    return [[0, 1, 2, 3], [1, 0, 3, 2], [2, 2, 1, 1], [3, 3, 0, 0]]


def line_rounds(held, beside):
    ends, middle, out = [(0, 1), (1, 0), (2, 3), (3, 2)], [(1, 2), (2, 1)], [(1, 0), (2, 3)]
    send = lambda chunk, pairs: lax.ppermute(chunk, "head", pairs)
    near, over, third, fourth = [], [], [], []
    for chunk in held:
        near.append(send(chunk, ends))
        over.append(send(chunk, middle))
    near[0], beside = lax.optimization_barrier((near[0], beside))
    for i in range(len(held)):
        far = send(near[i], middle)
        third.append((over[i], send(over[i], out)))
        fourth += [(piece, send(piece, out)) for piece in split(far, 1 if i < len(held) - 1 else 2)]
    return [held, near, third, fourth], beside


def links_of(count):
    if count == 2:
        return [[(0, 1), (1, 0)]]
    return [[(i, i + 1) for i in range(count - 1)], [(i + 1, i) for i in range(count - 1)]]


def dot_t(a, b):
    return lax.dot_general(a, b, (((1,), (1,)), ((), ())), preferred_element_type=F32)


def dot(a, b):
    return jnp.dot(a, b, preferred_element_type=F32)


def head_columns(h):
    return slice(h * HEAD_DIM, (h + 1) * HEAD_DIM)


def down_lanes(row):
    return jnp.transpose(jnp.broadcast_to(row, (LANES, row.shape[1])))


def same_mark(down, row):
    return jnp.concatenate([down == row[:, i : i + LANES] for i in range(0, row.shape[1], LANES)], axis=1)


def softmax_block(scores, same):
    scores = jnp.where(same, scores * SCALE, NEG_FILL)
    top = jnp.max(scores, axis=1, keepdims=True)
    weights = jnp.exp(scores - top)
    return top, weights, jnp.sum(weights, axis=1, keepdims=True)


def call(kernel, name, outs, operands, flops=0, exps=0, specs=None, scratch=(), limit=8 << 20):
    out_shape = [jax.ShapeDtypeStruct(*o) for o in outs]
    moved = sum(x.size * x.dtype.itemsize for x in [*operands, *out_shape])
    return pl.pallas_call(
        kernel,
        in_specs=specs or [VMEM] * len(operands),
        out_specs=[VMEM] * len(outs),
        out_shape=out_shape,
        scratch_shapes=list(scratch),
        compiler_params=pltpu.CompilerParams(vmem_limit_bytes=limit),
        cost_estimate=pl.CostEstimate(flops=flops, bytes_accessed=moved, transcendentals=exps),
        name=name,
    )(*operands)


def run_all(copies):
    for copy in copies:
        copy.start()
    for copy in copies:
        copy.wait()


def fetch_kernel(count, *refs):
    sources, targets, sems = refs[:count], refs[count : 2 * count], refs[-1]
    run_all([pltpu.make_async_copy(s, t, sems.at[i]) for i, (s, t) in enumerate(zip(sources, targets))])


def fetch(*arrays):
    return call(
        functools.partial(fetch_kernel, len(arrays)),
        "fetch",
        [(x.shape, x.dtype) for x in arrays],
        [pltpu.with_memory_space_constraint(x, pltpu.HBM) for x in arrays],
        specs=[HBM] * len(arrays),
        scratch=[pltpu.SemaphoreType.DMA((len(arrays),))],
    )


def pack_kernel(*refs):
    sources, out_ref, sems = refs[:-2], refs[-2], refs[-1]
    copies, row = [], 0
    for i, source in enumerate(sources):
        rows = source.shape[0]
        copies.append(pltpu.make_async_copy(source, out_ref.at[pl.ds(row, rows), :], sems.at[i]))
        row += rows
    run_all(copies)


def pack(*arrays):
    rows = sum(x.shape[0] for x in arrays)
    return call(
        pack_kernel,
        "pack",
        [((rows, arrays[0].shape[1]), arrays[0].dtype)],
        [pltpu.with_memory_space_constraint(x, pltpu.HBM) for x in arrays],
        specs=[HBM] * len(arrays),
        scratch=[pltpu.SemaphoreType.DMA((len(arrays),))],
    )[0]


def weigh_kernel(blocks, first, heads, *refs):
    marks, q_ref, keys = refs[:blocks], refs[blocks], refs[blocks + 1 : 2 * blocks + 1]
    weight_ref, total_ref = refs[2 * blocks + 1 :]
    down = down_lanes(marks[0][...])
    same = jnp.concatenate([same_mark(down, m[...]) for m in marks], axis=1)
    span = same.shape[1]
    lane = lax.broadcasted_iota(jnp.int32, total_ref.shape, 1)
    totals = jnp.zeros(total_ref.shape, F32)
    for h in range(heads):
        at = head_columns(first + h)
        scores = jnp.concatenate([dot_t(q_ref[:, at], k[:, at]) for k in keys], axis=1)
        _, weights, total = softmax_block(scores, same)
        weight_ref[:, h * span : (h + 1) * span] = weights.astype(BF16)
        totals = jnp.where(lane == h, total, totals)
    total_ref[...] = totals


def weigh(query, keys, marks, first, heads):
    rows, span = query.shape[0], query.shape[0] * len(keys)
    return call(
        functools.partial(weigh_kernel, len(keys), first, heads),
        "weigh",
        [((rows, heads * span), BF16), ((rows, LANES), F32)],
        [*marks, query, *keys],
        flops=WEIGH_FLOPS,
        exps=rows * span * heads,
    )


def mix_kernel(first, heads, weight_ref, total_ref, *refs):
    values, out_ref = refs[:-1], refs[-1]
    rows = total_ref.shape[0]
    for h in range(heads):
        start = h * rows * len(values)
        summed = sum(
            dot(weight_ref[:, start + i * rows : start + (i + 1) * rows], v[:, head_columns(first + h)])
            for i, v in enumerate(values)
        )
        out_ref[:, head_columns(h)] = (summed / total_ref[:, h : h + 1]).astype(BF16)


def mix(weights, totals, values, first, heads):
    rows = totals.shape[0]
    return call(
        functools.partial(mix_kernel, first, heads),
        "mix",
        [((rows, heads * HEAD_DIM), BF16)],
        [weights, totals, *values],
        flops=2 * weights.size * HEAD_DIM,
    )[0]


def in_shard(shards, shard, act):
    if len(shards) == 1:
        act(shards[0])
    else:
        for i, maps in enumerate(shards):
            pl.when(shard == i)(functools.partial(act, maps))


def split_kernel(source, *outs):
    width = outs[0].shape[1]
    for i, out in enumerate(outs):
        out[...] = source[:, i * width : (i + 1) * width]


def split(chunk, parts):
    rows, width = chunk.shape
    return call(split_kernel, "split", [((rows, width // parts), chunk.dtype)] * parts, [chunk], flops=SPLIT_FLOPS)


def flat(chunks):
    pairs = isinstance(chunks[0], tuple)
    return ([x for pair in chunks for x in pair] if pairs else list(chunks)), pairs


def joined(refs, pairs):
    chunks = [r[...] for r in refs]
    if pairs:
        chunks = [a + b for a, b in zip(chunks[::2], chunks[1::2])]
    return jnp.concatenate(chunks, axis=1)


def project_kernel(chunks, pairs, shards, map_rows, has_acc, place, *refs):
    e_refs, maps, out_ref = refs[:chunks], refs[chunks : chunks + shards], refs[-1]
    half = out_ref.shape[1] // 2
    depth = e_refs[0].shape[1]
    shard, row = place()
    row = pl.multiple_of(row, depth)
    chunk = joined(e_refs, pairs)

    def add(map_ref):
        for side in range(2):
            columns = slice(side * half, (side + 1) * half)
            product = dot(chunk, map_ref[pl.ds(side * map_rows + row, chunk.shape[1]), :])
            out_ref[:, columns] = refs[-2][:, columns] + product if has_acc else product

    in_shard(maps, shard, add)


def project(acc, chunks, place, shards, map_rows):
    chunks, pairs = flat(chunks)
    rows, depth = chunks[0].shape
    width = shards[0].shape[1]
    operands = [*chunks, *shards] + ([] if acc is None else [acc])
    return call(
        functools.partial(project_kernel, len(chunks), pairs, len(shards), map_rows, acc is not None, place),
        "project",
        [((rows, 2 * width), F32)],
        operands,
        flops=4 * rows * depth * width * len(chunks),
    )[0]


def prepare_kernel(shards, parts, map_rows, step, place, *refs):
    maps, marks, near = refs[:shards], refs[shards : shards + parts], refs[shards + parts : -4]
    map_ref, tgt_ref, mask_ref, down_ref = refs[-4:]
    shard, row = place()
    depth, width = map_ref.shape[0], map_ref.shape[1] // 2
    row = pl.multiple_of(row, depth)

    def copy(source):
        for side in range(2):
            map_ref[:, side * width : (side + 1) * width] = source[pl.ds(side * map_rows + row, depth), :]

    in_shard(maps, shard, copy)
    own = marks[0][...]
    count = tgt_ref.shape[0] // parts
    below = slice(2 * map_rows, 2 * map_rows + count)
    targets = [maps[0][below, :]] + ([r[...] for r in near] if near else [m[below, :] for m in maps[1:]])
    for i, (target, mark_ref) in enumerate(zip(targets, marks)):
        part = slice(i * count, (i + 1) * count)
        tgt_ref[part, :] = target
        down_ref[...] = down_lanes(mark_ref[...])
        down = down_ref[pl.ds(0, count, stride=step), :]
        mask_ref[part, :] = same_mark(down, own).astype(F32)


def prepare(place, depth, shards, map_rows, count, near_targets, marks):
    rows, width = marks[0].shape[1], shards[0].shape[1]
    total = count * len(marks)
    return call(
        functools.partial(prepare_kernel, len(shards), len(marks), map_rows, rows // count, place),
        "prepare",
        [((depth, 2 * width), BF16), ((total, width), BF16), ((total, rows), F32)],
        [*shards, *marks, *near_targets],
        scratch=[pltpu.VMEM((rows, LANES), jnp.int32)],
    )


def cross_kernel(pieces, pairs, *refs):
    chunk = joined(refs[:pieces], pairs)
    acc_ref, map_ref, tgt_ref, mask_ref, *outs = refs[pieces:]
    heads = map_ref.shape[1] // 2 // HEAD_DIM
    memory = []
    for h in range(2 * heads):
        at = head_columns(h)
        memory.append((acc_ref[:, at] + dot(chunk, map_ref[:, at])).astype(BF16))
    keys, values = memory[:heads], memory[heads:]
    count = outs[0].shape[0]
    same = mask_ref[...] > 0
    lane = lax.broadcasted_iota(jnp.int32, (same.shape[0], LANES), 1)
    stats = jnp.zeros(lane.shape, F32)
    for h in range(heads):
        at = head_columns(h)
        top, weights, total = softmax_block(dot_t(tgt_ref[:, at], keys[h]), same)
        summed = dot(weights.astype(BF16), values[h])
        for i, out_ref in enumerate(outs):
            out_ref[:, at] = summed[i * count : (i + 1) * count]
        stats = jnp.where(lane == h, top, jnp.where(lane == heads + h, total, stats))
    for i, out_ref in enumerate(outs):
        out_ref[:, heads * HEAD_DIM :] = stats[i * count : (i + 1) * count]


def cross_attend(acc, chunk, maps, targets, mask, parts):
    width = targets.shape[1]
    count = targets.shape[0] // parts
    pieces, pairs = flat([chunk])
    return call(
        functools.partial(cross_kernel, len(pieces), pairs),
        "cross_attend",
        [((count, width + LANES), F32)] * parts,
        [*pieces, acc, maps, targets, mask],
        flops=2 * maps.size * acc.shape[0],
    )


def combine_kernel(*refs):
    parts, out_ref = refs[:-1], refs[-1]
    width = out_ref.shape[1]
    heads = width // HEAD_DIM
    for h in range(heads):
        at = head_columns(h)
        tops = [r[:, width + h : width + h + 1] for r in parts]
        top = functools.reduce(jnp.maximum, tops)
        factors = [jnp.exp(t - top) for t in tops]
        total = sum(f * r[:, width + heads + h : width + heads + h + 1] for f, r in zip(factors, parts))
        summed = sum(f * r[:, at] for f, r in zip(factors, parts))
        out_ref[:, at] = (summed / total).astype(BF16)


def on_device(enc_query, enc_key, enc_value, doc_ids, key_map, value_map, tgt_query):
    rows, features = enc_query.shape
    tgt_rows, width = tgt_query.shape
    n_ctx, n_head = lax.axis_size("ctx"), lax.axis_size("head")
    links = links_of(n_ctx)
    bring = lambda x: [lax.ppermute(x, "ctx", pairs) for pairs in links]

    marks = (doc_ids if n_ctx == 2 else doc_ids + 1).reshape(1, rows)
    keys, near_marks, values = bring(enc_key), bring(marks), bring(enc_value)
    query, own_key, own_value, marks = fetch(enc_query, enc_key, enc_value, marks)
    chunks = 2
    heads = features // HEAD_DIM // chunks
    held = [None] * chunks
    for j in reversed(range(chunks)):
        weights, totals = weigh(query, [own_key, *keys], [marks, *near_marks], j * heads, heads)
        held[j] = mix(weights, totals, [own_value, *values], j * heads, heads)

    key_map, value_map, tgt_query, held[0] = lax.optimization_barrier((key_map, value_map, tgt_query, held[0]))
    if n_ctx == 2:
        own_maps, near_targets = pack(key_map, value_map, tgt_query), []
    else:
        whole = [lax.all_gather(x, "ctx", axis=0, tiled=True) for x in (key_map, value_map)]
        own_maps, near_targets = pack(*whole, tgt_query), bring(tgt_query)
    map_rows = (own_maps.shape[0] - tgt_rows) // 2

    if n_head == 4:
        owners, (rounds, own_maps) = line_owners(), line_rounds(held, own_maps)
    else:
        owners, rounds = ring_owners(n_head), ring_rounds(held, n_head)
    shards = [own_maps, *bring(own_maps)] if n_ctx == 2 else [own_maps]

    def place(turn, first):
        head, ctx = lax.axis_index("head"), lax.axis_index("ctx")
        owner = sum(jnp.where(head == i, source, 0) for i, source in enumerate(owners[turn]))
        row = owner * features + first
        if len(shards) == 1:
            return None, row
        return jnp.where(lax.div(row, map_rows) == ctx, 0, 1), lax.rem(row, map_rows)

    acc, last = None, n_head - 1
    for turn in range(last):
        acc = project(acc, rounds[turn], functools.partial(place, turn, 0), shards, map_rows)
    held = rounds[last]
    acc = project(acc, held[:-1], functools.partial(place, last, 0), shards, map_rows)
    depth = flat(held[-1:])[0][0].shape[1]
    last_maps, targets, mask = prepare(
        functools.partial(place, last, features - depth),
        depth,
        shards,
        map_rows,
        tgt_rows,
        near_targets,
        [marks, *near_marks],
    )
    own, *shares = cross_attend(acc, held[-1], last_maps, targets, mask, 1 + len(links))
    combined = [own]
    for i, (pairs, piece) in enumerate(zip(links, shares)):
        other = lax.ppermute(piece, "ctx", [(target, source) for source, target in pairs])
        if n_ctx > 2:
            end = n_ctx - 1 if i == 0 else 0
            column = lax.broadcasted_iota(jnp.int32, other.shape, 1)
            other = jnp.where((lax.axis_index("ctx") == end) & (column >= width), NEG_FILL, other)
        combined.append(other)
    return call(combine_kernel, "combine", [((tgt_rows, width), BF16)], combined, limit=4 << 20)[0]


def solution(mesh):
    in_specs = (
        P(("dp", "ctx"), "head"),
        P(("dp", "ctx"), "head"),
        P(("dp", "ctx"), "head"),
        P(("dp", "ctx")),
        P("ctx", "head"),
        P("ctx", "head"),
        P(("dp", "ctx"), "head"),
    )
    out_specs = P(("dp", "ctx"), "head")
    return jax.shard_map(
        on_device, mesh=mesh, in_specs=in_specs, out_specs=out_specs, check_vma=False
    )
```

```python
import functools

import jax
import jax.numpy as jnp
from jax import lax
from jax.experimental import pallas as pl
from jax.experimental.pallas import tpu as pltpu
from jax.sharding import PartitionSpec as P

HEAD_DIM = 256
NEG_FILL = -1e30
F32 = jnp.float32
BF16 = jnp.bfloat16
LANES = 128
SCALE = HEAD_DIM**-0.5
WEIGH_FLOPS = 6 * 10**9
VMEM = pl.BlockSpec(memory_space=pltpu.VMEM)
HBM = pl.BlockSpec(memory_space=pltpu.HBM)


def ring_order(count):
    return list(range(0, count, 2)) + list(range(1, count, 2))[::-1]


def links_of(count):
    if count == 2:
        return [[(0, 1), (1, 0)]]
    return [[(i, i + 1) for i in range(count - 1)], [(i + 1, i) for i in range(count - 1)]]


def dot_t(a, b):
    return lax.dot_general(a, b, (((1,), (1,)), ((), ())), preferred_element_type=F32)


def dot(a, b):
    return jnp.dot(a, b, preferred_element_type=F32)


def head_columns(h):
    return slice(h * HEAD_DIM, (h + 1) * HEAD_DIM)


def down_lanes(row):
    return jnp.transpose(jnp.broadcast_to(row, (LANES, row.shape[1])))


def same_mark(down, row):
    return jnp.concatenate([down == row[:, i : i + LANES] for i in range(0, row.shape[1], LANES)], axis=1)


def softmax_block(scores, same):
    scores = jnp.where(same, scores * SCALE, NEG_FILL)
    top = jnp.max(scores, axis=1, keepdims=True)
    weights = jnp.exp(scores - top)
    return top, weights, jnp.sum(weights, axis=1, keepdims=True)


def call(kernel, name, outs, operands, flops=0, exps=0, specs=None, scratch=(), limit=8 << 20):
    out_shape = [jax.ShapeDtypeStruct(*o) for o in outs]
    moved = sum(x.size * x.dtype.itemsize for x in [*operands, *out_shape])
    return pl.pallas_call(
        kernel,
        in_specs=specs or [VMEM] * len(operands),
        out_specs=[VMEM] * len(outs),
        out_shape=out_shape,
        scratch_shapes=list(scratch),
        compiler_params=pltpu.CompilerParams(vmem_limit_bytes=limit),
        cost_estimate=pl.CostEstimate(flops=flops, bytes_accessed=moved, transcendentals=exps),
        name=name,
    )(*operands)


def run_all(copies):
    for copy in copies:
        copy.start()
    for copy in copies:
        copy.wait()


def fetch_kernel(count, *refs):
    sources, targets, sems = refs[:count], refs[count : 2 * count], refs[-1]
    run_all([pltpu.make_async_copy(s, t, sems.at[i]) for i, (s, t) in enumerate(zip(sources, targets))])


def fetch(*arrays):
    return call(
        functools.partial(fetch_kernel, len(arrays)),
        "fetch",
        [(x.shape, x.dtype) for x in arrays],
        [pltpu.with_memory_space_constraint(x, pltpu.HBM) for x in arrays],
        specs=[HBM] * len(arrays),
        scratch=[pltpu.SemaphoreType.DMA((len(arrays),))],
    )


def pack_kernel(*refs):
    sources, out_ref, sems = refs[:-2], refs[-2], refs[-1]
    copies, row = [], 0
    for i, source in enumerate(sources):
        rows = source.shape[0]
        copies.append(pltpu.make_async_copy(source, out_ref.at[pl.ds(row, rows), :], sems.at[i]))
        row += rows
    run_all(copies)


def pack(*arrays):
    rows = sum(x.shape[0] for x in arrays)
    return call(
        pack_kernel,
        "pack",
        [((rows, arrays[0].shape[1]), arrays[0].dtype)],
        [pltpu.with_memory_space_constraint(x, pltpu.HBM) for x in arrays],
        specs=[HBM] * len(arrays),
        scratch=[pltpu.SemaphoreType.DMA((len(arrays),))],
    )[0]


def weigh_kernel(blocks, first, heads, *refs):
    marks, q_ref, keys = refs[:blocks], refs[blocks], refs[blocks + 1 : 2 * blocks + 1]
    weight_ref, total_ref = refs[2 * blocks + 1 :]
    down = down_lanes(marks[0][...])
    same = jnp.concatenate([same_mark(down, m[...]) for m in marks], axis=1)
    span = same.shape[1]
    lane = lax.broadcasted_iota(jnp.int32, total_ref.shape, 1)
    totals = jnp.zeros(total_ref.shape, F32)
    for h in range(heads):
        at = head_columns(first + h)
        scores = jnp.concatenate([dot_t(q_ref[:, at], k[:, at]) for k in keys], axis=1)
        _, weights, total = softmax_block(scores, same)
        weight_ref[:, h * span : (h + 1) * span] = weights.astype(BF16)
        totals = jnp.where(lane == h, total, totals)
    total_ref[...] = totals


def weigh(query, keys, marks, first, heads):
    rows, span = query.shape[0], query.shape[0] * len(keys)
    return call(
        functools.partial(weigh_kernel, len(keys), first, heads),
        "weigh",
        [((rows, heads * span), BF16), ((rows, LANES), F32)],
        [*marks, query, *keys],
        flops=WEIGH_FLOPS,
        exps=rows * span * heads,
    )


def mix_kernel(first, heads, weight_ref, total_ref, *refs):
    values, out_ref = refs[:-1], refs[-1]
    rows = total_ref.shape[0]
    for h in range(heads):
        start = h * rows * len(values)
        summed = sum(
            dot(weight_ref[:, start + i * rows : start + (i + 1) * rows], v[:, head_columns(first + h)])
            for i, v in enumerate(values)
        )
        out_ref[:, head_columns(h)] = (summed / total_ref[:, h : h + 1]).astype(BF16)


def mix(weights, totals, values, first, heads):
    rows = totals.shape[0]
    return call(
        functools.partial(mix_kernel, first, heads),
        "mix",
        [((rows, heads * HEAD_DIM), BF16)],
        [weights, totals, *values],
        flops=2 * weights.size * HEAD_DIM,
    )[0]


def in_shard(shards, shard, act):
    if len(shards) == 1:
        act(shards[0])
    else:
        for i, maps in enumerate(shards):
            pl.when(shard == i)(functools.partial(act, maps))


def halve_kernel(source, *outs):
    width = outs[0].shape[1]
    for i, out in enumerate(outs):
        out[...] = source[:, i * width : (i + 1) * width]


def halve(chunk):
    rows, width = chunk.shape
    return call(halve_kernel, "halve", [((rows, width // 2), chunk.dtype)] * 2, [chunk], flops=3 * 10**10)


def project_kernel(chunks, shards, map_rows, has_acc, place, *refs):
    e_refs, maps, out_ref = refs[:chunks], refs[chunks : chunks + shards], refs[-1]
    half = out_ref.shape[1] // 2
    depth = e_refs[0].shape[1]
    shard, row = place()
    row = pl.multiple_of(row, depth)
    chunk = jnp.concatenate([r[...] for r in e_refs], axis=1)

    def add(map_ref):
        for side in range(2):
            columns = slice(side * half, (side + 1) * half)
            product = dot(chunk, map_ref[pl.ds(side * map_rows + row, depth * chunks), :])
            out_ref[:, columns] = refs[-2][:, columns] + product if has_acc else product

    in_shard(maps, shard, add)


def project(acc, chunks, place, shards, map_rows):
    rows, depth = chunks[0].shape
    width = shards[0].shape[1]
    operands = [*chunks, *shards] + ([] if acc is None else [acc])
    return call(
        functools.partial(project_kernel, len(chunks), len(shards), map_rows, acc is not None, place),
        "project",
        [((rows, 2 * width), F32)],
        operands,
        flops=4 * rows * depth * width * len(chunks),
    )[0]


def prepare_kernel(shards, parts, map_rows, step, place, *refs):
    maps, marks, near = refs[:shards], refs[shards : shards + parts], refs[shards + parts : -4]
    map_ref, tgt_ref, mask_ref, down_ref = refs[-4:]
    shard, row = place()
    depth, width = map_ref.shape[0], map_ref.shape[1] // 2
    row = pl.multiple_of(row, depth)

    def copy(source):
        for side in range(2):
            map_ref[:, side * width : (side + 1) * width] = source[pl.ds(side * map_rows + row, depth), :]

    in_shard(maps, shard, copy)
    own = marks[0][...]
    count = tgt_ref.shape[0] // parts
    below = slice(2 * map_rows, 2 * map_rows + count)
    targets = [maps[0][below, :]] + ([r[...] for r in near] if near else [m[below, :] for m in maps[1:]])
    for i, (target, mark_ref) in enumerate(zip(targets, marks)):
        part = slice(i * count, (i + 1) * count)
        tgt_ref[part, :] = target
        down_ref[...] = down_lanes(mark_ref[...])
        down = down_ref[pl.ds(0, count, stride=step), :]
        mask_ref[part, :] = same_mark(down, own).astype(F32)


def prepare(place, depth, shards, map_rows, count, near_targets, marks):
    rows, width = marks[0].shape[1], shards[0].shape[1]
    total = count * len(marks)
    return call(
        functools.partial(prepare_kernel, len(shards), len(marks), map_rows, rows // count, place),
        "prepare",
        [((depth, 2 * width), BF16), ((total, width), BF16), ((total, rows), F32)],
        [*shards, *marks, *near_targets],
        scratch=[pltpu.VMEM((rows, LANES), jnp.int32)],
    )


def cross_kernel(e_ref, acc_ref, map_ref, tgt_ref, mask_ref, *outs):
    heads = map_ref.shape[1] // 2 // HEAD_DIM
    chunk = e_ref[...]
    memory = []
    for h in range(2 * heads):
        at = head_columns(h)
        memory.append((acc_ref[:, at] + dot(chunk, map_ref[:, at])).astype(BF16))
    keys, values = memory[:heads], memory[heads:]
    count = outs[0].shape[0]
    same = mask_ref[...] > 0
    lane = lax.broadcasted_iota(jnp.int32, (same.shape[0], LANES), 1)
    stats = jnp.zeros(lane.shape, F32)
    for h in range(heads):
        at = head_columns(h)
        top, weights, total = softmax_block(dot_t(tgt_ref[:, at], keys[h]), same)
        summed = dot(weights.astype(BF16), values[h])
        for i, out_ref in enumerate(outs):
            out_ref[:, at] = summed[i * count : (i + 1) * count]
        stats = jnp.where(lane == h, top, jnp.where(lane == heads + h, total, stats))
    for i, out_ref in enumerate(outs):
        out_ref[:, heads * HEAD_DIM :] = stats[i * count : (i + 1) * count]


def cross_attend(acc, chunk, maps, targets, mask, parts):
    width = targets.shape[1]
    count = targets.shape[0] // parts
    return call(
        cross_kernel,
        "cross_attend",
        [((count, width + LANES), F32)] * parts,
        [chunk, acc, maps, targets, mask],
        flops=2 * chunk.size * 2 * width,
    )


def combine_kernel(*refs):
    parts, out_ref = refs[:-1], refs[-1]
    width = out_ref.shape[1]
    heads = width // HEAD_DIM
    for h in range(heads):
        at = head_columns(h)
        tops = [r[:, width + h : width + h + 1] for r in parts]
        top = functools.reduce(jnp.maximum, tops)
        factors = [jnp.exp(t - top) for t in tops]
        total = sum(f * r[:, width + heads + h : width + heads + h + 1] for f, r in zip(factors, parts))
        summed = sum(f * r[:, at] for f, r in zip(factors, parts))
        out_ref[:, at] = (summed / total).astype(BF16)


def on_device(enc_query, enc_key, enc_value, doc_ids, key_map, value_map, tgt_query):
    rows, features = enc_query.shape
    tgt_rows, width = tgt_query.shape
    n_ctx, n_head = lax.axis_size("ctx"), lax.axis_size("head")
    links = links_of(n_ctx)
    bring = lambda x: [lax.ppermute(x, "ctx", pairs) for pairs in links]

    marks = (doc_ids if n_ctx == 2 else doc_ids + 1).reshape(1, rows)
    keys, near_marks, values = bring(enc_key), bring(marks), bring(enc_value)
    query, own_key, own_value, marks = fetch(enc_query, enc_key, enc_value, marks)
    near_targets = []
    if n_ctx == 2:
        own_maps = pack(key_map, value_map, tgt_query)
        shards = [own_maps, *bring(own_maps)]
    else:
        whole = [lax.all_gather(x, "ctx", axis=0, tiled=True) for x in (key_map, value_map)]
        shards, near_targets = [pack(*whole, tgt_query)], bring(tgt_query)
    map_rows = (shards[0].shape[0] - tgt_rows) // 2

    chunks = 2
    heads = features // HEAD_DIM // chunks
    held = [None] * chunks
    for j in range(chunks):
        weights, totals = weigh(query, [own_key, *keys], [marks, *near_marks], j * heads, heads)
        held[j] = mix(weights, totals, [own_value, *values], j * heads, heads)

    order = ring_order(n_head)
    ring = [(order[i], order[(i + 1) % n_head]) for i in range(n_head)]
    before = {target: source for source, target in ring}

    def place(turn, first):
        head, ctx = lax.axis_index("head"), lax.axis_index("ctx")
        owner = 0
        for i in range(n_head):
            source = i
            for _ in range(turn):
                source = before[source]
            owner = owner + jnp.where(head == i, source, 0)
        row = owner * features + first
        if len(shards) == 1:
            return None, row
        return jnp.where(lax.div(row, map_rows) == ctx, 0, 1), lax.rem(row, map_rows)

    acc, last = None, n_head - 1
    for turn in range(last):
        if turn == last - 1:
            pieces = [p for h in held for p in halve(h)]
        else:
            pieces = held
        later = [lax.ppermute(p, "head", ring) for p in pieces]
        acc = project(acc, held, functools.partial(place, turn, 0), shards, map_rows)
        held = later
    acc = project(acc, held[:-1], functools.partial(place, last, 0), shards, map_rows)
    depth = held[-1].shape[1]
    last_maps, targets, mask = prepare(
        functools.partial(place, last, features - depth),
        depth,
        shards,
        map_rows,
        tgt_rows,
        near_targets,
        [marks, *near_marks],
    )
    own, *shares = cross_attend(acc, held[-1], last_maps, targets, mask, 1 + len(links))
    combined = [own]
    for i, (pairs, piece) in enumerate(zip(links, shares)):
        other = lax.ppermute(piece, "ctx", [(target, source) for source, target in pairs])
        if n_ctx > 2:
            end = n_ctx - 1 if i == 0 else 0
            column = lax.broadcasted_iota(jnp.int32, other.shape, 1)
            other = jnp.where((lax.axis_index("ctx") == end) & (column >= width), NEG_FILL, other)
        combined.append(other)
    return call(combine_kernel, "combine", [((tgt_rows, width), BF16)], combined, limit=4 << 20)[0]


def solution(mesh):
    in_specs = (
        P(("dp", "ctx"), "head"),
        P(("dp", "ctx"), "head"),
        P(("dp", "ctx"), "head"),
        P(("dp", "ctx")),
        P("ctx", "head"),
        P("ctx", "head"),
        P(("dp", "ctx"), "head"),
    )
    out_specs = P(("dp", "ctx"), "head")
    return jax.shard_map(
        on_device, mesh=mesh, in_specs=in_specs, out_specs=out_specs, check_vma=False
    )
```

```python
import functools

import jax
import jax.numpy as jnp
from jax import lax
from jax.experimental import pallas as pl
from jax.experimental.pallas import tpu as pltpu
from jax.sharding import PartitionSpec as P

HEAD_DIM = 256
NEG_FILL = -1e30
F32 = jnp.float32
BF16 = jnp.bfloat16
LANES = 128
SCALE = HEAD_DIM**-0.5
WEIGH_FLOPS = 6 * 10**9
SPLIT_FLOPS = 15 * 10**9
VMEM = pl.BlockSpec(memory_space=pltpu.VMEM)
HBM = pl.BlockSpec(memory_space=pltpu.HBM)


def ring_order(count):
    return list(range(0, count, 2)) + list(range(1, count, 2))[::-1]


def links_of(count):
    if count == 2:
        return [[(0, 1), (1, 0)]]
    return [[(i, i + 1) for i in range(count - 1)], [(i + 1, i) for i in range(count - 1)]]


def dot_t(a, b):
    return lax.dot_general(a, b, (((1,), (1,)), ((), ())), preferred_element_type=F32)


def dot(a, b):
    return jnp.dot(a, b, preferred_element_type=F32)


def head_columns(h):
    return slice(h * HEAD_DIM, (h + 1) * HEAD_DIM)


def down_lanes(row):
    return jnp.transpose(jnp.broadcast_to(row, (LANES, row.shape[1])))


def same_mark(down, row):
    return jnp.concatenate([down == row[:, i : i + LANES] for i in range(0, row.shape[1], LANES)], axis=1)


def softmax_block(scores, same):
    scores = jnp.where(same, scores * SCALE, NEG_FILL)
    top = jnp.max(scores, axis=1, keepdims=True)
    weights = jnp.exp(scores - top)
    return top, weights, jnp.sum(weights, axis=1, keepdims=True)


def call(kernel, name, outs, operands, flops=0, exps=0, specs=None, scratch=(), limit=8 << 20):
    out_shape = [jax.ShapeDtypeStruct(*o) for o in outs]
    moved = sum(x.size * x.dtype.itemsize for x in [*operands, *out_shape])
    return pl.pallas_call(
        kernel,
        in_specs=specs or [VMEM] * len(operands),
        out_specs=[VMEM] * len(outs),
        out_shape=out_shape,
        scratch_shapes=list(scratch),
        compiler_params=pltpu.CompilerParams(vmem_limit_bytes=limit),
        cost_estimate=pl.CostEstimate(flops=flops, bytes_accessed=moved, transcendentals=exps),
        name=name,
    )(*operands)


def run_all(copies):
    for copy in copies:
        copy.start()
    for copy in copies:
        copy.wait()


def fetch_kernel(count, *refs):
    sources, targets, sems = refs[:count], refs[count : 2 * count], refs[-1]
    run_all([pltpu.make_async_copy(s, t, sems.at[i]) for i, (s, t) in enumerate(zip(sources, targets))])


def fetch(*arrays):
    return call(
        functools.partial(fetch_kernel, len(arrays)),
        "fetch",
        [(x.shape, x.dtype) for x in arrays],
        [pltpu.with_memory_space_constraint(x, pltpu.HBM) for x in arrays],
        specs=[HBM] * len(arrays),
        scratch=[pltpu.SemaphoreType.DMA((len(arrays),))],
    )


def pack_kernel(*refs):
    sources, out_ref, sems = refs[:-2], refs[-2], refs[-1]
    copies, row = [], 0
    for i, source in enumerate(sources):
        rows = source.shape[0]
        copies.append(pltpu.make_async_copy(source, out_ref.at[pl.ds(row, rows), :], sems.at[i]))
        row += rows
    run_all(copies)


def pack(*arrays):
    rows = sum(x.shape[0] for x in arrays)
    return call(
        pack_kernel,
        "pack",
        [((rows, arrays[0].shape[1]), arrays[0].dtype)],
        [pltpu.with_memory_space_constraint(x, pltpu.HBM) for x in arrays],
        specs=[HBM] * len(arrays),
        scratch=[pltpu.SemaphoreType.DMA((len(arrays),))],
    )[0]


def weigh_kernel(blocks, first, heads, *refs):
    marks, q_ref, keys = refs[:blocks], refs[blocks], refs[blocks + 1 : 2 * blocks + 1]
    weight_ref, total_ref = refs[2 * blocks + 1 :]
    down = down_lanes(marks[0][...])
    same = jnp.concatenate([same_mark(down, m[...]) for m in marks], axis=1)
    span = same.shape[1]
    lane = lax.broadcasted_iota(jnp.int32, total_ref.shape, 1)
    totals = jnp.zeros(total_ref.shape, F32)
    for h in range(heads):
        at = head_columns(first + h)
        scores = jnp.concatenate([dot_t(q_ref[:, at], k[:, at]) for k in keys], axis=1)
        _, weights, total = softmax_block(scores, same)
        weight_ref[:, h * span : (h + 1) * span] = weights.astype(BF16)
        totals = jnp.where(lane == h, total, totals)
    total_ref[...] = totals


def weigh(query, keys, marks, first, heads):
    rows, span = query.shape[0], query.shape[0] * len(keys)
    return call(
        functools.partial(weigh_kernel, len(keys), first, heads),
        "weigh",
        [((rows, heads * span), BF16), ((rows, LANES), F32)],
        [*marks, query, *keys],
        flops=WEIGH_FLOPS,
        exps=rows * span * heads,
    )


def mix_kernel(first, heads, weight_ref, total_ref, *refs):
    values, out_ref = refs[:-1], refs[-1]
    rows = total_ref.shape[0]
    for h in range(heads):
        start = h * rows * len(values)
        summed = sum(
            dot(weight_ref[:, start + i * rows : start + (i + 1) * rows], v[:, head_columns(first + h)])
            for i, v in enumerate(values)
        )
        out_ref[:, head_columns(h)] = (summed / total_ref[:, h : h + 1]).astype(BF16)


def mix(weights, totals, values, first, heads):
    rows = totals.shape[0]
    return call(
        functools.partial(mix_kernel, first, heads),
        "mix",
        [((rows, heads * HEAD_DIM), BF16)],
        [weights, totals, *values],
        flops=2 * weights.size * HEAD_DIM,
    )[0]


def in_shard(shards, shard, act):
    if len(shards) == 1:
        act(shards[0])
    else:
        for i, maps in enumerate(shards):
            pl.when(shard == i)(functools.partial(act, maps))


def split_kernel(source, *outs):
    width = outs[0].shape[1]
    for i, out in enumerate(outs):
        out[...] = source[:, i * width : (i + 1) * width]


def split(chunk, parts):
    rows, width = chunk.shape
    return call(split_kernel, "split", [((rows, width // parts), chunk.dtype)] * parts, [chunk], flops=SPLIT_FLOPS)


def project_kernel(chunks, shards, map_rows, has_acc, place, *refs):
    e_refs, maps, out_ref = refs[:chunks], refs[chunks : chunks + shards], refs[-1]
    half = out_ref.shape[1] // 2
    depth = e_refs[0].shape[1]
    shard, row = place()
    row = pl.multiple_of(row, depth)
    chunk = jnp.concatenate([r[...] for r in e_refs], axis=1)

    def add(map_ref):
        for side in range(2):
            columns = slice(side * half, (side + 1) * half)
            product = dot(chunk, map_ref[pl.ds(side * map_rows + row, depth * chunks), :])
            out_ref[:, columns] = refs[-2][:, columns] + product if has_acc else product

    in_shard(maps, shard, add)


def project(acc, chunks, place, shards, map_rows):
    rows, depth = chunks[0].shape
    width = shards[0].shape[1]
    operands = [*chunks, *shards] + ([] if acc is None else [acc])
    return call(
        functools.partial(project_kernel, len(chunks), len(shards), map_rows, acc is not None, place),
        "project",
        [((rows, 2 * width), F32)],
        operands,
        flops=4 * rows * depth * width * len(chunks),
    )[0]


def prepare_kernel(shards, parts, map_rows, step, place, *refs):
    maps, marks, near = refs[:shards], refs[shards : shards + parts], refs[shards + parts : -4]
    map_ref, tgt_ref, mask_ref, down_ref = refs[-4:]
    shard, row = place()
    depth, width = map_ref.shape[0], map_ref.shape[1] // 2
    row = pl.multiple_of(row, depth)

    def copy(source):
        for side in range(2):
            map_ref[:, side * width : (side + 1) * width] = source[pl.ds(side * map_rows + row, depth), :]

    in_shard(maps, shard, copy)
    own = marks[0][...]
    count = tgt_ref.shape[0] // parts
    below = slice(2 * map_rows, 2 * map_rows + count)
    targets = [maps[0][below, :]] + ([r[...] for r in near] if near else [m[below, :] for m in maps[1:]])
    for i, (target, mark_ref) in enumerate(zip(targets, marks)):
        part = slice(i * count, (i + 1) * count)
        tgt_ref[part, :] = target
        down_ref[...] = down_lanes(mark_ref[...])
        down = down_ref[pl.ds(0, count, stride=step), :]
        mask_ref[part, :] = same_mark(down, own).astype(F32)


def prepare(place, depth, shards, map_rows, count, near_targets, marks):
    rows, width = marks[0].shape[1], shards[0].shape[1]
    total = count * len(marks)
    return call(
        functools.partial(prepare_kernel, len(shards), len(marks), map_rows, rows // count, place),
        "prepare",
        [((depth, 2 * width), BF16), ((total, width), BF16), ((total, rows), F32)],
        [*shards, *marks, *near_targets],
        scratch=[pltpu.VMEM((rows, LANES), jnp.int32)],
    )


def cross_kernel(acc_ref, e_ref, map_ref, tgt_ref, mask_ref, *outs):
    heads = map_ref.shape[1] // 2 // HEAD_DIM
    chunk = e_ref[...]
    memory = []
    for h in range(2 * heads):
        at = head_columns(h)
        memory.append((acc_ref[:, at] + dot(chunk, map_ref[:, at])).astype(BF16))
    keys, values = memory[:heads], memory[heads:]
    count = outs[0].shape[0]
    same = mask_ref[...] > 0
    lane = lax.broadcasted_iota(jnp.int32, (same.shape[0], LANES), 1)
    stats = jnp.zeros(lane.shape, F32)
    for h in range(heads):
        at = head_columns(h)
        top, weights, total = softmax_block(dot_t(tgt_ref[:, at], keys[h]), same)
        summed = dot(weights.astype(BF16), values[h])
        for i, out_ref in enumerate(outs):
            out_ref[:, at] = summed[i * count : (i + 1) * count]
        stats = jnp.where(lane == h, top, jnp.where(lane == heads + h, total, stats))
    for i, out_ref in enumerate(outs):
        out_ref[:, heads * HEAD_DIM :] = stats[i * count : (i + 1) * count]


def cross_attend(acc, chunk, maps, targets, mask, parts):
    width = targets.shape[1]
    count = targets.shape[0] // parts
    return call(
        cross_kernel,
        "cross_attend",
        [((count, width + LANES), F32)] * parts,
        [acc, chunk, maps, targets, mask],
        flops=2 * chunk.size * 2 * width,
    )


def combine_kernel(*refs):
    parts, out_ref = refs[:-1], refs[-1]
    width = out_ref.shape[1]
    heads = width // HEAD_DIM
    for h in range(heads):
        at = head_columns(h)
        tops = [r[:, width + h : width + h + 1] for r in parts]
        top = functools.reduce(jnp.maximum, tops)
        factors = [jnp.exp(t - top) for t in tops]
        total = sum(f * r[:, width + heads + h : width + heads + h + 1] for f, r in zip(factors, parts))
        summed = sum(f * r[:, at] for f, r in zip(factors, parts))
        out_ref[:, at] = (summed / total).astype(BF16)


def on_device(enc_query, enc_key, enc_value, doc_ids, key_map, value_map, tgt_query):
    rows, features = enc_query.shape
    tgt_rows, width = tgt_query.shape
    n_ctx, n_head = lax.axis_size("ctx"), lax.axis_size("head")
    links = links_of(n_ctx)
    bring = lambda x: [lax.ppermute(x, "ctx", pairs) for pairs in links]

    marks = (doc_ids if n_ctx == 2 else doc_ids + 1).reshape(1, rows)
    keys, near_marks, values = bring(enc_key), bring(marks), bring(enc_value)
    query, own_key, own_value, marks = fetch(enc_query, enc_key, enc_value, marks)
    chunks = 2
    heads = features // HEAD_DIM // chunks
    held = [None] * chunks
    for j in range(chunks):
        weights, totals = weigh(query, [own_key, *keys], [marks, *near_marks], j * heads, heads)
        held[j] = mix(weights, totals, [own_value, *values], j * heads, heads)

    key_map, value_map, tgt_query, held[1] = lax.optimization_barrier((key_map, value_map, tgt_query, held[1]))
    near_targets = []
    if n_ctx == 2:
        own_maps = pack(key_map, value_map, tgt_query)
        shards = [own_maps, *bring(own_maps)]
    else:
        whole = [lax.all_gather(x, "ctx", axis=0, tiled=True) for x in (key_map, value_map)]
        shards, near_targets = [pack(*whole, tgt_query)], bring(tgt_query)
    map_rows = (shards[0].shape[0] - tgt_rows) // 2

    order = ring_order(n_head)
    ring = [(order[i], order[(i + 1) % n_head]) for i in range(n_head)]
    before = {target: source for source, target in ring}

    def place(turn, first):
        head, ctx = lax.axis_index("head"), lax.axis_index("ctx")
        owner = 0
        for i in range(n_head):
            source = i
            for _ in range(turn):
                source = before[source]
            owner = owner + jnp.where(head == i, source, 0)
        row = owner * features + first
        if len(shards) == 1:
            return None, row
        return jnp.where(lax.div(row, map_rows) == ctx, 0, 1), lax.rem(row, map_rows)

    acc, last = None, n_head - 1
    for turn in range(last):
        pieces = [p for h in held for p in split(h, 2 if turn == 1 else 1)] if turn else held
        later = [lax.ppermute(p, "head", ring) for p in pieces]
        acc = project(acc, held, functools.partial(place, turn, 0), shards, map_rows)
        held = later
    acc = project(acc, held[:-1], functools.partial(place, last, 0), shards, map_rows)
    depth = held[-1].shape[1]
    last_maps, targets, mask = prepare(
        functools.partial(place, last, features - depth),
        depth,
        shards,
        map_rows,
        tgt_rows,
        near_targets,
        [marks, *near_marks],
    )
    own, *shares = cross_attend(acc, held[-1], last_maps, targets, mask, 1 + len(links))
    combined = [own]
    for i, (pairs, piece) in enumerate(zip(links, shares)):
        other = lax.ppermute(piece, "ctx", [(target, source) for source, target in pairs])
        if n_ctx > 2:
            end = n_ctx - 1 if i == 0 else 0
            column = lax.broadcasted_iota(jnp.int32, other.shape, 1)
            other = jnp.where((lax.axis_index("ctx") == end) & (column >= width), NEG_FILL, other)
        combined.append(other)
    return call(combine_kernel, "combine", [((tgt_rows, width), BF16)], combined, limit=4 << 20)[0]


def solution(mesh):
    in_specs = (
        P(("dp", "ctx"), "head"),
        P(("dp", "ctx"), "head"),
        P(("dp", "ctx"), "head"),
        P(("dp", "ctx")),
        P("ctx", "head"),
        P("ctx", "head"),
        P(("dp", "ctx"), "head"),
    )
    out_specs = P(("dp", "ctx"), "head")
    return jax.shard_map(
        on_device, mesh=mesh, in_specs=in_specs, out_specs=out_specs, check_vma=False
    )
```

```python
import functools

import jax
import jax.numpy as jnp
from jax import lax
from jax.experimental import pallas as pl
from jax.experimental.pallas import tpu as pltpu
from jax.sharding import PartitionSpec as P

HEAD_DIM = 256
NEG_FILL = -1e30
F32 = jnp.float32
BF16 = jnp.bfloat16
LANES = 128
SCALE = HEAD_DIM**-0.5
WEIGH_FLOPS = 6 * 10**9
SPLIT_FLOPS = 15 * 10**9
VMEM = pl.BlockSpec(memory_space=pltpu.VMEM)
HBM = pl.BlockSpec(memory_space=pltpu.HBM)


def ring_order(count):
    return list(range(0, count, 2)) + list(range(1, count, 2))[::-1]


def links_of(count):
    if count == 2:
        return [[(0, 1), (1, 0)]]
    return [[(i, i + 1) for i in range(count - 1)], [(i + 1, i) for i in range(count - 1)]]


def dot_t(a, b):
    return lax.dot_general(a, b, (((1,), (1,)), ((), ())), preferred_element_type=F32)


def dot(a, b):
    return jnp.dot(a, b, preferred_element_type=F32)


def head_columns(h):
    return slice(h * HEAD_DIM, (h + 1) * HEAD_DIM)


def down_lanes(row):
    return jnp.transpose(jnp.broadcast_to(row, (LANES, row.shape[1])))


def same_mark(down, row):
    return jnp.concatenate([down == row[:, i : i + LANES] for i in range(0, row.shape[1], LANES)], axis=1)


def softmax_block(scores, same):
    scores = jnp.where(same, scores * SCALE, NEG_FILL)
    top = jnp.max(scores, axis=1, keepdims=True)
    weights = jnp.exp(scores - top)
    return top, weights, jnp.sum(weights, axis=1, keepdims=True)


def call(kernel, name, outs, operands, flops=0, exps=0, specs=None, scratch=(), limit=8 << 20):
    out_shape = [jax.ShapeDtypeStruct(*o) for o in outs]
    moved = sum(x.size * x.dtype.itemsize for x in [*operands, *out_shape])
    return pl.pallas_call(
        kernel,
        in_specs=specs or [VMEM] * len(operands),
        out_specs=[VMEM] * len(outs),
        out_shape=out_shape,
        scratch_shapes=list(scratch),
        compiler_params=pltpu.CompilerParams(vmem_limit_bytes=limit),
        cost_estimate=pl.CostEstimate(flops=flops, bytes_accessed=moved, transcendentals=exps),
        name=name,
    )(*operands)


def run_all(copies):
    for copy in copies:
        copy.start()
    for copy in copies:
        copy.wait()


def fetch_kernel(count, *refs):
    sources, targets, sems = refs[:count], refs[count : 2 * count], refs[-1]
    run_all([pltpu.make_async_copy(s, t, sems.at[i]) for i, (s, t) in enumerate(zip(sources, targets))])


def fetch(*arrays):
    return call(
        functools.partial(fetch_kernel, len(arrays)),
        "fetch",
        [(x.shape, x.dtype) for x in arrays],
        [pltpu.with_memory_space_constraint(x, pltpu.HBM) for x in arrays],
        specs=[HBM] * len(arrays),
        scratch=[pltpu.SemaphoreType.DMA((len(arrays),))],
    )


def pack_kernel(*refs):
    sources, out_ref, sems = refs[:-2], refs[-2], refs[-1]
    copies, row = [], 0
    for i, source in enumerate(sources):
        rows = source.shape[0]
        copies.append(pltpu.make_async_copy(source, out_ref.at[pl.ds(row, rows), :], sems.at[i]))
        row += rows
    run_all(copies)


def pack(*arrays):
    rows = sum(x.shape[0] for x in arrays)
    return call(
        pack_kernel,
        "pack",
        [((rows, arrays[0].shape[1]), arrays[0].dtype)],
        [pltpu.with_memory_space_constraint(x, pltpu.HBM) for x in arrays],
        specs=[HBM] * len(arrays),
        scratch=[pltpu.SemaphoreType.DMA((len(arrays),))],
    )[0]


def weigh_kernel(blocks, first, heads, *refs):
    marks, q_ref, keys = refs[:blocks], refs[blocks], refs[blocks + 1 : 2 * blocks + 1]
    weight_ref, total_ref = refs[2 * blocks + 1 :]
    down = down_lanes(marks[0][...])
    same = jnp.concatenate([same_mark(down, m[...]) for m in marks], axis=1)
    span = same.shape[1]
    lane = lax.broadcasted_iota(jnp.int32, total_ref.shape, 1)
    totals = jnp.zeros(total_ref.shape, F32)
    results = []
    for h in range(heads):
        at = head_columns(first + h)
        scores = jnp.concatenate([dot_t(q_ref[:, at], k[:, at]) for k in keys], axis=1)
        _, weights, total = softmax_block(scores, same)
        results.append(weights.astype(BF16))
        totals = jnp.where(lane == h, total, totals)
    for h in range(heads):
        weight_ref[:, h * span : (h + 1) * span] = results[h]
    total_ref[...] = totals


def weigh(query, keys, marks, first, heads):
    rows, span = query.shape[0], query.shape[0] * len(keys)
    return call(
        functools.partial(weigh_kernel, len(keys), first, heads),
        "weigh",
        [((rows, heads * span), BF16), ((rows, LANES), F32)],
        [*marks, query, *keys],
        flops=WEIGH_FLOPS,
        exps=rows * span * heads,
    )


def mix_kernel(first, heads, weight_ref, total_ref, *refs):
    values, out_ref = refs[:-1], refs[-1]
    rows = total_ref.shape[0]
    results = []
    for h in range(heads):
        start = h * rows * len(values)
        summed = sum(
            dot(weight_ref[:, start + i * rows : start + (i + 1) * rows], v[:, head_columns(first + h)])
            for i, v in enumerate(values)
        )
        results.append((summed / total_ref[:, h : h + 1]).astype(BF16))
    for h in range(heads):
        out_ref[:, head_columns(h)] = results[h]


def mix(weights, totals, values, first, heads):
    rows = totals.shape[0]
    return call(
        functools.partial(mix_kernel, first, heads),
        "mix",
        [((rows, heads * HEAD_DIM), BF16)],
        [weights, totals, *values],
        flops=2 * weights.size * HEAD_DIM,
    )[0]


def in_shard(shards, shard, act):
    if len(shards) == 1:
        act(shards[0])
    else:
        for i, maps in enumerate(shards):
            pl.when(shard == i)(functools.partial(act, maps))


def split_kernel(source, *outs):
    width = outs[0].shape[1]
    for i, out in enumerate(outs):
        out[...] = source[:, i * width : (i + 1) * width]


def split(chunk, parts):
    rows, width = chunk.shape
    return call(split_kernel, "split", [((rows, width // parts), chunk.dtype)] * parts, [chunk], flops=SPLIT_FLOPS)


def project_kernel(chunks, shards, map_rows, has_acc, place, *refs):
    e_refs, maps, out_ref = refs[:chunks], refs[chunks : chunks + shards], refs[-1]
    half = out_ref.shape[1] // 2
    depth = e_refs[0].shape[1]
    shard, row = place()
    row = pl.multiple_of(row, depth)
    chunk = jnp.concatenate([r[...] for r in e_refs], axis=1)

    def add(map_ref):
        for side in range(2):
            columns = slice(side * half, (side + 1) * half)
            product = dot(chunk, map_ref[pl.ds(side * map_rows + row, depth * chunks), :])
            out_ref[:, columns] = refs[-2][:, columns] + product if has_acc else product

    in_shard(maps, shard, add)


def project(acc, chunks, place, shards, map_rows):
    rows, depth = chunks[0].shape
    width = shards[0].shape[1]
    operands = [*chunks, *shards] + ([] if acc is None else [acc])
    return call(
        functools.partial(project_kernel, len(chunks), len(shards), map_rows, acc is not None, place),
        "project",
        [((rows, 2 * width), F32)],
        operands,
        flops=4 * rows * depth * width * len(chunks),
    )[0]


def prepare_kernel(shards, parts, map_rows, step, place, *refs):
    maps, marks, near = refs[:shards], refs[shards : shards + parts], refs[shards + parts : -4]
    map_ref, tgt_ref, mask_ref, down_ref = refs[-4:]
    shard, row = place()
    depth, width = map_ref.shape[0], map_ref.shape[1] // 2
    row = pl.multiple_of(row, depth)

    def copy(source):
        for side in range(2):
            map_ref[:, side * width : (side + 1) * width] = source[pl.ds(side * map_rows + row, depth), :]

    in_shard(maps, shard, copy)
    own = marks[0][...]
    count = tgt_ref.shape[0] // parts
    below = slice(2 * map_rows, 2 * map_rows + count)
    targets = [maps[0][below, :]] + ([r[...] for r in near] if near else [m[below, :] for m in maps[1:]])
    for i, (target, mark_ref) in enumerate(zip(targets, marks)):
        part = slice(i * count, (i + 1) * count)
        tgt_ref[part, :] = target
        down_ref[...] = down_lanes(mark_ref[...])
        down = down_ref[pl.ds(0, count, stride=step), :]
        mask_ref[part, :] = same_mark(down, own).astype(F32)


def prepare(place, depth, shards, map_rows, count, near_targets, marks):
    rows, width = marks[0].shape[1], shards[0].shape[1]
    total = count * len(marks)
    return call(
        functools.partial(prepare_kernel, len(shards), len(marks), map_rows, rows // count, place),
        "prepare",
        [((depth, 2 * width), BF16), ((total, width), BF16), ((total, rows), F32)],
        [*shards, *marks, *near_targets],
        scratch=[pltpu.VMEM((rows, LANES), jnp.int32)],
    )


def cross_kernel(acc_ref, e_ref, map_ref, tgt_ref, mask_ref, *outs):
    heads = map_ref.shape[1] // 2 // HEAD_DIM
    chunk = e_ref[...]
    queries = [tgt_ref[:, head_columns(h)] for h in range(heads)]
    memory = []
    for h in range(2 * heads):
        at = head_columns(h)
        memory.append((acc_ref[:, at] + dot(chunk, map_ref[:, at])).astype(BF16))
    keys, values = memory[:heads], memory[heads:]
    count = outs[0].shape[0]
    same = mask_ref[...] > 0
    scores = [dot_t(queries[h], keys[h]) for h in range(heads)]
    tops, weights, totals = zip(*[softmax_block(x, same) for x in scores])
    summed = [dot(w.astype(BF16), v) for w, v in zip(weights, values)]
    lane = lax.broadcasted_iota(jnp.int32, (same.shape[0], LANES), 1)
    stats = jnp.zeros(lane.shape, F32)
    for h in range(heads):
        stats = jnp.where(lane == h, tops[h], jnp.where(lane == heads + h, totals[h], stats))
    for i, out_ref in enumerate(outs):
        part = slice(i * count, (i + 1) * count)
        for h in range(heads):
            out_ref[:, head_columns(h)] = summed[h][part]
        out_ref[:, heads * HEAD_DIM :] = stats[part]


def cross_attend(acc, chunk, maps, targets, mask, parts):
    width = targets.shape[1]
    count = targets.shape[0] // parts
    return call(
        cross_kernel,
        "cross_attend",
        [((count, width + LANES), F32)] * parts,
        [acc, chunk, maps, targets, mask],
        flops=2 * chunk.size * 2 * width,
    )


def combine_kernel(*refs):
    parts, out_ref = [r[...] for r in refs[:-1]], refs[-1]
    width = out_ref.shape[1]
    heads = width // HEAD_DIM
    results = []
    for h in range(heads):
        tops = [x[:, width + h : width + h + 1] for x in parts]
        totals = [x[:, width + heads + h : width + heads + h + 1] for x in parts]
        top = functools.reduce(jnp.maximum, tops)
        factors = [jnp.exp(t - top) for t in tops]
        share = 1.0 / sum(f * t for f, t in zip(factors, totals))
        results.append(sum((f * share) * x[:, head_columns(h)] for f, x in zip(factors, parts)))
    for h in range(heads):
        out_ref[:, head_columns(h)] = results[h].astype(BF16)


def on_device(enc_query, enc_key, enc_value, doc_ids, key_map, value_map, tgt_query):
    rows, features = enc_query.shape
    tgt_rows, width = tgt_query.shape
    n_ctx, n_head = lax.axis_size("ctx"), lax.axis_size("head")
    links = links_of(n_ctx)
    bring = lambda x: [lax.ppermute(x, "ctx", pairs) for pairs in links]

    marks = (doc_ids if n_ctx == 2 else doc_ids + 1).reshape(1, rows)
    keys, near_marks, values = bring(enc_key), bring(marks), bring(enc_value)
    query, own_key, own_value, marks = fetch(enc_query, enc_key, enc_value, marks)
    chunks = 2
    heads = features // HEAD_DIM // chunks
    held = [None] * chunks
    for j in range(chunks):
        weights, totals = weigh(query, [own_key, *keys], [marks, *near_marks], j * heads, heads)
        held[j] = mix(weights, totals, [own_value, *values], j * heads, heads)

    key_map, value_map, tgt_query, held[1] = lax.optimization_barrier((key_map, value_map, tgt_query, held[1]))
    near_targets = []
    if n_ctx == 2:
        own_maps = pack(key_map, value_map, tgt_query)
        shards = [own_maps, *bring(own_maps)]
    else:
        whole = [lax.all_gather(x, "ctx", axis=0, tiled=True) for x in (key_map, value_map)]
        shards, near_targets = [pack(*whole, tgt_query)], bring(tgt_query)
    map_rows = (shards[0].shape[0] - tgt_rows) // 2

    order = ring_order(n_head)
    ring = [(order[i], order[(i + 1) % n_head]) for i in range(n_head)]
    before = {target: source for source, target in ring}

    def place(turn, first):
        head, ctx = lax.axis_index("head"), lax.axis_index("ctx")
        owner = 0
        for i in range(n_head):
            source = i
            for _ in range(turn):
                source = before[source]
            owner = owner + jnp.where(head == i, source, 0)
        row = owner * features + first
        if len(shards) == 1:
            return None, row
        return jnp.where(lax.div(row, map_rows) == ctx, 0, 1), lax.rem(row, map_rows)

    acc, last = None, n_head - 1
    for turn in range(last):
        pieces = [p for h in held for p in split(h, 2 if turn == 1 else 1)] if turn else held
        later = [lax.ppermute(p, "head", ring) for p in pieces]
        acc = project(acc, held, functools.partial(place, turn, 0), shards, map_rows)
        held = later
    acc = project(acc, held[:-1], functools.partial(place, last, 0), shards, map_rows)
    depth = held[-1].shape[1]
    last_maps, targets, mask = prepare(
        functools.partial(place, last, features - depth),
        depth,
        shards,
        map_rows,
        tgt_rows,
        near_targets,
        [marks, *near_marks],
    )
    own, *shares = cross_attend(acc, held[-1], last_maps, targets, mask, 1 + len(links))
    combined = [own]
    for i, (pairs, piece) in enumerate(zip(links, shares)):
        other = lax.ppermute(piece, "ctx", [(target, source) for source, target in pairs])
        if n_ctx > 2:
            end = n_ctx - 1 if i == 0 else 0
            column = lax.broadcasted_iota(jnp.int32, other.shape, 1)
            other = jnp.where((lax.axis_index("ctx") == end) & (column >= width), NEG_FILL, other)
        combined.append(other)
    return call(combine_kernel, "combine", [((tgt_rows, width), BF16)], combined, limit=4 << 20)[0]


def solution(mesh):
    in_specs = (
        P(("dp", "ctx"), "head"),
        P(("dp", "ctx"), "head"),
        P(("dp", "ctx"), "head"),
        P(("dp", "ctx")),
        P("ctx", "head"),
        P("ctx", "head"),
        P(("dp", "ctx"), "head"),
    )
    out_specs = P(("dp", "ctx"), "head")
    return jax.shard_map(
        on_device, mesh=mesh, in_specs=in_specs, out_specs=out_specs, check_vma=False
    )
```

```python
import functools

import jax
import jax.numpy as jnp
from jax import lax
from jax.experimental import pallas as pl
from jax.experimental.pallas import tpu as pltpu
from jax.sharding import PartitionSpec as P

HEAD_DIM = 256
NEG_FILL = -1e30
F32 = jnp.float32
BF16 = jnp.bfloat16
LANES = 128
SCALE = HEAD_DIM**-0.5
WEIGH_FLOPS = 6 * 10**9
SPLIT_FLOPS = 15 * 10**9
VMEM = pl.BlockSpec(memory_space=pltpu.VMEM)
HBM = pl.BlockSpec(memory_space=pltpu.HBM)


def ring_order(count):
    return list(range(0, count, 2)) + list(range(1, count, 2))[::-1]


def links_of(count):
    if count == 2:
        return [[(0, 1), (1, 0)]]
    return [[(i, i + 1) for i in range(count - 1)], [(i + 1, i) for i in range(count - 1)]]


def dot_t(a, b):
    return lax.dot_general(a, b, (((1,), (1,)), ((), ())), preferred_element_type=F32)


def dot(a, b):
    return jnp.dot(a, b, preferred_element_type=F32)


def head_columns(h):
    return slice(h * HEAD_DIM, (h + 1) * HEAD_DIM)


def down_lanes(row):
    return jnp.transpose(jnp.broadcast_to(row, (LANES, row.shape[1])))


def same_mark(down, row):
    return jnp.concatenate([down == row[:, i : i + LANES] for i in range(0, row.shape[1], LANES)], axis=1)


def softmax_block(scores, same):
    scores = jnp.where(same, scores * SCALE, NEG_FILL)
    top = jnp.max(scores, axis=1, keepdims=True)
    weights = jnp.exp(scores - top)
    return top, weights, jnp.sum(weights, axis=1, keepdims=True)


def call(kernel, name, outs, operands, flops=0, exps=0, specs=None, scratch=(), limit=8 << 20):
    out_shape = [jax.ShapeDtypeStruct(*o) for o in outs]
    moved = sum(x.size * x.dtype.itemsize for x in [*operands, *out_shape])
    return pl.pallas_call(
        kernel,
        in_specs=specs or [VMEM] * len(operands),
        out_specs=[VMEM] * len(outs),
        out_shape=out_shape,
        scratch_shapes=list(scratch),
        compiler_params=pltpu.CompilerParams(vmem_limit_bytes=limit),
        cost_estimate=pl.CostEstimate(flops=flops, bytes_accessed=moved, transcendentals=exps),
        name=name,
    )(*operands)


def run_all(copies):
    for copy in copies:
        copy.start()
    for copy in copies:
        copy.wait()


def fetch_kernel(count, *refs):
    sources, targets, sems = refs[:count], refs[count : 2 * count], refs[-1]
    run_all([pltpu.make_async_copy(s, t, sems.at[i]) for i, (s, t) in enumerate(zip(sources, targets))])


def fetch(*arrays):
    return call(
        functools.partial(fetch_kernel, len(arrays)),
        "fetch",
        [(x.shape, x.dtype) for x in arrays],
        [pltpu.with_memory_space_constraint(x, pltpu.HBM) for x in arrays],
        specs=[HBM] * len(arrays),
        scratch=[pltpu.SemaphoreType.DMA((len(arrays),))],
    )


def pack_kernel(*refs):
    sources, out_ref, sems = refs[:-3], refs[-2], refs[-1]
    copies, row = [], 0
    for i, source in enumerate(sources):
        rows = source.shape[0]
        copies.append(pltpu.make_async_copy(source, out_ref.at[pl.ds(row, rows), :], sems.at[i]))
        row += rows
    run_all(copies)


def pack(*arrays, after):
    rows = sum(x.shape[0] for x in arrays)
    return call(
        pack_kernel,
        "pack",
        [((rows, arrays[0].shape[1]), arrays[0].dtype)],
        [pltpu.with_memory_space_constraint(x, pltpu.HBM) for x in arrays] + [after],
        specs=[HBM] * len(arrays) + [VMEM],
        scratch=[pltpu.SemaphoreType.DMA((len(arrays),))],
    )[0]


def weigh_kernel(blocks, first, heads, *refs):
    marks, q_ref, keys = refs[:blocks], refs[blocks], refs[blocks + 1 : 2 * blocks + 1]
    weight_ref, total_ref = refs[2 * blocks + 1 :]
    down = down_lanes(marks[0][...])
    same = jnp.concatenate([same_mark(down, m[...]) for m in marks], axis=1)
    span = same.shape[1]
    lane = lax.broadcasted_iota(jnp.int32, total_ref.shape, 1)
    totals = jnp.zeros(total_ref.shape, F32)
    results = []
    for h in range(heads):
        at = head_columns(first + h)
        scores = jnp.concatenate([dot_t(q_ref[:, at], k[:, at]) for k in keys], axis=1)
        _, weights, total = softmax_block(scores, same)
        results.append(weights.astype(BF16))
        totals = jnp.where(lane == h, total, totals)
    for h in range(heads):
        weight_ref[:, h * span : (h + 1) * span] = results[h]
    total_ref[...] = totals


def weigh(query, keys, marks, first, heads):
    rows, span = query.shape[0], query.shape[0] * len(keys)
    return call(
        functools.partial(weigh_kernel, len(keys), first, heads),
        "weigh",
        [((rows, heads * span), BF16), ((rows, LANES), F32)],
        [*marks, query, *keys],
        flops=WEIGH_FLOPS,
        exps=rows * span * heads,
    )


def mix_kernel(first, heads, weight_ref, total_ref, *refs):
    values, out_ref = refs[:-1], refs[-1]
    rows = total_ref.shape[0]
    results = []
    for h in range(heads):
        start = h * rows * len(values)
        summed = sum(
            dot(weight_ref[:, start + i * rows : start + (i + 1) * rows], v[:, head_columns(first + h)])
            for i, v in enumerate(values)
        )
        results.append((summed / total_ref[:, h : h + 1]).astype(BF16))
    for h in range(heads):
        out_ref[:, head_columns(h)] = results[h]


def mix(weights, totals, values, first, heads):
    rows = totals.shape[0]
    return call(
        functools.partial(mix_kernel, first, heads),
        "mix",
        [((rows, heads * HEAD_DIM), BF16)],
        [weights, totals, *values],
        flops=2 * weights.size * HEAD_DIM,
    )[0]


def in_shard(shards, shard, act):
    if len(shards) == 1:
        act(shards[0])
    else:
        for i, maps in enumerate(shards):
            pl.when(shard == i)(functools.partial(act, maps))


def split_kernel(source, *outs):
    width = outs[0].shape[1]
    for i, out in enumerate(outs):
        out[...] = source[:, i * width : (i + 1) * width]


def split(chunk, parts):
    rows, width = chunk.shape
    return call(split_kernel, "split", [((rows, width // parts), chunk.dtype)] * parts, [chunk], flops=SPLIT_FLOPS)


def project_kernel(chunks, shards, map_rows, has_acc, place, *refs):
    e_refs, maps, out_ref = refs[:chunks], refs[chunks : chunks + shards], refs[-1]
    half = out_ref.shape[1] // 2
    depth = e_refs[0].shape[1]
    shard, row = place()
    row = pl.multiple_of(row, depth)
    chunk = jnp.concatenate([r[...] for r in e_refs], axis=1)

    def add(map_ref):
        for side in range(2):
            columns = slice(side * half, (side + 1) * half)
            product = dot(chunk, map_ref[pl.ds(side * map_rows + row, depth * chunks), :])
            out_ref[:, columns] = refs[-2][:, columns] + product if has_acc else product

    in_shard(maps, shard, add)


def project(acc, chunks, place, shards, map_rows):
    rows, depth = chunks[0].shape
    width = shards[0].shape[1]
    operands = [*chunks, *shards] + ([] if acc is None else [acc])
    return call(
        functools.partial(project_kernel, len(chunks), len(shards), map_rows, acc is not None, place),
        "project",
        [((rows, 2 * width), F32)],
        operands,
        flops=4 * rows * depth * width * len(chunks),
    )[0]


def prepare_kernel(shards, parts, map_rows, step, place, *refs):
    maps, marks, near = refs[:shards], refs[shards : shards + parts], refs[shards + parts : -4]
    map_ref, tgt_ref, mask_ref, down_ref = refs[-4:]
    shard, row = place()
    depth, width = map_ref.shape[0], map_ref.shape[1] // 2
    row = pl.multiple_of(row, depth)

    def copy(source):
        for side in range(2):
            map_ref[:, side * width : (side + 1) * width] = source[pl.ds(side * map_rows + row, depth), :]

    in_shard(maps, shard, copy)
    own = marks[0][...]
    count = tgt_ref.shape[0] // parts
    below = slice(2 * map_rows, 2 * map_rows + count)
    targets = [maps[0][below, :]] + ([r[...] for r in near] if near else [m[below, :] for m in maps[1:]])
    for i, (target, mark_ref) in enumerate(zip(targets, marks)):
        part = slice(i * count, (i + 1) * count)
        tgt_ref[part, :] = target
        down_ref[...] = down_lanes(mark_ref[...])
        down = down_ref[pl.ds(0, count, stride=step), :]
        mask_ref[part, :] = same_mark(down, own).astype(F32)


def prepare(place, depth, shards, map_rows, count, near_targets, marks):
    rows, width = marks[0].shape[1], shards[0].shape[1]
    total = count * len(marks)
    return call(
        functools.partial(prepare_kernel, len(shards), len(marks), map_rows, rows // count, place),
        "prepare",
        [((depth, 2 * width), BF16), ((total, width), BF16), ((total, rows), F32)],
        [*shards, *marks, *near_targets],
        scratch=[pltpu.VMEM((rows, LANES), jnp.int32)],
    )


def cross_kernel(acc_ref, e_ref, map_ref, tgt_ref, mask_ref, *outs):
    heads = map_ref.shape[1] // 2 // HEAD_DIM
    chunk = e_ref[...]
    queries = [tgt_ref[:, head_columns(h)] for h in range(heads)]
    memory = []
    for h in range(2 * heads):
        at = head_columns(h)
        memory.append((acc_ref[:, at] + dot(chunk, map_ref[:, at])).astype(BF16))
    keys, values = memory[:heads], memory[heads:]
    count = outs[0].shape[0]
    same = mask_ref[...] > 0
    scores = [dot_t(queries[h], keys[h]) for h in range(heads)]
    tops, weights, totals = zip(*[softmax_block(x, same) for x in scores])
    summed = [dot(w.astype(BF16), v) for w, v in zip(weights, values)]
    lane = lax.broadcasted_iota(jnp.int32, (same.shape[0], LANES), 1)
    stats = jnp.zeros(lane.shape, F32)
    for h in range(heads):
        stats = jnp.where(lane == h, tops[h], jnp.where(lane == heads + h, totals[h], stats))
    for i, out_ref in enumerate(outs):
        part = slice(i * count, (i + 1) * count)
        for h in range(heads):
            out_ref[:, head_columns(h)] = summed[h][part]
        out_ref[:, heads * HEAD_DIM :] = stats[part]


def cross_attend(acc, chunk, maps, targets, mask, parts):
    width = targets.shape[1]
    count = targets.shape[0] // parts
    return call(
        cross_kernel,
        "cross_attend",
        [((count, width + LANES), F32)] * parts,
        [acc, chunk, maps, targets, mask],
        flops=2 * chunk.size * 2 * width,
    )


def combine_kernel(*refs):
    parts, out_ref = [r[...] for r in refs[:-1]], refs[-1]
    width = out_ref.shape[1]
    heads = width // HEAD_DIM
    results = []
    for h in range(heads):
        tops = [x[:, width + h : width + h + 1] for x in parts]
        totals = [x[:, width + heads + h : width + heads + h + 1] for x in parts]
        top = functools.reduce(jnp.maximum, tops)
        factors = [jnp.exp(t - top) for t in tops]
        share = 1.0 / sum(f * t for f, t in zip(factors, totals))
        results.append(sum((f * share) * x[:, head_columns(h)] for f, x in zip(factors, parts)))
    for h in range(heads):
        out_ref[:, head_columns(h)] = results[h].astype(BF16)


def on_device(enc_query, enc_key, enc_value, doc_ids, key_map, value_map, tgt_query):
    rows, features = enc_query.shape
    tgt_rows, width = tgt_query.shape
    n_ctx, n_head = lax.axis_size("ctx"), lax.axis_size("head")
    links = links_of(n_ctx)
    bring = lambda x: [lax.ppermute(x, "ctx", pairs) for pairs in links]

    marks = (doc_ids if n_ctx == 2 else doc_ids + 1).reshape(1, rows)
    keys, near_marks, values = bring(enc_key), bring(marks), bring(enc_value)
    opened = lax.ppermute(marks, "head", [(i + 1, i) for i in range(n_head - 1)])
    query, own_key, own_value, marks = fetch(enc_query, enc_key, enc_value, marks)
    chunks = 2
    heads = features // HEAD_DIM // chunks
    held = [None] * chunks
    for j in range(chunks):
        weights, totals = weigh(query, [own_key, *keys], [marks, *near_marks], j * heads, heads)
        held[j] = mix(weights, totals, [own_value, *values], j * heads, heads)

    key_map, value_map, tgt_query, held[1] = lax.optimization_barrier((key_map, value_map, tgt_query, held[1]))
    near_targets = []
    if n_ctx == 2:
        own_maps = pack(key_map, value_map, tgt_query, after=opened)
        shards = [own_maps, *bring(own_maps)]
    else:
        whole = [lax.all_gather(x, "ctx", axis=0, tiled=True) for x in (key_map, value_map)]
        shards, near_targets = [pack(*whole, tgt_query, after=opened)], bring(tgt_query)
    map_rows = (shards[0].shape[0] - tgt_rows) // 2

    order = ring_order(n_head)
    ring = [(order[i], order[(i + 1) % n_head]) for i in range(n_head)]
    before = {target: source for source, target in ring}

    def place(turn, first):
        head, ctx = lax.axis_index("head"), lax.axis_index("ctx")
        owner = 0
        for i in range(n_head):
            source = i
            for _ in range(turn):
                source = before[source]
            owner = owner + jnp.where(head == i, source, 0)
        row = owner * features + first
        if len(shards) == 1:
            return None, row
        return jnp.where(lax.div(row, map_rows) == ctx, 0, 1), lax.rem(row, map_rows)

    acc, last = None, n_head - 1
    for turn in range(last):
        pieces = [p for h in held for p in split(h, 2 if turn == 1 else 1)] if turn else held
        later = [lax.ppermute(p, "head", ring) for p in pieces]
        acc = project(acc, held, functools.partial(place, turn, 0), shards, map_rows)
        held = later
    acc = project(acc, held[:-1], functools.partial(place, last, 0), shards, map_rows)
    depth = held[-1].shape[1]
    last_maps, targets, mask = prepare(
        functools.partial(place, last, features - depth),
        depth,
        shards,
        map_rows,
        tgt_rows,
        near_targets,
        [marks, *near_marks],
    )
    own, *shares = cross_attend(acc, held[-1], last_maps, targets, mask, 1 + len(links))
    combined = [own]
    for i, (pairs, piece) in enumerate(zip(links, shares)):
        other = lax.ppermute(piece, "ctx", [(target, source) for source, target in pairs])
        if n_ctx > 2:
            end = n_ctx - 1 if i == 0 else 0
            column = lax.broadcasted_iota(jnp.int32, other.shape, 1)
            other = jnp.where((lax.axis_index("ctx") == end) & (column >= width), NEG_FILL, other)
        combined.append(other)
    return call(combine_kernel, "combine", [((tgt_rows, width), BF16)], combined, limit=4 << 20)[0]


def solution(mesh):
    in_specs = (
        P(("dp", "ctx"), "head"),
        P(("dp", "ctx"), "head"),
        P(("dp", "ctx"), "head"),
        P(("dp", "ctx")),
        P("ctx", "head"),
        P("ctx", "head"),
        P(("dp", "ctx"), "head"),
    )
    out_specs = P(("dp", "ctx"), "head")
    return jax.shard_map(
        on_device, mesh=mesh, in_specs=in_specs, out_specs=out_specs, check_vma=False
    )
```

```python
import functools

import jax
import jax.numpy as jnp
from jax import lax
from jax.experimental import pallas as pl
from jax.experimental.pallas import tpu as pltpu
from jax.sharding import PartitionSpec as P

HEAD_DIM = 256
NEG_FILL = -1e30
F32 = jnp.float32
BF16 = jnp.bfloat16
LANES = 128
SCALE = HEAD_DIM**-0.5
WEIGH_FLOPS = 6 * 10**9
SPLIT_FLOPS = 15 * 10**9
VMEM = pl.BlockSpec(memory_space=pltpu.VMEM)
HBM = pl.BlockSpec(memory_space=pltpu.HBM)


def ring_order(count):
    return list(range(0, count, 2)) + list(range(1, count, 2))[::-1]


def links_of(count):
    if count == 2:
        return [[(0, 1), (1, 0)]]
    return [[(i, i + 1) for i in range(count - 1)], [(i + 1, i) for i in range(count - 1)]]


def dot_t(a, b):
    return lax.dot_general(a, b, (((1,), (1,)), ((), ())), preferred_element_type=F32)


def dot(a, b):
    return jnp.dot(a, b, preferred_element_type=F32)


def head_columns(h):
    return slice(h * HEAD_DIM, (h + 1) * HEAD_DIM)


def down_lanes(row):
    return jnp.transpose(jnp.broadcast_to(row, (LANES, row.shape[1])))


def same_mark(down, row):
    return jnp.concatenate([down == row[:, i : i + LANES] for i in range(0, row.shape[1], LANES)], axis=1)


def softmax_block(scores, same):
    scores = jnp.where(same, scores * SCALE, NEG_FILL)
    top = jnp.max(scores, axis=1, keepdims=True)
    weights = jnp.exp(scores - top)
    return top, weights, jnp.sum(weights, axis=1, keepdims=True)


def call(kernel, name, outs, operands, flops=0, exps=0, specs=None, scratch=(), limit=8 << 20):
    out_shape = [jax.ShapeDtypeStruct(*o) for o in outs]
    moved = sum(x.size * x.dtype.itemsize for x in [*operands, *out_shape])
    return pl.pallas_call(
        kernel,
        in_specs=specs or [VMEM] * len(operands),
        out_specs=[VMEM] * len(outs),
        out_shape=out_shape,
        scratch_shapes=list(scratch),
        compiler_params=pltpu.CompilerParams(vmem_limit_bytes=limit),
        cost_estimate=pl.CostEstimate(flops=flops, bytes_accessed=moved, transcendentals=exps),
        name=name,
    )(*operands)


def run_all(copies):
    for copy in copies:
        copy.start()
    for copy in copies:
        copy.wait()


def fetch_kernel(count, *refs):
    sources, targets, sems = refs[:count], refs[count : 2 * count], refs[-1]
    run_all([pltpu.make_async_copy(s, t, sems.at[i]) for i, (s, t) in enumerate(zip(sources, targets))])


def fetch(*arrays):
    return call(
        functools.partial(fetch_kernel, len(arrays)),
        "fetch",
        [(x.shape, x.dtype) for x in arrays],
        [pltpu.with_memory_space_constraint(x, pltpu.HBM) for x in arrays],
        specs=[HBM] * len(arrays),
        scratch=[pltpu.SemaphoreType.DMA((len(arrays),))],
    )


def pack_kernel(*refs):
    sources, out_ref, sems = refs[:-2], refs[-2], refs[-1]
    copies, row = [], 0
    for i, source in enumerate(sources):
        rows = source.shape[0]
        copies.append(pltpu.make_async_copy(source, out_ref.at[pl.ds(row, rows), :], sems.at[i]))
        row += rows
    run_all(copies)


def pack(*arrays):
    rows = sum(x.shape[0] for x in arrays)
    return call(
        pack_kernel,
        "pack",
        [((rows, arrays[0].shape[1]), arrays[0].dtype)],
        [pltpu.with_memory_space_constraint(x, pltpu.HBM) for x in arrays],
        specs=[HBM] * len(arrays),
        scratch=[pltpu.SemaphoreType.DMA((len(arrays),))],
    )[0]


def weigh_kernel(blocks, first, heads, *refs):
    marks, q_ref, keys = refs[:blocks], refs[blocks], refs[blocks + 1 : 2 * blocks + 1]
    weight_ref, total_ref = refs[2 * blocks + 1 :]
    down = down_lanes(marks[0][...])
    same = jnp.concatenate([same_mark(down, m[...]) for m in marks], axis=1)
    span = same.shape[1]
    lane = lax.broadcasted_iota(jnp.int32, total_ref.shape, 1)
    totals = jnp.zeros(total_ref.shape, F32)
    results = []
    for h in range(heads):
        at = head_columns(first + h)
        scores = jnp.concatenate([dot_t(q_ref[:, at], k[:, at]) for k in keys], axis=1)
        _, weights, total = softmax_block(scores, same)
        results.append(weights.astype(BF16))
        totals = jnp.where(lane == h, 1.0 / total, totals)
    for h in range(heads):
        weight_ref[:, h * span : (h + 1) * span] = results[h]
    total_ref[...] = totals


def weigh(query, keys, marks, first, heads):
    rows, span = query.shape[0], query.shape[0] * len(keys)
    return call(
        functools.partial(weigh_kernel, len(keys), first, heads),
        "weigh",
        [((rows, heads * span), BF16), ((rows, LANES), F32)],
        [*marks, query, *keys],
        flops=WEIGH_FLOPS,
        exps=rows * span * heads,
    )


def mix_kernel(skip, first, heads, weight_ref, total_ref, *refs):
    values, out_ref = refs[:-1], refs[-1]
    rows = total_ref.shape[0]
    results = []
    for h in range(heads):
        start = (skip + h) * rows * len(values)
        summed = sum(
            dot(weight_ref[:, start + i * rows : start + (i + 1) * rows], v[:, head_columns(first + h)])
            for i, v in enumerate(values)
        )
        results.append((summed * total_ref[:, skip + h : skip + h + 1]).astype(BF16))
    for h in range(heads):
        out_ref[:, head_columns(h)] = results[h]


def mix(weights, totals, values, skip, first, heads):
    rows = totals.shape[0]
    return call(
        functools.partial(mix_kernel, skip, first, heads),
        "mix",
        [((rows, heads * HEAD_DIM), BF16)],
        [weights, totals, *values],
        flops=2 * rows * rows * len(values) * heads * HEAD_DIM,
    )[0]


def in_shard(shards, shard, act):
    if len(shards) == 1:
        act(shards[0])
    else:
        for i, maps in enumerate(shards):
            pl.when(shard == i)(functools.partial(act, maps))


def split_kernel(source, *outs):
    width = outs[0].shape[1]
    for i, out in enumerate(outs):
        out[...] = source[:, i * width : (i + 1) * width]


def split(chunk, parts):
    rows, width = chunk.shape
    return call(split_kernel, "split", [((rows, width // parts), chunk.dtype)] * parts, [chunk], flops=SPLIT_FLOPS)


def project_kernel(chunks, shards, map_rows, has_acc, place, *refs):
    e_refs, maps, out_ref = refs[:chunks], refs[chunks : chunks + shards], refs[-1]
    half = out_ref.shape[1] // 2
    depth = e_refs[0].shape[1]
    shard, row = place()
    row = pl.multiple_of(row, depth)
    chunk = jnp.concatenate([r[...] for r in e_refs], axis=1)

    def add(map_ref):
        for side in range(2):
            columns = slice(side * half, (side + 1) * half)
            product = dot(chunk, map_ref[pl.ds(side * map_rows + row, chunk.shape[1]), :])
            out_ref[:, columns] = refs[-2][:, columns] + product if has_acc else product

    in_shard(maps, shard, add)


def project(acc, chunks, place, shards, map_rows):
    rows, width = chunks[0].shape[0], shards[0].shape[1]
    operands = [*chunks, *shards] + ([] if acc is None else [acc])
    return call(
        functools.partial(project_kernel, len(chunks), len(shards), map_rows, acc is not None, place),
        "project",
        [((rows, 2 * width), F32)],
        operands,
        flops=4 * width * sum(x.size for x in chunks),
    )[0]


def prepare_kernel(shards, parts, map_rows, step, place, *refs):
    maps, marks, near = refs[:shards], refs[shards : shards + parts], refs[shards + parts : -4]
    map_ref, tgt_ref, mask_ref, down_ref = refs[-4:]
    shard, row = place()
    depth, width = map_ref.shape[0], map_ref.shape[1] // 2
    row = pl.multiple_of(row, depth)

    def copy(source):
        for side in range(2):
            map_ref[:, side * width : (side + 1) * width] = source[pl.ds(side * map_rows + row, depth), :]

    in_shard(maps, shard, copy)
    own = marks[0][...]
    count = tgt_ref.shape[0] // parts
    below = slice(2 * map_rows, 2 * map_rows + count)
    targets = [maps[0][below, :]] + ([r[...] for r in near] if near else [m[below, :] for m in maps[1:]])
    for i, (target, mark_ref) in enumerate(zip(targets, marks)):
        part = slice(i * count, (i + 1) * count)
        tgt_ref[part, :] = target
        down_ref[...] = down_lanes(mark_ref[...])
        down = down_ref[pl.ds(0, count, stride=step), :]
        mask_ref[part, :] = same_mark(down, own).astype(F32)


def prepare(place, depth, shards, map_rows, count, near_targets, marks):
    rows, width = marks[0].shape[1], shards[0].shape[1]
    total = count * len(marks)
    return call(
        functools.partial(prepare_kernel, len(shards), len(marks), map_rows, rows // count, place),
        "prepare",
        [((depth, 2 * width), BF16), ((total, width), BF16), ((total, rows), F32)],
        [*shards, *marks, *near_targets],
        scratch=[pltpu.VMEM((rows, LANES), jnp.int32)],
    )


def cross_kernel(acc_ref, e_ref, map_ref, tgt_ref, mask_ref, *outs):
    heads = map_ref.shape[1] // 2 // HEAD_DIM
    chunk = e_ref[...]
    queries = [tgt_ref[:, head_columns(h)] for h in range(heads)]
    memory = []
    for h in range(2 * heads):
        at = head_columns(h)
        memory.append((acc_ref[:, at] + dot(chunk, map_ref[:, at])).astype(BF16))
    keys, values = memory[:heads], memory[heads:]
    count = outs[0].shape[0]
    same = mask_ref[...] > 0
    scores = [dot_t(queries[h], keys[h]) for h in range(heads)]
    tops, weights, totals = zip(*[softmax_block(x, same) for x in scores])
    summed = [dot(w.astype(BF16), v) for w, v in zip(weights, values)]
    lane = lax.broadcasted_iota(jnp.int32, (same.shape[0], LANES), 1)
    stats = jnp.zeros(lane.shape, F32)
    for h in range(heads):
        stats = jnp.where(lane == h, tops[h], jnp.where(lane == heads + h, totals[h], stats))
    for i, out_ref in enumerate(outs):
        part = slice(i * count, (i + 1) * count)
        for h in range(heads):
            out_ref[:, head_columns(h)] = summed[h][part]
        out_ref[:, heads * HEAD_DIM :] = stats[part]


def cross_attend(acc, chunk, maps, targets, mask, parts):
    width = targets.shape[1]
    count = targets.shape[0] // parts
    return call(
        cross_kernel,
        "cross_attend",
        [((count, width + LANES), F32)] * parts,
        [acc, chunk, maps, targets, mask],
        flops=2 * chunk.size * 2 * width,
    )


def combine_kernel(*refs):
    parts, out_ref = [r[...] for r in refs[:-1]], refs[-1]
    width = out_ref.shape[1]
    heads = width // HEAD_DIM
    results = []
    for h in range(heads):
        tops = [x[:, width + h : width + h + 1] for x in parts]
        totals = [x[:, width + heads + h : width + heads + h + 1] for x in parts]
        top = functools.reduce(jnp.maximum, tops)
        factors = [jnp.exp(t - top) for t in tops]
        share = 1.0 / sum(f * t for f, t in zip(factors, totals))
        results.append(sum((f * share) * x[:, head_columns(h)] for f, x in zip(factors, parts)))
    for h in range(heads):
        out_ref[:, head_columns(h)] = results[h].astype(BF16)


def on_device(enc_query, enc_key, enc_value, doc_ids, key_map, value_map, tgt_query):
    rows, features = enc_query.shape
    tgt_rows, width = tgt_query.shape
    n_ctx, n_head = lax.axis_size("ctx"), lax.axis_size("head")
    links = links_of(n_ctx)
    bring = lambda x: [lax.ppermute(x, "ctx", pairs) for pairs in links]

    marks = (doc_ids if n_ctx == 2 else doc_ids + 1).reshape(1, rows)
    keys, near_marks, values = bring(enc_key), bring(marks), bring(enc_value)
    query, own_key, own_value, marks = fetch(enc_query, enc_key, enc_value, marks)
    chunks = 2
    heads = features // HEAD_DIM // chunks
    held = []
    for j in range(chunks):
        weights, totals = weigh(query, [own_key, *keys], [marks, *near_marks], j * heads, heads)
        size = heads if j else 1
        for skip in range(0, heads, size):
            held.append(mix(weights, totals, [own_value, *values], skip, j * heads + skip, size))

    key_map, value_map, tgt_query, held[-1] = lax.optimization_barrier((key_map, value_map, tgt_query, held[-1]))
    near_targets = []
    if n_ctx == 2:
        own_maps = pack(key_map, value_map, tgt_query)
        shards = [own_maps, *bring(own_maps)]
    else:
        whole = [lax.all_gather(x, "ctx", axis=0, tiled=True) for x in (key_map, value_map)]
        shards, near_targets = [pack(*whole, tgt_query)], bring(tgt_query)
    map_rows = (shards[0].shape[0] - tgt_rows) // 2

    order = ring_order(n_head)
    ring = [(order[i], order[(i + 1) % n_head]) for i in range(n_head)]
    before = {target: source for source, target in ring}

    def place(turn, first):
        head, ctx = lax.axis_index("head"), lax.axis_index("ctx")
        owner = 0
        for i in range(n_head):
            source = i
            for _ in range(turn):
                source = before[source]
            owner = owner + jnp.where(head == i, source, 0)
        row = owner * features + first
        if len(shards) == 1:
            return None, row
        return jnp.where(lax.div(row, map_rows) == ctx, 0, 1), lax.rem(row, map_rows)

    acc, last = None, n_head - 1
    for turn in range(last):
        pieces = [p for h in held for p in split(h, h.shape[1] // HEAD_DIM)] if turn else held
        later = [lax.ppermute(p, "head", ring) for p in pieces]
        acc = project(acc, held, functools.partial(place, turn, 0), shards, map_rows)
        held = later
    acc = project(acc, held[:-1], functools.partial(place, last, 0), shards, map_rows)
    depth = held[-1].shape[1]
    last_maps, targets, mask = prepare(
        functools.partial(place, last, features - depth),
        depth,
        shards,
        map_rows,
        tgt_rows,
        near_targets,
        [marks, *near_marks],
    )
    own, *shares = cross_attend(acc, held[-1], last_maps, targets, mask, 1 + len(links))
    combined = [own]
    for i, (pairs, piece) in enumerate(zip(links, shares)):
        other = lax.ppermute(piece, "ctx", [(target, source) for source, target in pairs])
        if n_ctx > 2:
            end = n_ctx - 1 if i == 0 else 0
            column = lax.broadcasted_iota(jnp.int32, other.shape, 1)
            other = jnp.where((lax.axis_index("ctx") == end) & (column >= width), NEG_FILL, other)
        combined.append(other)
    return call(combine_kernel, "combine", [((tgt_rows, width), BF16)], combined, limit=4 << 20)[0]


def solution(mesh):
    in_specs = (
        P(("dp", "ctx"), "head"),
        P(("dp", "ctx"), "head"),
        P(("dp", "ctx"), "head"),
        P(("dp", "ctx")),
        P("ctx", "head"),
        P("ctx", "head"),
        P(("dp", "ctx"), "head"),
    )
    out_specs = P(("dp", "ctx"), "head")
    return jax.shard_map(
        on_device, mesh=mesh, in_specs=in_specs, out_specs=out_specs, check_vma=False
    )
```

```python
import functools

import jax
import jax.numpy as jnp
from jax import lax
from jax.experimental import pallas as pl
from jax.experimental.pallas import tpu as pltpu
from jax.sharding import PartitionSpec as P

HEAD_DIM = 256
NEG_FILL = -1e30
F32 = jnp.float32
BF16 = jnp.bfloat16
LANES = 128
SCALE = HEAD_DIM**-0.5
WEIGH_FLOPS = 6 * 10**9
SPLIT_FLOPS = 15 * 10**9
VMEM = pl.BlockSpec(memory_space=pltpu.VMEM)
HBM = pl.BlockSpec(memory_space=pltpu.HBM)


def ring_order(count):
    return list(range(0, count, 2)) + list(range(1, count, 2))[::-1]


def links_of(count):
    if count == 2:
        return [[(0, 1), (1, 0)]]
    return [[(i, i + 1) for i in range(count - 1)], [(i + 1, i) for i in range(count - 1)]]


def dot_t(a, b):
    return lax.dot_general(a, b, (((1,), (1,)), ((), ())), preferred_element_type=F32)


def dot(a, b):
    return jnp.dot(a, b, preferred_element_type=F32)


def head_columns(h):
    return slice(h * HEAD_DIM, (h + 1) * HEAD_DIM)


def down_lanes(row):
    return jnp.transpose(jnp.broadcast_to(row, (LANES, row.shape[1])))


def same_mark(down, row):
    return jnp.concatenate([down == row[:, i : i + LANES] for i in range(0, row.shape[1], LANES)], axis=1)


def softmax_block(scores, same):
    scores = jnp.where(same, scores * SCALE, NEG_FILL)
    top = jnp.max(scores, axis=1, keepdims=True)
    weights = jnp.exp(scores - top)
    return top, weights, jnp.sum(weights, axis=1, keepdims=True)


def call(kernel, name, outs, operands, flops=0, exps=0, specs=None, scratch=(), limit=8 << 20, out_specs=None):
    out_shape = [jax.ShapeDtypeStruct(*o) for o in outs]
    moved = sum(x.size * x.dtype.itemsize for x in [*operands, *out_shape])
    return pl.pallas_call(
        kernel,
        in_specs=specs or [VMEM] * len(operands),
        out_specs=out_specs or [VMEM] * len(outs),
        out_shape=out_shape,
        scratch_shapes=list(scratch),
        compiler_params=pltpu.CompilerParams(vmem_limit_bytes=limit),
        cost_estimate=pl.CostEstimate(flops=flops, bytes_accessed=moved, transcendentals=exps),
        name=name,
    )(*operands)


def run_all(copies):
    for copy in copies:
        copy.start()
    for copy in copies:
        copy.wait()


def fetch_kernel(count, *refs):
    sources, targets, sems = refs[:count], refs[count : 2 * count], refs[-1]
    run_all([pltpu.make_async_copy(s, t, sems.at[i]) for i, (s, t) in enumerate(zip(sources, targets))])


def fetch(*arrays):
    return call(
        functools.partial(fetch_kernel, len(arrays)),
        "fetch",
        [(x.shape, x.dtype) for x in arrays],
        [pltpu.with_memory_space_constraint(x, pltpu.HBM) for x in arrays],
        specs=[HBM] * len(arrays),
        scratch=[pltpu.SemaphoreType.DMA((len(arrays),))],
    )


def pack_kernel(*refs):
    sources, out_ref, sems = refs[:-2], refs[-2], refs[-1]
    copies, row = [], 0
    for i, source in enumerate(sources):
        rows = source.shape[0]
        copies.append(pltpu.make_async_copy(source, out_ref.at[pl.ds(row, rows), :], sems.at[i]))
        row += rows
    run_all(copies)


def pack(*arrays):
    rows = sum(x.shape[0] for x in arrays)
    return call(
        pack_kernel,
        "pack",
        [((rows, arrays[0].shape[1]), arrays[0].dtype)],
        [pltpu.with_memory_space_constraint(x, pltpu.HBM) for x in arrays],
        specs=[HBM] * len(arrays),
        scratch=[pltpu.SemaphoreType.DMA((len(arrays),))],
    )[0]


def weigh_kernel(blocks, first, heads, *refs):
    marks, q_ref, keys = refs[:blocks], refs[blocks], refs[blocks + 1 : 2 * blocks + 1]
    weight_ref, total_ref = refs[2 * blocks + 1 :]
    down = down_lanes(marks[0][...])
    same = jnp.concatenate([same_mark(down, m[...]) for m in marks], axis=1)
    span = same.shape[1]
    lane = lax.broadcasted_iota(jnp.int32, total_ref.shape, 1)
    totals = jnp.zeros(total_ref.shape, F32)
    results = []
    for h in range(heads):
        at = head_columns(first + h)
        scores = jnp.concatenate([dot_t(q_ref[:, at], k[:, at]) for k in keys], axis=1)
        _, weights, total = softmax_block(scores, same)
        results.append(weights.astype(BF16))
        totals = jnp.where(lane == h, 1.0 / total, totals)
    for h in range(heads):
        weight_ref[:, h * span : (h + 1) * span] = results[h]
    total_ref[...] = totals


def weigh(query, keys, marks, first, heads):
    rows, span = query.shape[0], query.shape[0] * len(keys)
    return call(
        functools.partial(weigh_kernel, len(keys), first, heads),
        "weigh",
        [((rows, heads * span), BF16), ((rows, LANES), F32)],
        [*marks, query, *keys],
        flops=WEIGH_FLOPS,
        exps=rows * span * heads,
    )


def mix_kernel(skip, first, heads, weight_ref, total_ref, *refs):
    values, out_ref = refs[:-1], refs[-1]
    rows = total_ref.shape[0]
    results = []
    for h in range(heads):
        start = (skip + h) * rows * len(values)
        summed = sum(
            dot(weight_ref[:, start + i * rows : start + (i + 1) * rows], v[:, head_columns(first + h)])
            for i, v in enumerate(values)
        )
        results.append((summed * total_ref[:, skip + h : skip + h + 1]).astype(BF16))
    for h in range(heads):
        out_ref[:, head_columns(h)] = results[h]


def mix(weights, totals, values, skip, first, heads):
    rows = totals.shape[0]
    return call(
        functools.partial(mix_kernel, skip, first, heads),
        "mix",
        [((rows, heads * HEAD_DIM), BF16)],
        [weights, totals, *values],
        flops=2 * rows * rows * len(values) * heads * HEAD_DIM,
    )[0]


def in_shard(shards, shard, act):
    if len(shards) == 1:
        act(shards[0])
    else:
        for i, maps in enumerate(shards):
            pl.when(shard == i)(functools.partial(act, maps))


def split_kernel(source, *outs):
    width = outs[0].shape[1]
    for i, out in enumerate(outs):
        out[...] = source[:, i * width : (i + 1) * width]


def split(chunk, parts):
    rows, width = chunk.shape
    return call(split_kernel, "split", [((rows, width // parts), chunk.dtype)] * parts, [chunk], flops=SPLIT_FLOPS)


def project_kernel(chunks, shards, map_rows, has_acc, place, *refs):
    e_refs, maps, out_ref = refs[:chunks], refs[chunks : chunks + shards], refs[-1]
    half = out_ref.shape[1] // 2
    depth = e_refs[0].shape[1]
    shard, row = place()
    row = pl.multiple_of(row, depth)
    chunk = jnp.concatenate([r[...] for r in e_refs], axis=1)

    def add(map_ref):
        for side in range(2):
            columns = slice(side * half, (side + 1) * half)
            product = dot(chunk, map_ref[pl.ds(side * map_rows + row, chunk.shape[1]), :])
            out_ref[:, columns] = refs[-2][:, columns] + product if has_acc else product

    in_shard(maps, shard, add)


def project(acc, chunks, place, shards, map_rows):
    rows, width = chunks[0].shape[0], shards[0].shape[1]
    operands = [*chunks, *shards] + ([] if acc is None else [acc])
    return call(
        functools.partial(project_kernel, len(chunks), len(shards), map_rows, acc is not None, place),
        "project",
        [((rows, 2 * width), F32)],
        operands,
        flops=4 * width * sum(x.size for x in chunks),
    )[0]


def prepare_kernel(shards, parts, map_rows, step, place, *refs):
    maps, marks, near = refs[:shards], refs[shards : shards + parts], refs[shards + parts : -4]
    map_ref, tgt_ref, mask_ref, down_ref = refs[-4:]
    shard, row = place()
    depth, width = map_ref.shape[0], map_ref.shape[1] // 2
    row = pl.multiple_of(row, depth)

    def copy(source):
        for side in range(2):
            map_ref[:, side * width : (side + 1) * width] = source[pl.ds(side * map_rows + row, depth), :]

    in_shard(maps, shard, copy)
    own = marks[0][...]
    count = tgt_ref.shape[0] // parts
    below = slice(2 * map_rows, 2 * map_rows + count)
    targets = [maps[0][below, :]] + ([r[...] for r in near] if near else [m[below, :] for m in maps[1:]])
    for i, (target, mark_ref) in enumerate(zip(targets, marks)):
        part = slice(i * count, (i + 1) * count)
        tgt_ref[part, :] = target
        down_ref[...] = down_lanes(mark_ref[...])
        down = down_ref[pl.ds(0, count, stride=step), :]
        mask_ref[part, :] = same_mark(down, own).astype(F32)


def prepare(place, depth, shards, map_rows, count, near_targets, marks):
    rows, width = marks[0].shape[1], shards[0].shape[1]
    total = count * len(marks)
    return call(
        functools.partial(prepare_kernel, len(shards), len(marks), map_rows, rows // count, place),
        "prepare",
        [((depth, 2 * width), BF16), ((total, width), BF16), ((total, rows), F32)],
        [*shards, *marks, *near_targets],
        scratch=[pltpu.VMEM((rows, LANES), jnp.int32)],
    )


def cross_kernel(acc_ref, e_ref, map_ref, tgt_ref, mask_ref, *outs):
    heads = map_ref.shape[1] // 2 // HEAD_DIM
    chunk = e_ref[...]
    queries = [tgt_ref[:, head_columns(h)] for h in range(heads)]
    memory = []
    for h in range(2 * heads):
        at = head_columns(h)
        memory.append((acc_ref[:, at] + dot(chunk, map_ref[:, at])).astype(BF16))
    keys, values = memory[:heads], memory[heads:]
    count = outs[0].shape[0]
    same = mask_ref[...] > 0
    scores = [dot_t(queries[h], keys[h]) for h in range(heads)]
    tops, weights, totals = zip(*[softmax_block(x, same) for x in scores])
    summed = [dot(w.astype(BF16), v) for w, v in zip(weights, values)]
    lane = lax.broadcasted_iota(jnp.int32, (same.shape[0], LANES), 1)
    stats = jnp.zeros(lane.shape, F32)
    for h in range(heads):
        stats = jnp.where(lane == h, tops[h], jnp.where(lane == heads + h, totals[h], stats))
    for i, out_ref in enumerate(outs):
        part = slice(i * count, (i + 1) * count)
        for h in range(heads):
            out_ref[:, head_columns(h)] = summed[h][part]
        out_ref[:, heads * HEAD_DIM :] = stats[part]


def cross_attend(acc, chunk, maps, targets, mask, parts):
    width = targets.shape[1]
    count = targets.shape[0] // parts
    return call(
        cross_kernel,
        "cross_attend",
        [((count, width + LANES), F32)] * parts,
        [acc, chunk, maps, targets, mask],
        flops=2 * chunk.size * 2 * width,
    )


def combine_kernel(*refs):
    parts, (out_hbm, out_ref, sems) = [r[...] for r in refs[:-3]], refs[-3:]
    width = out_ref.shape[1]
    heads = width // HEAD_DIM
    copies = []
    for h in range(heads):
        at = head_columns(h)
        tops = [x[:, width + h : width + h + 1] for x in parts]
        totals = [x[:, width + heads + h : width + heads + h + 1] for x in parts]
        top = functools.reduce(jnp.maximum, tops)
        factors = [jnp.exp(t - top) for t in tops]
        share = 1.0 / sum(f * t for f, t in zip(factors, totals))
        out_ref[:, at] = sum((f * share) * x[:, at] for f, x in zip(factors, parts)).astype(BF16)
        copies.append(pltpu.make_async_copy(out_ref.at[:, at], out_hbm.at[:, at], sems.at[h]))
        copies[-1].start()
    for copy in copies:
        copy.wait()


def combine(parts, width):
    count = parts[0].shape[0]
    return call(
        combine_kernel,
        "combine",
        [((count, width), BF16)],
        parts,
        scratch=[pltpu.VMEM((count, width), BF16), pltpu.SemaphoreType.DMA((width // HEAD_DIM,))],
        limit=4 << 20,
        out_specs=[HBM],
    )[0]


def on_device(enc_query, enc_key, enc_value, doc_ids, key_map, value_map, tgt_query):
    rows, features = enc_query.shape
    tgt_rows, width = tgt_query.shape
    n_ctx, n_head = lax.axis_size("ctx"), lax.axis_size("head")
    links = links_of(n_ctx)
    bring = lambda x: [lax.ppermute(x, "ctx", pairs) for pairs in links]

    marks = (doc_ids if n_ctx == 2 else doc_ids + 1).reshape(1, rows)
    keys, near_marks, values = bring(enc_key), bring(marks), bring(enc_value)
    query, own_key, own_value, marks = fetch(enc_query, enc_key, enc_value, marks)
    chunks = 2
    heads = features // HEAD_DIM // chunks
    held = []
    for j in range(chunks):
        weights, totals = weigh(query, [own_key, *keys], [marks, *near_marks], j * heads, heads)
        size = heads if j else 1
        for skip in range(0, heads, size):
            held.append(mix(weights, totals, [own_value, *values], skip, j * heads + skip, size))

    key_map, value_map, tgt_query, held[-1] = lax.optimization_barrier((key_map, value_map, tgt_query, held[-1]))
    near_targets = []
    if n_ctx == 2:
        own_maps = pack(key_map, value_map, tgt_query)
        shards = [own_maps, *bring(own_maps)]
    else:
        whole = [lax.all_gather(x, "ctx", axis=0, tiled=True) for x in (key_map, value_map)]
        shards, near_targets = [pack(*whole, tgt_query)], bring(tgt_query)
    map_rows = (shards[0].shape[0] - tgt_rows) // 2

    order = ring_order(n_head)
    ring = [(order[i], order[(i + 1) % n_head]) for i in range(n_head)]
    before = {target: source for source, target in ring}

    def place(turn, first):
        head, ctx = lax.axis_index("head"), lax.axis_index("ctx")
        owner = 0
        for i in range(n_head):
            source = i
            for _ in range(turn):
                source = before[source]
            owner = owner + jnp.where(head == i, source, 0)
        row = owner * features + first
        if len(shards) == 1:
            return None, row
        return jnp.where(lax.div(row, map_rows) == ctx, 0, 1), lax.rem(row, map_rows)

    acc, last = None, n_head - 1
    for turn in range(last):
        pieces = [p for h in held for p in split(h, h.shape[1] // HEAD_DIM)] if turn else held
        later = [lax.ppermute(p, "head", ring) for p in pieces]
        acc = project(acc, held, functools.partial(place, turn, 0), shards, map_rows)
        held = later
    acc = project(acc, held[:-1], functools.partial(place, last, 0), shards, map_rows)
    depth = held[-1].shape[1]
    last_maps, targets, mask = prepare(
        functools.partial(place, last, features - depth),
        depth,
        shards,
        map_rows,
        tgt_rows,
        near_targets,
        [marks, *near_marks],
    )
    own, *shares = cross_attend(acc, held[-1], last_maps, targets, mask, 1 + len(links))
    combined = [own]
    for i, (pairs, piece) in enumerate(zip(links, shares)):
        other = lax.ppermute(piece, "ctx", [(target, source) for source, target in pairs])
        if n_ctx > 2:
            end = n_ctx - 1 if i == 0 else 0
            column = lax.broadcasted_iota(jnp.int32, other.shape, 1)
            other = jnp.where((lax.axis_index("ctx") == end) & (column >= width), NEG_FILL, other)
        combined.append(other)
    return combine(combined, width)


def solution(mesh):
    in_specs = (
        P(("dp", "ctx"), "head"),
        P(("dp", "ctx"), "head"),
        P(("dp", "ctx"), "head"),
        P(("dp", "ctx")),
        P("ctx", "head"),
        P("ctx", "head"),
        P(("dp", "ctx"), "head"),
    )
    out_specs = P(("dp", "ctx"), "head")
    return jax.shard_map(
        on_device, mesh=mesh, in_specs=in_specs, out_specs=out_specs, check_vma=False
    )
```

```python
import functools

import jax
import jax.numpy as jnp
from jax import lax
from jax.experimental import pallas as pl
from jax.experimental.pallas import tpu as pltpu
from jax.sharding import PartitionSpec as P

HEAD_DIM = 256
NEG_FILL = -1e30
F32 = jnp.float32
BF16 = jnp.bfloat16
LANES = 128
SCALE = HEAD_DIM**-0.5
WEIGH_FLOPS = 6 * 10**9
SPLIT_FLOPS = 15 * 10**9
VMEM = pl.BlockSpec(memory_space=pltpu.VMEM)
HBM = pl.BlockSpec(memory_space=pltpu.HBM)


def ring_order(count):
    return list(range(0, count, 2)) + list(range(1, count, 2))[::-1]


def links_of(count):
    if count == 2:
        return [[(0, 1), (1, 0)]]
    return [[(i, i + 1) for i in range(count - 1)], [(i + 1, i) for i in range(count - 1)]]


def dot_t(a, b):
    return lax.dot_general(a, b, (((1,), (1,)), ((), ())), preferred_element_type=F32)


def dot(a, b):
    return jnp.dot(a, b, preferred_element_type=F32)


def head_columns(h):
    return slice(h * HEAD_DIM, (h + 1) * HEAD_DIM)


def down_lanes(row):
    return jnp.transpose(jnp.broadcast_to(row, (LANES, row.shape[1])))


def same_mark(down, row):
    return jnp.concatenate([down == row[:, i : i + LANES] for i in range(0, row.shape[1], LANES)], axis=1)


def softmax_block(scores, same):
    scores = jnp.where(same, scores * SCALE, NEG_FILL)
    top = jnp.max(scores, axis=1, keepdims=True)
    weights = jnp.exp(scores - top)
    return top, weights, jnp.sum(weights, axis=1, keepdims=True)


def call(kernel, name, outs, operands, flops=0, exps=0, specs=None, scratch=(), limit=8 << 20):
    out_shape = [jax.ShapeDtypeStruct(*o) for o in outs]
    moved = sum(x.size * x.dtype.itemsize for x in [*operands, *out_shape])
    return pl.pallas_call(
        kernel,
        in_specs=specs or [VMEM] * len(operands),
        out_specs=[VMEM] * len(outs),
        out_shape=out_shape,
        scratch_shapes=list(scratch),
        compiler_params=pltpu.CompilerParams(vmem_limit_bytes=limit),
        cost_estimate=pl.CostEstimate(flops=flops, bytes_accessed=moved, transcendentals=exps),
        name=name,
    )(*operands)


def run_all(copies):
    for copy in copies:
        copy.start()
    for copy in copies:
        copy.wait()


def fetch_kernel(count, *refs):
    sources, targets, sems = refs[:count], refs[count : 2 * count], refs[-1]
    run_all([pltpu.make_async_copy(s, t, sems.at[i]) for i, (s, t) in enumerate(zip(sources, targets))])


def fetch(*arrays):
    return call(
        functools.partial(fetch_kernel, len(arrays)),
        "fetch",
        [(x.shape, x.dtype) for x in arrays],
        [pltpu.with_memory_space_constraint(x, pltpu.HBM) for x in arrays],
        specs=[HBM] * len(arrays),
        scratch=[pltpu.SemaphoreType.DMA((len(arrays),))],
    )


def pack_kernel(*refs):
    sources, out_ref, sems = refs[:-2], refs[-2], refs[-1]
    copies, row = [], 0
    for i, source in enumerate(sources):
        rows = source.shape[0]
        copies.append(pltpu.make_async_copy(source, out_ref.at[pl.ds(row, rows), :], sems.at[i]))
        row += rows
    run_all(copies)


def pack(*arrays):
    rows = sum(x.shape[0] for x in arrays)
    return call(
        pack_kernel,
        "pack",
        [((rows, arrays[0].shape[1]), arrays[0].dtype)],
        [pltpu.with_memory_space_constraint(x, pltpu.HBM) for x in arrays],
        specs=[HBM] * len(arrays),
        scratch=[pltpu.SemaphoreType.DMA((len(arrays),))],
    )[0]


def weigh_kernel(blocks, first, heads, *refs):
    marks, q_ref, keys = refs[:blocks], refs[blocks], refs[blocks + 1 : 2 * blocks + 1]
    weight_ref, total_ref = refs[2 * blocks + 1 :]
    down = down_lanes(marks[0][...])
    same = jnp.concatenate([same_mark(down, m[...]) for m in marks], axis=1)
    span = same.shape[1]
    lane = lax.broadcasted_iota(jnp.int32, total_ref.shape, 1)
    totals = jnp.zeros(total_ref.shape, F32)
    results = []
    for h in range(heads):
        at = head_columns(first + h)
        scores = jnp.concatenate([dot_t(q_ref[:, at], k[:, at]) for k in keys], axis=1)
        _, weights, total = softmax_block(scores, same)
        results.append(weights.astype(BF16))
        totals = jnp.where(lane == h, 1.0 / total, totals)
    for h in range(heads):
        weight_ref[:, h * span : (h + 1) * span] = results[h]
    total_ref[...] = totals


def weigh(query, keys, marks, first, heads):
    rows, span = query.shape[0], query.shape[0] * len(keys)
    return call(
        functools.partial(weigh_kernel, len(keys), first, heads),
        "weigh",
        [((rows, heads * span), BF16), ((rows, LANES), F32)],
        [*marks, query, *keys],
        flops=WEIGH_FLOPS,
        exps=rows * span * heads,
    )


def mix_kernel(skip, first, heads, weight_ref, total_ref, *refs):
    values, out_ref = refs[:-1], refs[-1]
    rows = total_ref.shape[0]
    results = []
    for h in range(heads):
        start = (skip + h) * rows * len(values)
        summed = sum(
            dot(weight_ref[:, start + i * rows : start + (i + 1) * rows], v[:, head_columns(first + h)])
            for i, v in enumerate(values)
        )
        results.append((summed * total_ref[:, skip + h : skip + h + 1]).astype(BF16))
    for h in range(heads):
        out_ref[:, head_columns(h)] = results[h]


def mix(weights, totals, values, skip, first, heads):
    rows = totals.shape[0]
    return call(
        functools.partial(mix_kernel, skip, first, heads),
        "mix",
        [((rows, heads * HEAD_DIM), BF16)],
        [weights, totals, *values],
        flops=2 * rows * rows * len(values) * heads * HEAD_DIM,
    )[0]


def in_shard(shards, shard, act):
    if len(shards) == 1:
        act(shards[0])
    else:
        for i, maps in enumerate(shards):
            pl.when(shard == i)(functools.partial(act, maps))


def split_kernel(source, *outs):
    width = outs[0].shape[1]
    for i, out in enumerate(outs):
        out[...] = source[:, i * width : (i + 1) * width]


def split(chunk, parts):
    rows, width = chunk.shape
    return call(split_kernel, "split", [((rows, width // parts), chunk.dtype)] * parts, [chunk], flops=SPLIT_FLOPS)


def project_kernel(chunks, shards, map_rows, has_acc, place, *refs):
    e_refs, maps, out_ref = refs[:chunks], refs[chunks : chunks + shards], refs[-1]
    half = out_ref.shape[1] // 2
    depth = e_refs[0].shape[1]
    shard, row = place()
    row = pl.multiple_of(row, depth)
    chunk = jnp.concatenate([r[...] for r in e_refs], axis=1)

    def add(map_ref):
        for side in range(2):
            columns = slice(side * half, (side + 1) * half)
            product = dot(chunk, map_ref[pl.ds(side * map_rows + row, chunk.shape[1]), :])
            out_ref[:, columns] = refs[-2][:, columns] + product if has_acc else product

    in_shard(maps, shard, add)


def project(acc, chunks, place, shards, map_rows):
    rows, width = chunks[0].shape[0], shards[0].shape[1]
    operands = [*chunks, *shards] + ([] if acc is None else [acc])
    return call(
        functools.partial(project_kernel, len(chunks), len(shards), map_rows, acc is not None, place),
        "project",
        [((rows, 2 * width), F32)],
        operands,
        flops=4 * width * sum(x.size for x in chunks),
    )[0]


def prepare_kernel(shards, parts, map_rows, step, place, *refs):
    maps, marks, near = refs[:shards], refs[shards : shards + parts], refs[shards + parts : -4]
    map_ref, tgt_ref, mask_ref, down_ref = refs[-4:]
    shard, row = place()
    depth, width = map_ref.shape[0], map_ref.shape[1] // 2
    row = pl.multiple_of(row, depth)

    def copy(source):
        for side in range(2):
            map_ref[:, side * width : (side + 1) * width] = source[pl.ds(side * map_rows + row, depth), :]

    in_shard(maps, shard, copy)
    own = marks[0][...]
    count = tgt_ref.shape[0] // parts
    below = slice(2 * map_rows, 2 * map_rows + count)
    targets = [maps[0][below, :]] + ([r[...] for r in near] if near else [m[below, :] for m in maps[1:]])
    for i, (target, mark_ref) in enumerate(zip(targets, marks)):
        part = slice(i * count, (i + 1) * count)
        tgt_ref[part, :] = target
        down_ref[...] = down_lanes(mark_ref[...])
        down = down_ref[pl.ds(0, count, stride=step), :]
        mask_ref[part, :] = same_mark(down, own).astype(F32)


def prepare(place, depth, shards, map_rows, count, near_targets, marks):
    rows, width = marks[0].shape[1], shards[0].shape[1]
    total = count * len(marks)
    return call(
        functools.partial(prepare_kernel, len(shards), len(marks), map_rows, rows // count, place),
        "prepare",
        [((depth, 2 * width), BF16), ((total, width), BF16), ((total, rows), F32)],
        [*shards, *marks, *near_targets],
        scratch=[pltpu.VMEM((rows, LANES), jnp.int32)],
    )


def cross_kernel(acc_ref, e_ref, map_ref, tgt_ref, mask_ref, *outs):
    heads = map_ref.shape[1] // 2 // HEAD_DIM
    chunk = e_ref[...]
    queries = [tgt_ref[:, head_columns(h)] for h in range(heads)]
    memory = []
    for h in range(2 * heads):
        at = head_columns(h)
        memory.append((acc_ref[:, at] + dot(chunk, map_ref[:, at])).astype(BF16))
    keys, values = memory[:heads], memory[heads:]
    count = outs[0].shape[0]
    same = mask_ref[...] > 0
    scores = [dot_t(queries[h], keys[h]) for h in range(heads)]
    tops, weights, totals = zip(*[softmax_block(x, same) for x in scores])
    summed = [dot(w.astype(BF16), v) for w, v in zip(weights, values)]
    lane = lax.broadcasted_iota(jnp.int32, (same.shape[0], LANES), 1)
    stats = jnp.zeros(lane.shape, F32)
    for h in range(heads):
        stats = jnp.where(lane == h, tops[h], jnp.where(lane == heads + h, totals[h], stats))
    for i, out_ref in enumerate(outs):
        part = slice(i * count, (i + 1) * count)
        for h in range(heads):
            out_ref[:, head_columns(h)] = summed[h][part]
        out_ref[:, heads * HEAD_DIM :] = stats[part]


def cross_attend(acc, chunk, maps, targets, mask, parts):
    width = targets.shape[1]
    count = targets.shape[0] // parts
    return call(
        cross_kernel,
        "cross_attend",
        [((count, width + LANES), F32)] * parts,
        [acc, chunk, maps, targets, mask],
        flops=2 * chunk.size * 2 * width,
    )


def combine_kernel(*refs):
    parts, out_ref = [r[...] for r in refs[:-1]], refs[-1]
    width = out_ref.shape[1]
    heads = width // HEAD_DIM
    results = []
    for h in range(heads):
        tops = [x[:, width + h : width + h + 1] for x in parts]
        totals = [x[:, width + heads + h : width + heads + h + 1] for x in parts]
        top = functools.reduce(jnp.maximum, tops)
        factors = [jnp.exp(t - top) for t in tops]
        share = 1.0 / sum(f * t for f, t in zip(factors, totals))
        results.append(sum((f * share) * x[:, head_columns(h)] for f, x in zip(factors, parts)))
    for h in range(heads):
        out_ref[:, head_columns(h)] = results[h].astype(BF16)


def on_device(enc_query, enc_key, enc_value, doc_ids, key_map, value_map, tgt_query):
    rows, features = enc_query.shape
    tgt_rows, width = tgt_query.shape
    n_ctx, n_head = lax.axis_size("ctx"), lax.axis_size("head")
    links = links_of(n_ctx)
    bring = lambda x: [lax.ppermute(x, "ctx", pairs) for pairs in links]

    marks = (doc_ids if n_ctx == 2 else doc_ids + 1).reshape(1, rows)
    keys, near_marks, values = bring(enc_key), bring(marks), bring(enc_value)
    query, own_key, own_value, marks = fetch(enc_query, enc_key, enc_value, marks)
    chunks = 2
    heads = features // HEAD_DIM // chunks
    held = []
    for j in range(chunks):
        weights, totals = weigh(query, [own_key, *keys], [marks, *near_marks], j * heads, heads)
        size = heads if j else 1
        for skip in range(0, heads, size):
            held.append(mix(weights, totals, [own_value, *values], skip, j * heads + skip, size))

    key_map, value_map, tgt_query, held[-1] = lax.optimization_barrier((key_map, value_map, tgt_query, held[-1]))
    near_targets = []
    if n_ctx == 2:
        own_maps = pack(key_map, value_map, tgt_query)
        shards = [own_maps, *bring(own_maps)]
    else:
        whole = [lax.all_gather(x, "ctx", axis=0, tiled=True) for x in (key_map, value_map)]
        shards, near_targets = [pack(*whole, tgt_query)], bring(tgt_query)
    map_rows = (shards[0].shape[0] - tgt_rows) // 2

    order = ring_order(n_head)[::-1]
    ring = [(order[i], order[(i + 1) % n_head]) for i in range(n_head)]
    before = {target: source for source, target in ring}

    def place(turn, first):
        head, ctx = lax.axis_index("head"), lax.axis_index("ctx")
        owner = 0
        for i in range(n_head):
            source = i
            for _ in range(turn):
                source = before[source]
            owner = owner + jnp.where(head == i, source, 0)
        row = owner * features + first
        if len(shards) == 1:
            return None, row
        return jnp.where(lax.div(row, map_rows) == ctx, 0, 1), lax.rem(row, map_rows)

    acc, last = None, n_head - 1
    for turn in range(last):
        pieces = [p for h in held for p in split(h, h.shape[1] // HEAD_DIM)] if turn else held
        later = [lax.ppermute(p, "head", ring) for p in pieces]
        acc = project(acc, held, functools.partial(place, turn, 0), shards, map_rows)
        held = later
    acc = project(acc, held[:-1], functools.partial(place, last, 0), shards, map_rows)
    depth = held[-1].shape[1]
    last_maps, targets, mask = prepare(
        functools.partial(place, last, features - depth),
        depth,
        shards,
        map_rows,
        tgt_rows,
        near_targets,
        [marks, *near_marks],
    )
    own, *shares = cross_attend(acc, held[-1], last_maps, targets, mask, 1 + len(links))
    combined = [own]
    for i, (pairs, piece) in enumerate(zip(links, shares)):
        other = lax.ppermute(piece, "ctx", [(target, source) for source, target in pairs])
        if n_ctx > 2:
            end = n_ctx - 1 if i == 0 else 0
            column = lax.broadcasted_iota(jnp.int32, other.shape, 1)
            other = jnp.where((lax.axis_index("ctx") == end) & (column >= width), NEG_FILL, other)
        combined.append(other)
    return call(combine_kernel, "combine", [((tgt_rows, width), BF16)], combined, limit=4 << 20)[0]


def solution(mesh):
    in_specs = (
        P(("dp", "ctx"), "head"),
        P(("dp", "ctx"), "head"),
        P(("dp", "ctx"), "head"),
        P(("dp", "ctx")),
        P("ctx", "head"),
        P("ctx", "head"),
        P(("dp", "ctx"), "head"),
    )
    out_specs = P(("dp", "ctx"), "head")
    return jax.shard_map(
        on_device, mesh=mesh, in_specs=in_specs, out_specs=out_specs, check_vma=False
    )
```

```python
import functools

import jax
import jax.numpy as jnp
from jax import lax
from jax.experimental import pallas as pl
from jax.experimental.pallas import tpu as pltpu
from jax.sharding import PartitionSpec as P

HEAD_DIM = 256
NEG_FILL = -1e30
F32 = jnp.float32
BF16 = jnp.bfloat16
LANES = 128
SCALE = HEAD_DIM**-0.5
WEIGH_FLOPS = 6 * 10**9
SPLIT_FLOPS = 15 * 10**9
VMEM = pl.BlockSpec(memory_space=pltpu.VMEM)
HBM = pl.BlockSpec(memory_space=pltpu.HBM)


def ring_order(count):
    return list(range(0, count, 2)) + list(range(1, count, 2))[::-1]


def links_of(count):
    if count == 2:
        return [[(0, 1), (1, 0)]]
    return [[(i, i + 1) for i in range(count - 1)], [(i + 1, i) for i in range(count - 1)]]


def dot_t(a, b):
    return lax.dot_general(a, b, (((1,), (1,)), ((), ())), preferred_element_type=F32)


def dot(a, b):
    return jnp.dot(a, b, preferred_element_type=F32)


def head_columns(h):
    return slice(h * HEAD_DIM, (h + 1) * HEAD_DIM)


def down_lanes(row):
    return jnp.transpose(jnp.broadcast_to(row, (LANES, row.shape[1])))


def same_mark(down, row):
    return jnp.concatenate([down == row[:, i : i + LANES] for i in range(0, row.shape[1], LANES)], axis=1)


def softmax_block(scores, same):
    scores = jnp.where(same, scores * SCALE, NEG_FILL)
    top = jnp.max(scores, axis=1, keepdims=True)
    weights = jnp.exp(scores - top)
    return top, weights, jnp.sum(weights, axis=1, keepdims=True)


def call(kernel, name, outs, operands, flops=0, exps=0, specs=None, scratch=(), limit=8 << 20):
    out_shape = [jax.ShapeDtypeStruct(*o) for o in outs]
    moved = sum(x.size * x.dtype.itemsize for x in [*operands, *out_shape])
    return pl.pallas_call(
        kernel,
        in_specs=specs or [VMEM] * len(operands),
        out_specs=[VMEM] * len(outs),
        out_shape=out_shape,
        scratch_shapes=list(scratch),
        compiler_params=pltpu.CompilerParams(vmem_limit_bytes=limit),
        cost_estimate=pl.CostEstimate(flops=flops, bytes_accessed=moved, transcendentals=exps),
        name=name,
    )(*operands)


def run_all(copies):
    for copy in copies:
        copy.start()
    for copy in copies:
        copy.wait()


def fetch_kernel(count, *refs):
    sources, targets, sems = refs[:count], refs[count : 2 * count], refs[-1]
    run_all([pltpu.make_async_copy(s, t, sems.at[i]) for i, (s, t) in enumerate(zip(sources, targets))])


def fetch(*arrays):
    return call(
        functools.partial(fetch_kernel, len(arrays)),
        "fetch",
        [(x.shape, x.dtype) for x in arrays],
        [pltpu.with_memory_space_constraint(x, pltpu.HBM) for x in arrays],
        specs=[HBM] * len(arrays),
        scratch=[pltpu.SemaphoreType.DMA((len(arrays),))],
    )


def pack_kernel(*refs):
    sources, out_ref, sems = refs[:-2], refs[-2], refs[-1]
    copies, row = [], 0
    for i, source in enumerate(sources):
        rows = source.shape[0]
        copies.append(pltpu.make_async_copy(source, out_ref.at[pl.ds(row, rows), :], sems.at[i]))
        row += rows
    run_all(copies)


def pack(*arrays):
    rows = sum(x.shape[0] for x in arrays)
    return call(
        pack_kernel,
        "pack",
        [((rows, arrays[0].shape[1]), arrays[0].dtype)],
        [pltpu.with_memory_space_constraint(x, pltpu.HBM) for x in arrays],
        specs=[HBM] * len(arrays),
        scratch=[pltpu.SemaphoreType.DMA((len(arrays),))],
    )[0]


def weigh_kernel(blocks, first, heads, *refs):
    marks, q_ref, keys = refs[:blocks], refs[blocks], refs[blocks + 1 : 2 * blocks + 1]
    weight_ref, total_ref = refs[2 * blocks + 1 :]
    down = down_lanes(marks[0][...])
    same = jnp.concatenate([same_mark(down, m[...]) for m in marks], axis=1)
    span = same.shape[1]
    lane = lax.broadcasted_iota(jnp.int32, total_ref.shape, 1)
    totals = jnp.zeros(total_ref.shape, F32)
    results = []
    for h in range(heads):
        at = head_columns(first + h)
        scores = jnp.concatenate([dot_t(q_ref[:, at], k[:, at]) for k in keys], axis=1)
        _, weights, total = softmax_block(scores, same)
        results.append(weights.astype(BF16))
        totals = jnp.where(lane == h, 1.0 / total, totals)
    for h in range(heads):
        weight_ref[:, h * span : (h + 1) * span] = results[h]
    total_ref[...] = totals


def weigh(query, keys, marks, first, heads):
    rows, span = query.shape[0], query.shape[0] * len(keys)
    return call(
        functools.partial(weigh_kernel, len(keys), first, heads),
        "weigh",
        [((rows, heads * span), BF16), ((rows, LANES), F32)],
        [*marks, query, *keys],
        flops=WEIGH_FLOPS,
        exps=rows * span * heads,
    )


def mix_kernel(skip, first, heads, weight_ref, total_ref, *refs):
    values, out_ref = refs[:-1], refs[-1]
    rows = total_ref.shape[0]
    results = []
    for h in range(heads):
        start = (skip + h) * rows * len(values)
        summed = sum(
            dot(weight_ref[:, start + i * rows : start + (i + 1) * rows], v[:, head_columns(first + h)])
            for i, v in enumerate(values)
        )
        results.append((summed * total_ref[:, skip + h : skip + h + 1]).astype(BF16))
    for h in range(heads):
        out_ref[:, head_columns(h)] = results[h]


def mix(weights, totals, values, skip, first, heads):
    rows = totals.shape[0]
    return call(
        functools.partial(mix_kernel, skip, first, heads),
        "mix",
        [((rows, heads * HEAD_DIM), BF16)],
        [weights, totals, *values],
        flops=2 * rows * rows * len(values) * heads * HEAD_DIM,
    )[0]


def in_shard(shards, shard, act):
    if len(shards) == 1:
        act(shards[0])
    else:
        for i, maps in enumerate(shards):
            pl.when(shard == i)(functools.partial(act, maps))


def split_kernel(source, *outs):
    width = outs[0].shape[1]
    for i, out in enumerate(outs):
        out[...] = source[:, i * width : (i + 1) * width]


def split(chunk, parts):
    rows, width = chunk.shape
    return call(split_kernel, "split", [((rows, width // parts), chunk.dtype)] * parts, [chunk], flops=SPLIT_FLOPS)


def project_kernel(sizes, shards, map_rows, has_acc, places, *refs):
    count, out_ref = sum(sizes), refs[-1]
    maps = refs[count : count + shards]
    half = out_ref.shape[1] // 2
    before = refs[-2] if has_acc else None
    start = 0
    for size, place in zip(sizes, places):
        e_refs = refs[start : start + size]
        start += size
        shard, row = place()
        row = pl.multiple_of(row, e_refs[0].shape[1])
        chunk = jnp.concatenate([r[...] for r in e_refs], axis=1)

        def add(map_ref, chunk=chunk, row=row, before=before):
            for side in range(2):
                columns = slice(side * half, (side + 1) * half)
                product = dot(chunk, map_ref[pl.ds(side * map_rows + row, chunk.shape[1]), :])
                out_ref[:, columns] = product if before is None else before[:, columns] + product

        in_shard(maps, shard, add)
        before = out_ref


def project(acc, groups, shards, map_rows):
    chunks = [x for group, _ in groups for x in group]
    rows, width = chunks[0].shape[0], shards[0].shape[1]
    operands = [*chunks, *shards] + ([] if acc is None else [acc])
    sizes = [len(group) for group, _ in groups]
    places = [place for _, place in groups]
    return call(
        functools.partial(project_kernel, sizes, len(shards), map_rows, acc is not None, places),
        "project",
        [((rows, 2 * width), F32)],
        operands,
        flops=4 * width * sum(x.size for x in chunks),
    )[0]


def prepare_kernel(shards, parts, map_rows, step, place, *refs):
    maps, marks, near = refs[:shards], refs[shards : shards + parts], refs[shards + parts : -4]
    map_ref, tgt_ref, mask_ref, down_ref = refs[-4:]
    shard, row = place()
    depth, width = map_ref.shape[0], map_ref.shape[1] // 2
    row = pl.multiple_of(row, depth)

    def copy(source):
        for side in range(2):
            map_ref[:, side * width : (side + 1) * width] = source[pl.ds(side * map_rows + row, depth), :]

    in_shard(maps, shard, copy)
    own = marks[0][...]
    count = tgt_ref.shape[0] // parts
    below = slice(2 * map_rows, 2 * map_rows + count)
    targets = [maps[0][below, :]] + ([r[...] for r in near] if near else [m[below, :] for m in maps[1:]])
    for i, (target, mark_ref) in enumerate(zip(targets, marks)):
        part = slice(i * count, (i + 1) * count)
        tgt_ref[part, :] = target
        down_ref[...] = down_lanes(mark_ref[...])
        down = down_ref[pl.ds(0, count, stride=step), :]
        mask_ref[part, :] = same_mark(down, own).astype(F32)


def prepare(place, depth, shards, map_rows, count, near_targets, marks):
    rows, width = marks[0].shape[1], shards[0].shape[1]
    total = count * len(marks)
    return call(
        functools.partial(prepare_kernel, len(shards), len(marks), map_rows, rows // count, place),
        "prepare",
        [((depth, 2 * width), BF16), ((total, width), BF16), ((total, rows), F32)],
        [*shards, *marks, *near_targets],
        scratch=[pltpu.VMEM((rows, LANES), jnp.int32)],
    )


def cross_kernel(acc_ref, e_ref, map_ref, tgt_ref, mask_ref, *outs):
    heads = map_ref.shape[1] // 2 // HEAD_DIM
    chunk = e_ref[...]
    queries = [tgt_ref[:, head_columns(h)] for h in range(heads)]
    memory = []
    for h in range(2 * heads):
        at = head_columns(h)
        memory.append((acc_ref[:, at] + dot(chunk, map_ref[:, at])).astype(BF16))
    keys, values = memory[:heads], memory[heads:]
    count = outs[0].shape[0]
    same = mask_ref[...] > 0
    scores = [dot_t(queries[h], keys[h]) for h in range(heads)]
    tops, weights, totals = zip(*[softmax_block(x, same) for x in scores])
    summed = [dot(w.astype(BF16), v) for w, v in zip(weights, values)]
    lane = lax.broadcasted_iota(jnp.int32, (same.shape[0], LANES), 1)
    stats = jnp.zeros(lane.shape, F32)
    for h in range(heads):
        stats = jnp.where(lane == h, tops[h], jnp.where(lane == heads + h, totals[h], stats))
    for i, out_ref in enumerate(outs):
        part = slice(i * count, (i + 1) * count)
        for h in range(heads):
            out_ref[:, head_columns(h)] = summed[h][part]
        out_ref[:, heads * HEAD_DIM :] = stats[part]


def cross_attend(acc, chunk, maps, targets, mask, parts):
    width = targets.shape[1]
    count = targets.shape[0] // parts
    return call(
        cross_kernel,
        "cross_attend",
        [((count, width + LANES), F32)] * parts,
        [acc, chunk, maps, targets, mask],
        flops=2 * chunk.size * 2 * width,
    )


def combine_kernel(*refs):
    parts, out_ref = [r[...] for r in refs[:-1]], refs[-1]
    width = out_ref.shape[1]
    heads = width // HEAD_DIM
    results = []
    for h in range(heads):
        tops = [x[:, width + h : width + h + 1] for x in parts]
        totals = [x[:, width + heads + h : width + heads + h + 1] for x in parts]
        top = functools.reduce(jnp.maximum, tops)
        factors = [jnp.exp(t - top) for t in tops]
        share = 1.0 / sum(f * t for f, t in zip(factors, totals))
        results.append(sum((f * share) * x[:, head_columns(h)] for f, x in zip(factors, parts)))
    for h in range(heads):
        out_ref[:, head_columns(h)] = results[h].astype(BF16)


def on_device(enc_query, enc_key, enc_value, doc_ids, key_map, value_map, tgt_query):
    rows, features = enc_query.shape
    tgt_rows, width = tgt_query.shape
    n_ctx, n_head = lax.axis_size("ctx"), lax.axis_size("head")
    links = links_of(n_ctx)
    bring = lambda x: [lax.ppermute(x, "ctx", pairs) for pairs in links]

    marks = (doc_ids if n_ctx == 2 else doc_ids + 1).reshape(1, rows)
    keys, near_marks, values = bring(enc_key), bring(marks), bring(enc_value)
    query, own_key, own_value, marks = fetch(enc_query, enc_key, enc_value, marks)
    chunks = 2
    heads = features // HEAD_DIM // chunks
    held = []
    for j in range(chunks):
        weights, totals = weigh(query, [own_key, *keys], [marks, *near_marks], j * heads, heads)
        size = heads if j else 1
        for skip in range(0, heads, size):
            held.append(mix(weights, totals, [own_value, *values], skip, j * heads + skip, size))

    key_map, value_map, tgt_query, held[-1] = lax.optimization_barrier((key_map, value_map, tgt_query, held[-1]))
    near_targets = []
    if n_ctx == 2:
        own_maps = pack(key_map, value_map, tgt_query)
        shards = [own_maps, *bring(own_maps)]
    else:
        whole = [lax.all_gather(x, "ctx", axis=0, tiled=True) for x in (key_map, value_map)]
        shards, near_targets = [pack(*whole, tgt_query)], bring(tgt_query)
    map_rows = (shards[0].shape[0] - tgt_rows) // 2

    order = ring_order(n_head)
    rings = [[(o[i], o[(i + 1) % n_head]) for i in range(n_head)] for o in (order, order[::-1])]

    def place(way, turn, first):
        head, ctx = lax.axis_index("head"), lax.axis_index("ctx")
        before = {target: source for source, target in rings[way]}
        owner = 0
        for i in range(n_head):
            source = i
            for _ in range(turn):
                source = before[source]
            owner = owner + jnp.where(head == i, source, 0)
        row = owner * features + first
        if len(shards) == 1:
            return None, row
        return jnp.where(lax.div(row, map_rows) == ctx, 0, 1), lax.rem(row, map_rows)

    def grouped(turn, pieces):
        first = heads * HEAD_DIM
        at = [0 if p < first else 1 for p in offsets(pieces)]
        groups = [[x for x, w in zip(pieces, at) if w == way] for way in range(2)]
        return [(g, functools.partial(place, way, turn, way * first)) for way, g in enumerate(groups) if g]

    def offsets(pieces):
        return [sum(x.shape[1] for x in pieces[:i]) for i in range(len(pieces))]

    acc, last = None, n_head - 1
    for turn in range(last):
        pieces = [p for h in held for p in split(h, h.shape[1] // HEAD_DIM)] if turn else held
        ways = [0 if p < heads * HEAD_DIM else 1 for p in offsets(pieces)]
        later = [lax.ppermute(p, "head", rings[way]) for p, way in zip(pieces, ways)]
        acc = project(acc, grouped(turn, held), shards, map_rows)
        held = later
    acc = project(acc, grouped(last, held[:-1]), shards, map_rows)
    depth = held[-1].shape[1]
    last_maps, targets, mask = prepare(
        functools.partial(place, 1, last, features - depth),
        depth,
        shards,
        map_rows,
        tgt_rows,
        near_targets,
        [marks, *near_marks],
    )
    own, *shares = cross_attend(acc, held[-1], last_maps, targets, mask, 1 + len(links))
    combined = [own]
    for i, (pairs, piece) in enumerate(zip(links, shares)):
        other = lax.ppermute(piece, "ctx", [(target, source) for source, target in pairs])
        if n_ctx > 2:
            end = n_ctx - 1 if i == 0 else 0
            column = lax.broadcasted_iota(jnp.int32, other.shape, 1)
            other = jnp.where((lax.axis_index("ctx") == end) & (column >= width), NEG_FILL, other)
        combined.append(other)
    return call(combine_kernel, "combine", [((tgt_rows, width), BF16)], combined, limit=4 << 20)[0]


def solution(mesh):
    in_specs = (
        P(("dp", "ctx"), "head"),
        P(("dp", "ctx"), "head"),
        P(("dp", "ctx"), "head"),
        P(("dp", "ctx")),
        P("ctx", "head"),
        P("ctx", "head"),
        P(("dp", "ctx"), "head"),
    )
    out_specs = P(("dp", "ctx"), "head")
    return jax.shard_map(
        on_device, mesh=mesh, in_specs=in_specs, out_specs=out_specs, check_vma=False
    )
```

```python
import functools

import jax
import jax.numpy as jnp
from jax import lax
from jax.experimental import pallas as pl
from jax.experimental.pallas import tpu as pltpu
from jax.sharding import PartitionSpec as P

HEAD_DIM = 256
NEG_FILL = -1e30
F32 = jnp.float32
BF16 = jnp.bfloat16
LANES = 128
SCALE = HEAD_DIM**-0.5
WEIGH_FLOPS = 6 * 10**9
SPLIT_FLOPS = 15 * 10**9
VMEM = pl.BlockSpec(memory_space=pltpu.VMEM)
HBM = pl.BlockSpec(memory_space=pltpu.HBM)


def ring_order(count):
    return list(range(0, count, 2)) + list(range(1, count, 2))[::-1]


def links_of(count):
    if count == 2:
        return [[(0, 1), (1, 0)]]
    return [[(i, i + 1) for i in range(count - 1)], [(i + 1, i) for i in range(count - 1)]]


def dot_t(a, b):
    return lax.dot_general(a, b, (((1,), (1,)), ((), ())), preferred_element_type=F32)


def dot(a, b):
    return jnp.dot(a, b, preferred_element_type=F32)


def head_columns(h):
    return slice(h * HEAD_DIM, (h + 1) * HEAD_DIM)


def down_lanes(row):
    return jnp.transpose(jnp.broadcast_to(row, (LANES, row.shape[1])))


def same_mark(down, row):
    return jnp.concatenate([down == row[:, i : i + LANES] for i in range(0, row.shape[1], LANES)], axis=1)


def softmax_block(scores, same):
    scores = jnp.where(same, scores * SCALE, NEG_FILL)
    top = jnp.max(scores, axis=1, keepdims=True)
    weights = jnp.exp(scores - top)
    return top, weights, jnp.sum(weights, axis=1, keepdims=True)


def call(kernel, name, outs, operands, flops=0, exps=0, specs=None, scratch=(), limit=8 << 20):
    out_shape = [jax.ShapeDtypeStruct(*o) for o in outs]
    moved = sum(x.size * x.dtype.itemsize for x in [*operands, *out_shape])
    return pl.pallas_call(
        kernel,
        in_specs=specs or [VMEM] * len(operands),
        out_specs=[VMEM] * len(outs),
        out_shape=out_shape,
        scratch_shapes=list(scratch),
        compiler_params=pltpu.CompilerParams(vmem_limit_bytes=limit),
        cost_estimate=pl.CostEstimate(flops=flops, bytes_accessed=moved, transcendentals=exps),
        name=name,
    )(*operands)


def run_all(copies):
    for copy in copies:
        copy.start()
    for copy in copies:
        copy.wait()


def fetch_kernel(count, *refs):
    sources, targets, sems = refs[:count], refs[count : 2 * count], refs[-1]
    run_all([pltpu.make_async_copy(s, t, sems.at[i]) for i, (s, t) in enumerate(zip(sources, targets))])


def fetch(*arrays):
    return call(
        functools.partial(fetch_kernel, len(arrays)),
        "fetch",
        [(x.shape, x.dtype) for x in arrays],
        [pltpu.with_memory_space_constraint(x, pltpu.HBM) for x in arrays],
        specs=[HBM] * len(arrays),
        scratch=[pltpu.SemaphoreType.DMA((len(arrays),))],
    )


def pack_kernel(*refs):
    sources, out_ref, sems = refs[:-2], refs[-2], refs[-1]
    copies, row = [], 0
    for i, source in enumerate(sources):
        rows = source.shape[0]
        copies.append(pltpu.make_async_copy(source, out_ref.at[pl.ds(row, rows), :], sems.at[i]))
        row += rows
    run_all(copies)


def pack(*arrays):
    rows = sum(x.shape[0] for x in arrays)
    return call(
        pack_kernel,
        "pack",
        [((rows, arrays[0].shape[1]), arrays[0].dtype)],
        [pltpu.with_memory_space_constraint(x, pltpu.HBM) for x in arrays],
        specs=[HBM] * len(arrays),
        scratch=[pltpu.SemaphoreType.DMA((len(arrays),))],
    )[0]


def weigh_kernel(blocks, first, heads, *refs):
    marks, q_ref, keys = refs[:blocks], refs[blocks], refs[blocks + 1 : 2 * blocks + 1]
    weight_ref, total_ref = refs[2 * blocks + 1 :]
    down = down_lanes(marks[0][...])
    same = jnp.concatenate([same_mark(down, m[...]) for m in marks], axis=1)
    span = same.shape[1]
    lane = lax.broadcasted_iota(jnp.int32, total_ref.shape, 1)
    totals = jnp.zeros(total_ref.shape, F32)
    results = []
    for h in range(heads):
        at = head_columns(first + h)
        scores = jnp.concatenate([dot_t(q_ref[:, at], k[:, at]) for k in keys], axis=1)
        _, weights, total = softmax_block(scores, same)
        results.append(weights.astype(BF16))
        totals = jnp.where(lane == h, 1.0 / total, totals)
    for h in range(heads):
        weight_ref[:, h * span : (h + 1) * span] = results[h]
    total_ref[...] = totals


def weigh(query, keys, marks, first, heads):
    rows, span = query.shape[0], query.shape[0] * len(keys)
    return call(
        functools.partial(weigh_kernel, len(keys), first, heads),
        "weigh",
        [((rows, heads * span), BF16), ((rows, LANES), F32)],
        [*marks, query, *keys],
        flops=WEIGH_FLOPS,
        exps=rows * span * heads,
    )


def mix_kernel(skip, first, heads, weight_ref, total_ref, *refs):
    values, out_ref = refs[:-1], refs[-1]
    rows = total_ref.shape[0]
    results = []
    for h in range(heads):
        start = (skip + h) * rows * len(values)
        summed = sum(
            dot(weight_ref[:, start + i * rows : start + (i + 1) * rows], v[:, head_columns(first + h)])
            for i, v in enumerate(values)
        )
        results.append((summed * total_ref[:, skip + h : skip + h + 1]).astype(BF16))
    for h in range(heads):
        out_ref[:, head_columns(h)] = results[h]


def mix(weights, totals, values, skip, first, heads):
    rows = totals.shape[0]
    return call(
        functools.partial(mix_kernel, skip, first, heads),
        "mix",
        [((rows, heads * HEAD_DIM), BF16)],
        [weights, totals, *values],
        flops=2 * rows * rows * len(values) * heads * HEAD_DIM,
    )[0]


def in_shard(shards, shard, act):
    if len(shards) == 1:
        act(shards[0])
    else:
        for i, maps in enumerate(shards):
            pl.when(shard == i)(functools.partial(act, maps))


def split_kernel(source, *outs):
    width = outs[0].shape[1]
    for i, out in enumerate(outs):
        out[...] = source[:, i * width : (i + 1) * width]


def split(chunk, parts):
    rows, width = chunk.shape
    return call(split_kernel, "split", [((rows, width // parts), chunk.dtype)] * parts, [chunk], flops=SPLIT_FLOPS)


def project_kernel(chunks, shards, map_rows, has_acc, place, *refs):
    e_refs, maps, out_ref = refs[:chunks], refs[chunks : chunks + shards], refs[-1]
    half = out_ref.shape[1] // 2
    depth = e_refs[0].shape[1]
    shard, row = place()
    row = pl.multiple_of(row, depth)
    chunk = jnp.concatenate([r[...] for r in e_refs], axis=1)

    def add(map_ref):
        for side in range(2):
            columns = slice(side * half, (side + 1) * half)
            product = dot(chunk, map_ref[pl.ds(side * map_rows + row, chunk.shape[1]), :])
            out_ref[:, columns] = refs[-2][:, columns] + product if has_acc else product

    in_shard(maps, shard, add)


def project(acc, chunks, place, shards, map_rows):
    rows, width = chunks[0].shape[0], shards[0].shape[1]
    operands = [*chunks, *shards] + ([] if acc is None else [acc])
    return call(
        functools.partial(project_kernel, len(chunks), len(shards), map_rows, acc is not None, place),
        "project",
        [((rows, 2 * width), F32)],
        operands,
        flops=4 * width * sum(x.size for x in chunks),
    )[0]


def prepare_kernel(shards, parts, map_rows, step, place, *refs):
    maps, marks, near = refs[:shards], refs[shards : shards + parts], refs[shards + parts : -4]
    map_ref, tgt_ref, mask_ref, down_ref = refs[-4:]
    shard, row = place()
    depth, width = map_ref.shape[0], map_ref.shape[1] // 2
    row = pl.multiple_of(row, depth)

    def copy(source):
        for side in range(2):
            map_ref[:, side * width : (side + 1) * width] = source[pl.ds(side * map_rows + row, depth), :]

    in_shard(maps, shard, copy)
    own = marks[0][...]
    count = tgt_ref.shape[0] // parts
    below = slice(2 * map_rows, 2 * map_rows + count)
    targets = [maps[0][below, :]] + ([r[...] for r in near] if near else [m[below, :] for m in maps[1:]])
    for i, (target, mark_ref) in enumerate(zip(targets, marks)):
        part = slice(i * count, (i + 1) * count)
        tgt_ref[part, :] = target
        down_ref[...] = down_lanes(mark_ref[...])
        down = down_ref[pl.ds(0, count, stride=step), :]
        mask_ref[part, :] = same_mark(down, own).astype(F32)


def prepare(place, depth, shards, map_rows, count, near_targets, marks):
    rows, width = marks[0].shape[1], shards[0].shape[1]
    total = count * len(marks)
    return call(
        functools.partial(prepare_kernel, len(shards), len(marks), map_rows, rows // count, place),
        "prepare",
        [((depth, 2 * width), BF16), ((total, width), BF16), ((total, rows), F32)],
        [*shards, *marks, *near_targets],
        scratch=[pltpu.VMEM((rows, LANES), jnp.int32)],
    )


def cross_kernel(acc_ref, e_ref, map_ref, tgt_ref, mask_ref, *outs):
    heads = map_ref.shape[1] // 2 // HEAD_DIM
    chunk = e_ref[...]
    queries = [tgt_ref[:, head_columns(h)] for h in range(heads)]
    memory = []
    for h in range(2 * heads):
        at = head_columns(h)
        memory.append((acc_ref[:, at] + dot(chunk, map_ref[:, at])).astype(BF16))
    keys, values = memory[:heads], memory[heads:]
    count = outs[0].shape[0]
    same = mask_ref[...] > 0
    scores = [dot_t(queries[h], keys[h]) for h in range(heads)]
    tops, weights, totals = zip(*[softmax_block(x, same) for x in scores])
    summed = [dot(w.astype(BF16), v) for w, v in zip(weights, values)]
    lane = lax.broadcasted_iota(jnp.int32, (same.shape[0], LANES), 1)
    stats = jnp.zeros(lane.shape, F32)
    for h in range(heads):
        stats = jnp.where(lane == h, tops[h], jnp.where(lane == heads + h, totals[h], stats))
    for i, out_ref in enumerate(outs):
        part = slice(i * count, (i + 1) * count)
        for h in range(heads):
            out_ref[:, head_columns(h)] = summed[h][part]
        out_ref[:, heads * HEAD_DIM :] = stats[part]


def cross_attend(acc, chunk, maps, targets, mask, parts):
    width = targets.shape[1]
    count = targets.shape[0] // parts
    return call(
        cross_kernel,
        "cross_attend",
        [((count, width + LANES), F32)] * parts,
        [acc, chunk, maps, targets, mask],
        flops=2 * chunk.size * 2 * width,
    )


def combine_kernel(*refs):
    parts, out_ref = [r[...] for r in refs[:-1]], refs[-1]
    width = out_ref.shape[1]
    heads = width // HEAD_DIM
    results = []
    for h in range(heads):
        tops = [x[:, width + h : width + h + 1] for x in parts]
        totals = [x[:, width + heads + h : width + heads + h + 1] for x in parts]
        top = functools.reduce(jnp.maximum, tops)
        factors = [jnp.exp(t - top) for t in tops]
        share = 1.0 / sum(f * t for f, t in zip(factors, totals))
        results.append(sum((f * share) * x[:, head_columns(h)] for f, x in zip(factors, parts)))
    for h in range(heads):
        out_ref[:, head_columns(h)] = results[h].astype(BF16)


def on_device(enc_query, enc_key, enc_value, doc_ids, key_map, value_map, tgt_query):
    rows, features = enc_query.shape
    tgt_rows, width = tgt_query.shape
    n_ctx, n_head = lax.axis_size("ctx"), lax.axis_size("head")
    links = links_of(n_ctx)
    bring = lambda x: [lax.ppermute(x, "ctx", pairs) for pairs in links]

    marks = (doc_ids if n_ctx == 2 else doc_ids + 1).reshape(1, rows)
    keys, near_marks, values = bring(enc_key), bring(marks), bring(enc_value)
    query, own_key, own_value, marks = fetch(enc_query, enc_key, enc_value, marks)
    chunks = 2
    heads = features // HEAD_DIM // chunks
    held = []
    for j in range(chunks):
        weights, totals = weigh(query, [own_key, *keys], [marks, *near_marks], j * heads, heads)
        size = 1
        for skip in range(0, heads, size):
            held.append(mix(weights, totals, [own_value, *values], skip, j * heads + skip, size))

    order = ring_order(n_head)
    ring = [(order[i], order[(i + 1) % n_head]) for i in range(n_head)]
    before = {target: source for source, target in ring}

    sent, held = held, [lax.ppermute(h, "head", ring) for h in held]
    key_map, value_map, tgt_query, arrived = lax.optimization_barrier((key_map, value_map, tgt_query, held[0]))
    near_targets = []
    if n_ctx == 2:
        own_maps = pack(key_map, value_map, tgt_query)
        shards = [own_maps, *bring(own_maps)]
    else:
        whole = [lax.all_gather(x, "ctx", axis=0, tiled=True) for x in (key_map, value_map)]
        shards, near_targets = [pack(*whole, tgt_query)], bring(tgt_query)
    map_rows = (shards[0].shape[0] - tgt_rows) // 2

    def place(turn, first):
        head, ctx = lax.axis_index("head"), lax.axis_index("ctx")
        owner = 0
        for i in range(n_head):
            source = i
            for _ in range(turn):
                source = before[source]
            owner = owner + jnp.where(head == i, source, 0)
        row = owner * features + first
        if len(shards) == 1:
            return None, row
        return jnp.where(lax.div(row, map_rows) == ctx, 0, 1), lax.rem(row, map_rows)

    last = n_head - 1
    acc = project(None, sent, functools.partial(place, 0, 0), shards, map_rows)
    arrived = [arrived, *held[1:]]
    for turn in range(1, last):
        pieces = [p for h in held for p in split(h, h.shape[1] // HEAD_DIM)]
        later = [lax.ppermute(p, "head", ring) for p in pieces]
        acc = project(acc, arrived, functools.partial(place, turn, 0), shards, map_rows)
        held = arrived = later
    acc = project(acc, held[:-1], functools.partial(place, last, 0), shards, map_rows)
    depth = held[-1].shape[1]
    last_maps, targets, mask = prepare(
        functools.partial(place, last, features - depth),
        depth,
        shards,
        map_rows,
        tgt_rows,
        near_targets,
        [marks, *near_marks],
    )
    own, *shares = cross_attend(acc, held[-1], last_maps, targets, mask, 1 + len(links))
    combined = [own]
    for i, (pairs, piece) in enumerate(zip(links, shares)):
        other = lax.ppermute(piece, "ctx", [(target, source) for source, target in pairs])
        if n_ctx > 2:
            end = n_ctx - 1 if i == 0 else 0
            column = lax.broadcasted_iota(jnp.int32, other.shape, 1)
            other = jnp.where((lax.axis_index("ctx") == end) & (column >= width), NEG_FILL, other)
        combined.append(other)
    return call(combine_kernel, "combine", [((tgt_rows, width), BF16)], combined, limit=4 << 20)[0]


def solution(mesh):
    in_specs = (
        P(("dp", "ctx"), "head"),
        P(("dp", "ctx"), "head"),
        P(("dp", "ctx"), "head"),
        P(("dp", "ctx")),
        P("ctx", "head"),
        P("ctx", "head"),
        P(("dp", "ctx"), "head"),
    )
    out_specs = P(("dp", "ctx"), "head")
    return jax.shard_map(
        on_device, mesh=mesh, in_specs=in_specs, out_specs=out_specs, check_vma=False
    )
```

```python
import functools

import jax
import jax.numpy as jnp
from jax import lax
from jax.experimental import pallas as pl
from jax.experimental.pallas import tpu as pltpu
from jax.sharding import PartitionSpec as P

HEAD_DIM = 256
NEG_FILL = -1e30
F32 = jnp.float32
BF16 = jnp.bfloat16
LANES = 128
SCALE = HEAD_DIM**-0.5
WEIGH_FLOPS = 6 * 10**9
SPLIT_FLOPS = 15 * 10**9
VMEM = pl.BlockSpec(memory_space=pltpu.VMEM)
HBM = pl.BlockSpec(memory_space=pltpu.HBM)


def ring_order(count):
    return list(range(0, count, 2)) + list(range(1, count, 2))[::-1]


def links_of(count):
    if count == 2:
        return [[(0, 1), (1, 0)]]
    return [[(i, i + 1) for i in range(count - 1)], [(i + 1, i) for i in range(count - 1)]]


def dot_t(a, b):
    return lax.dot_general(a, b, (((1,), (1,)), ((), ())), preferred_element_type=F32)


def dot(a, b):
    return jnp.dot(a, b, preferred_element_type=F32)


def head_columns(h):
    return slice(h * HEAD_DIM, (h + 1) * HEAD_DIM)


def down_lanes(row):
    return jnp.transpose(jnp.broadcast_to(row, (LANES, row.shape[1])))


def same_mark(down, row):
    return jnp.concatenate([down == row[:, i : i + LANES] for i in range(0, row.shape[1], LANES)], axis=1)


def softmax_block(scores, same):
    scores = jnp.where(same, scores * SCALE, NEG_FILL)
    top = jnp.max(scores, axis=1, keepdims=True)
    weights = jnp.exp(scores - top)
    return top, weights, jnp.sum(weights, axis=1, keepdims=True)


def call(kernel, name, outs, operands, flops=0, exps=0, specs=None, scratch=(), limit=8 << 20):
    out_shape = [jax.ShapeDtypeStruct(*o) for o in outs]
    moved = sum(x.size * x.dtype.itemsize for x in [*operands, *out_shape])
    return pl.pallas_call(
        kernel,
        in_specs=specs or [VMEM] * len(operands),
        out_specs=[VMEM] * len(outs),
        out_shape=out_shape,
        scratch_shapes=list(scratch),
        compiler_params=pltpu.CompilerParams(vmem_limit_bytes=limit),
        cost_estimate=pl.CostEstimate(flops=flops, bytes_accessed=moved, transcendentals=exps),
        name=name,
    )(*operands)


def run_all(copies):
    for copy in copies:
        copy.start()
    for copy in copies:
        copy.wait()


def fetch_kernel(count, *refs):
    sources, targets, sems = refs[:count], refs[count : 2 * count], refs[-1]
    run_all([pltpu.make_async_copy(s, t, sems.at[i]) for i, (s, t) in enumerate(zip(sources, targets))])


def fetch(*arrays):
    return call(
        functools.partial(fetch_kernel, len(arrays)),
        "fetch",
        [(x.shape, x.dtype) for x in arrays],
        [pltpu.with_memory_space_constraint(x, pltpu.HBM) for x in arrays],
        specs=[HBM] * len(arrays),
        scratch=[pltpu.SemaphoreType.DMA((len(arrays),))],
    )


def pack_kernel(*refs):
    sources, out_ref, sems = refs[:-2], refs[-2], refs[-1]
    copies, row = [], 0
    for i, source in enumerate(sources):
        rows = source.shape[0]
        copies.append(pltpu.make_async_copy(source, out_ref.at[pl.ds(row, rows), :], sems.at[i]))
        row += rows
    run_all(copies)


def pack(*arrays):
    rows = sum(x.shape[0] for x in arrays)
    return call(
        pack_kernel,
        "pack",
        [((rows, arrays[0].shape[1]), arrays[0].dtype)],
        [pltpu.with_memory_space_constraint(x, pltpu.HBM) for x in arrays],
        specs=[HBM] * len(arrays),
        scratch=[pltpu.SemaphoreType.DMA((len(arrays),))],
    )[0]


def weigh_kernel(blocks, first, heads, *refs):
    marks, q_ref, keys = refs[:blocks], refs[blocks], refs[blocks + 1 : 2 * blocks + 1]
    weight_ref, total_ref = refs[2 * blocks + 1 :]
    down = down_lanes(marks[0][...])
    same = jnp.concatenate([same_mark(down, m[...]) for m in marks], axis=1)
    span = same.shape[1]
    lane = lax.broadcasted_iota(jnp.int32, total_ref.shape, 1)
    totals = jnp.zeros(total_ref.shape, F32)
    results = []
    for h in range(heads):
        at = head_columns(first + h)
        scores = jnp.concatenate([dot_t(q_ref[:, at], k[:, at]) for k in keys], axis=1)
        _, weights, total = softmax_block(scores, same)
        results.append(weights.astype(BF16))
        totals = jnp.where(lane == h, 1.0 / total, totals)
    for h in range(heads):
        weight_ref[:, h * span : (h + 1) * span] = results[h]
    total_ref[...] = totals


def weigh(query, keys, marks, first, heads):
    rows, span = query.shape[0], query.shape[0] * len(keys)
    return call(
        functools.partial(weigh_kernel, len(keys), first, heads),
        "weigh",
        [((rows, heads * span), BF16), ((rows, LANES), F32)],
        [*marks, query, *keys],
        flops=WEIGH_FLOPS,
        exps=rows * span * heads,
    )


def mix_kernel(skip, first, heads, weight_ref, total_ref, *refs):
    values, out_ref = refs[:-1], refs[-1]
    rows = total_ref.shape[0]
    results = []
    for h in range(heads):
        start = (skip + h) * rows * len(values)
        summed = sum(
            dot(weight_ref[:, start + i * rows : start + (i + 1) * rows], v[:, head_columns(first + h)])
            for i, v in enumerate(values)
        )
        results.append((summed * total_ref[:, skip + h : skip + h + 1]).astype(BF16))
    for h in range(heads):
        out_ref[:, head_columns(h)] = results[h]


def mix(weights, totals, values, skip, first, heads):
    rows = totals.shape[0]
    return call(
        functools.partial(mix_kernel, skip, first, heads),
        "mix",
        [((rows, heads * HEAD_DIM), BF16)],
        [weights, totals, *values],
        flops=2 * rows * rows * len(values) * heads * HEAD_DIM,
    )[0]


def in_shard(shards, shard, act):
    if len(shards) == 1:
        act(shards[0])
    else:
        for i, maps in enumerate(shards):
            pl.when(shard == i)(functools.partial(act, maps))


def split_kernel(source, *outs):
    width = outs[0].shape[1]
    for i, out in enumerate(outs):
        out[...] = source[:, i * width : (i + 1) * width]


def split(chunk, parts):
    rows, width = chunk.shape
    return call(split_kernel, "split", [((rows, width // parts), chunk.dtype)] * parts, [chunk], flops=SPLIT_FLOPS)


def project_kernel(chunks, shards, map_rows, has_acc, place, *refs):
    e_refs, maps, out_ref = refs[:chunks], refs[chunks : chunks + shards], refs[-1]
    half = out_ref.shape[1] // 2
    depth = e_refs[0].shape[1]
    shard, row = place()
    row = pl.multiple_of(row, depth)
    chunk = jnp.concatenate([r[...] for r in e_refs], axis=1)

    def add(map_ref):
        for side in range(2):
            columns = slice(side * half, (side + 1) * half)
            product = dot(chunk, map_ref[pl.ds(side * map_rows + row, chunk.shape[1]), :])
            out_ref[:, columns] = refs[-2][:, columns] + product if has_acc else product

    in_shard(maps, shard, add)


def project(acc, chunks, place, shards, map_rows):
    rows, width = chunks[0].shape[0], shards[0].shape[1]
    operands = [*chunks, *shards] + ([] if acc is None else [acc])
    return call(
        functools.partial(project_kernel, len(chunks), len(shards), map_rows, acc is not None, place),
        "project",
        [((rows, 2 * width), F32)],
        operands,
        flops=4 * width * sum(x.size for x in chunks),
    )[0]


def prepare_kernel(shards, parts, map_rows, step, place, *refs):
    maps, marks, near = refs[:shards], refs[shards : shards + parts], refs[shards + parts : -4]
    map_ref, tgt_ref, mask_ref, down_ref = refs[-4:]
    shard, row = place()
    depth, width = map_ref.shape[0], map_ref.shape[1] // 2
    row = pl.multiple_of(row, depth)

    def copy(source):
        for side in range(2):
            map_ref[:, side * width : (side + 1) * width] = source[pl.ds(side * map_rows + row, depth), :]

    in_shard(maps, shard, copy)
    own = marks[0][...]
    count = tgt_ref.shape[0] // parts
    below = slice(2 * map_rows, 2 * map_rows + count)
    targets = [maps[0][below, :]] + ([r[...] for r in near] if near else [m[below, :] for m in maps[1:]])
    for i, (target, mark_ref) in enumerate(zip(targets, marks)):
        part = slice(i * count, (i + 1) * count)
        tgt_ref[part, :] = target
        down_ref[...] = down_lanes(mark_ref[...])
        down = down_ref[pl.ds(0, count, stride=step), :]
        mask_ref[part, :] = same_mark(down, own).astype(F32)


def prepare(place, depth, shards, map_rows, count, near_targets, marks):
    rows, width = marks[0].shape[1], shards[0].shape[1]
    total = count * len(marks)
    return call(
        functools.partial(prepare_kernel, len(shards), len(marks), map_rows, rows // count, place),
        "prepare",
        [((depth, 2 * width), BF16), ((total, width), BF16), ((total, rows), F32)],
        [*shards, *marks, *near_targets],
        scratch=[pltpu.VMEM((rows, LANES), jnp.int32)],
    )


def attend_memory(queries, memory, same):
    heads = len(queries)
    scores = [dot_t(q, k) for q, k in zip(queries, memory[:heads])]
    tops, weights, totals = zip(*[softmax_block(x, same) for x in scores])
    summed = [dot(w.astype(BF16), v) for w, v in zip(weights, memory[heads:])]
    lane = lax.broadcasted_iota(jnp.int32, (same.shape[0], LANES), 1)
    stats = jnp.zeros(lane.shape, F32)
    for h in range(heads):
        stats = jnp.where(lane == h, tops[h], jnp.where(lane == heads + h, totals[h], stats))
    return jnp.concatenate([*summed, stats], axis=1)


def cross_near_kernel(acc_ref, e_ref, map_ref, tgt_ref, mask_ref, mem_ref, *outs):
    heads = map_ref.shape[1] // 2 // HEAD_DIM
    count = outs[0].shape[0]
    chunk = e_ref[...]
    parts = [slice((i + 1) * count, (i + 2) * count) for i in range(len(outs))]
    queries = [[tgt_ref[part, head_columns(h)] for h in range(heads)] for part in parts]
    same = [mask_ref[part, :] > 0 for part in parts]
    memory = []
    for h in range(2 * heads):
        at = head_columns(h)
        memory.append((acc_ref[:, at] + dot(chunk, map_ref[:, at])).astype(BF16))
    shares = [attend_memory(q, memory, m) for q, m in zip(queries, same)]
    for out_ref, share in zip(outs, shares):
        out_ref[...] = share
    for h in range(2 * heads):
        mem_ref[:, head_columns(h)] = memory[h]


def cross_near(acc, chunk, maps, targets, mask, parts):
    width = targets.shape[1]
    share = ((targets.shape[0] // parts, width + LANES), F32)
    return call(
        cross_near_kernel,
        "cross_near",
        [((acc.shape[0], 2 * width), BF16)] + [share] * (parts - 1),
        [acc, chunk, maps, targets, mask],
        flops=2 * chunk.size * 2 * width,
    )


def cross_own_kernel(mem_ref, tgt_ref, mask_ref, out_ref):
    heads = mem_ref.shape[1] // 2 // HEAD_DIM
    count = out_ref.shape[0]
    memory = [mem_ref[:, head_columns(h)] for h in range(2 * heads)]
    queries = [tgt_ref[:count, head_columns(h)] for h in range(heads)]
    out_ref[...] = attend_memory(queries, memory, mask_ref[:count, :] > 0)


def cross_own(memory, targets, mask, parts):
    count, width = targets.shape[0] // parts, targets.shape[1]
    return call(
        cross_own_kernel,
        "cross_own",
        [((count, width + LANES), F32)],
        [memory, targets, mask],
        flops=4 * count * width * memory.shape[0],
    )[0]


def combine_kernel(*refs):
    parts, out_ref = [r[...] for r in refs[:-1]], refs[-1]
    width = out_ref.shape[1]
    heads = width // HEAD_DIM
    results = []
    for h in range(heads):
        tops = [x[:, width + h : width + h + 1] for x in parts]
        totals = [x[:, width + heads + h : width + heads + h + 1] for x in parts]
        top = functools.reduce(jnp.maximum, tops)
        factors = [jnp.exp(t - top) for t in tops]
        share = 1.0 / sum(f * t for f, t in zip(factors, totals))
        results.append(sum((f * share) * x[:, head_columns(h)] for f, x in zip(factors, parts)))
    for h in range(heads):
        out_ref[:, head_columns(h)] = results[h].astype(BF16)


def on_device(enc_query, enc_key, enc_value, doc_ids, key_map, value_map, tgt_query):
    rows, features = enc_query.shape
    tgt_rows, width = tgt_query.shape
    n_ctx, n_head = lax.axis_size("ctx"), lax.axis_size("head")
    links = links_of(n_ctx)
    bring = lambda x: [lax.ppermute(x, "ctx", pairs) for pairs in links]

    marks = (doc_ids if n_ctx == 2 else doc_ids + 1).reshape(1, rows)
    keys, near_marks, values = bring(enc_key), bring(marks), bring(enc_value)
    query, own_key, own_value, marks = fetch(enc_query, enc_key, enc_value, marks)
    chunks = 2
    heads = features // HEAD_DIM // chunks
    held = []
    for j in range(chunks):
        weights, totals = weigh(query, [own_key, *keys], [marks, *near_marks], j * heads, heads)
        size = 1
        for skip in range(0, heads, size):
            held.append(mix(weights, totals, [own_value, *values], skip, j * heads + skip, size))

    order = ring_order(n_head)
    ring = [(order[i], order[(i + 1) % n_head]) for i in range(n_head)]
    before = {target: source for source, target in ring}

    sent, held = held, [lax.ppermute(h, "head", ring) for h in held]
    key_map, value_map, tgt_query, arrived = lax.optimization_barrier((key_map, value_map, tgt_query, held[0]))
    near_targets = []
    if n_ctx == 2:
        own_maps = pack(key_map, value_map, tgt_query)
        shards = [own_maps, *bring(own_maps)]
    else:
        whole = [lax.all_gather(x, "ctx", axis=0, tiled=True) for x in (key_map, value_map)]
        shards, near_targets = [pack(*whole, tgt_query)], bring(tgt_query)
    map_rows = (shards[0].shape[0] - tgt_rows) // 2

    def place(turn, first):
        head, ctx = lax.axis_index("head"), lax.axis_index("ctx")
        owner = 0
        for i in range(n_head):
            source = i
            for _ in range(turn):
                source = before[source]
            owner = owner + jnp.where(head == i, source, 0)
        row = owner * features + first
        if len(shards) == 1:
            return None, row
        return jnp.where(lax.div(row, map_rows) == ctx, 0, 1), lax.rem(row, map_rows)

    last = n_head - 1
    acc = project(None, sent, functools.partial(place, 0, 0), shards, map_rows)
    arrived = [arrived, *held[1:]]
    for turn in range(1, last):
        pieces = [p for h in held for p in split(h, h.shape[1] // HEAD_DIM)]
        later = [lax.ppermute(p, "head", ring) for p in pieces]
        acc = project(acc, arrived, functools.partial(place, turn, 0), shards, map_rows)
        held = arrived = later
    acc = project(acc, held[:-1], functools.partial(place, last, 0), shards, map_rows)
    depth = held[-1].shape[1]
    last_maps, targets, mask = prepare(
        functools.partial(place, last, features - depth),
        depth,
        shards,
        map_rows,
        tgt_rows,
        near_targets,
        [marks, *near_marks],
    )
    memory, *shares = cross_near(acc, held[-1], last_maps, targets, mask, 1 + len(links))
    combined = [cross_own(memory, targets, mask, 1 + len(links))]
    for i, (pairs, piece) in enumerate(zip(links, shares)):
        other = lax.ppermute(piece, "ctx", [(target, source) for source, target in pairs])
        if n_ctx > 2:
            end = n_ctx - 1 if i == 0 else 0
            column = lax.broadcasted_iota(jnp.int32, other.shape, 1)
            other = jnp.where((lax.axis_index("ctx") == end) & (column >= width), NEG_FILL, other)
        combined.append(other)
    return call(combine_kernel, "combine", [((tgt_rows, width), BF16)], combined, limit=4 << 20)[0]


def solution(mesh):
    in_specs = (
        P(("dp", "ctx"), "head"),
        P(("dp", "ctx"), "head"),
        P(("dp", "ctx"), "head"),
        P(("dp", "ctx")),
        P("ctx", "head"),
        P("ctx", "head"),
        P(("dp", "ctx"), "head"),
    )
    out_specs = P(("dp", "ctx"), "head")
    return jax.shard_map(
        on_device, mesh=mesh, in_specs=in_specs, out_specs=out_specs, check_vma=False
    )
```

```python
import functools

import jax
import jax.numpy as jnp
from jax import lax
from jax.experimental import pallas as pl
from jax.experimental.pallas import tpu as pltpu
from jax.sharding import PartitionSpec as P

HEAD_DIM = 256
NEG_FILL = -1e30
F32 = jnp.float32
BF16 = jnp.bfloat16
LANES = 128
SCALE = HEAD_DIM**-0.5
WEIGH_FLOPS = 6 * 10**9
SPLIT_FLOPS = 15 * 10**9
VMEM = pl.BlockSpec(memory_space=pltpu.VMEM)
HBM = pl.BlockSpec(memory_space=pltpu.HBM)


def ring_order(count):
    return list(range(0, count, 2)) + list(range(1, count, 2))[::-1]


def links_of(count):
    if count == 2:
        return [[(0, 1), (1, 0)]]
    return [[(i, i + 1) for i in range(count - 1)], [(i + 1, i) for i in range(count - 1)]]


def dot_t(a, b):
    return lax.dot_general(a, b, (((1,), (1,)), ((), ())), preferred_element_type=F32)


def dot(a, b):
    return jnp.dot(a, b, preferred_element_type=F32)


def head_columns(h):
    return slice(h * HEAD_DIM, (h + 1) * HEAD_DIM)


def down_lanes(row):
    return jnp.transpose(jnp.broadcast_to(row, (LANES, row.shape[1])))


def same_mark(down, row):
    return jnp.concatenate([down == row[:, i : i + LANES] for i in range(0, row.shape[1], LANES)], axis=1)


def softmax_block(scores, same):
    scores = jnp.where(same, scores * SCALE, NEG_FILL)
    top = jnp.max(scores, axis=1, keepdims=True)
    weights = jnp.exp(scores - top)
    return top, weights, jnp.sum(weights, axis=1, keepdims=True)


def call(kernel, name, outs, operands, flops=0, exps=0, specs=None, scratch=(), limit=8 << 20):
    out_shape = [jax.ShapeDtypeStruct(*o) for o in outs]
    moved = sum(x.size * x.dtype.itemsize for x in [*operands, *out_shape])
    return pl.pallas_call(
        kernel,
        in_specs=specs or [VMEM] * len(operands),
        out_specs=[VMEM] * len(outs),
        out_shape=out_shape,
        scratch_shapes=list(scratch),
        compiler_params=pltpu.CompilerParams(vmem_limit_bytes=limit),
        cost_estimate=pl.CostEstimate(flops=flops, bytes_accessed=moved, transcendentals=exps),
        name=name,
    )(*operands)


def run_all(copies):
    for copy in copies:
        copy.start()
    for copy in copies:
        copy.wait()


def fetch_kernel(count, *refs):
    sources, targets, sems = refs[:count], refs[count : 2 * count], refs[-1]
    run_all([pltpu.make_async_copy(s, t, sems.at[i]) for i, (s, t) in enumerate(zip(sources, targets))])


def fetch(*arrays):
    return call(
        functools.partial(fetch_kernel, len(arrays)),
        "fetch",
        [(x.shape, x.dtype) for x in arrays],
        [pltpu.with_memory_space_constraint(x, pltpu.HBM) for x in arrays],
        specs=[HBM] * len(arrays),
        scratch=[pltpu.SemaphoreType.DMA((len(arrays),))],
    )


def pack_kernel(*refs):
    sources, out_ref, sems = refs[:-2], refs[-2], refs[-1]
    copies, row = [], 0
    for i, source in enumerate(sources):
        rows = source.shape[0]
        copies.append(pltpu.make_async_copy(source, out_ref.at[pl.ds(row, rows), :], sems.at[i]))
        row += rows
    run_all(copies)


def pack(*arrays):
    rows = sum(x.shape[0] for x in arrays)
    return call(
        pack_kernel,
        "pack",
        [((rows, arrays[0].shape[1]), arrays[0].dtype)],
        [pltpu.with_memory_space_constraint(x, pltpu.HBM) for x in arrays],
        specs=[HBM] * len(arrays),
        scratch=[pltpu.SemaphoreType.DMA((len(arrays),))],
    )[0]


def weigh_kernel(blocks, first, heads, *refs):
    marks, q_ref, keys = refs[:blocks], refs[blocks], refs[blocks + 1 : 2 * blocks + 1]
    weight_ref, total_ref = refs[2 * blocks + 1 :]
    down = down_lanes(marks[0][...])
    same = jnp.concatenate([same_mark(down, m[...]) for m in marks], axis=1)
    span = same.shape[1]
    lane = lax.broadcasted_iota(jnp.int32, total_ref.shape, 1)
    totals = jnp.zeros(total_ref.shape, F32)
    results = []
    for h in range(heads):
        at = head_columns(first + h)
        scores = jnp.concatenate([dot_t(q_ref[:, at], k[:, at]) for k in keys], axis=1)
        _, weights, total = softmax_block(scores, same)
        results.append(weights.astype(BF16))
        totals = jnp.where(lane == h, 1.0 / total, totals)
    for h in range(heads):
        weight_ref[:, h * span : (h + 1) * span] = results[h]
    total_ref[...] = totals


def weigh(query, keys, marks, first, heads):
    rows, span = query.shape[0], query.shape[0] * len(keys)
    return call(
        functools.partial(weigh_kernel, len(keys), first, heads),
        "weigh",
        [((rows, heads * span), BF16), ((rows, LANES), F32)],
        [*marks, query, *keys],
        flops=WEIGH_FLOPS,
        exps=rows * span * heads,
    )


def mix_kernel(skip, first, heads, weight_ref, total_ref, *refs):
    values, out_ref = refs[:-1], refs[-1]
    rows = total_ref.shape[0]
    results = []
    for h in range(heads):
        start = (skip + h) * rows * len(values)
        summed = sum(
            dot(weight_ref[:, start + i * rows : start + (i + 1) * rows], v[:, head_columns(first + h)])
            for i, v in enumerate(values)
        )
        results.append((summed * total_ref[:, skip + h : skip + h + 1]).astype(BF16))
    for h in range(heads):
        out_ref[:, head_columns(h)] = results[h]


def mix(weights, totals, values, skip, first, heads):
    rows = totals.shape[0]
    return call(
        functools.partial(mix_kernel, skip, first, heads),
        "mix",
        [((rows, heads * HEAD_DIM), BF16)],
        [weights, totals, *values],
        flops=2 * rows * rows * len(values) * heads * HEAD_DIM,
    )[0]


def in_shard(shards, shard, act):
    if len(shards) == 1:
        act(shards[0])
    else:
        for i, maps in enumerate(shards):
            pl.when(shard == i)(functools.partial(act, maps))


def split_kernel(source, *outs):
    width = outs[0].shape[1]
    for i, out in enumerate(outs):
        out[...] = source[:, i * width : (i + 1) * width]


def split(chunk, parts):
    rows, width = chunk.shape
    return call(split_kernel, "split", [((rows, width // parts), chunk.dtype)] * parts, [chunk], flops=SPLIT_FLOPS)


def project_kernel(chunks, shards, map_rows, has_acc, place, *refs):
    e_refs, maps, out_ref = refs[:chunks], refs[chunks : chunks + shards], refs[-1]
    half = out_ref.shape[1] // 2
    depth = e_refs[0].shape[1]
    shard, row = place()
    row = pl.multiple_of(row, depth)
    chunk = jnp.concatenate([r[...] for r in e_refs], axis=1)

    def add(map_ref):
        for side in range(2):
            columns = slice(side * half, (side + 1) * half)
            product = dot(chunk, map_ref[pl.ds(side * map_rows + row, chunk.shape[1]), :])
            out_ref[:, columns] = refs[-2][:, columns] + product if has_acc else product

    in_shard(maps, shard, add)


def project(acc, chunks, place, shards, map_rows):
    rows, width = chunks[0].shape[0], shards[0].shape[1]
    operands = [*chunks, *shards] + ([] if acc is None else [acc])
    return call(
        functools.partial(project_kernel, len(chunks), len(shards), map_rows, acc is not None, place),
        "project",
        [((rows, 2 * width), F32)],
        operands,
        flops=4 * width * sum(x.size for x in chunks),
    )[0]


def prepare_kernel(shards, parts, map_rows, step, place, *refs):
    maps, marks, near = refs[:shards], refs[shards : shards + parts], refs[shards + parts : -4]
    map_ref, tgt_ref, mask_ref, down_ref = refs[-4:]
    shard, row = place()
    depth, width = map_ref.shape[0], map_ref.shape[1] // 2
    row = pl.multiple_of(row, depth)

    def copy(source):
        for side in range(2):
            map_ref[:, side * width : (side + 1) * width] = source[pl.ds(side * map_rows + row, depth), :]

    in_shard(maps, shard, copy)
    own = marks[0][...]
    count = tgt_ref.shape[0] // parts
    below = slice(2 * map_rows, 2 * map_rows + count)
    targets = [maps[0][below, :]] + ([r[...] for r in near] if near else [m[below, :] for m in maps[1:]])
    for i, (target, mark_ref) in enumerate(zip(targets, marks)):
        part = slice(i * count, (i + 1) * count)
        tgt_ref[part, :] = target
        down_ref[...] = down_lanes(mark_ref[...])
        down = down_ref[pl.ds(0, count, stride=step), :]
        mask_ref[part, :] = same_mark(down, own).astype(F32)


def prepare(place, depth, shards, map_rows, count, near_targets, marks):
    rows, width = marks[0].shape[1], shards[0].shape[1]
    total = count * len(marks)
    return call(
        functools.partial(prepare_kernel, len(shards), len(marks), map_rows, rows // count, place),
        "prepare",
        [((depth, 2 * width), BF16), ((total, width), BF16), ((total, rows), F32)],
        [*shards, *marks, *near_targets],
        scratch=[pltpu.VMEM((rows, LANES), jnp.int32)],
    )


def attend_memory(queries, memory, same):
    heads = len(queries)
    scores = [dot_t(q, k) for q, k in zip(queries, memory[:heads])]
    tops, weights, totals = zip(*[softmax_block(x, same) for x in scores])
    summed = [dot(w.astype(BF16), v) for w, v in zip(weights, memory[heads:])]
    lane = lax.broadcasted_iota(jnp.int32, (same.shape[0], LANES), 1)
    stats = jnp.zeros(lane.shape, F32)
    for h in range(heads):
        stats = jnp.where(lane == h, tops[h], jnp.where(lane == heads + h, totals[h], stats))
    return jnp.concatenate([*summed, stats], axis=1)


def cross_near_kernel(acc_ref, e_ref, map_ref, tgt_ref, mask_ref, mem_ref, *outs):
    heads = map_ref.shape[1] // 2 // HEAD_DIM
    count = outs[0].shape[0]
    chunk = e_ref[...]
    parts = [slice((i + 1) * count, (i + 2) * count) for i in range(len(outs))]
    queries = [[tgt_ref[part, head_columns(h)] for h in range(heads)] for part in parts]
    same = [mask_ref[part, :] > 0 for part in parts]
    memory = []
    for h in range(2 * heads):
        at = head_columns(h)
        memory.append((acc_ref[:, at] + dot(chunk, map_ref[:, at])).astype(BF16))
    shares = [attend_memory(q, memory, m) for q, m in zip(queries, same)]
    for out_ref, share in zip(outs, shares):
        out_ref[...] = share
    for h in range(2 * heads):
        mem_ref[:, head_columns(h)] = memory[h]


def cross_near(acc, chunk, maps, targets, mask, parts):
    width = targets.shape[1]
    share = ((targets.shape[0] // parts, width + LANES), F32)
    return call(
        cross_near_kernel,
        "cross_near",
        [((acc.shape[0], 2 * width), BF16)] + [share] * (parts - 1),
        [acc, chunk, maps, targets, mask],
        flops=2 * chunk.size * 2 * width,
    )


def cross_own_kernel(mem_ref, tgt_ref, mask_ref, out_ref):
    heads = mem_ref.shape[1] // 2 // HEAD_DIM
    count = out_ref.shape[0]
    memory = [mem_ref[:, head_columns(h)] for h in range(2 * heads)]
    queries = [tgt_ref[:count, head_columns(h)] for h in range(heads)]
    out_ref[...] = attend_memory(queries, memory, mask_ref[:count, :] > 0)


def cross_own(memory, targets, mask, parts):
    count, width = targets.shape[0] // parts, targets.shape[1]
    return call(
        cross_own_kernel,
        "cross_own",
        [((count, width + LANES), F32)],
        [memory, targets, mask],
        flops=4 * count * width * memory.shape[0],
    )[0]


def combine_kernel(*refs):
    parts, out_ref = [r[...] for r in refs[:-1]], refs[-1]
    width = out_ref.shape[1]
    heads = width // HEAD_DIM
    results = []
    for h in range(heads):
        tops = [x[:, width + h : width + h + 1] for x in parts]
        totals = [x[:, width + heads + h : width + heads + h + 1] for x in parts]
        top = functools.reduce(jnp.maximum, tops)
        factors = [jnp.exp(t - top) for t in tops]
        share = 1.0 / sum(f * t for f, t in zip(factors, totals))
        results.append(sum((f * share) * x[:, head_columns(h)] for f, x in zip(factors, parts)))
    for h in range(heads):
        out_ref[:, head_columns(h)] = results[h].astype(BF16)


def on_device(enc_query, enc_key, enc_value, doc_ids, key_map, value_map, tgt_query):
    rows, features = enc_query.shape
    tgt_rows, width = tgt_query.shape
    n_ctx, n_head = lax.axis_size("ctx"), lax.axis_size("head")
    links = links_of(n_ctx)
    bring = lambda x: [lax.ppermute(x, "ctx", pairs) for pairs in links]

    marks = (doc_ids if n_ctx == 2 else doc_ids + 1).reshape(1, rows)
    keys, near_marks, values = bring(enc_key), bring(marks), bring(enc_value)
    query, own_key, own_value, marks = fetch(enc_query, enc_key, enc_value, marks)
    chunks = 2
    heads = features // HEAD_DIM // chunks
    held = []
    for j in range(chunks):
        weights, totals = weigh(query, [own_key, *keys], [marks, *near_marks], j * heads, heads)
        size = 1
        for skip in range(0, heads, size):
            held.append(mix(weights, totals, [own_value, *values], skip, j * heads + skip, size))

    order = ring_order(n_head)
    ring = [(order[i], order[(i + 1) % n_head]) for i in range(n_head)]
    before = {target: source for source, target in ring}

    sent, held = held, [lax.ppermute(h, "head", ring) for h in held]
    key_map, value_map, tgt_query, arrived = lax.optimization_barrier((key_map, value_map, tgt_query, held[0]))
    near_targets = []
    if n_ctx == 2:
        own_maps = pack(key_map, value_map, tgt_query)
        shards = [own_maps, *bring(own_maps)]
    else:
        whole = [lax.all_gather(x, "ctx", axis=0, tiled=True) for x in (key_map, value_map)]
        shards, near_targets = [pack(*whole, tgt_query)], bring(tgt_query)
    map_rows = (shards[0].shape[0] - tgt_rows) // 2

    def place(turn, first):
        head, ctx = lax.axis_index("head"), lax.axis_index("ctx")
        owner = 0
        for i in range(n_head):
            source = i
            for _ in range(turn):
                source = before[source]
            owner = owner + jnp.where(head == i, source, 0)
        row = owner * features + first
        if len(shards) == 1:
            return None, row
        return jnp.where(lax.div(row, map_rows) == ctx, 0, 1), lax.rem(row, map_rows)

    last = n_head - 1
    acc = project(None, sent, functools.partial(place, 0, 0), shards, map_rows)
    arrived = [arrived, *held[1:]]
    for turn in range(1, last):
        pieces = [p for h in held[:-1] for p in split(h, 1)] + list(split(held[-1], 2 if turn == last - 1 else 1))
        later = [lax.ppermute(p, "head", ring) for p in pieces]
        acc = project(acc, arrived, functools.partial(place, turn, 0), shards, map_rows)
        held = arrived = later
    acc = project(acc, held[:-1], functools.partial(place, last, 0), shards, map_rows)
    depth = held[-1].shape[1]
    last_maps, targets, mask = prepare(
        functools.partial(place, last, features - depth),
        depth,
        shards,
        map_rows,
        tgt_rows,
        near_targets,
        [marks, *near_marks],
    )
    memory, *shares = cross_near(acc, held[-1], last_maps, targets, mask, 1 + len(links))
    combined = [cross_own(memory, targets, mask, 1 + len(links))]
    for i, (pairs, piece) in enumerate(zip(links, shares)):
        other = lax.ppermute(piece, "ctx", [(target, source) for source, target in pairs])
        if n_ctx > 2:
            end = n_ctx - 1 if i == 0 else 0
            column = lax.broadcasted_iota(jnp.int32, other.shape, 1)
            other = jnp.where((lax.axis_index("ctx") == end) & (column >= width), NEG_FILL, other)
        combined.append(other)
    return call(combine_kernel, "combine", [((tgt_rows, width), BF16)], combined, limit=4 << 20)[0]


def solution(mesh):
    in_specs = (
        P(("dp", "ctx"), "head"),
        P(("dp", "ctx"), "head"),
        P(("dp", "ctx"), "head"),
        P(("dp", "ctx")),
        P("ctx", "head"),
        P("ctx", "head"),
        P(("dp", "ctx"), "head"),
    )
    out_specs = P(("dp", "ctx"), "head")
    return jax.shard_map(
        on_device, mesh=mesh, in_specs=in_specs, out_specs=out_specs, check_vma=False
    )
```

```python
import functools

import jax
import jax.numpy as jnp
from jax import lax
from jax.experimental import pallas as pl
from jax.experimental.pallas import tpu as pltpu
from jax.sharding import PartitionSpec as P

HEAD_DIM = 256
NEG_FILL = -1e30
F32 = jnp.float32
BF16 = jnp.bfloat16
LANES = 128
SCALE = HEAD_DIM**-0.5
WEIGH_FLOPS = 6 * 10**9
SPLIT_FLOPS = 15 * 10**9
VMEM = pl.BlockSpec(memory_space=pltpu.VMEM)
HBM = pl.BlockSpec(memory_space=pltpu.HBM)


def ring_order(count):
    return list(range(0, count, 2)) + list(range(1, count, 2))[::-1]


def links_of(count):
    if count == 2:
        return [[(0, 1), (1, 0)]]
    return [[(i, i + 1) for i in range(count - 1)], [(i + 1, i) for i in range(count - 1)]]


def dot_t(a, b):
    return lax.dot_general(a, b, (((1,), (1,)), ((), ())), preferred_element_type=F32)


def dot(a, b):
    return jnp.dot(a, b, preferred_element_type=F32)


def head_columns(h):
    return slice(h * HEAD_DIM, (h + 1) * HEAD_DIM)


def down_lanes(row):
    return jnp.transpose(jnp.broadcast_to(row, (LANES, row.shape[1])))


def same_mark(down, row):
    return jnp.concatenate([down == row[:, i : i + LANES] for i in range(0, row.shape[1], LANES)], axis=1)


def softmax_block(scores, same):
    scores = jnp.where(same, scores * SCALE, NEG_FILL)
    top = jnp.max(scores, axis=1, keepdims=True)
    weights = jnp.exp(scores - top)
    return top, weights, jnp.sum(weights, axis=1, keepdims=True)


def call(kernel, name, outs, operands, flops=0, exps=0, specs=None, scratch=(), limit=8 << 20):
    out_shape = [jax.ShapeDtypeStruct(*o) for o in outs]
    moved = sum(x.size * x.dtype.itemsize for x in [*operands, *out_shape])
    return pl.pallas_call(
        kernel,
        in_specs=specs or [VMEM] * len(operands),
        out_specs=[VMEM] * len(outs),
        out_shape=out_shape,
        scratch_shapes=list(scratch),
        compiler_params=pltpu.CompilerParams(vmem_limit_bytes=limit),
        cost_estimate=pl.CostEstimate(flops=flops, bytes_accessed=moved, transcendentals=exps),
        name=name,
    )(*operands)


def run_all(copies):
    for copy in copies:
        copy.start()
    for copy in copies:
        copy.wait()


def fetch_kernel(count, *refs):
    sources, targets, sems = refs[:count], refs[count : 2 * count], refs[-1]
    run_all([pltpu.make_async_copy(s, t, sems.at[i]) for i, (s, t) in enumerate(zip(sources, targets))])


def fetch(*arrays):
    return call(
        functools.partial(fetch_kernel, len(arrays)),
        "fetch",
        [(x.shape, x.dtype) for x in arrays],
        [pltpu.with_memory_space_constraint(x, pltpu.HBM) for x in arrays],
        specs=[HBM] * len(arrays),
        scratch=[pltpu.SemaphoreType.DMA((len(arrays),))],
    )


def pack_kernel(*refs):
    sources, out_ref, sems = refs[:-2], refs[-2], refs[-1]
    copies, row = [], 0
    for i, source in enumerate(sources):
        rows = source.shape[0]
        copies.append(pltpu.make_async_copy(source, out_ref.at[pl.ds(row, rows), :], sems.at[i]))
        row += rows
    run_all(copies)


def pack(*arrays):
    rows = sum(x.shape[0] for x in arrays)
    return call(
        pack_kernel,
        "pack",
        [((rows, arrays[0].shape[1]), arrays[0].dtype)],
        [pltpu.with_memory_space_constraint(x, pltpu.HBM) for x in arrays],
        specs=[HBM] * len(arrays),
        scratch=[pltpu.SemaphoreType.DMA((len(arrays),))],
    )[0]


def weigh_kernel(blocks, first, heads, *refs):
    marks, q_ref, keys = refs[:blocks], refs[blocks], refs[blocks + 1 : 2 * blocks + 1]
    weight_ref, total_ref = refs[2 * blocks + 1 :]
    down = down_lanes(marks[0][...])
    same = jnp.concatenate([same_mark(down, m[...]) for m in marks], axis=1)
    span = same.shape[1]
    lane = lax.broadcasted_iota(jnp.int32, total_ref.shape, 1)
    totals = jnp.zeros(total_ref.shape, F32)
    results = []
    for h in range(heads):
        at = head_columns(first + h)
        scores = jnp.concatenate([dot_t(q_ref[:, at], k[:, at]) for k in keys], axis=1)
        _, weights, total = softmax_block(scores, same)
        results.append(weights.astype(BF16))
        totals = jnp.where(lane == h, 1.0 / total, totals)
    for h in range(heads):
        weight_ref[:, h * span : (h + 1) * span] = results[h]
    total_ref[...] = totals


def weigh(query, keys, marks, first, heads):
    rows, span = query.shape[0], query.shape[0] * len(keys)
    return call(
        functools.partial(weigh_kernel, len(keys), first, heads),
        "weigh",
        [((rows, heads * span), BF16), ((rows, LANES), F32)],
        [*marks, query, *keys],
        flops=WEIGH_FLOPS,
        exps=rows * span * heads,
    )


def mix_kernel(skip, first, heads, weight_ref, total_ref, *refs):
    values, out_ref = refs[:-1], refs[-1]
    rows = total_ref.shape[0]
    results = []
    for h in range(heads):
        start = (skip + h) * rows * len(values)
        summed = sum(
            dot(weight_ref[:, start + i * rows : start + (i + 1) * rows], v[:, head_columns(first + h)])
            for i, v in enumerate(values)
        )
        results.append((summed * total_ref[:, skip + h : skip + h + 1]).astype(BF16))
    for h in range(heads):
        out_ref[:, head_columns(h)] = results[h]


def mix(weights, totals, values, skip, first, heads):
    rows = totals.shape[0]
    return call(
        functools.partial(mix_kernel, skip, first, heads),
        "mix",
        [((rows, heads * HEAD_DIM), BF16)],
        [weights, totals, *values],
        flops=2 * rows * rows * len(values) * heads * HEAD_DIM,
    )[0]


def in_shard(shards, shard, act):
    if len(shards) == 1:
        act(shards[0])
    else:
        for i, maps in enumerate(shards):
            pl.when(shard == i)(functools.partial(act, maps))


def split_kernel(source, *outs):
    width = outs[0].shape[1]
    for i, out in enumerate(outs):
        out[...] = source[:, i * width : (i + 1) * width]


def split(chunk, parts):
    rows, width = chunk.shape
    return call(split_kernel, "split", [((rows, width // parts), chunk.dtype)] * parts, [chunk], flops=SPLIT_FLOPS)


def project_kernel(chunks, shards, map_rows, has_acc, place, *refs):
    e_refs, maps, out_ref = refs[:chunks], refs[chunks : chunks + shards], refs[-1]
    half = out_ref.shape[1] // 2
    depth = e_refs[0].shape[1]
    shard, row = place()
    row = pl.multiple_of(row, depth)
    chunk = jnp.concatenate([r[...] for r in e_refs], axis=1)

    def add(map_ref):
        for side in range(2):
            columns = slice(side * half, (side + 1) * half)
            product = dot(chunk, map_ref[pl.ds(side * map_rows + row, chunk.shape[1]), :])
            out_ref[:, columns] = refs[-2][:, columns] + product if has_acc else product

    in_shard(maps, shard, add)


def project(acc, chunks, place, shards, map_rows):
    rows, width = chunks[0].shape[0], shards[0].shape[1]
    operands = [*chunks, *shards] + ([] if acc is None else [acc])
    return call(
        functools.partial(project_kernel, len(chunks), len(shards), map_rows, acc is not None, place),
        "project",
        [((rows, 2 * width), F32)],
        operands,
        flops=4 * width * sum(x.size for x in chunks),
    )[0]


def prepare_kernel(shards, parts, map_rows, step, place, *refs):
    maps, marks, near = refs[:shards], refs[shards : shards + parts], refs[shards + parts : -4]
    map_ref, tgt_ref, mask_ref, down_ref = refs[-4:]
    shard, row = place()
    depth, width = map_ref.shape[0], map_ref.shape[1] // 2
    row = pl.multiple_of(row, depth)

    def copy(source):
        for side in range(2):
            map_ref[:, side * width : (side + 1) * width] = source[pl.ds(side * map_rows + row, depth), :]

    in_shard(maps, shard, copy)
    own = marks[0][...]
    count = tgt_ref.shape[0] // parts
    below = slice(2 * map_rows, 2 * map_rows + count)
    targets = [maps[0][below, :]] + ([r[...] for r in near] if near else [m[below, :] for m in maps[1:]])
    for i, (target, mark_ref) in enumerate(zip(targets, marks)):
        part = slice(i * count, (i + 1) * count)
        tgt_ref[part, :] = target
        down_ref[...] = down_lanes(mark_ref[...])
        down = down_ref[pl.ds(0, count, stride=step), :]
        mask_ref[part, :] = same_mark(down, own).astype(F32)


def prepare(place, depth, shards, map_rows, count, near_targets, marks):
    rows, width = marks[0].shape[1], shards[0].shape[1]
    total = count * len(marks)
    return call(
        functools.partial(prepare_kernel, len(shards), len(marks), map_rows, rows // count, place),
        "prepare",
        [((depth, 2 * width), BF16), ((total, width), BF16), ((total, rows), F32)],
        [*shards, *marks, *near_targets],
        scratch=[pltpu.VMEM((rows, LANES), jnp.int32)],
    )


def attend_memory(queries, memory, same):
    heads = len(queries)
    scores = [dot_t(q, k) for q, k in zip(queries, memory[:heads])]
    tops, weights, totals = zip(*[softmax_block(x, same) for x in scores])
    summed = [dot(w.astype(BF16), v) for w, v in zip(weights, memory[heads:])]
    lane = lax.broadcasted_iota(jnp.int32, (same.shape[0], LANES), 1)
    stats = jnp.zeros(lane.shape, F32)
    for h in range(heads):
        stats = jnp.where(lane == h, tops[h], jnp.where(lane == heads + h, totals[h], stats))
    return jnp.concatenate([*summed, stats], axis=1)


def cross_near_kernel(acc_ref, e_ref, map_ref, tgt_ref, mask_ref, mem_ref, *outs):
    heads = map_ref.shape[1] // 2 // HEAD_DIM
    count = outs[0].shape[0]
    chunk = e_ref[...]
    parts = [slice((i + 1) * count, (i + 2) * count) for i in range(len(outs))]
    queries = [[tgt_ref[part, head_columns(h)] for h in range(heads)] for part in parts]
    same = [mask_ref[part, :] > 0 for part in parts]
    memory = []
    for h in range(2 * heads):
        at = head_columns(h)
        memory.append((acc_ref[:, at] + dot(chunk, map_ref[:, at])).astype(BF16))
    shares = [attend_memory(q, memory, m) for q, m in zip(queries, same)]
    for out_ref, share in zip(outs, shares):
        out_ref[...] = share
    for h in range(2 * heads):
        mem_ref[:, head_columns(h)] = memory[h]


def cross_near(acc, chunk, maps, targets, mask, parts):
    width = targets.shape[1]
    share = ((targets.shape[0] // parts, width + LANES), F32)
    return call(
        cross_near_kernel,
        "cross_near",
        [((acc.shape[0], 2 * width), BF16)] + [share] * (parts - 1),
        [acc, chunk, maps, targets, mask],
        flops=2 * chunk.size * 2 * width,
    )


def cross_own_kernel(mem_ref, tgt_ref, mask_ref, out_ref):
    heads = mem_ref.shape[1] // 2 // HEAD_DIM
    count = out_ref.shape[0]
    memory = [mem_ref[:, head_columns(h)] for h in range(2 * heads)]
    queries = [tgt_ref[:count, head_columns(h)] for h in range(heads)]
    out_ref[...] = attend_memory(queries, memory, mask_ref[:count, :] > 0)


def cross_own(memory, targets, mask, parts):
    count, width = targets.shape[0] // parts, targets.shape[1]
    return call(
        cross_own_kernel,
        "cross_own",
        [((count, width + LANES), F32)],
        [memory, targets, mask],
        flops=4 * count * width * memory.shape[0],
    )[0]


def combine_kernel(*refs):
    parts, out_ref = [r[...] for r in refs[:-1]], refs[-1]
    width = out_ref.shape[1]
    heads = width // HEAD_DIM
    results = []
    for h in range(heads):
        tops = [x[:, width + h : width + h + 1] for x in parts]
        totals = [x[:, width + heads + h : width + heads + h + 1] for x in parts]
        top = functools.reduce(jnp.maximum, tops)
        factors = [jnp.exp(t - top) for t in tops]
        share = 1.0 / sum(f * t for f, t in zip(factors, totals))
        results.append(sum((f * share) * x[:, head_columns(h)] for f, x in zip(factors, parts)))
    for h in range(heads):
        out_ref[:, head_columns(h)] = results[h].astype(BF16)


def on_device(enc_query, enc_key, enc_value, doc_ids, key_map, value_map, tgt_query):
    rows, features = enc_query.shape
    tgt_rows, width = tgt_query.shape
    n_ctx, n_head = lax.axis_size("ctx"), lax.axis_size("head")
    links = links_of(n_ctx)
    bring = lambda x: [lax.ppermute(x, "ctx", pairs) for pairs in links]

    marks = (doc_ids if n_ctx == 2 else doc_ids + 1).reshape(1, rows)
    keys, near_marks, values = bring(enc_key), bring(marks), bring(enc_value)
    query, own_key, own_value, marks = fetch(enc_query, enc_key, enc_value, marks)
    chunks = 2
    heads = features // HEAD_DIM // chunks
    held = []
    for j in range(chunks):
        weights, totals = weigh(query, [own_key, *keys], [marks, *near_marks], j * heads, heads)
        size = 1
        for skip in range(0, heads, size):
            held.append(mix(weights, totals, [own_value, *values], skip, j * heads + skip, size))

    order = ring_order(n_head)
    ring = [(order[i], order[(i + 1) % n_head]) for i in range(n_head)]
    before = {target: source for source, target in ring}

    sent, held = held, [lax.ppermute(h, "head", ring) for h in held]
    key_map, value_map, tgt_query, arrived = lax.optimization_barrier((key_map, value_map, tgt_query, held[0]))
    near_targets = []
    if n_ctx == 2:
        own_maps = pack(key_map, value_map, tgt_query)
        shards = [own_maps, *bring(own_maps)]
    else:
        whole = [lax.all_gather(x, "ctx", axis=0, tiled=True) for x in (key_map, value_map)]
        shards, near_targets = [pack(*whole, tgt_query)], bring(tgt_query)
    map_rows = (shards[0].shape[0] - tgt_rows) // 2

    def place(turn, first):
        head, ctx = lax.axis_index("head"), lax.axis_index("ctx")
        owner = 0
        for i in range(n_head):
            source = i
            for _ in range(turn):
                source = before[source]
            owner = owner + jnp.where(head == i, source, 0)
        row = owner * features + first
        if len(shards) == 1:
            return None, row
        return jnp.where(lax.div(row, map_rows) == ctx, 0, 1), lax.rem(row, map_rows)

    last = n_head - 1
    acc = project(None, sent, functools.partial(place, 0, 0), shards, map_rows)
    arrived = [arrived, *held[1:]]
    for turn in range(1, last):
        pieces = [p for h in held[:-1] for p in split(h, 1)] + list(split(held[-1], 2 if turn == last - 1 else 1))
        later = [lax.ppermute(p, "head", ring) for p in pieces]
        acc = project(acc, arrived, functools.partial(place, turn, 0), shards, map_rows)
        held = arrived = later
    depth = held[-1].shape[1]
    acc = project(acc, held[:-2], functools.partial(place, last, 0), shards, map_rows)
    near_last = functools.partial(place, last, features - depth - held[-2].shape[1])
    acc = project(acc, held[-2:-1], near_last, shards, map_rows)
    last_maps, targets, mask = prepare(
        functools.partial(place, last, features - depth),
        depth,
        shards,
        map_rows,
        tgt_rows,
        near_targets,
        [marks, *near_marks],
    )
    memory, *shares = cross_near(acc, held[-1], last_maps, targets, mask, 1 + len(links))
    combined = [cross_own(memory, targets, mask, 1 + len(links))]
    for i, (pairs, piece) in enumerate(zip(links, shares)):
        other = lax.ppermute(piece, "ctx", [(target, source) for source, target in pairs])
        if n_ctx > 2:
            end = n_ctx - 1 if i == 0 else 0
            column = lax.broadcasted_iota(jnp.int32, other.shape, 1)
            other = jnp.where((lax.axis_index("ctx") == end) & (column >= width), NEG_FILL, other)
        combined.append(other)
    return call(combine_kernel, "combine", [((tgt_rows, width), BF16)], combined, limit=4 << 20)[0]


def solution(mesh):
    in_specs = (
        P(("dp", "ctx"), "head"),
        P(("dp", "ctx"), "head"),
        P(("dp", "ctx"), "head"),
        P(("dp", "ctx")),
        P("ctx", "head"),
        P("ctx", "head"),
        P(("dp", "ctx"), "head"),
    )
    out_specs = P(("dp", "ctx"), "head")
    return jax.shard_map(
        on_device, mesh=mesh, in_specs=in_specs, out_specs=out_specs, check_vma=False
    )
```

```python
import functools

import jax
import jax.numpy as jnp
from jax import lax
from jax.experimental import pallas as pl
from jax.experimental.pallas import tpu as pltpu
from jax.sharding import PartitionSpec as P

HEAD_DIM = 256
NEG_FILL = -1e30
F32 = jnp.float32
BF16 = jnp.bfloat16
LANES = 128
SCALE = HEAD_DIM**-0.5
WEIGH_FLOPS = 6 * 10**9
SPLIT_FLOPS = 15 * 10**9
VMEM = pl.BlockSpec(memory_space=pltpu.VMEM)
HBM = pl.BlockSpec(memory_space=pltpu.HBM)


def ring_order(count):
    return list(range(0, count, 2)) + list(range(1, count, 2))[::-1]


def links_of(count):
    if count == 2:
        return [[(0, 1), (1, 0)]]
    return [[(i, i + 1) for i in range(count - 1)], [(i + 1, i) for i in range(count - 1)]]


def dot_t(a, b):
    return lax.dot_general(a, b, (((1,), (1,)), ((), ())), preferred_element_type=F32)


def dot(a, b):
    return jnp.dot(a, b, preferred_element_type=F32)


def head_columns(h):
    return slice(h * HEAD_DIM, (h + 1) * HEAD_DIM)


def down_lanes(row):
    return jnp.transpose(jnp.broadcast_to(row, (LANES, row.shape[1])))


def same_mark(down, row):
    return jnp.concatenate([down == row[:, i : i + LANES] for i in range(0, row.shape[1], LANES)], axis=1)


def softmax_block(scores, same):
    scores = jnp.where(same, scores, NEG_FILL)
    top = jnp.max(scores, axis=1, keepdims=True)
    weights = jnp.exp(scores - top)
    return top, weights, jnp.sum(weights, axis=1, keepdims=True)


def call(kernel, name, outs, operands, flops=0, exps=0, specs=None, scratch=(), limit=8 << 20):
    out_shape = [jax.ShapeDtypeStruct(*o) for o in outs]
    moved = sum(x.size * x.dtype.itemsize for x in [*operands, *out_shape])
    return pl.pallas_call(
        kernel,
        in_specs=specs or [VMEM] * len(operands),
        out_specs=[VMEM] * len(outs),
        out_shape=out_shape,
        scratch_shapes=list(scratch),
        compiler_params=pltpu.CompilerParams(vmem_limit_bytes=limit),
        cost_estimate=pl.CostEstimate(flops=flops, bytes_accessed=moved, transcendentals=exps),
        name=name,
    )(*operands)


def run_all(copies):
    for copy in copies:
        copy.start()
    for copy in copies:
        copy.wait()


def fetch_kernel(count, *refs):
    sources, targets, sems = refs[:count], refs[count : 2 * count], refs[-1]
    run_all([pltpu.make_async_copy(s, t, sems.at[i]) for i, (s, t) in enumerate(zip(sources, targets))])


def fetch(*arrays):
    return call(
        functools.partial(fetch_kernel, len(arrays)),
        "fetch",
        [(x.shape, x.dtype) for x in arrays],
        [pltpu.with_memory_space_constraint(x, pltpu.HBM) for x in arrays],
        specs=[HBM] * len(arrays),
        scratch=[pltpu.SemaphoreType.DMA((len(arrays),))],
    )


def pack_kernel(*refs):
    sources, out_ref, sems = refs[:-2], refs[-2], refs[-1]
    copies, row = [], 0
    for i, source in enumerate(sources):
        rows = source.shape[0]
        copies.append(pltpu.make_async_copy(source, out_ref.at[pl.ds(row, rows), :], sems.at[i]))
        row += rows
    run_all(copies)


def pack(*arrays):
    rows = sum(x.shape[0] for x in arrays)
    return call(
        pack_kernel,
        "pack",
        [((rows, arrays[0].shape[1]), arrays[0].dtype)],
        [pltpu.with_memory_space_constraint(x, pltpu.HBM) for x in arrays],
        specs=[HBM] * len(arrays),
        scratch=[pltpu.SemaphoreType.DMA((len(arrays),))],
    )[0]


def weigh_kernel(blocks, first, heads, *refs):
    marks, q_ref, keys = refs[:blocks], refs[blocks], refs[blocks + 1 : 2 * blocks + 1]
    weight_ref, total_ref = refs[2 * blocks + 1 :]
    down = down_lanes(marks[0][...])
    same = jnp.concatenate([same_mark(down, m[...]) for m in marks], axis=1)
    span = same.shape[1]
    lane = lax.broadcasted_iota(jnp.int32, total_ref.shape, 1)
    totals = jnp.zeros(total_ref.shape, F32)
    results = []
    for h in range(heads):
        at = head_columns(first + h)
        scores = jnp.concatenate([dot_t(q_ref[:, at], k[:, at]) for k in keys], axis=1)
        _, weights, total = softmax_block(scores * SCALE, same)
        results.append(weights.astype(BF16))
        totals = jnp.where(lane == h, 1.0 / total, totals)
    for h in range(heads):
        weight_ref[:, h * span : (h + 1) * span] = results[h]
    total_ref[...] = totals


def weigh(query, keys, marks, first, heads):
    rows, span = query.shape[0], query.shape[0] * len(keys)
    return call(
        functools.partial(weigh_kernel, len(keys), first, heads),
        "weigh",
        [((rows, heads * span), BF16), ((rows, LANES), F32)],
        [*marks, query, *keys],
        flops=WEIGH_FLOPS,
        exps=rows * span * heads,
    )


def mix_kernel(skip, first, heads, weight_ref, total_ref, *refs):
    values, out_ref = refs[:-1], refs[-1]
    rows = total_ref.shape[0]
    results = []
    for h in range(heads):
        start = (skip + h) * rows * len(values)
        summed = sum(
            dot(weight_ref[:, start + i * rows : start + (i + 1) * rows], v[:, head_columns(first + h)])
            for i, v in enumerate(values)
        )
        results.append((summed * total_ref[:, skip + h : skip + h + 1]).astype(BF16))
    for h in range(heads):
        out_ref[:, head_columns(h)] = results[h]


def mix(weights, totals, values, skip, first, heads):
    rows = totals.shape[0]
    return call(
        functools.partial(mix_kernel, skip, first, heads),
        "mix",
        [((rows, heads * HEAD_DIM), BF16)],
        [weights, totals, *values],
        flops=2 * rows * rows * len(values) * heads * HEAD_DIM,
    )[0]


def in_shard(shards, shard, act):
    if len(shards) == 1:
        act(shards[0])
    else:
        for i, maps in enumerate(shards):
            pl.when(shard == i)(functools.partial(act, maps))


def split_kernel(source, *outs):
    width = outs[0].shape[1]
    for i, out in enumerate(outs):
        out[...] = source[:, i * width : (i + 1) * width]


def split(chunk, parts):
    rows, width = chunk.shape
    return call(split_kernel, "split", [((rows, width // parts), chunk.dtype)] * parts, [chunk], flops=SPLIT_FLOPS)


def project_kernel(chunks, shards, map_rows, has_acc, place, *refs):
    e_refs, maps, out_ref = refs[:chunks], refs[chunks : chunks + shards], refs[-1]
    half = out_ref.shape[1] // 2
    depth = e_refs[0].shape[1]
    shard, row = place()
    row = pl.multiple_of(row, depth)
    chunk = jnp.concatenate([r[...] for r in e_refs], axis=1)

    def add(map_ref):
        for side in range(2):
            columns = slice(side * half, (side + 1) * half)
            product = dot(chunk, map_ref[pl.ds(side * map_rows + row, chunk.shape[1]), :])
            out_ref[:, columns] = refs[-2][:, columns] + product if has_acc else product

    in_shard(maps, shard, add)


def project(acc, chunks, place, shards, map_rows):
    rows, width = chunks[0].shape[0], shards[0].shape[1]
    operands = [*chunks, *shards] + ([] if acc is None else [acc])
    return call(
        functools.partial(project_kernel, len(chunks), len(shards), map_rows, acc is not None, place),
        "project",
        [((rows, 2 * width), F32)],
        operands,
        flops=4 * width * sum(x.size for x in chunks),
    )[0]


def prepare_kernel(shards, parts, map_rows, step, place, *refs):
    maps, marks, near = refs[:shards], refs[shards : shards + parts], refs[shards + parts : -4]
    map_ref, tgt_ref, mask_ref, down_ref = refs[-4:]
    shard, row = place()
    depth, width = map_ref.shape[0], map_ref.shape[1] // 2
    row = pl.multiple_of(row, depth)

    def copy(source):
        for side in range(2):
            map_ref[:, side * width : (side + 1) * width] = source[pl.ds(side * map_rows + row, depth), :]

    in_shard(maps, shard, copy)
    own = marks[0][...]
    count = tgt_ref.shape[0] // parts
    below = slice(2 * map_rows, 2 * map_rows + count)
    targets = [maps[0][below, :]] + ([r[...] for r in near] if near else [m[below, :] for m in maps[1:]])
    for i, (target, mark_ref) in enumerate(zip(targets, marks)):
        part = slice(i * count, (i + 1) * count)
        tgt_ref[part, :] = target * SCALE
        down_ref[...] = down_lanes(mark_ref[...])
        down = down_ref[pl.ds(0, count, stride=step), :]
        mask_ref[part, :] = same_mark(down, own).astype(F32)


def prepare(place, depth, shards, map_rows, count, near_targets, marks):
    rows, width = marks[0].shape[1], shards[0].shape[1]
    total = count * len(marks)
    return call(
        functools.partial(prepare_kernel, len(shards), len(marks), map_rows, rows // count, place),
        "prepare",
        [((depth, 2 * width), BF16), ((total, width), BF16), ((total, rows), F32)],
        [*shards, *marks, *near_targets],
        scratch=[pltpu.VMEM((rows, LANES), jnp.int32)],
    )


def attend_memory(queries, memory, same):
    heads = len(queries)
    scores = [dot_t(q, k) for q, k in zip(queries, memory[:heads])]
    tops, weights, totals = zip(*[softmax_block(x, same) for x in scores])
    summed = [dot(w.astype(BF16), v) for w, v in zip(weights, memory[heads:])]
    lane = lax.broadcasted_iota(jnp.int32, (same.shape[0], LANES), 1)
    stats = jnp.zeros(lane.shape, F32)
    for h in range(heads):
        stats = jnp.where(lane == h, tops[h], jnp.where(lane == heads + h, totals[h], stats))
    return jnp.concatenate([*summed, stats], axis=1)


def cross_near_kernel(acc_ref, e_ref, map_ref, tgt_ref, mask_ref, mem_ref, *outs):
    heads = map_ref.shape[1] // 2 // HEAD_DIM
    count = outs[0].shape[0]
    chunk = e_ref[...]
    parts = [slice((i + 1) * count, (i + 2) * count) for i in range(len(outs))]
    queries = [[tgt_ref[part, head_columns(h)] for h in range(heads)] for part in parts]
    same = [mask_ref[part, :] > 0 for part in parts]
    memory = []
    for h in range(2 * heads):
        at = head_columns(h)
        memory.append((acc_ref[:, at] + dot(chunk, map_ref[:, at])).astype(BF16))
    shares = [attend_memory(q, memory, m) for q, m in zip(queries, same)]
    for out_ref, share in zip(outs, shares):
        out_ref[...] = share
    for h in range(2 * heads):
        mem_ref[:, head_columns(h)] = memory[h]


def cross_near(acc, chunk, maps, targets, mask, parts):
    width = targets.shape[1]
    share = ((targets.shape[0] // parts, width + LANES), F32)
    return call(
        cross_near_kernel,
        "cross_near",
        [((acc.shape[0], 2 * width), BF16)] + [share] * (parts - 1),
        [acc, chunk, maps, targets, mask],
        flops=2 * chunk.size * 2 * width,
    )


def cross_own_kernel(mem_ref, tgt_ref, mask_ref, out_ref):
    heads = mem_ref.shape[1] // 2 // HEAD_DIM
    count = out_ref.shape[0]
    memory = [mem_ref[:, head_columns(h)] for h in range(2 * heads)]
    queries = [tgt_ref[:count, head_columns(h)] for h in range(heads)]
    out_ref[...] = attend_memory(queries, memory, mask_ref[:count, :] > 0)


def cross_own(memory, targets, mask, parts):
    count, width = targets.shape[0] // parts, targets.shape[1]
    return call(
        cross_own_kernel,
        "cross_own",
        [((count, width + LANES), F32)],
        [memory, targets, mask],
        flops=4 * count * width * memory.shape[0],
    )[0]


def combine_kernel(*refs):
    parts, out_ref = [r[...] for r in refs[:-1]], refs[-1]
    width = out_ref.shape[1]
    heads = width // HEAD_DIM
    results = []
    for h in range(heads):
        tops = [x[:, width + h : width + h + 1] for x in parts]
        totals = [x[:, width + heads + h : width + heads + h + 1] for x in parts]
        top = functools.reduce(jnp.maximum, tops)
        factors = [jnp.exp(t - top) for t in tops]
        share = 1.0 / sum(f * t for f, t in zip(factors, totals))
        results.append(sum((f * share) * x[:, head_columns(h)] for f, x in zip(factors, parts)))
    for h in range(heads):
        out_ref[:, head_columns(h)] = results[h].astype(BF16)


def on_device(enc_query, enc_key, enc_value, doc_ids, key_map, value_map, tgt_query):
    rows, features = enc_query.shape
    tgt_rows, width = tgt_query.shape
    n_ctx, n_head = lax.axis_size("ctx"), lax.axis_size("head")
    links = links_of(n_ctx)
    bring = lambda x: [lax.ppermute(x, "ctx", pairs) for pairs in links]

    marks = (doc_ids if n_ctx == 2 else doc_ids + 1).reshape(1, rows)
    keys, near_marks, values = bring(enc_key), bring(marks), bring(enc_value)
    query, own_key, own_value, marks = fetch(enc_query, enc_key, enc_value, marks)
    chunks = 2
    heads = features // HEAD_DIM // chunks
    held = []
    for j in range(chunks):
        weights, totals = weigh(query, [own_key, *keys], [marks, *near_marks], j * heads, heads)
        size = 1
        for skip in range(0, heads, size):
            held.append(mix(weights, totals, [own_value, *values], skip, j * heads + skip, size))

    order = ring_order(n_head)
    ring = [(order[i], order[(i + 1) % n_head]) for i in range(n_head)]
    before = {target: source for source, target in ring}

    sent, held = held, [lax.ppermute(h, "head", ring) for h in held]
    key_map, value_map, tgt_query, arrived = lax.optimization_barrier((key_map, value_map, tgt_query, held[0]))
    near_targets = []
    if n_ctx == 2:
        own_maps = pack(key_map, value_map, tgt_query)
        shards = [own_maps, *bring(own_maps)]
    else:
        whole = [lax.all_gather(x, "ctx", axis=0, tiled=True) for x in (key_map, value_map)]
        shards, near_targets = [pack(*whole, tgt_query)], bring(tgt_query)
    map_rows = (shards[0].shape[0] - tgt_rows) // 2

    def place(turn, first):
        head, ctx = lax.axis_index("head"), lax.axis_index("ctx")
        owner = 0
        for i in range(n_head):
            source = i
            for _ in range(turn):
                source = before[source]
            owner = owner + jnp.where(head == i, source, 0)
        row = owner * features + first
        if len(shards) == 1:
            return None, row
        return jnp.where(lax.div(row, map_rows) == ctx, 0, 1), lax.rem(row, map_rows)

    last = n_head - 1
    acc = project(None, sent, functools.partial(place, 0, 0), shards, map_rows)
    arrived = [arrived, *held[1:]]
    for turn in range(1, last):
        pieces = [p for h in held for p in split(h, h.shape[1] // HEAD_DIM)]
        later = [lax.ppermute(p, "head", ring) for p in pieces]
        acc = project(acc, arrived, functools.partial(place, turn, 0), shards, map_rows)
        held = arrived = later
    acc = project(acc, held[:-1], functools.partial(place, last, 0), shards, map_rows)
    depth = held[-1].shape[1]
    last_maps, targets, mask = prepare(
        functools.partial(place, last, features - depth),
        depth,
        shards,
        map_rows,
        tgt_rows,
        near_targets,
        [marks, *near_marks],
    )
    memory, *shares = cross_near(acc, held[-1], last_maps, targets, mask, 1 + len(links))
    combined = [cross_own(memory, targets, mask, 1 + len(links))]
    for i, (pairs, piece) in enumerate(zip(links, shares)):
        other = lax.ppermute(piece, "ctx", [(target, source) for source, target in pairs])
        if n_ctx > 2:
            end = n_ctx - 1 if i == 0 else 0
            column = lax.broadcasted_iota(jnp.int32, other.shape, 1)
            other = jnp.where((lax.axis_index("ctx") == end) & (column >= width), NEG_FILL, other)
        combined.append(other)
    return call(combine_kernel, "combine", [((tgt_rows, width), BF16)], combined, limit=4 << 20)[0]


def solution(mesh):
    in_specs = (
        P(("dp", "ctx"), "head"),
        P(("dp", "ctx"), "head"),
        P(("dp", "ctx"), "head"),
        P(("dp", "ctx")),
        P("ctx", "head"),
        P("ctx", "head"),
        P(("dp", "ctx"), "head"),
    )
    out_specs = P(("dp", "ctx"), "head")
    return jax.shard_map(
        on_device, mesh=mesh, in_specs=in_specs, out_specs=out_specs, check_vma=False
    )
```
